128 devices in a mesh: roll: 8 (over y, core), frame: 16 (over z, x).
Axes of the slice: x: 4, y: 4, z: 4, core: 2. Of those that a mesh axis runs over, the one named last changes fastest.
Arguments:
- patch_activation_tensor: bfloat16 [8, 16, 576, 2048], P('roll', 'frame'), may hold values from -900 to 900
- conditioning_affine: float32 [8, 16, 2, 2048], P('roll', 'frame'), may hold values from -3 to 3
- entry_projection_matrix: bfloat16 [2048, 3072], replicated, may hold values from -0.125 to 0.125
- exit_projection_matrix: bfloat16 [1024, 2048], replicated, may hold values from -0.1875 to 0.1875
- softmax_sharpness: float32 [2, 4], replicated, may hold values from 15 to 45
- cached_past_pairs: bfloat16 [64, 576, 2, 512], P('roll', 'frame'), may hold values from -6 to 6
- recalled_picture_holder: int32 [8, 16, 6, 1], P('roll', 'frame'), may hold values from 0 to 7; in each aligned block of 6 rows (0 to 5, 6 to 11, ..., all dimensions but the last counted through in order) at most 2 rows name the same one
- recalled_picture_position: int32 [8, 16, 6], P('roll', 'frame'), may hold values from 0 to 7
- lookback_lengths: int32 [8], P('roll'), may hold values from 2 to 16, as said below
Outputs:
- attended: bfloat16 [8, 16, 576, 2048], P('roll', 'frame')
The draws below stay inside these ranges and needn't reach their ends.
Inputs may be any that keep to these rules, and one draw needn't show every extreme that they name: `recalled_picture_holder`: among the 6 retrievals of one frame no owner appears more than 2 times, and some frames name one owner exactly 2 times. `lookback_lengths`: some rollout has context 16 and some has 2.
All inputs are finite; a program needn't handle non-finite values.
Results may differ from the reference program's by a relative error of at most 0.011.
Values may be sent and summed in bfloat16 or wider, within the bound.
No kernel may reach another device: no remote copies, remote signals or barrier semaphores. Data moves between devices by JAX's collectives and lax.ppermute only.
A program may use at most 192 MiB of HBM per device.

```python
import math
import jax
import jax.numpy as jnp
import numpy as np
from jax import lax

D = 2048
PLANAR_GROUPS = 4
ATTN_CHANNELS = 128
P_SIZE = 576
TOPM = 6
CAP = 2
HIST_DEV = 8
ROLLS = 8
FRAMES = 16
HIST = 64
N_ROLL = 8


def draw_patch_activation_tensor(key, part):
    key = jax.random.fold_in(key, 11)
    base_key, row_key, column_key = jax.random.split(key, 3)
    shape = (ROLLS, FRAMES, P_SIZE, D)
    base = jnp.clip(jax.random.normal(base_key, shape, jnp.float32), -4.0, 4.0)
    spread = math.log(10.0)
    row_scale = jnp.exp(jax.random.uniform(row_key, (ROLLS, FRAMES, P_SIZE, 1), jnp.float32, 0.0, spread))
    column_scale = jnp.exp(jax.random.uniform(column_key, (1, 1, 1, D), jnp.float32, 0.0, spread))
    return (base * row_scale * column_scale).astype(jnp.bfloat16)


def draw_lookback_lengths(key, part):
    key = jax.random.fold_in(key, 23)
    value_key, order_key = jax.random.split(key, 2)
    lengths = jax.random.randint(value_key, (ROLLS,), 2, FRAMES + 1, jnp.int32)
    order = jax.random.permutation(order_key, ROLLS)
    lengths = lengths.at[order[0]].set(FRAMES)
    lengths = lengths.at[order[1]].set(2)
    return lengths.astype(jnp.int32)


def plant(values, key, smallest, high):
    index_at = [jax.random.randint(jax.random.fold_in(key, axis), (), 0, length) for axis, length in enumerate(values.shape)]
    widest = values.shape.index(max(values.shape))
    neighbour = index_at[:widest] + [(index_at[widest] + 1) % values.shape[widest]] + index_at[widest + 1:]
    return values.at[tuple(index_at)].set(smallest).at[tuple(neighbour)].set(high)


def block_levels(key, shape, cuts, low, largest):
    loudness, own = 1.0, jax.random.fold_in(key, 6)
    for axis_at, shards_of in cuts:
        draws = jnp.exp(jax.random.uniform(jax.random.fold_in(own, axis_at), (shards_of,), jnp.float32, low / len(cuts), largest / len(cuts)))
        loudness = loudness * jnp.repeat(draws, shape[axis_at] // shards_of).reshape([-1 if axis == axis_at else 1 for axis in range(len(shape))])
    return loudness


def deal_out(key, own, number, rows, amount, top, limit, slope):
    sequence = jax.random.permutation(key, amount)
    packed, usual = portions_of(amount, rows * top, limit, slope, True), portions_of(amount, rows * top, limit, slope, False)
    places = jnp.arange(amount)

    def named(sizes, offset_by):
        used = int((sizes > 0).sum())
        fixed = max(1, used // 4)
        moved = fixed + (places - fixed + offset_by * (used - fixed)) % max(1, amount - fixed)
        return jnp.zeros((amount,), jnp.int32).at[sequence[jnp.where(places < fixed, places, moved)]].set(jnp.asarray(sizes, jnp.int32))

    sizes = jnp.where(number % 4 == 0, named(packed, number // 4), named(usual, number - number // 4 - 1))
    mixed = jax.random.permutation(jax.random.fold_in(own, 3), amount)
    source_of, receiver = mixed[0:amount // 2 * 2:2], mixed[1:amount // 2 * 2:2]
    margin = jnp.minimum(sizes[source_of] - 1, limit - sizes[receiver]) // 2
    margin = jnp.where((source_of == sequence[0]) | (receiver == sequence[0]) | (sizes[receiver] == 0), 0, jnp.maximum(margin, 0))
    moved = jax.random.randint(jax.random.fold_in(own, 4), (amount // 2,), 0, 1 << 20) % (margin + 1)
    sizes = sizes.at[source_of].add(-moved).at[receiver].add(moved)
    members = jnp.searchsorted(jnp.cumsum(sizes), jnp.arange(rows * top), side="right").astype(jnp.int32)
    grid = members.reshape(top, rows).T
    grid = grid[jax.random.permutation(jax.random.fold_in(own, 1), rows)]
    offset_by = jax.random.randint(jax.random.fold_in(own, 2), (rows, 1), 0, top)
    return jnp.take_along_axis(grid, (jnp.arange(top)[None, :] + offset_by) % top, axis=1)


def portions_of(amount, total, limit, slope, full):
    weights = [(1 << 20) // math.isqrt(standing ** slope) + 1 for standing in range(1, amount + 1)]
    largest = limit if full else min(limit, max(-(-total // amount), total * weights[0] // sum(weights)))
    least = 1 if total - largest >= amount - 1 else 0
    holding, spare = [largest] + [least] * (amount - 1), total - largest - least * (amount - 1)
    while spare > 0:
        candidates = [i for i in range(1, amount) if holding[i] < largest] or [i for i in range(1, amount) if holding[i] < limit]
        mass, left = sum([weights[i] for i in candidates]), spare
        for i in candidates:
            more = min(limit - holding[i], max(1, left * weights[i] // mass), spare)
            holding[i] = holding[i] + more
            spare = spare - more
    return np.array(holding)


def gaussian(own_key, shape, width, limit, cuts=(), kind=jnp.bfloat16):
    level = block_levels(own_key, shape, cuts, -0.22, 0.18) if cuts else 1.0
    array = jax.random.normal(own_key, shape, jnp.float32) * width * level
    return jnp.minimum(jnp.maximum(array, -limit), limit).astype(kind)


def setup_inputs(seed: int = 0) -> dict:
    key_of = jax.random.split(jax.random.key(seed), 10)
    patch_activation_tensor = draw_patch_activation_tensor(jax.random.fold_in(key_of[9], 71), 0)
    conditioning_affine = gaussian(key_of[1], (ROLLS, FRAMES, 2, D), 0.5, 3.0, ((0, 8), (1, 16)), jnp.float32)
    entry_projection_matrix = gaussian(key_of[2], (D, 6 * PLANAR_GROUPS * ATTN_CHANNELS), D ** -0.5, 0.125)
    exit_projection_matrix = gaussian(key_of[3], (2 * PLANAR_GROUPS * ATTN_CHANNELS, D), (2 * PLANAR_GROUPS * ATTN_CHANNELS) ** -0.5, 0.1875)
    softmax_sharpness = jnp.clip(jnp.exp(jax.random.uniform(key_of[4], (2, PLANAR_GROUPS), jnp.float32, math.log(15.0), math.log(45.0))), 15.0, 45.0)
    cached_past_pairs = gaussian(key_of[5], (HIST, P_SIZE, 2, PLANAR_GROUPS * ATTN_CHANNELS), 1.0, 6.0, ((0, 8), (1, 16)))
    recalled_picture_holder_keys = jax.random.split(jax.random.fold_in(key_of[6], 1), ROLLS * FRAMES * TOPM // TOPM)
    recalled_picture_holder_turns = jax.random.permutation(jax.random.fold_in(key_of[6], 3), ROLLS * FRAMES * TOPM // TOPM)
    recalled_picture_holder = jax.vmap(lambda own, number: deal_out(jax.random.fold_in(key_of[6], 2), own, number, TOPM, N_ROLL, 1, CAP, 2))(recalled_picture_holder_keys, recalled_picture_holder_turns).reshape((ROLLS, FRAMES, TOPM, 1))
    recalled_picture_position = plant(jax.random.randint(key_of[7], (ROLLS, FRAMES, TOPM), 0, HIST_DEV), jax.random.fold_in(key_of[7], 1), 0, HIST_DEV - 1).astype(jnp.int32)
    lookback_lengths = draw_lookback_lengths(jax.random.fold_in(key_of[9], 71), 0)
    return {"patch_activation_tensor": patch_activation_tensor, "conditioning_affine": conditioning_affine, "entry_projection_matrix": entry_projection_matrix, "exit_projection_matrix": exit_projection_matrix, "softmax_sharpness": softmax_sharpness, "cached_past_pairs": cached_past_pairs, "recalled_picture_holder": recalled_picture_holder, "recalled_picture_position": recalled_picture_position, "lookback_lengths": lookback_lengths}


EPSILON = 1e-06

def normed(values):
    return values * lax.rsqrt(lax.optimization_barrier(jnp.mean(values * values, axis=-1, keepdims=True)) + EPSILON)

def reference(patch_activation_tensor, conditioning_affine, entry_projection_matrix, exit_projection_matrix, softmax_sharpness, cached_past_pairs, recalled_picture_holder, recalled_picture_position, lookback_lengths):
    roll_count = patch_activation_tensor.shape[0]
    frame_count = patch_activation_tensor.shape[1]
    head_width = PLANAR_GROUPS * ATTN_CHANNELS
    activation = patch_activation_tensor.astype(jnp.float32)
    hidden = (normed(activation) * (1.0 + conditioning_affine[:, :, 0:1, :]) + conditioning_affine[:, :, 1:2, :]).astype(jnp.bfloat16)
    planar_mapped_result = jnp.dot(hidden.reshape(-1, D), entry_projection_matrix, preferred_element_type=jnp.float32).astype(jnp.bfloat16)
    planar_mapped_result = planar_mapped_result.reshape(roll_count, frame_count, P_SIZE, 6, PLANAR_GROUPS, ATTN_CHANNELS)
    planar_score_factor = softmax_sharpness[0][:, None] / ATTN_CHANNELS
    chronal_score_factor = softmax_sharpness[1][:, None] / ATTN_CHANNELS
    planar_probe_vector = (normed(planar_mapped_result[:, :, :, 0].astype(jnp.float32)) * planar_score_factor).astype(jnp.bfloat16)
    space_key = normed(planar_mapped_result[:, :, :, 1].astype(jnp.float32)).astype(jnp.bfloat16)
    space_value = planar_mapped_result[:, :, :, 2]
    chronal_probe_vector = (normed(planar_mapped_result[:, :, :, 3].astype(jnp.float32)) * chronal_score_factor).astype(jnp.bfloat16)
    time_key = normed(planar_mapped_result[:, :, :, 4].astype(jnp.float32)).astype(jnp.bfloat16)
    time_value = planar_mapped_result[:, :, :, 5]
    memory_index = (recalled_picture_holder[..., 0] * HIST_DEV + recalled_picture_position).astype(jnp.int32)

    def spatial(operands):
        queries, own_keys, own_values, chosen = operands
        stored = cached_past_pairs[chosen]
        memory_key = normed(stored[:, :, 0, :].reshape(TOPM * P_SIZE, PLANAR_GROUPS, ATTN_CHANNELS).astype(jnp.float32)).astype(jnp.bfloat16)
        memory_value = stored[:, :, 1, :].reshape(TOPM * P_SIZE, PLANAR_GROUPS, ATTN_CHANNELS)
        key_rows = jnp.concatenate([own_keys, memory_key], axis=0)
        value_rows = jnp.concatenate([own_values, memory_value], axis=0)
        scores = jnp.einsum('qhd,khd->hqk', queries.astype(jnp.float32), key_rows.astype(jnp.float32))
        weights = jnp.exp(scores)
        shares = (weights / lax.optimization_barrier(jnp.sum(weights, axis=-1, keepdims=True))).astype(jnp.bfloat16)
        result = jnp.einsum('hqk,khd->qhd', shares.astype(jnp.float32), value_rows.astype(jnp.float32))
        return result.astype(jnp.bfloat16).reshape(P_SIZE, head_width)
    space_out = lax.map(spatial, (planar_probe_vector.reshape(-1, P_SIZE, PLANAR_GROUPS, ATTN_CHANNELS), space_key.reshape(-1, P_SIZE, PLANAR_GROUPS, ATTN_CHANNELS), space_value.reshape(-1, P_SIZE, PLANAR_GROUPS, ATTN_CHANNELS), memory_index.reshape(-1, TOPM)))
    space_out = space_out.reshape(roll_count, frame_count, P_SIZE, head_width)
    scores = jnp.einsum('rtphd,rsphd->rphts', chronal_probe_vector.astype(jnp.float32), time_key.astype(jnp.float32))
    target = jnp.arange(frame_count, dtype=jnp.int32)[:, None]
    source = jnp.arange(frame_count, dtype=jnp.int32)[None, :]
    window_mask = (source <= target)[None] & (source[None] > target[None] - lookback_lengths[:, None, None])
    weights = jnp.where(window_mask[:, None, None], jnp.exp(scores), 0.0)
    shares = (weights / lax.optimization_barrier(jnp.sum(weights, axis=-1, keepdims=True))).astype(jnp.bfloat16)
    time_out = jnp.einsum('rphts,rsphd->rtphd', shares.astype(jnp.float32), time_value.astype(jnp.float32))
    time_out = time_out.astype(jnp.bfloat16).reshape(roll_count, frame_count, P_SIZE, head_width)
    combined = jnp.concatenate([space_out, time_out], axis=-1).reshape(-1, 2 * head_width)
    attended = jnp.dot(combined, exit_projection_matrix, preferred_element_type=jnp.float32).astype(jnp.bfloat16)
    return attended.reshape(roll_count, frame_count, P_SIZE, D)
```

```python
import functools

import jax
import jax.numpy as jnp
from jax import lax
from jax.experimental import pallas as pl
from jax.experimental.pallas import tpu as pltpu
from jax.sharding import Mesh
from jax.sharding import PartitionSpec as P

G = 4
C = 128
HW = G * C
TOPM = 6
EPSILON = 1e-06
BF = jnp.bfloat16
F32 = jnp.float32
PAD = 16
VMEM_LIMIT = 50 * 1024 * 1024


def params(**more):
    return pltpu.CompilerParams(vmem_limit_bytes=VMEM_LIMIT, **more)


def inverse_rms(values):
    return lax.rsqrt(jnp.mean(values * values, axis=-1, keepdims=True) + EPSILON)


def dot(a, b):
    return jnp.dot(a, b, preferred_element_type=F32)


def dot_t(a, b):
    return lax.dot_general(a, b, (((1,), (1,)), ((), ())), preferred_element_type=F32)


def split_store_kernel(rows_ref, out_ref):
    for h in range(G):
        key = rows_ref[:, h * C : (h + 1) * C].astype(F32)
        out_ref[h, :, :C] = (key * inverse_rms(key)).astype(BF)
        out_ref[h, :, C:] = rows_ref[:, HW + h * C : HW + (h + 1) * C]


def split_store(rows):
    n = rows.shape[0]
    return pl.pallas_call(
        split_store_kernel,
        out_shape=jax.ShapeDtypeStruct((G, n, 2 * C), BF),
        compiler_params=params(),
        name="split_store",
        cost_estimate=pl.CostEstimate(
            flops=8 * n * HW, bytes_accessed=8 * n * HW, transcendentals=n * G
        ),
    )(rows)


def join_pieces_kernel(piece, in_ref, out_ref, wide_ref, joined_ref):
    pieces = in_ref.shape[0]
    wide_ref[...] = in_ref[...].astype(F32)
    for m in range(out_ref.shape[0]):
        for i in range(pieces):
            joined_ref[m, i * piece : (i + 1) * piece, :] = wide_ref[
                i, m * piece : (m + 1) * piece, :
            ]
    out_ref[...] = joined_ref[...].astype(BF)


def join_pieces(parts, frames):
    pieces, rows, width = parts.shape
    piece = rows // frames
    return pl.pallas_call(
        functools.partial(join_pieces_kernel, piece),
        out_shape=jax.ShapeDtypeStruct((frames, pieces * piece, width), BF),
        scratch_shapes=[
            pltpu.VMEM((pieces, rows, width), F32),
            pltpu.VMEM((frames, pieces * piece, width), F32),
        ],
        compiler_params=params(),
        name="join_pieces",
        cost_estimate=pl.CostEstimate(
            flops=0, bytes_accessed=4 * pieces * rows * width, transcendentals=0
        ),
    )(parts)


def modulate_kernel(act_ref, affine_ref, weight_ref, factor_ref, tail_ref, hidden_ref, query_ref):
    step = pl.program_id(0)
    rows = act_ref.shape[0]
    patches = query_ref.shape[1] - PAD
    act = act_ref[...].astype(F32)
    hidden = act * inverse_rms(act) * (1.0 + affine_ref[0:1, :]) + affine_ref[1:2, :]
    hidden = hidden.astype(BF)
    hidden_ref[...] = hidden
    mapped = dot(hidden, weight_ref[...]).astype(BF).astype(F32)
    for h in range(G):
        one = mapped[:, h * C : (h + 1) * C]
        query_ref[h, pl.ds(pl.multiple_of(step * rows, 16), rows), :] = (
            one * inverse_rms(one) * factor_ref[0, h]
        ).astype(BF)

    @pl.when(step == 0)
    def _():
        for h in range(G):
            query_ref[h, patches:, :] = tail_ref[...]


def modulate(act, affine, weight, factor, tail):
    patches, depth = act.shape
    steps = 2
    rows = patches // steps
    return pl.pallas_call(
        modulate_kernel,
        grid=(steps,),
        in_specs=[
            pl.BlockSpec((rows, depth), lambda i: (i, 0)),
            pl.BlockSpec((2, depth), lambda i: (0, 0)),
            pl.BlockSpec((depth, HW), lambda i: (0, 0)),
            pl.BlockSpec(memory_space=pltpu.SMEM),
            pl.BlockSpec((PAD, C), lambda i: (0, 0)),
        ],
        out_specs=[
            pl.BlockSpec((rows, depth), lambda i: (i, 0)),
            pl.BlockSpec((G, patches + PAD, C), lambda i: (0, 0, 0)),
        ],
        out_shape=[
            jax.ShapeDtypeStruct((patches, depth), BF),
            jax.ShapeDtypeStruct((G, patches + PAD, C), BF),
        ],
        compiler_params=params(),
        name="modulate",
        cost_estimate=pl.CostEstimate(
            flops=2 * patches * depth * HW,
            bytes_accessed=4 * patches * depth + 2 * depth * HW + 2 * patches * HW,
            transcendentals=patches,
        ),
    )(act, affine, weight, factor, tail)


def temporal_entry_kernel(quarters, hidden_ref, weight_ref, factor_ref, out_ref):
    part = pl.program_id(0)
    rows = hidden_ref.shape[0] // quarters
    mapped = dot(hidden_ref[...], weight_ref[...]).astype(BF).astype(F32)
    for h in range(G):
        one = mapped[:, h * C : (h + 1) * C]
        scale = jnp.where(part < 2, inverse_rms(one), 1.0)
        factor = jnp.where(part == 0, factor_ref[1, h], 1.0)
        done = (one * scale * factor).astype(BF)
        for z in range(quarters):
            out_ref[z, h, 0] = done[z * rows : (z + 1) * rows, :]


def temporal_entry(hidden, weight, factor, quarters):
    patches, depth = hidden.shape
    rows = patches // quarters
    return pl.pallas_call(
        functools.partial(temporal_entry_kernel, quarters),
        grid=(3,),
        in_specs=[
            pl.BlockSpec((patches, depth), lambda i: (0, 0)),
            pl.BlockSpec((depth, HW), lambda i: (0, 3 + i)),
            pl.BlockSpec(memory_space=pltpu.SMEM),
        ],
        out_specs=pl.BlockSpec((quarters, G, 1, rows, C), lambda i: (0, 0, i, 0, 0)),
        out_shape=jax.ShapeDtypeStruct((quarters, G, 3, rows, C), BF),
        compiler_params=params(),
        name="temporal_entry",
        cost_estimate=pl.CostEstimate(
            flops=6 * patches * depth * HW,
            bytes_accessed=2 * patches * depth + 6 * depth * HW + 6 * patches * HW,
            transcendentals=patches,
        ),
    )(hidden, weight, factor)


def temporal_attend_kernel(length_ref, in_ref, out_ref):
    frames, _, rows, _ = in_ref.shape
    group = 16
    size = frames * group
    length = length_ref[0]
    row = lax.broadcasted_iota(jnp.int32, (size, size), 0)
    column = lax.broadcasted_iota(jnp.int32, (size, size), 1)
    target, source = row // group, column // group
    keep = (row % group == column % group) & (source <= target) & (source > target - length)
    for g in range(rows // group):
        at = slice(g * group, (g + 1) * group)
        query = in_ref[:, 0, at, :].reshape(size, C)
        key = in_ref[:, 1, at, :].reshape(size, C)
        value = in_ref[:, 2, at, :].reshape(size, C)
        weights = jnp.where(keep, jnp.exp(dot_t(query, key)), 0.0)
        shares = weights / jnp.sum(weights, axis=-1, keepdims=True)
        result = dot(shares.astype(BF), value).astype(BF)
        out_ref[:, at, :] = result.reshape(frames, group, C)


def temporal_attend(length, parts):
    frames, _, rows, _ = parts.shape
    return pl.pallas_call(
        temporal_attend_kernel,
        in_specs=[
            pl.BlockSpec(memory_space=pltpu.SMEM),
            pl.BlockSpec(memory_space=pltpu.VMEM),
        ],
        out_shape=jax.ShapeDtypeStruct((frames, rows, C), BF),
        compiler_params=params(),
        name="temporal_attend",
        cost_estimate=pl.CostEstimate(
            flops=4 * frames * rows * 256 * C,
            bytes_accessed=8 * frames * rows * C,
            transcendentals=frames * rows * 256,
        ),
    )(length, parts)


def own_attend_kernel(hidden_ref, key_weight_ref, value_weight_ref, query_ref, out_ref):
    heads = query_ref.shape[0]
    patches = hidden_ref.shape[0]
    hidden = hidden_ref[...]
    keys = dot(hidden, key_weight_ref[...]).astype(BF).astype(F32)
    values = dot(hidden, value_weight_ref[...]).astype(BF)
    ones = jnp.ones((patches, C), BF)
    for h in range(heads):
        key = keys[:, h * C : (h + 1) * C]
        key = (key * inverse_rms(key)).astype(BF)
        both = jnp.concatenate([values[:, h * C : (h + 1) * C], ones], axis=1)
        weights = jnp.exp(dot_t(query_ref[h, :patches, :], key)).astype(BF)
        out_ref[h] = dot(weights, both)


def own_attend(hidden, weight, query):
    patches, depth = hidden.shape
    heads = 2
    wide = heads * C
    per = HW // wide
    return pl.pallas_call(
        own_attend_kernel,
        grid=(G // heads,),
        in_specs=[
            pl.BlockSpec((patches, depth), lambda i: (0, 0)),
            pl.BlockSpec((depth, wide), lambda i: (0, per + i)),
            pl.BlockSpec((depth, wide), lambda i: (0, 2 * per + i)),
            pl.BlockSpec((heads, patches + PAD, C), lambda i: (i, 0, 0)),
        ],
        out_specs=pl.BlockSpec((heads, patches, 2 * C), lambda i: (i, 0, 0)),
        out_shape=jax.ShapeDtypeStruct((G, patches, 2 * C), F32),
        compiler_params=params(),
        name="own_attend",
        cost_estimate=pl.CostEstimate(
            flops=4 * patches * depth * HW + 6 * patches * patches * HW,
            bytes_accessed=2 * patches * depth + 4 * depth * HW + 10 * patches * HW,
            transcendentals=G * patches * patches,
        ),
    )(hidden, weight, weight, query)


def memory_attend_kernel(index_ref, query_ref, *refs):
    stores, out_ref = refs[:TOPM], refs[TOPM]
    patches = query_ref.shape[1] - PAD
    keys = jnp.concatenate([ref[0, :, :C] for ref in stores], axis=0)
    values = jnp.concatenate([ref[0, :, C:] for ref in stores], axis=0)
    both = jnp.concatenate([values, jnp.ones(values.shape, BF)], axis=1)
    row = lax.broadcasted_iota(jnp.int32, (C, C), 0)
    column = lax.broadcasted_iota(jnp.int32, (C, C), 1)
    rows = []
    start = 0
    while start < patches:
        size = min(C, patches - start)
        weights = jnp.exp(dot_t(query_ref[0, start : start + size, :], keys)).astype(BF)
        result = dot(weights, both)
        out_ref[0, start : start + size, :] = result[:, :C].astype(BF)
        diagonal = jnp.where(row[:size] == column[:size], result[:, C:], 0.0)
        rows.append(jnp.sum(diagonal, axis=0, keepdims=True))
        start += size
    rows.append(jnp.zeros((8 - len(rows), C), F32))
    total = jnp.concatenate(rows, axis=0)
    high = total.astype(BF).astype(F32)
    out_ref[0, patches:, :] = jnp.concatenate([high, total - high], axis=0).astype(BF)


def memory_attend(index, query, store):
    frames, rows, _ = query.shape
    patches = rows - PAD
    quarter = store.shape[1]

    def place(j):
        return lambda i, index_ref: (index_ref[i, j], 0, 0)

    return pl.pallas_call(
        memory_attend_kernel,
        grid_spec=pltpu.PrefetchScalarGridSpec(
            num_scalar_prefetch=1,
            grid=(frames,),
            in_specs=[pl.BlockSpec((1, rows, C), lambda i, index_ref: (i, 0, 0))]
            + [pl.BlockSpec((1, quarter, 2 * C), place(j)) for j in range(TOPM)],
            out_specs=pl.BlockSpec((1, rows, C), lambda i, index_ref: (i, 0, 0)),
        ),
        out_shape=jax.ShapeDtypeStruct(query.shape, BF),
        compiler_params=params(),
        name="memory_attend",
        cost_estimate=pl.CostEstimate(
            flops=8 * frames * patches * TOPM * quarter * C,
            bytes_accessed=4 * query.size + 4 * frames * TOPM * quarter * C,
            transcendentals=frames * patches * TOPM * quarter,
        ),
    )(index, query, *([store] * TOPM))


def add_partials_kernel(*refs):
    ins, out_ref = refs[:-1], refs[-1]
    patches = out_ref.shape[1] - PAD
    total = ins[0][0, :patches, :].astype(F32)
    tail = ins[0][0, patches:, :].astype(F32)
    for ref in ins[1:]:
        total += ref[0, :patches, :].astype(F32)
        tail += ref[0, patches:, :].astype(F32)
    out_ref[0, :patches, :] = total.astype(BF)
    denominator = tail[:8] + tail[8:]
    high = denominator.astype(BF).astype(F32)
    out_ref[0, patches:, :] = jnp.concatenate([high, denominator - high], axis=0).astype(BF)


def add_partials(parts):
    frames, rows, _ = parts[0].shape
    spec = pl.BlockSpec((1, rows, C), lambda i: (i, 0, 0))
    return pl.pallas_call(
        add_partials_kernel,
        grid=(frames,),
        in_specs=[spec] * len(parts),
        out_specs=spec,
        out_shape=jax.ShapeDtypeStruct(parts[0].shape, BF),
        compiler_params=params(),
        name="add_partials",
        cost_estimate=pl.CostEstimate(
            flops=4 * parts[0].size, bytes_accessed=10 * parts[0].size, transcendentals=0
        ),
    )(*parts)


def leave_kernel(own_ref, memory_ref, time_ref, weight_ref, out_ref, combined_ref):
    patches = own_ref.shape[1]
    quarters = time_ref.shape[0] // G
    rows = time_ref.shape[1]

    @pl.when(pl.program_id(0) == 0)
    def _():
        row = lax.broadcasted_iota(jnp.int32, (C, C), 0)
        column = lax.broadcasted_iota(jnp.int32, (C, C), 1)
        for h in range(G):
            tail = memory_ref[h, patches:, :].astype(F32)
            denominators = tail[:8] + tail[8:]
            for j in range(-(-patches // C)):
                start = j * C
                size = min(C, patches - start)
                at = slice(start, start + size)
                line = jnp.broadcast_to(denominators[j : j + 1, :], (size, C))
                memory_sum = jnp.sum(
                    jnp.where(row[:size] == column[:size], line, 0.0), axis=1, keepdims=True
                )
                top = own_ref[h, at, :C] + memory_ref[h, at, :].astype(F32)
                combined_ref[at, h * C : (h + 1) * C] = (
                    top / (own_ref[h, at, C:] + memory_sum)
                ).astype(BF)
            for z in range(quarters):
                combined_ref[z * rows : (z + 1) * rows, HW + h * C : HW + (h + 1) * C] = time_ref[
                    z * G + h
                ]

    out_ref[...] = dot(combined_ref[...], weight_ref[...]).astype(BF)


def leave(own, memory, time, weight):
    patches = own.shape[1]
    depth, width = weight.shape
    step = 512
    return pl.pallas_call(
        leave_kernel,
        grid=(width // step,),
        in_specs=[
            pl.BlockSpec(own.shape, lambda i: (0, 0, 0)),
            pl.BlockSpec(memory.shape, lambda i: (0, 0, 0)),
            pl.BlockSpec(time.shape, lambda i: (0, 0, 0)),
            pl.BlockSpec((depth, step), lambda i: (0, i)),
        ],
        out_specs=pl.BlockSpec((patches, step), lambda i: (0, i)),
        out_shape=jax.ShapeDtypeStruct((patches, width), BF),
        scratch_shapes=[pltpu.VMEM((patches, depth), BF)],
        compiler_params=params(),
        name="leave",
        cost_estimate=pl.CostEstimate(
            flops=2 * patches * depth * width,
            bytes_accessed=2 * depth * width + 2 * patches * width + 6 * patches * depth,
            transcendentals=0,
        ),
    )(own, memory, time, weight)


def on_device(
    patch_activation_tensor,
    conditioning_affine,
    entry_projection_matrix,
    exit_projection_matrix,
    softmax_sharpness,
    cached_past_pairs,
    recalled_picture_holder,
    recalled_picture_position,
    lookback_lengths,
):
    rings = lax.axis_size("z")
    patches, depth = patch_activation_tensor.shape[2:]
    held, piece = cached_past_pairs.shape[:2]

    with jax.named_scope("store"):
        store = split_store(cached_past_pairs.reshape(held * piece, 2 * HW))
        store = lax.all_to_all(store, "x", split_axis=0, concat_axis=0, tiled=True)
        store = join_pieces(store, held)
        store = lax.all_gather(store, ("y", "c"), axis=0, tiled=True)

    with jax.named_scope("queries"):
        factor = softmax_sharpness / C
        index = recalled_picture_holder.reshape(TOPM) * held + recalled_picture_position.reshape(
            TOPM
        )
        tail = jnp.zeros((PAD, C), BF).at[0, :TOPM].set(index.astype(BF))
        hidden, query = modulate(
            patch_activation_tensor.reshape(patches, depth),
            conditioning_affine.reshape(2, depth),
            entry_projection_matrix,
            factor,
            tail,
        )
        group = lax.all_to_all(query, "x", split_axis=0, concat_axis=0, tiled=True)
        groups = [group]
        for step in range(1, rings):
            groups.append(
                lax.ppermute(group, "z", [(s, (s + step) % rings) for s in range(rings)])
            )

    with jax.named_scope("temporal"):
        parts = temporal_entry(hidden, entry_projection_matrix, factor, rings)
        parts = parts.reshape((rings * G,) + parts.shape[2:])
        parts = lax.all_to_all(parts, ("z", "x"), split_axis=0, concat_axis=0, tiled=True)

    with jax.named_scope("own"):
        own = own_attend(hidden, entry_projection_matrix, query)

    with jax.named_scope("temporal"):
        time = temporal_attend(lookback_lengths, parts)
        time = lax.all_to_all(time, ("z", "x"), split_axis=0, concat_axis=0, tiled=True)

    with jax.named_scope("memory"):
        partials = []
        for step, group in enumerate(groups):
            chosen = group[:, patches, :TOPM].astype(jnp.int32)
            partial = memory_attend(chosen, group, store)
            if step:
                partial = lax.ppermute(
                    partial, "z", [(s, (s - step) % rings) for s in range(rings)]
                )
            partials.append(partial)
        memory = add_partials(partials)
        memory = lax.all_to_all(memory, "x", split_axis=0, concat_axis=0, tiled=True)

    with jax.named_scope("exit"):
        attended = leave(own, memory, time, exit_projection_matrix)
    return attended.reshape(1, 1, patches, depth)


def solution(mesh):
    apart = Mesh(mesh.devices.reshape(4, 2, 4, 4), ("y", "c", "z", "x"))
    roll, frame = ("y", "c"), ("z", "x")
    return jax.shard_map(
        on_device,
        mesh=apart,
        in_specs=(
            P(roll, frame, None, None),
            P(roll, frame, None, None),
            P(),
            P(),
            P(),
            P(roll, frame, None, None),
            P(roll, frame, None, None),
            P(roll, frame, None),
            P(roll),
        ),
        out_specs=P(roll, frame, None, None),
        check_vma=False,
    )
```

```python
import functools

import jax
import jax.numpy as jnp
from jax import lax
from jax.experimental import pallas as pl
from jax.experimental.pallas import tpu as pltpu
from jax.sharding import Mesh
from jax.sharding import PartitionSpec as P

G = 4
C = 128
HW = G * C
TOPM = 6
EPSILON = 1e-06
BF = jnp.bfloat16
F32 = jnp.float32
PAD = 16
VMEM_LIMIT = 28 * 1024 * 1024
ANY = pl.BlockSpec(memory_space=pl.ANY)
WHOLE = pl.BlockSpec(memory_space=pltpu.VMEM)
SCALARS = pl.BlockSpec(memory_space=pltpu.SMEM)


def params(**more):
    return pltpu.CompilerParams(vmem_limit_bytes=VMEM_LIMIT, **more)


def cost(flops, bytes_accessed):
    return pl.CostEstimate(
        flops=flops // 16, bytes_accessed=bytes_accessed // 16, transcendentals=0
    )


def inverse_rms(values):
    return lax.rsqrt(jnp.mean(values * values, axis=-1, keepdims=True) + EPSILON)


def dot(a, b):
    return jnp.dot(a, b, preferred_element_type=F32)


def dot_t(a, b):
    return lax.dot_general(a, b, (((1,), (1,)), ((), ())), preferred_element_type=F32)


def split_store_kernel(rows_ref, out_ref):
    for h in range(G):
        key = rows_ref[:, h * C : (h + 1) * C].astype(F32)
        out_ref[h, :, :C] = (key * inverse_rms(key)).astype(BF)
        out_ref[h, :, C:] = rows_ref[:, HW + h * C : HW + (h + 1) * C]


def split_store(rows):
    n = rows.shape[0]
    return pl.pallas_call(
        split_store_kernel,
        out_shape=jax.ShapeDtypeStruct((G, n, 2 * C), BF),
        compiler_params=params(),
        name="split_store",
        cost_estimate=cost(8 * n * HW, 8 * n * HW),
    )(rows)


def join_pieces_kernel(piece, in_ref, _, out_ref, wide_ref, joined_ref):
    pieces = in_ref.shape[0]
    wide_ref[...] = in_ref[...].astype(F32)
    for m in range(out_ref.shape[0]):
        for i in range(pieces):
            joined_ref[m, i * piece : (i + 1) * piece, :] = wide_ref[
                i, m * piece : (m + 1) * piece, :
            ]
    out_ref[...] = joined_ref[...].astype(BF)


def join_pieces(parts, frames, after):
    pieces, rows, width = parts.shape
    piece = rows // frames
    return pl.pallas_call(
        functools.partial(join_pieces_kernel, piece),
        in_specs=[WHOLE, ANY],
        out_shape=jax.ShapeDtypeStruct((frames, pieces * piece, width), BF),
        scratch_shapes=[
            pltpu.VMEM((pieces, rows, width), F32),
            pltpu.VMEM((frames, pieces * piece, width), F32),
        ],
        compiler_params=params(),
        name="join_pieces",
        cost_estimate=cost(parts.size, 4 * parts.size),
    )(parts, after)


def modulate_kernel(
    act_ref, affine_ref, weight_ref, factor_ref, tail_ref, _, hidden_ref, query_ref
):
    step = pl.program_id(0)
    rows = act_ref.shape[0]
    patches = query_ref.shape[1] - PAD
    act = act_ref[...].astype(F32)
    hidden = act * inverse_rms(act) * (1.0 + affine_ref[0:1, :]) + affine_ref[1:2, :]
    hidden = hidden.astype(BF)
    hidden_ref[...] = hidden
    mapped = dot(hidden, weight_ref[...]).astype(BF).astype(F32)
    for h in range(G):
        one = mapped[:, h * C : (h + 1) * C]
        query_ref[h, pl.ds(pl.multiple_of(step * rows, 16), rows), :] = (
            one * inverse_rms(one) * factor_ref[0, h]
        ).astype(BF)

    @pl.when(step == 0)
    def _():
        for h in range(G):
            query_ref[h, patches:, :] = tail_ref[...]


def modulate(act, affine, weight, factor, tail, after):
    patches, depth = act.shape
    steps = 2
    rows = patches // steps
    return pl.pallas_call(
        modulate_kernel,
        grid=(steps,),
        in_specs=[
            pl.BlockSpec((rows, depth), lambda i: (i, 0)),
            pl.BlockSpec((2, depth), lambda i: (0, 0)),
            pl.BlockSpec((depth, HW), lambda i: (0, 0)),
            SCALARS,
            pl.BlockSpec((PAD, C), lambda i: (0, 0)),
            ANY,
        ],
        out_specs=[
            pl.BlockSpec((rows, depth), lambda i: (i, 0)),
            pl.BlockSpec((G, patches + PAD, C), lambda i: (0, 0, 0)),
        ],
        out_shape=[
            jax.ShapeDtypeStruct((patches, depth), BF),
            jax.ShapeDtypeStruct((G, patches + PAD, C), BF),
        ],
        compiler_params=params(),
        name="modulate",
        cost_estimate=cost(
            2 * patches * depth * HW, 4 * patches * depth + 2 * depth * HW + 2 * patches * HW
        ),
    )(act, affine, weight, factor, tail, after)


def temporal_entry_kernel(quarters, hidden_ref, weight_ref, factor_ref, _, out_ref):
    part = pl.program_id(0)
    rows = hidden_ref.shape[0] // quarters
    mapped = dot(hidden_ref[...], weight_ref[...]).astype(BF).astype(F32)
    for h in range(G):
        one = mapped[:, h * C : (h + 1) * C]
        scale = jnp.where(part < 2, inverse_rms(one), 1.0)
        factor = jnp.where(part == 0, factor_ref[1, h], 1.0)
        done = (one * scale * factor).astype(BF)
        for z in range(quarters):
            out_ref[z, h, 0] = done[z * rows : (z + 1) * rows, :]


def temporal_entry(hidden, weight, factor, quarters, after):
    patches, depth = hidden.shape
    rows = patches // quarters
    return pl.pallas_call(
        functools.partial(temporal_entry_kernel, quarters),
        grid=(3,),
        in_specs=[
            pl.BlockSpec((patches, depth), lambda i: (0, 0)),
            pl.BlockSpec((depth, HW), lambda i: (0, 3 + i)),
            SCALARS,
            ANY,
        ],
        out_specs=pl.BlockSpec((quarters, G, 1, rows, C), lambda i: (0, 0, i, 0, 0)),
        out_shape=jax.ShapeDtypeStruct((quarters, G, 3, rows, C), BF),
        compiler_params=params(),
        name="temporal_entry",
        cost_estimate=cost(
            6 * patches * depth * HW, 2 * patches * depth + 6 * depth * HW + 6 * patches * HW
        ),
    )(hidden, weight, factor, after)


def temporal_attend_kernel(length_ref, in_ref, _, out_ref):
    frames, _, rows, _ = in_ref.shape
    group = 16
    size = frames * group
    length = length_ref[0]
    row = lax.broadcasted_iota(jnp.int32, (size, size), 0)
    column = lax.broadcasted_iota(jnp.int32, (size, size), 1)
    target, source = row // group, column // group
    keep = (row % group == column % group) & (source <= target) & (source > target - length)
    for g in range(rows // group):
        at = slice(g * group, (g + 1) * group)
        query = in_ref[:, 0, at, :].reshape(size, C)
        key = in_ref[:, 1, at, :].reshape(size, C)
        value = in_ref[:, 2, at, :].reshape(size, C)
        weights = jnp.where(keep, jnp.exp(dot_t(query, key)), 0.0)
        shares = weights / jnp.sum(weights, axis=-1, keepdims=True)
        result = dot(shares.astype(BF), value).astype(BF)
        out_ref[:, at, :] = result.reshape(frames, group, C)


def temporal_attend(length, parts, after):
    frames, _, rows, _ = parts.shape
    return pl.pallas_call(
        temporal_attend_kernel,
        in_specs=[SCALARS, WHOLE, ANY],
        out_shape=jax.ShapeDtypeStruct((frames, rows, C), BF),
        compiler_params=params(),
        name="temporal_attend",
        cost_estimate=cost(4 * frames * rows * 256 * C, 8 * frames * rows * C),
    )(length, parts, after)


def own_attend_kernel(hidden_ref, key_weight_ref, value_weight_ref, query_ref, out_ref):
    heads = query_ref.shape[0]
    patches = hidden_ref.shape[0]
    hidden = hidden_ref[...]
    keys = dot(hidden, key_weight_ref[...]).astype(BF).astype(F32)
    values = dot(hidden, value_weight_ref[...]).astype(BF)
    ones = jnp.ones((patches, C), BF)
    for h in range(heads):
        key = keys[:, h * C : (h + 1) * C]
        key = (key * inverse_rms(key)).astype(BF)
        both = jnp.concatenate([values[:, h * C : (h + 1) * C], ones], axis=1)
        weights = jnp.exp(dot_t(query_ref[h, :patches, :], key)).astype(BF)
        out_ref[h] = dot(weights, both)


def own_attend(hidden, weight, query):
    patches, depth = hidden.shape
    heads = 2
    wide = heads * C
    per = HW // wide
    return pl.pallas_call(
        own_attend_kernel,
        grid=(G // heads,),
        in_specs=[
            pl.BlockSpec((patches, depth), lambda i: (0, 0)),
            pl.BlockSpec((depth, wide), lambda i: (0, per + i)),
            pl.BlockSpec((depth, wide), lambda i: (0, 2 * per + i)),
            pl.BlockSpec((heads, patches + PAD, C), lambda i: (i, 0, 0)),
        ],
        out_specs=pl.BlockSpec((heads, patches, 2 * C), lambda i: (i, 0, 0)),
        out_shape=jax.ShapeDtypeStruct((G, patches, 2 * C), F32),
        compiler_params=params(),
        name="own_attend",
        cost_estimate=cost(
            4 * patches * depth * HW + 6 * patches * patches * HW,
            2 * patches * depth + 4 * depth * HW + 10 * patches * HW,
        ),
    )(hidden, weight, weight, query)


LINE = 96


def halves(denominators):
    high = denominators.astype(BF).astype(F32)
    return jnp.concatenate([high, denominators - high], axis=0).astype(BF)


def memory_attend_kernel(carried, index_ref, query_ref, *refs):
    stores, out_ref = refs[:TOPM], refs[-1]
    patches = query_ref.shape[1] - PAD
    chunk = 3 * LINE
    keys = jnp.concatenate([ref[0, :, :C] for ref in stores], axis=0)
    values = jnp.concatenate([ref[0, :, C:] for ref in stores], axis=0)
    both = jnp.concatenate([values, jnp.ones(values.shape, BF)], axis=1)
    row = lax.broadcasted_iota(jnp.int32, (LINE, C), 0)
    column = lax.broadcasted_iota(jnp.int32, (LINE, C), 1)
    carry = None
    if carried is not None:
        first, count = carried
        step = pl.program_id(0)
        here = jnp.logical_and(step >= first, step < first + count).astype(F32)
        carry_ref = refs[TOPM]
        carry = here * carry_ref[0].astype(F32)
    lines = []
    for start in range(0, patches, chunk):
        at = slice(start, start + chunk)
        weights = jnp.exp(dot_t(query_ref[0, at, :], keys)).astype(BF)
        result = dot(weights, both)
        top = result[:, :C]
        if carry is not None:
            top = top + carry[at]
        out_ref[0, at, :] = top.astype(BF)
        for j in range(0, chunk, LINE):
            diagonal = jnp.where(row == column, result[j : j + LINE, C:], 0.0)
            lines.append(jnp.sum(diagonal, axis=0, keepdims=True))
    lines.append(jnp.zeros((8 - len(lines), C), F32))
    total = jnp.concatenate(lines, axis=0)
    if carry is not None:
        total = total + carry[patches : patches + 8] + carry[patches + 8 :]
    out_ref[0, patches:, :] = halves(total)


def memory_attend(index, query, store, after, carry=None, first=0):
    frames, rows, _ = query.shape
    patches = rows - PAD
    quarter = store.shape[1]
    block = pl.BlockSpec((1, rows, C), lambda i, index_ref: (i, 0, 0))
    carried, extra, extra_specs = None, [], []
    if carry is not None:
        count = carry.shape[0]
        carried, extra = (first, count), [carry]
        extra_specs = [
            pl.BlockSpec(
                (1, rows, C),
                lambda i, index_ref: (jnp.clip(i - first, 0, count - 1), 0, 0),
            )
        ]

    def place(j):
        return lambda i, index_ref: (index_ref[i, j], 0, 0)

    return pl.pallas_call(
        functools.partial(memory_attend_kernel, carried),
        grid_spec=pltpu.PrefetchScalarGridSpec(
            num_scalar_prefetch=1,
            grid=(frames,),
            in_specs=[block]
            + [pl.BlockSpec((1, quarter, 2 * C), place(j)) for j in range(TOPM)]
            + extra_specs
            + [ANY],
            out_specs=block,
        ),
        out_shape=jax.ShapeDtypeStruct(query.shape, BF),
        compiler_params=params(),
        name="memory_attend",
        cost_estimate=cost(
            8 * frames * patches * TOPM * quarter * C,
            4 * query.size + 4 * frames * TOPM * quarter * C,
        ),
    )(index, query, *([store] * TOPM), *extra, after)


def add_partials_kernel(*refs):
    ins, out_ref = refs[:-1], refs[-1]
    patches = out_ref.shape[1] - PAD
    total = ins[0][:, :patches, :].astype(F32)
    tail = ins[0][:, patches:, :].astype(F32)
    for ref in ins[1:]:
        total += ref[:, :patches, :].astype(F32)
        tail += ref[:, patches:, :].astype(F32)
    out_ref[:, :patches, :] = total.astype(BF)
    for i in range(out_ref.shape[0]):
        out_ref[i, patches:, :] = halves(tail[i, :8] + tail[i, 8:])


def add_partials(parts):
    return pl.pallas_call(
        add_partials_kernel,
        out_shape=jax.ShapeDtypeStruct(parts[0].shape, BF),
        compiler_params=params(),
        name="add_partials",
        cost_estimate=cost(4 * parts[0].size, 8 * parts[0].size),
    )(*parts)


def leave_kernel(own_ref, memory_ref, time_ref, weight_ref, out_ref, combined_ref):
    patches = own_ref.shape[1]
    quarters = time_ref.shape[0] // G
    rows = time_ref.shape[1]

    @pl.when(pl.program_id(0) == 0)
    def _():
        row = lax.broadcasted_iota(jnp.int32, (LINE, C), 0)
        column = lax.broadcasted_iota(jnp.int32, (LINE, C), 1)
        for h in range(G):
            tail = memory_ref[h, patches:, :].astype(F32)
            denominators = tail[:8] + tail[8:]
            for j in range(patches // LINE):
                at = slice(j * LINE, (j + 1) * LINE)
                line = jnp.broadcast_to(denominators[j : j + 1, :], (LINE, C))
                memory_sum = jnp.sum(
                    jnp.where(row == column, line, 0.0), axis=1, keepdims=True
                )
                top = own_ref[h, at, :C] + memory_ref[h, at, :].astype(F32)
                combined_ref[at, h * C : (h + 1) * C] = (
                    top / (own_ref[h, at, C:] + memory_sum)
                ).astype(BF)
            for z in range(quarters):
                combined_ref[z * rows : (z + 1) * rows, HW + h * C : HW + (h + 1) * C] = time_ref[
                    z * G + h
                ]

    out_ref[...] = dot(combined_ref[...], weight_ref[...]).astype(BF)


def leave(own, memory, time, weight):
    patches = own.shape[1]
    depth, width = weight.shape
    step = 512
    return pl.pallas_call(
        leave_kernel,
        grid=(width // step,),
        in_specs=[
            pl.BlockSpec(own.shape, lambda i: (0, 0, 0)),
            pl.BlockSpec(memory.shape, lambda i: (0, 0, 0)),
            pl.BlockSpec(time.shape, lambda i: (0, 0, 0)),
            pl.BlockSpec((depth, step), lambda i: (0, i)),
        ],
        out_specs=pl.BlockSpec((patches, step), lambda i: (0, i)),
        out_shape=jax.ShapeDtypeStruct((patches, width), BF),
        scratch_shapes=[pltpu.VMEM((patches, depth), BF)],
        compiler_params=params(),
        name="leave",
        cost_estimate=cost(
            2 * patches * depth * width,
            2 * depth * width + 2 * patches * width + 6 * patches * depth,
        ),
    )(own, memory, time, weight)


def on_device(
    patch_activation_tensor,
    conditioning_affine,
    entry_projection_matrix,
    exit_projection_matrix,
    softmax_sharpness,
    cached_past_pairs,
    recalled_picture_holder,
    recalled_picture_position,
    lookback_lengths,
):
    rings = lax.axis_size("z")
    patches, depth = patch_activation_tensor.shape[2:]
    held, piece = cached_past_pairs.shape[:2]
    up = [(s, (s + 1) % rings) for s in range(rings)]
    down = [(s, (s - 1) % rings) for s in range(rings)]

    def swap(blocks, axes):
        return lax.all_to_all(blocks, axes, split_axis=0, concat_axis=0, tiled=True)

    def attend(group, store, after, **more):
        chosen = group[:, patches, :TOPM].astype(jnp.int32)
        return memory_attend(chosen, group, store, after, **more)

    with jax.named_scope("store"):
        split = split_store(cached_past_pairs.reshape(held * piece, 2 * HW))
        pieces = swap(split, "x")

    with jax.named_scope("queries"):
        factor = softmax_sharpness / C
        index = recalled_picture_holder.reshape(TOPM) * held + recalled_picture_position.reshape(
            TOPM
        )
        tail = jnp.zeros((PAD, C), BF).at[0, :TOPM].set(index.astype(BF))
        hidden, query = modulate(
            patch_activation_tensor.reshape(patches, depth),
            conditioning_affine.reshape(2, depth),
            entry_projection_matrix,
            factor,
            tail,
            after=split,
        )
        here = swap(query, "x")

    with jax.named_scope("own"):
        own = own_attend(hidden, entry_projection_matrix, query)

    with jax.named_scope("store"):
        joined = join_pieces(pieces, held, after=own)
        store = lax.all_gather(joined, ("y", "c"), axis=0, tiled=True)

    with jax.named_scope("queries"):
        below = lax.ppermute(here, "z", up)
        above = lax.ppermute(here, "z", down)
        half = here.shape[0] // 2
        far_first = lax.ppermute(below[:half], "z", up)
        far_last = lax.ppermute(above[half:], "z", down)

    with jax.named_scope("temporal"):
        parts = temporal_entry(hidden, entry_projection_matrix, factor, rings, after=joined)
        sent = swap(parts.reshape((rings * G,) + parts.shape[2:]), ("z", "x"))

    with jax.named_scope("memory"):
        sum_first = attend(far_first, store, parts)
        sum_last = attend(far_last, store, sum_first)
        carry_first = lax.ppermute(sum_first, "z", down)
        carry_last = lax.ppermute(sum_last, "z", up)
        sum_below = attend(below, store, sum_last, carry=carry_first, first=0)
        from_above = lax.ppermute(sum_below, "z", down)
        sum_above = attend(above, store, sum_below, carry=carry_last, first=half)
        from_below = lax.ppermute(sum_above, "z", up)

    with jax.named_scope("temporal"):
        timed = temporal_attend(lookback_lengths, sent, after=sum_above)
        time = swap(timed, ("z", "x"))

    with jax.named_scope("memory"):
        sum_here = attend(here, store, timed)
        memory = swap(add_partials([sum_here, from_above, from_below]), "x")

    with jax.named_scope("exit"):
        attended = leave(own, memory, time, exit_projection_matrix)
    return attended.reshape(1, 1, patches, depth)


def solution(mesh):
    apart = Mesh(mesh.devices.reshape(4, 2, 4, 4), ("y", "c", "z", "x"))
    roll, frame = ("y", "c"), ("z", "x")
    return jax.shard_map(
        on_device,
        mesh=apart,
        in_specs=(
            P(roll, frame, None, None),
            P(roll, frame, None, None),
            P(),
            P(),
            P(),
            P(roll, frame, None, None),
            P(roll, frame, None, None),
            P(roll, frame, None),
            P(roll),
        ),
        out_specs=P(roll, frame, None, None),
        check_vma=False,
    )
```

```python
import functools

import jax
import jax.numpy as jnp
from jax import lax
from jax.experimental import pallas as pl
from jax.experimental.pallas import tpu as pltpu
from jax.sharding import Mesh
from jax.sharding import PartitionSpec as P

G = 4
C = 128
HW = G * C
TOPM = 6
EPSILON = 1e-06
BF = jnp.bfloat16
F32 = jnp.float32
PAD = 16
VMEM_LIMIT = 28 * 1024 * 1024
ANY = pl.BlockSpec(memory_space=pl.ANY)
HBM = pl.BlockSpec(memory_space=pltpu.HBM)
WHOLE = pl.BlockSpec(memory_space=pltpu.VMEM)
SCALARS = pl.BlockSpec(memory_space=pltpu.SMEM)


def params(**more):
    return pltpu.CompilerParams(vmem_limit_bytes=VMEM_LIMIT, **more)


def cost(flops, bytes_accessed):
    return pl.CostEstimate(
        flops=flops // 16, bytes_accessed=bytes_accessed // 16, transcendentals=0
    )


def in_hbm(array):
    return pltpu.with_memory_space_constraint(array, pltpu.HBM)


def inverse_rms(values):
    return lax.rsqrt(jnp.mean(values * values, axis=-1, keepdims=True) + EPSILON)


def dot(a, b):
    return jnp.dot(a, b, preferred_element_type=F32)


def dot_t(a, b):
    return lax.dot_general(a, b, (((1,), (1,)), ((), ())), preferred_element_type=F32)


def split_store_kernel(rows_ref, out_ref):
    for h in range(G):
        key = rows_ref[:, h * C : (h + 1) * C].astype(F32)
        out_ref[h, :, :C] = (key * inverse_rms(key)).astype(BF)
        out_ref[h, :, C:] = rows_ref[:, HW + h * C : HW + (h + 1) * C]


def split_store(rows):
    n = rows.shape[0]
    return pl.pallas_call(
        split_store_kernel,
        out_shape=jax.ShapeDtypeStruct((G, n, 2 * C), BF),
        compiler_params=params(),
        name="split_store",
        cost_estimate=cost(8 * n * HW, 8 * n * HW),
    )(rows)


def join_pieces_kernel(piece, in_ref, _, out_ref, wide_ref, joined_ref):
    pieces = in_ref.shape[0]
    wide_ref[...] = in_ref[...].astype(F32)
    for m in range(out_ref.shape[0]):
        for i in range(pieces):
            joined_ref[m, i * piece : (i + 1) * piece, :] = wide_ref[
                i, m * piece : (m + 1) * piece, :
            ]
    out_ref[...] = joined_ref[...].astype(BF)


def join_pieces(parts, frames, after):
    pieces, rows, width = parts.shape
    piece = rows // frames
    return pl.pallas_call(
        functools.partial(join_pieces_kernel, piece),
        in_specs=[WHOLE, ANY],
        out_shape=jax.ShapeDtypeStruct((frames, pieces * piece, width), BF),
        scratch_shapes=[
            pltpu.VMEM((pieces, rows, width), F32),
            pltpu.VMEM((frames, pieces * piece, width), F32),
        ],
        compiler_params=params(),
        name="join_pieces",
        cost_estimate=cost(parts.size, 4 * parts.size),
    )(parts, after)


def modulate_kernel(
    act_hbm, affine_ref, weight_hbm, factor_ref, tail_ref, _, hidden_ref, query_ref,
    act_ref, weight_ref, act_sem, weight_sem,
):
    steps, rows, _ = act_ref.shape
    patches = query_ref.shape[1] - PAD
    loads = [
        pltpu.make_async_copy(act_hbm.at[pl.ds(i * rows, rows), :], act_ref.at[i], act_sem.at[i])
        for i in range(steps)
    ]
    weight_load = pltpu.make_async_copy(weight_hbm.at[:, pl.ds(0, HW)], weight_ref, weight_sem)
    loads[0].start()
    weight_load.start()
    for load in loads[1:]:
        load.start()
    for h in range(G):
        query_ref[h, patches:, :] = tail_ref[...]
    for i in range(steps):
        at = slice(i * rows, (i + 1) * rows)
        loads[i].wait()
        act = act_ref[i].astype(F32)
        hidden = act * inverse_rms(act) * (1.0 + affine_ref[0:1, :]) + affine_ref[1:2, :]
        hidden = hidden.astype(BF)
        hidden_ref[at, :] = hidden
        if i == 0:
            weight_load.wait()
        mapped = dot(hidden, weight_ref[...]).astype(BF).astype(F32)
        for h in range(G):
            one = mapped[:, h * C : (h + 1) * C]
            query_ref[h, at, :] = (one * inverse_rms(one) * factor_ref[0, h]).astype(BF)


def modulate(act, affine, weight, factor, tail, after):
    patches, depth = act.shape
    steps = 2
    rows = patches // steps
    return pl.pallas_call(
        modulate_kernel,
        in_specs=[HBM, WHOLE, HBM, SCALARS, WHOLE, ANY],
        out_specs=[WHOLE, WHOLE],
        out_shape=[
            jax.ShapeDtypeStruct((patches, depth), BF),
            jax.ShapeDtypeStruct((G, patches + PAD, C), BF),
        ],
        scratch_shapes=[
            pltpu.VMEM((steps, rows, depth), BF),
            pltpu.VMEM((depth, HW), BF),
            pltpu.SemaphoreType.DMA((steps,)),
            pltpu.SemaphoreType.DMA,
        ],
        compiler_params=params(),
        name="modulate",
        cost_estimate=cost(
            2 * patches * depth * HW, 4 * patches * depth + 2 * depth * HW + 2 * patches * HW
        ),
    )(in_hbm(act), affine, in_hbm(weight), factor, tail, after)


def temporal_entry_kernel(
    quarters, hidden_ref, weight_hbm, factor_ref, _, out_ref, weight_ref, sem
):
    rows = hidden_ref.shape[0] // quarters
    loads = [
        pltpu.make_async_copy(
            weight_hbm.at[:, pl.ds((3 + part) * HW, HW)], weight_ref.at[part], sem.at[part]
        )
        for part in range(3)
    ]
    for load in loads:
        load.start()
    for part in range(3):
        loads[part].wait()
        mapped = dot(hidden_ref[...], weight_ref[part]).astype(BF)
        for h in range(G):
            done = mapped[:, h * C : (h + 1) * C]
            if part < 2:
                one = done.astype(F32)
                one = one * inverse_rms(one)
                if part == 0:
                    one = one * factor_ref[1, h]
                done = one.astype(BF)
            for z in range(quarters):
                out_ref[z, h, part] = done[z * rows : (z + 1) * rows, :]


def temporal_entry(hidden, weight, factor, quarters, after):
    patches, depth = hidden.shape
    rows = patches // quarters
    return pl.pallas_call(
        functools.partial(temporal_entry_kernel, quarters),
        in_specs=[WHOLE, HBM, SCALARS, ANY],
        out_specs=WHOLE,
        out_shape=jax.ShapeDtypeStruct((quarters, G, 3, rows, C), BF),
        scratch_shapes=[pltpu.VMEM((3, depth, HW), BF), pltpu.SemaphoreType.DMA((3,))],
        compiler_params=params(),
        name="temporal_entry",
        cost_estimate=cost(
            6 * patches * depth * HW, 2 * patches * depth + 6 * depth * HW + 6 * patches * HW
        ),
    )(hidden, in_hbm(weight), factor, after)


def temporal_attend_kernel(length_ref, in_ref, _, out_ref):
    frames, _, rows, _ = in_ref.shape
    group = 16
    size = frames * group
    length = length_ref[0]
    row = lax.broadcasted_iota(jnp.int32, (size, size), 0)
    column = lax.broadcasted_iota(jnp.int32, (size, size), 1)
    target, source = row // group, column // group
    keep = (row % group == column % group) & (source <= target) & (source > target - length)
    for g in range(rows // group):
        at = slice(g * group, (g + 1) * group)
        query = in_ref[:, 0, at, :].reshape(size, C)
        key = in_ref[:, 1, at, :].reshape(size, C)
        value = in_ref[:, 2, at, :].reshape(size, C)
        weights = jnp.where(keep, jnp.exp(dot_t(query, key)), 0.0)
        shares = weights / jnp.sum(weights, axis=-1, keepdims=True)
        result = dot(shares.astype(BF), value).astype(BF)
        out_ref[:, at, :] = result.reshape(frames, group, C)


def temporal_attend(length, parts, after):
    frames, _, rows, _ = parts.shape
    return pl.pallas_call(
        temporal_attend_kernel,
        in_specs=[SCALARS, WHOLE, ANY],
        out_shape=jax.ShapeDtypeStruct((frames, rows, C), BF),
        compiler_params=params(),
        name="temporal_attend",
        cost_estimate=cost(4 * frames * rows * 256 * C, 8 * frames * rows * C),
    )(length, parts, after)


def own_attend_kernel(hidden_ref, weight_hbm, query_ref, _, out_ref, weight_ref, sem):
    patches = hidden_ref.shape[0]
    loads = [
        pltpu.make_async_copy(
            weight_hbm.at[:, pl.ds((1 + part) * HW, HW)], weight_ref.at[part], sem.at[part]
        )
        for part in range(2)
    ]
    for load in loads:
        load.start()
    loads[0].wait()
    keys = dot(hidden_ref[...], weight_ref[0]).astype(BF)
    loads[1].wait()
    values = dot(hidden_ref[...], weight_ref[1]).astype(BF)
    ones = jnp.ones((patches, C), BF)
    for h in range(G):
        key = keys[:, h * C : (h + 1) * C].astype(F32)
        key = (key * inverse_rms(key)).astype(BF)
        both = jnp.concatenate([values[:, h * C : (h + 1) * C], ones], axis=1)
        weights = jnp.exp(dot_t(query_ref[h, :patches, :], key)).astype(BF)
        out_ref[h] = dot(weights, both)


def own_attend(hidden, weight, query, after):
    patches, depth = hidden.shape
    return pl.pallas_call(
        own_attend_kernel,
        in_specs=[WHOLE, HBM, WHOLE, ANY],
        out_specs=WHOLE,
        out_shape=jax.ShapeDtypeStruct((G, patches, 2 * C), F32),
        scratch_shapes=[pltpu.VMEM((2, depth, HW), BF), pltpu.SemaphoreType.DMA((2,))],
        compiler_params=params(),
        name="own_attend",
        cost_estimate=cost(
            4 * patches * depth * HW + 6 * patches * patches * HW,
            2 * patches * depth + 4 * depth * HW + 10 * patches * HW,
        ),
    )(hidden, in_hbm(weight), query, after)


LINE = 96


def halves(denominators):
    high = denominators.astype(BF).astype(F32)
    return jnp.concatenate([high, denominators - high], axis=0).astype(BF)


def memory_attend_kernel(carried, index_ref, query_ref, store_ref, *refs):
    out_ref = refs[-1]
    frames = query_ref.shape[0]
    patches = query_ref.shape[1] - PAD
    chunk = 3 * LINE
    row = lax.broadcasted_iota(jnp.int32, (LINE, C), 0)
    column = lax.broadcasted_iota(jnp.int32, (LINE, C), 1)
    for i in range(frames):
        blocks = [store_ref[index_ref[i, j]] for j in range(TOPM)]
        keys = jnp.concatenate([block[:, :C] for block in blocks], axis=0)
        values = jnp.concatenate([block[:, C:] for block in blocks], axis=0)
        both = jnp.concatenate([values, jnp.ones(values.shape, BF)], axis=1)
        carry = None
        if carried is not None and carried[0] <= i < carried[1]:
            carry = refs[0].at[i - carried[0]]
        lines = []
        for start in range(0, patches, chunk):
            at = slice(start, start + chunk)
            weights = jnp.exp(dot_t(query_ref[i, at, :], keys)).astype(BF)
            result = dot(weights, both)
            top = result[:, :C]
            if carry is not None:
                top = top + carry[at, :].astype(F32)
            out_ref[i, at, :] = top.astype(BF)
            for j in range(0, chunk, LINE):
                diagonal = jnp.where(row == column, result[j : j + LINE, C:], 0.0)
                lines.append(jnp.sum(diagonal, axis=0, keepdims=True))
        lines.append(jnp.zeros((8 - len(lines), C), F32))
        total = jnp.concatenate(lines, axis=0)
        if carry is not None:
            tail = carry[patches:, :].astype(F32)
            total = total + tail[:8] + tail[8:]
        out_ref[i, patches:, :] = halves(total)


def memory_attend(query, store, after, carry=None, first=0):
    frames, rows, _ = query.shape
    patches = rows - PAD
    quarter = store.shape[1]
    index = query[:, patches, :TOPM].astype(jnp.int32)
    carried, extra = None, []
    if carry is not None:
        carried, extra = (first, first + carry.shape[0]), [carry]
    return pl.pallas_call(
        functools.partial(memory_attend_kernel, carried),
        in_specs=[SCALARS, WHOLE, WHOLE] + [WHOLE] * len(extra) + [ANY],
        out_specs=WHOLE,
        out_shape=jax.ShapeDtypeStruct(query.shape, BF),
        compiler_params=params(),
        name="memory_attend",
        cost_estimate=cost(
            8 * frames * patches * TOPM * quarter * C,
            4 * query.size + 4 * frames * TOPM * quarter * C,
        ),
    )(index, query, store, *extra, after)


def add_partials_kernel(*refs):
    ins, out_ref = refs[:-1], refs[-1]
    patches = out_ref.shape[1] - PAD
    total = ins[0][:, :patches, :].astype(F32)
    tail = ins[0][:, patches:, :].astype(F32)
    for ref in ins[1:]:
        total += ref[:, :patches, :].astype(F32)
        tail += ref[:, patches:, :].astype(F32)
    out_ref[:, :patches, :] = total.astype(BF)
    for i in range(out_ref.shape[0]):
        out_ref[i, patches:, :] = halves(tail[i, :8] + tail[i, 8:])


def add_partials(parts):
    return pl.pallas_call(
        add_partials_kernel,
        out_shape=jax.ShapeDtypeStruct(parts[0].shape, BF),
        compiler_params=params(),
        name="add_partials",
        cost_estimate=cost(4 * parts[0].size, 8 * parts[0].size),
    )(*parts)


def leave_kernel(
    own_ref, memory_ref, time_ref, weight_hbm, out_hbm,
    combined_ref, weight_ref, out_ref, load_sem, store_sem,
):
    patches = own_ref.shape[1]
    quarters = time_ref.shape[0] // G
    rows = time_ref.shape[1]
    steps, _, width = weight_ref.shape
    loads, stores = [], []
    for i in range(steps):
        at = pl.ds(i * width, width)
        loads.append(
            pltpu.make_async_copy(weight_hbm.at[:, at], weight_ref.at[i], load_sem.at[i])
        )
        stores.append(pltpu.make_async_copy(out_ref.at[i], out_hbm.at[:, at], store_sem.at[i]))
    for load in loads:
        load.start()
    row = lax.broadcasted_iota(jnp.int32, (LINE, C), 0)
    column = lax.broadcasted_iota(jnp.int32, (LINE, C), 1)
    for h in range(G):
        tail = memory_ref[h, patches:, :].astype(F32)
        denominators = tail[:8] + tail[8:]
        for j in range(patches // LINE):
            at = slice(j * LINE, (j + 1) * LINE)
            line = jnp.broadcast_to(denominators[j : j + 1, :], (LINE, C))
            memory_sum = jnp.sum(jnp.where(row == column, line, 0.0), axis=1, keepdims=True)
            top = own_ref[h, at, :C] + memory_ref[h, at, :].astype(F32)
            combined_ref[at, h * C : (h + 1) * C] = (
                top / (own_ref[h, at, C:] + memory_sum)
            ).astype(BF)
        for z in range(quarters):
            combined_ref[z * rows : (z + 1) * rows, HW + h * C : HW + (h + 1) * C] = time_ref[
                z * G + h
            ]
    for i in range(steps):
        loads[i].wait()
        out_ref[i] = dot(combined_ref[...], weight_ref[i]).astype(BF)
        stores[i].start()
    for store in stores:
        store.wait()


def leave(own, memory, time, weight):
    patches = own.shape[1]
    depth, width = weight.shape
    steps = 4
    step = width // steps
    return pl.pallas_call(
        leave_kernel,
        in_specs=[WHOLE, WHOLE, WHOLE, HBM],
        out_specs=HBM,
        out_shape=jax.ShapeDtypeStruct((patches, width), BF),
        scratch_shapes=[
            pltpu.VMEM((patches, depth), BF),
            pltpu.VMEM((steps, depth, step), BF),
            pltpu.VMEM((steps, patches, step), BF),
            pltpu.SemaphoreType.DMA((steps,)),
            pltpu.SemaphoreType.DMA((steps,)),
        ],
        compiler_params=params(),
        name="leave",
        cost_estimate=cost(
            2 * patches * depth * width,
            2 * depth * width + 2 * patches * width + 6 * patches * depth,
        ),
    )(own, memory, time, in_hbm(weight))


def on_device(
    patch_activation_tensor,
    conditioning_affine,
    entry_projection_matrix,
    exit_projection_matrix,
    softmax_sharpness,
    cached_past_pairs,
    recalled_picture_holder,
    recalled_picture_position,
    lookback_lengths,
):
    rings = lax.axis_size("z")
    patches, depth = patch_activation_tensor.shape[2:]
    held, piece = cached_past_pairs.shape[:2]
    up = [(s, (s + 1) % rings) for s in range(rings)]
    down = [(s, (s - 1) % rings) for s in range(rings)]

    def swap(blocks, axes):
        return lax.all_to_all(blocks, axes, split_axis=0, concat_axis=0, tiled=True)

    with jax.named_scope("store"):
        split = split_store(cached_past_pairs.reshape(held * piece, 2 * HW))
        pieces = swap(split, "x")

    with jax.named_scope("queries"):
        factor = softmax_sharpness / C
        index = recalled_picture_holder.reshape(TOPM) * held + recalled_picture_position.reshape(
            TOPM
        )
        tail = jnp.zeros((PAD, C), BF).at[0, :TOPM].set(index.astype(BF))
        hidden, query = modulate(
            patch_activation_tensor.reshape(patches, depth),
            conditioning_affine.reshape(2, depth),
            entry_projection_matrix,
            factor,
            tail,
            after=split,
        )
        here = swap(query, "x")

    with jax.named_scope("store"):
        joined = join_pieces(pieces, held, after=hidden)
        store = lax.all_gather(joined, ("y", "c"), axis=0, tiled=True)

    with jax.named_scope("own"):
        own = own_attend(hidden, entry_projection_matrix, query, after=joined)

    with jax.named_scope("queries"):
        half = here.shape[0] // 2
        below = lax.ppermute(here, "z", up)
        above = lax.ppermute(here, "z", down)
        far_first = lax.ppermute(below[:half], "z", up)
        far_last = lax.ppermute(above[half:], "z", down)

    with jax.named_scope("temporal"):
        parts = temporal_entry(hidden, entry_projection_matrix, factor, rings, after=own)
        parts, far_first, far_last = lax.optimization_barrier((parts, far_first, far_last))
        sent = swap(parts.reshape((rings * G,) + parts.shape[2:]), ("z", "x"))

    with jax.named_scope("memory"):
        sum_first = memory_attend(far_first, store, parts)
        carry_first = lax.ppermute(sum_first, "z", down)
        sum_last = memory_attend(far_last, store, sum_first)
        carry_last = lax.ppermute(sum_last, "z", up)
        sum_below = memory_attend(below, store, sum_last, carry=carry_first, first=0)
        from_above = lax.ppermute(sum_below, "z", down)
        sum_above = memory_attend(above, store, sum_below, carry=carry_last, first=half)
        from_below = lax.ppermute(sum_above, "z", up)

    with jax.named_scope("temporal"):
        timed = temporal_attend(lookback_lengths, sent, after=sum_above)
        time = swap(timed, ("z", "x"))

    with jax.named_scope("memory"):
        sum_here = memory_attend(here, store, timed)
        memory = swap(add_partials([sum_here, from_above, from_below]), "x")

    with jax.named_scope("exit"):
        attended = leave(own, memory, time, exit_projection_matrix)
    return attended.reshape(1, 1, patches, depth)


def solution(mesh):
    apart = Mesh(mesh.devices.reshape(4, 2, 4, 4), ("y", "c", "z", "x"))
    roll, frame = ("y", "c"), ("z", "x")
    return jax.shard_map(
        on_device,
        mesh=apart,
        in_specs=(
            P(roll, frame, None, None),
            P(roll, frame, None, None),
            P(),
            P(),
            P(),
            P(roll, frame, None, None),
            P(roll, frame, None, None),
            P(roll, frame, None),
            P(roll),
        ),
        out_specs=P(roll, frame, None, None),
        check_vma=False,
    )
```

```python
import functools

import jax
import jax.numpy as jnp
from jax import lax
from jax.experimental import pallas as pl
from jax.experimental.pallas import tpu as pltpu
from jax.sharding import Mesh
from jax.sharding import PartitionSpec as P

G = 4
C = 128
HW = G * C
TOPM = 6
EPSILON = 1e-06
BF = jnp.bfloat16
F32 = jnp.float32
PAD = 16
VMEM_LIMIT = 28 * 1024 * 1024
ANY = pl.BlockSpec(memory_space=pl.ANY)
HBM = pl.BlockSpec(memory_space=pltpu.HBM)
WHOLE = pl.BlockSpec(memory_space=pltpu.VMEM)
SCALARS = pl.BlockSpec(memory_space=pltpu.SMEM)


def params(**more):
    return pltpu.CompilerParams(vmem_limit_bytes=VMEM_LIMIT, **more)


def cost(flops, bytes_accessed):
    return pl.CostEstimate(
        flops=flops // 16, bytes_accessed=bytes_accessed // 16, transcendentals=0
    )


def in_hbm(array):
    return pltpu.with_memory_space_constraint(array, pltpu.HBM)


def inverse_rms(values):
    return lax.rsqrt(jnp.mean(values * values, axis=-1, keepdims=True) + EPSILON)


def dot(a, b):
    return jnp.dot(a, b, preferred_element_type=F32)


def dot_t(a, b):
    return lax.dot_general(a, b, (((1,), (1,)), ((), ())), preferred_element_type=F32)


def split_store_kernel(rows_ref, out_ref):
    for h in range(G):
        key = rows_ref[:, h * C : (h + 1) * C].astype(F32)
        out_ref[h, :, :C] = (key * inverse_rms(key)).astype(BF)
        out_ref[h, :, C:] = rows_ref[:, HW + h * C : HW + (h + 1) * C]


def split_store(rows):
    n = rows.shape[0]
    return pl.pallas_call(
        split_store_kernel,
        out_shape=jax.ShapeDtypeStruct((G, n, 2 * C), BF),
        compiler_params=params(),
        name="split_store",
        cost_estimate=cost(8 * n * HW, 8 * n * HW),
    )(rows)


def join_pieces_kernel(piece, in_ref, _, out_ref, wide_ref, joined_ref):
    pieces = in_ref.shape[0]
    wide_ref[...] = in_ref[...].astype(F32)
    for m in range(out_ref.shape[0]):
        for i in range(pieces):
            joined_ref[m, i * piece : (i + 1) * piece, :] = wide_ref[
                i, m * piece : (m + 1) * piece, :
            ]
    out_ref[...] = joined_ref[...].astype(BF)


def join_pieces(parts, frames, after):
    pieces, rows, width = parts.shape
    piece = rows // frames
    return pl.pallas_call(
        functools.partial(join_pieces_kernel, piece),
        in_specs=[WHOLE, ANY],
        out_shape=jax.ShapeDtypeStruct((frames, pieces * piece, width), BF),
        scratch_shapes=[
            pltpu.VMEM((pieces, rows, width), F32),
            pltpu.VMEM((frames, pieces * piece, width), F32),
        ],
        compiler_params=params(),
        name="join_pieces",
        cost_estimate=cost(parts.size, 4 * parts.size),
    )(parts, after)


def modulate_kernel(
    act_hbm, affine_ref, weight_hbm, factor_ref, tail_ref, _, hidden_ref, query_ref,
    act_ref, weight_ref, act_sem, weight_sem,
):
    steps, rows, _ = act_ref.shape
    patches = query_ref.shape[1] - PAD
    loads = [
        pltpu.make_async_copy(act_hbm.at[pl.ds(i * rows, rows), :], act_ref.at[i], act_sem.at[i])
        for i in range(steps)
    ]
    weight_load = pltpu.make_async_copy(weight_hbm.at[:, pl.ds(0, HW)], weight_ref, weight_sem)
    loads[0].start()
    weight_load.start()
    for load in loads[1:]:
        load.start()
    for h in range(G):
        query_ref[h, patches:, :] = tail_ref[...]
    for i in range(steps):
        at = slice(i * rows, (i + 1) * rows)
        loads[i].wait()
        act = act_ref[i].astype(F32)
        hidden = act * inverse_rms(act) * (1.0 + affine_ref[0:1, :]) + affine_ref[1:2, :]
        hidden = hidden.astype(BF)
        hidden_ref[at, :] = hidden
        if i == 0:
            weight_load.wait()
        mapped = dot(hidden, weight_ref[...]).astype(BF).astype(F32)
        for h in range(G):
            one = mapped[:, h * C : (h + 1) * C]
            query_ref[h, at, :] = (one * inverse_rms(one) * factor_ref[0, h]).astype(BF)


def modulate(act, affine, weight, factor, tail, after):
    patches, depth = act.shape
    steps = 2
    rows = patches // steps
    return pl.pallas_call(
        modulate_kernel,
        in_specs=[HBM, WHOLE, HBM, SCALARS, WHOLE, ANY],
        out_specs=[WHOLE, WHOLE],
        out_shape=[
            jax.ShapeDtypeStruct((patches, depth), BF),
            jax.ShapeDtypeStruct((G, patches + PAD, C), BF),
        ],
        scratch_shapes=[
            pltpu.VMEM((steps, rows, depth), BF),
            pltpu.VMEM((depth, HW), BF),
            pltpu.SemaphoreType.DMA((steps,)),
            pltpu.SemaphoreType.DMA,
        ],
        compiler_params=params(),
        name="modulate",
        cost_estimate=cost(
            2 * patches * depth * HW, 4 * patches * depth + 2 * depth * HW + 2 * patches * HW
        ),
    )(in_hbm(act), affine, in_hbm(weight), factor, tail, after)


def temporal_entry_kernel(
    quarters, hidden_ref, weight_hbm, factor_ref, _, out_ref, weight_ref, sem
):
    rows = hidden_ref.shape[0] // quarters
    loads = [
        pltpu.make_async_copy(
            weight_hbm.at[:, pl.ds((3 + part) * HW, HW)], weight_ref.at[part], sem.at[part]
        )
        for part in range(3)
    ]
    for load in loads:
        load.start()
    for part in range(3):
        loads[part].wait()
        mapped = dot(hidden_ref[...], weight_ref[part]).astype(BF)
        for h in range(G):
            done = mapped[:, h * C : (h + 1) * C]
            if part < 2:
                one = done.astype(F32)
                one = one * inverse_rms(one)
                if part == 0:
                    one = one * factor_ref[1, h]
                done = one.astype(BF)
            for z in range(quarters):
                out_ref[z, h, part] = done[z * rows : (z + 1) * rows, :]


def temporal_entry(hidden, weight, factor, quarters, after):
    patches, depth = hidden.shape
    rows = patches // quarters
    return pl.pallas_call(
        functools.partial(temporal_entry_kernel, quarters),
        in_specs=[WHOLE, HBM, SCALARS, ANY],
        out_specs=WHOLE,
        out_shape=jax.ShapeDtypeStruct((quarters, G, 3, rows, C), BF),
        scratch_shapes=[pltpu.VMEM((3, depth, HW), BF), pltpu.SemaphoreType.DMA((3,))],
        compiler_params=params(),
        name="temporal_entry",
        cost_estimate=cost(
            6 * patches * depth * HW, 2 * patches * depth + 6 * depth * HW + 6 * patches * HW
        ),
    )(hidden, in_hbm(weight), factor, after)


def temporal_attend_kernel(length_ref, in_ref, _, out_ref):
    frames, _, rows, _ = in_ref.shape
    group = 16
    size = frames * group
    length = length_ref[0]
    row = lax.broadcasted_iota(jnp.int32, (size, size), 0)
    column = lax.broadcasted_iota(jnp.int32, (size, size), 1)
    target, source = row // group, column // group
    keep = (row % group == column % group) & (source <= target) & (source > target - length)
    for g in range(rows // group):
        at = slice(g * group, (g + 1) * group)
        query = in_ref[:, 0, at, :].reshape(size, C)
        key = in_ref[:, 1, at, :].reshape(size, C)
        value = in_ref[:, 2, at, :].reshape(size, C)
        weights = jnp.where(keep, jnp.exp(dot_t(query, key)), 0.0)
        shares = weights / jnp.sum(weights, axis=-1, keepdims=True)
        result = dot(shares.astype(BF), value).astype(BF)
        out_ref[:, at, :] = result.reshape(frames, group, C)


def temporal_attend(length, parts, after):
    frames, _, rows, _ = parts.shape
    return pl.pallas_call(
        temporal_attend_kernel,
        in_specs=[SCALARS, WHOLE, ANY],
        out_shape=jax.ShapeDtypeStruct((frames, rows, C), BF),
        compiler_params=params(),
        name="temporal_attend",
        cost_estimate=cost(4 * frames * rows * 256 * C, 8 * frames * rows * C),
    )(length, parts, after)


def own_attend_kernel(hidden_ref, weight_hbm, query_ref, _, out_ref, weight_ref, sem):
    patches = hidden_ref.shape[0]
    loads = [
        pltpu.make_async_copy(
            weight_hbm.at[:, pl.ds((1 + part) * HW, HW)], weight_ref.at[part], sem.at[part]
        )
        for part in range(2)
    ]
    for load in loads:
        load.start()
    loads[0].wait()
    keys = dot(hidden_ref[...], weight_ref[0]).astype(BF)
    loads[1].wait()
    values = dot(hidden_ref[...], weight_ref[1]).astype(BF)
    ones = jnp.ones((patches, C), BF)
    for h in range(G):
        key = keys[:, h * C : (h + 1) * C].astype(F32)
        key = (key * inverse_rms(key)).astype(BF)
        both = jnp.concatenate([values[:, h * C : (h + 1) * C], ones], axis=1)
        weights = jnp.exp(dot_t(query_ref[h, :patches, :], key)).astype(BF)
        out_ref[h] = dot(weights, both)


def own_attend(hidden, weight, query, after):
    patches, depth = hidden.shape
    return pl.pallas_call(
        own_attend_kernel,
        in_specs=[WHOLE, HBM, WHOLE, ANY],
        out_specs=WHOLE,
        out_shape=jax.ShapeDtypeStruct((G, patches, 2 * C), F32),
        scratch_shapes=[pltpu.VMEM((2, depth, HW), BF), pltpu.SemaphoreType.DMA((2,))],
        compiler_params=params(),
        name="own_attend",
        cost_estimate=cost(
            4 * patches * depth * HW + 6 * patches * patches * HW,
            2 * patches * depth + 4 * depth * HW + 10 * patches * HW,
        ),
    )(hidden, in_hbm(weight), query, after)


LINE = 96


def halves(denominators):
    high = denominators.astype(BF).astype(F32)
    return jnp.concatenate([high, denominators - high], axis=0).astype(BF)


def memory_attend_kernel(carried, index_ref, query_ref, store_ref, *refs):
    out_ref = refs[-1]
    frames = query_ref.shape[0]
    patches = query_ref.shape[1] - PAD
    chunk = 3 * LINE
    row = lax.broadcasted_iota(jnp.int32, (LINE, C), 0)
    column = lax.broadcasted_iota(jnp.int32, (LINE, C), 1)
    for i in range(frames):
        blocks = [store_ref[index_ref[i, j]] for j in range(TOPM)]
        keys = jnp.concatenate([block[:, :C] for block in blocks], axis=0)
        values = jnp.concatenate([block[:, C:] for block in blocks], axis=0)
        both = jnp.concatenate([values, jnp.ones(values.shape, BF)], axis=1)
        carry = None
        if carried is not None and carried[0] <= i < carried[1]:
            carry = refs[0].at[i - carried[0]]
        lines = []
        for start in range(0, patches, chunk):
            at = slice(start, start + chunk)
            weights = jnp.exp(dot_t(query_ref[i, at, :], keys)).astype(BF)
            result = dot(weights, both)
            top = result[:, :C]
            if carry is not None:
                top = top + carry[at, :].astype(F32)
            out_ref[i, at, :] = top.astype(BF)
            for j in range(0, chunk, LINE):
                diagonal = jnp.where(row == column, result[j : j + LINE, C:], 0.0)
                lines.append(jnp.sum(diagonal, axis=0, keepdims=True))
        lines.append(jnp.zeros((8 - len(lines), C), F32))
        total = jnp.concatenate(lines, axis=0)
        if carry is not None:
            tail = carry[patches:, :].astype(F32)
            total = total + tail[:8] + tail[8:]
        out_ref[i, patches:, :] = halves(total)


def memory_attend(index, query, store, after, carry=None, first=0):
    frames, rows, _ = query.shape
    patches = rows - PAD
    quarter = store.shape[1]
    carried, extra = None, []
    if carry is not None:
        carried, extra = (first, first + carry.shape[0]), [carry]
    return pl.pallas_call(
        functools.partial(memory_attend_kernel, carried),
        in_specs=[SCALARS, WHOLE, WHOLE] + [WHOLE] * len(extra) + [ANY],
        out_specs=WHOLE,
        out_shape=jax.ShapeDtypeStruct(query.shape, BF),
        compiler_params=params(),
        name="memory_attend",
        cost_estimate=cost(
            8 * frames * patches * TOPM * quarter * C,
            4 * query.size + 4 * frames * TOPM * quarter * C,
        ),
    )(index, query, store, *extra, after)


def add_partials_kernel(*refs):
    ins, out_ref = refs[:-1], refs[-1]
    patches = out_ref.shape[1] - PAD
    total = ins[0][:, :patches, :].astype(F32)
    tail = ins[0][:, patches:, :].astype(F32)
    for ref in ins[1:]:
        total += ref[:, :patches, :].astype(F32)
        tail += ref[:, patches:, :].astype(F32)
    out_ref[:, :patches, :] = total.astype(BF)
    for i in range(out_ref.shape[0]):
        out_ref[i, patches:, :] = halves(tail[i, :8] + tail[i, 8:])


def add_partials(parts):
    return pl.pallas_call(
        add_partials_kernel,
        out_shape=jax.ShapeDtypeStruct(parts[0].shape, BF),
        compiler_params=params(),
        name="add_partials",
        cost_estimate=cost(4 * parts[0].size, 8 * parts[0].size),
    )(*parts)


def leave_kernel(
    own_ref, memory_ref, time_ref, weight_hbm, out_hbm,
    combined_ref, weight_ref, out_ref, load_sem, store_sem,
):
    patches = own_ref.shape[1]
    quarters = time_ref.shape[0] // G
    rows = time_ref.shape[1]
    steps, _, width = weight_ref.shape
    loads, stores = [], []
    for i in range(steps):
        at = pl.ds(i * width, width)
        loads.append(
            pltpu.make_async_copy(weight_hbm.at[:, at], weight_ref.at[i], load_sem.at[i])
        )
        stores.append(pltpu.make_async_copy(out_ref.at[i], out_hbm.at[:, at], store_sem.at[i]))
    for load in loads:
        load.start()
    row = lax.broadcasted_iota(jnp.int32, (LINE, C), 0)
    column = lax.broadcasted_iota(jnp.int32, (LINE, C), 1)
    for h in range(G):
        tail = memory_ref[h, patches:, :].astype(F32)
        denominators = tail[:8] + tail[8:]
        for j in range(patches // LINE):
            at = slice(j * LINE, (j + 1) * LINE)
            line = jnp.broadcast_to(denominators[j : j + 1, :], (LINE, C))
            memory_sum = jnp.sum(jnp.where(row == column, line, 0.0), axis=1, keepdims=True)
            top = own_ref[h, at, :C] + memory_ref[h, at, :].astype(F32)
            combined_ref[at, h * C : (h + 1) * C] = (
                top / (own_ref[h, at, C:] + memory_sum)
            ).astype(BF)
        for z in range(quarters):
            combined_ref[z * rows : (z + 1) * rows, HW + h * C : HW + (h + 1) * C] = time_ref[
                z * G + h
            ]
    for i in range(steps):
        loads[i].wait()
        out_ref[i] = dot(combined_ref[...], weight_ref[i]).astype(BF)
        stores[i].start()
    for store in stores:
        store.wait()


def leave(own, memory, time, weight):
    patches = own.shape[1]
    depth, width = weight.shape
    steps = 4
    step = width // steps
    return pl.pallas_call(
        leave_kernel,
        in_specs=[WHOLE, WHOLE, WHOLE, HBM],
        out_specs=HBM,
        out_shape=jax.ShapeDtypeStruct((patches, width), BF),
        scratch_shapes=[
            pltpu.VMEM((patches, depth), BF),
            pltpu.VMEM((steps, depth, step), BF),
            pltpu.VMEM((steps, patches, step), BF),
            pltpu.SemaphoreType.DMA((steps,)),
            pltpu.SemaphoreType.DMA((steps,)),
        ],
        compiler_params=params(),
        name="leave",
        cost_estimate=cost(
            2 * patches * depth * width,
            2 * depth * width + 2 * patches * width + 6 * patches * depth,
        ),
    )(own, memory, time, in_hbm(weight))


def on_device(
    patch_activation_tensor,
    conditioning_affine,
    entry_projection_matrix,
    exit_projection_matrix,
    softmax_sharpness,
    cached_past_pairs,
    recalled_picture_holder,
    recalled_picture_position,
    lookback_lengths,
):
    rings = lax.axis_size("z")
    patches, depth = patch_activation_tensor.shape[2:]
    held, piece = cached_past_pairs.shape[:2]
    rolls_y, cores = lax.axis_size("y"), lax.axis_size("c")
    up = [(s, (s + 1) % rings) for s in range(rings)]
    down = [(s, (s - 1) % rings) for s in range(rings)]
    other = [(s, cores - 1 - s) for s in range(cores)]

    def swap(blocks, axes):
        return lax.all_to_all(blocks, axes, split_axis=0, concat_axis=0, tiled=True)

    with jax.named_scope("store"):
        split = split_store(cached_past_pairs.reshape(held * piece, 2 * HW))
        pieces = swap(split, "x")

    with jax.named_scope("queries"):
        factor = softmax_sharpness / C
        index = recalled_picture_holder.reshape(TOPM) * held + recalled_picture_position.reshape(
            TOPM
        )
        tail = jnp.zeros((PAD, C), BF).at[0, :TOPM].set(index.astype(BF))
        hidden, query = modulate(
            patch_activation_tensor.reshape(patches, depth),
            conditioning_affine.reshape(2, depth),
            entry_projection_matrix,
            factor,
            tail,
            after=split,
        )
        here = swap(query, "x")

    with jax.named_scope("store"):
        joined = join_pieces(pieces, held, after=hidden)
        store_above = lax.ppermute(joined, "y", down)
        store_below = lax.ppermute(joined, "y", up)
        store_far = lax.ppermute(store_above, "y", down)
        near = [joined, store_above, store_far, store_below]
        beside = [lax.ppermute(block, "c", other) for block in near]
        store = jnp.concatenate(near + beside, axis=0)

    with jax.named_scope("own"):
        own = own_attend(hidden, entry_projection_matrix, query, after=joined)

    with jax.named_scope("queries"):
        here, own = lax.optimization_barrier((here, own))
        above = lax.ppermute(here, "z", down)
        below = lax.ppermute(here, "z", up)
        far = lax.ppermute(above, "z", down)

    with jax.named_scope("temporal"):
        parts = temporal_entry(hidden, entry_projection_matrix, factor, rings, after=own)
        sent = swap(parts.reshape((rings * G,) + parts.shape[2:]), ("z", "x"))

    def attend(group, after, **more):
        named = group[:, patches, :TOPM].astype(jnp.int32)
        y = (named // (cores * held) - lax.axis_index("y")) & (rolls_y - 1)
        c = (named // held & (cores - 1)) ^ lax.axis_index("c")
        index = (c * rolls_y + y) * held + (named & (held - 1))
        return memory_attend(index, group, store, after, **more)

    with jax.named_scope("memory"):
        sum_far = attend(far, parts)
        carry = lax.ppermute(sum_far, "z", down)
        sum_above = attend(above, sum_far)
        from_below = lax.ppermute(sum_above, "z", up)
        sum_below = attend(below, sum_above, carry=carry)
        from_above = lax.ppermute(sum_below, "z", down)

    with jax.named_scope("temporal"):
        timed = temporal_attend(lookback_lengths, sent, after=sum_below)
        time = swap(timed, ("z", "x"))

    with jax.named_scope("memory"):
        sum_here = attend(here, timed)
        memory = swap(add_partials([sum_here, from_above, from_below]), "x")

    with jax.named_scope("exit"):
        attended = leave(own, memory, time, exit_projection_matrix)
    return attended.reshape(1, 1, patches, depth)


def solution(mesh):
    apart = Mesh(mesh.devices.reshape(4, 2, 4, 4), ("y", "c", "z", "x"))
    roll, frame = ("y", "c"), ("z", "x")
    return jax.shard_map(
        on_device,
        mesh=apart,
        in_specs=(
            P(roll, frame, None, None),
            P(roll, frame, None, None),
            P(),
            P(),
            P(),
            P(roll, frame, None, None),
            P(roll, frame, None, None),
            P(roll, frame, None),
            P(roll),
        ),
        out_specs=P(roll, frame, None, None),
        check_vma=False,
    )
```

```python
import functools

import jax
import jax.numpy as jnp
from jax import lax
from jax.experimental import pallas as pl
from jax.experimental.pallas import tpu as pltpu
from jax.sharding import Mesh
from jax.sharding import PartitionSpec as P

G = 4
C = 128
HW = G * C
TOPM = 6
EPSILON = 1e-06
BF = jnp.bfloat16
F32 = jnp.float32
PAD = 16
VMEM_LIMIT = 28 * 1024 * 1024
ANY = pl.BlockSpec(memory_space=pl.ANY)
HBM = pl.BlockSpec(memory_space=pltpu.HBM)
WHOLE = pl.BlockSpec(memory_space=pltpu.VMEM)
SCALARS = pl.BlockSpec(memory_space=pltpu.SMEM)


def params(**more):
    return pltpu.CompilerParams(vmem_limit_bytes=VMEM_LIMIT, **more)


def cost(flops, bytes_accessed):
    return pl.CostEstimate(
        flops=flops // 16, bytes_accessed=bytes_accessed // 16, transcendentals=0
    )


def in_hbm(array):
    return pltpu.with_memory_space_constraint(array, pltpu.HBM)


def hbm_out(shape, dtype=BF):
    return pltpu.HBM(shape, dtype)


def inverse_rms(values):
    return lax.rsqrt(jnp.mean(values * values, axis=-1, keepdims=True) + EPSILON)


def dot(a, b):
    return jnp.dot(a, b, preferred_element_type=F32)


def dot_t(a, b):
    return lax.dot_general(a, b, (((1,), (1,)), ((), ())), preferred_element_type=F32)


DMA = pltpu.SemaphoreType.DMA
copy = pltpu.make_async_copy


def split_store_kernel(rows_ref, out_hbm, out_ref, sem):
    sends = []
    for h in range(G):
        key = rows_ref[:, h * C : (h + 1) * C].astype(F32)
        out_ref[h, :, :C] = (key * inverse_rms(key)).astype(BF)
        out_ref[h, :, C:] = rows_ref[:, HW + h * C : HW + (h + 1) * C]
        sends.append(copy(out_ref.at[h], out_hbm.at[h], sem.at[h]))
        sends[-1].start()
    for send in sends:
        send.wait()


def split_store(rows):
    n = rows.shape[0]
    return pl.pallas_call(
        split_store_kernel,
        in_specs=[WHOLE],
        out_specs=HBM,
        out_shape=hbm_out((G, n, 2 * C)),
        scratch_shapes=[pltpu.VMEM((G, n, 2 * C), BF), DMA((G,))],
        compiler_params=params(),
        name="split_store",
        cost_estimate=cost(8 * n * HW, 8 * n * HW),
    )(rows)


def join_pieces_kernel(piece, in_hbm, _, out_hbm, in_ref, wide_ref, joined_ref, out_ref, sem):
    pieces = in_ref.shape[0]
    loads = [copy(in_hbm.at[i], in_ref.at[i], sem.at[i]) for i in range(pieces)]
    for load in loads:
        load.start()
    for i in range(pieces):
        loads[i].wait()
        wide_ref[i] = in_ref[i].astype(F32)
        for m in range(out_ref.shape[0]):
            joined_ref[m, i * piece : (i + 1) * piece, :] = wide_ref[
                i, m * piece : (m + 1) * piece, :
            ]
    out_ref[...] = joined_ref[...].astype(BF)
    send = copy(out_ref, out_hbm, sem.at[0])
    send.start()
    send.wait()


def join_pieces(parts, frames, after):
    pieces, rows, width = parts.shape
    piece = rows // frames
    shape = (frames, pieces * piece, width)
    return pl.pallas_call(
        functools.partial(join_pieces_kernel, piece),
        in_specs=[ANY, ANY],
        out_specs=HBM,
        out_shape=hbm_out(shape),
        scratch_shapes=[
            pltpu.VMEM(parts.shape, BF),
            pltpu.VMEM(parts.shape, F32),
            pltpu.VMEM(shape, F32),
            pltpu.VMEM(shape, BF),
            DMA((pieces,)),
        ],
        compiler_params=params(),
        name="join_pieces",
        cost_estimate=cost(parts.size, 4 * parts.size),
    )(parts, in_hbm(after))


def modulate_kernel(
    act_hbm, affine_ref, weight_hbm, factor_ref, tail_ref, _, hidden_hbm, query_hbm,
    act_ref, weight_ref, hidden_ref, query_ref, load_sem, weight_sem, store_sem, query_sem,
):
    steps, rows, _ = act_ref.shape
    patches = query_ref.shape[1] - PAD
    loads, stores = [], []
    for i in range(steps):
        at = pl.ds(i * rows, rows)
        loads.append(copy(act_hbm.at[at, :], act_ref.at[i], load_sem.at[i]))
        stores.append(copy(hidden_ref.at[i], hidden_hbm.at[at, :], store_sem.at[i]))
    weight_load = copy(weight_hbm.at[:, pl.ds(0, HW)], weight_ref, weight_sem)
    loads[0].start()
    weight_load.start()
    for load in loads[1:]:
        load.start()
    for h in range(G):
        query_ref[h, patches:, :] = tail_ref[...]
    for i in range(steps):
        at = slice(i * rows, (i + 1) * rows)
        loads[i].wait()
        act = act_ref[i].astype(F32)
        hidden = act * inverse_rms(act) * (1.0 + affine_ref[0:1, :]) + affine_ref[1:2, :]
        hidden = hidden.astype(BF)
        hidden_ref[i] = hidden
        stores[i].start()
        if i == 0:
            weight_load.wait()
        mapped = dot(hidden, weight_ref[...]).astype(BF).astype(F32)
        for h in range(G):
            one = mapped[:, h * C : (h + 1) * C]
            query_ref[h, at, :] = (one * inverse_rms(one) * factor_ref[0, h]).astype(BF)
    send = copy(query_ref, query_hbm, query_sem)
    send.start()
    for store in stores:
        store.wait()
    send.wait()


def modulate(act, affine, weight, factor, tail, after):
    patches, depth = act.shape
    steps = 2
    rows = patches // steps
    shape = (G, patches + PAD, C)
    return pl.pallas_call(
        modulate_kernel,
        in_specs=[HBM, WHOLE, HBM, SCALARS, WHOLE, ANY],
        out_specs=[HBM, HBM],
        out_shape=[hbm_out((patches, depth)), hbm_out(shape)],
        scratch_shapes=[
            pltpu.VMEM((steps, rows, depth), BF),
            pltpu.VMEM((depth, HW), BF),
            pltpu.VMEM((steps, rows, depth), BF),
            pltpu.VMEM(shape, BF),
            DMA((steps,)),
            DMA,
            DMA((steps,)),
            DMA,
        ],
        compiler_params=params(),
        name="modulate",
        cost_estimate=cost(
            2 * patches * depth * HW, 4 * patches * depth + 2 * depth * HW + 2 * patches * HW
        ),
    )(in_hbm(act), affine, in_hbm(weight), factor, tail, in_hbm(after))


def temporal_entry_kernel(
    quarters, hidden_hbm, weight_hbm, factor_ref, out_hbm,
    hidden_ref, weight_ref, out_ref, hidden_sem, weight_sem, store_sem,
):
    rows = hidden_ref.shape[0] // quarters
    hidden_load = copy(hidden_hbm, hidden_ref, hidden_sem)
    loads = [
        copy(
            weight_hbm.at[:, pl.ds((3 + part) * HW, HW)], weight_ref.at[part], weight_sem.at[part]
        )
        for part in range(3)
    ]
    loads[0].start()
    hidden_load.start()
    for load in loads[1:]:
        load.start()
    hidden_load.wait()
    stores = []
    for part in range(3):
        loads[part].wait()
        mapped = dot(hidden_ref[...], weight_ref[part]).astype(BF)
        for h in range(G):
            done = mapped[:, h * C : (h + 1) * C]
            if part < 2:
                one = done.astype(F32)
                one = one * inverse_rms(one)
                if part == 0:
                    one = one * factor_ref[1, h]
                done = one.astype(BF)
            for z in range(quarters):
                out_ref[part, z, h] = done[z * rows : (z + 1) * rows, :]
        stores.append(copy(out_ref.at[part], out_hbm.at[:, :, part], store_sem.at[part]))
        stores[-1].start()
    for store in stores:
        store.wait()


def temporal_entry(hidden, weight, factor, quarters):
    patches, depth = hidden.shape
    rows = patches // quarters
    return pl.pallas_call(
        functools.partial(temporal_entry_kernel, quarters),
        in_specs=[HBM, HBM, SCALARS],
        out_specs=HBM,
        out_shape=hbm_out((quarters, G, 3, rows, C)),
        scratch_shapes=[
            pltpu.VMEM((patches, depth), BF),
            pltpu.VMEM((3, depth, HW), BF),
            pltpu.VMEM((3, quarters, G, rows, C), BF),
            DMA,
            DMA((3,)),
            DMA((3,)),
        ],
        compiler_params=params(),
        name="temporal_entry",
        cost_estimate=cost(
            6 * patches * depth * HW, 2 * patches * depth + 6 * depth * HW + 6 * patches * HW
        ),
    )(in_hbm(hidden), in_hbm(weight), factor)


def temporal_attend_kernel(length_ref, in_hbm_ref, _, out_hbm, in_ref, out_ref, sem):
    frames, _, rows, _ = in_ref.shape
    group = 16
    size = frames * group
    load = copy(in_hbm_ref, in_ref, sem)
    load.start()
    length = length_ref[0]
    row = lax.broadcasted_iota(jnp.int32, (size, size), 0)
    column = lax.broadcasted_iota(jnp.int32, (size, size), 1)
    target, source = row // group, column // group
    keep = (row % group == column % group) & (source <= target) & (source > target - length)
    load.wait()
    for g in range(rows // group):
        at = slice(g * group, (g + 1) * group)
        query = in_ref[:, 0, at, :].reshape(size, C)
        key = in_ref[:, 1, at, :].reshape(size, C)
        value = in_ref[:, 2, at, :].reshape(size, C)
        weights = jnp.where(keep, jnp.exp(dot_t(query, key)), 0.0)
        shares = weights / jnp.sum(weights, axis=-1, keepdims=True)
        result = dot(shares.astype(BF), value).astype(BF)
        out_ref[:, at, :] = result.reshape(frames, group, C)
    store = copy(out_ref, out_hbm, sem)
    store.start()
    store.wait()


def temporal_attend(length, parts, after):
    frames, _, rows, _ = parts.shape
    shape = (frames, rows, C)
    return pl.pallas_call(
        temporal_attend_kernel,
        in_specs=[SCALARS, ANY, ANY],
        out_specs=HBM,
        out_shape=hbm_out(shape),
        scratch_shapes=[pltpu.VMEM(parts.shape, BF), pltpu.VMEM(shape, BF), DMA],
        compiler_params=params(),
        name="temporal_attend",
        cost_estimate=cost(4 * frames * rows * 256 * C, 8 * frames * rows * C),
    )(length, parts, in_hbm(after))


LINE = 96
CHUNK = 3 * LINE


def halves(denominators):
    high = denominators.astype(BF).astype(F32)
    return jnp.concatenate([high, denominators - high], axis=0).astype(BF)


def attend_rows(query, keys, both, out_ref):
    patches = out_ref.shape[0] - PAD
    row = lax.broadcasted_iota(jnp.int32, (LINE, C), 0)
    column = lax.broadcasted_iota(jnp.int32, (LINE, C), 1)
    lines = []
    for start in range(0, patches, CHUNK):
        at = slice(start, start + CHUNK)
        weights = jnp.exp(dot_t(query(at), keys)).astype(BF)
        result = dot(weights, both)
        out_ref[at, :] = result[:, :C].astype(BF)
        for j in range(0, CHUNK, LINE):
            diagonal = jnp.where(row == column, result[j : j + LINE, C:], 0.0)
            lines.append(jnp.sum(diagonal, axis=0, keepdims=True))
    lines.append(jnp.zeros((8 - len(lines), C), F32))
    out_ref[patches:, :] = halves(jnp.concatenate(lines, axis=0))


def with_ones(values):
    return jnp.concatenate([values, jnp.ones(values.shape, BF)], axis=1)


def own_attend_kernel(
    hidden_hbm, weight_hbm, query_hbm, _, out_hbm,
    hidden_ref, weight_ref, query_ref, out_ref, hidden_sem, weight_sem, query_sem, store_sem,
):
    hidden_load = copy(hidden_hbm, hidden_ref, hidden_sem)
    query_load = copy(query_hbm, query_ref, query_sem)
    loads = [
        copy(
            weight_hbm.at[:, pl.ds((1 + part) * HW, HW)], weight_ref.at[part], weight_sem.at[part]
        )
        for part in range(2)
    ]
    loads[0].start()
    hidden_load.start()
    loads[1].start()
    query_load.start()
    hidden_load.wait()
    loads[0].wait()
    keys = dot(hidden_ref[...], weight_ref[0]).astype(BF)
    loads[1].wait()
    values = dot(hidden_ref[...], weight_ref[1]).astype(BF)
    query_load.wait()
    stores = []
    for h in range(G):
        key = keys[:, h * C : (h + 1) * C].astype(F32)
        key = (key * inverse_rms(key)).astype(BF)
        both = with_ones(values[:, h * C : (h + 1) * C])
        attend_rows(lambda at, h=h: query_ref[h, at, :], key, both, out_ref.at[h])
        stores.append(copy(out_ref.at[h], out_hbm.at[h], store_sem.at[h]))
        stores[-1].start()
    for store in stores:
        store.wait()


def own_attend(hidden, weight, query, after):
    patches, depth = hidden.shape
    return pl.pallas_call(
        own_attend_kernel,
        in_specs=[HBM, HBM, HBM, ANY],
        out_specs=HBM,
        out_shape=hbm_out(query.shape),
        scratch_shapes=[
            pltpu.VMEM((patches, depth), BF),
            pltpu.VMEM((2, depth, HW), BF),
            pltpu.VMEM(query.shape, BF),
            pltpu.VMEM(query.shape, BF),
            DMA,
            DMA((2,)),
            DMA,
            DMA((G,)),
        ],
        compiler_params=params(),
        name="own_attend",
        cost_estimate=cost(
            4 * patches * depth * HW + 6 * patches * patches * HW,
            2 * patches * depth + 4 * depth * HW + 10 * patches * HW,
        ),
    )(in_hbm(hidden), in_hbm(weight), in_hbm(query), in_hbm(after))


def memory_attend_kernel(count, index_ref, query_hbm, *refs):
    blocks = refs[:count]
    out_hbm, query_ref, store_ref, out_ref, query_sem, block_sem, store_sem = refs[count + 1 :]
    frames = query_ref.shape[0]
    held = blocks[0].shape[0]
    loads = [
        copy(blocks[i], store_ref.at[pl.ds(i * held, held)], block_sem.at[i]) for i in range(count)
    ]
    query_load = copy(query_hbm, query_ref, query_sem)
    for load in loads:
        load.start()
    query_load.start()
    for load in loads:
        load.wait()
    query_load.wait()
    stores = []
    for i in range(frames):
        chosen = [store_ref[index_ref[i, j]] for j in range(TOPM)]
        keys = jnp.concatenate([block[:, :C] for block in chosen], axis=0)
        values = jnp.concatenate([block[:, C:] for block in chosen], axis=0)
        attend_rows(lambda at, i=i: query_ref[i, at, :], keys, with_ones(values), out_ref.at[i])
        stores.append(copy(out_ref.at[i], out_hbm.at[i], store_sem.at[i]))
        stores[-1].start()
    for store in stores:
        store.wait()


def memory_attend(index, query, blocks, after):
    frames, rows, _ = query.shape
    held, quarter, width = blocks[0].shape
    count = len(blocks)
    return pl.pallas_call(
        functools.partial(memory_attend_kernel, count),
        in_specs=[SCALARS, ANY] + [ANY] * count + [ANY],
        out_specs=HBM,
        out_shape=hbm_out(query.shape),
        scratch_shapes=[
            pltpu.VMEM(query.shape, BF),
            pltpu.VMEM((count * held, quarter, width), BF),
            pltpu.VMEM(query.shape, BF),
            DMA,
            DMA((count,)),
            DMA((frames,)),
        ],
        compiler_params=params(),
        name="memory_attend",
        cost_estimate=cost(
            8 * frames * rows * TOPM * quarter * C,
            4 * query.size + 2 * count * held * quarter * width,
        ),
    )(index, query, *blocks, in_hbm(after))


def add_partials_kernel(*refs):
    ins, out_hbm, parts_ref, out_ref, load_sem, store_sem = (
        refs[: len(refs) - 5], *refs[len(refs) - 5 :],
    )
    frames = out_ref.shape[0]
    patches = out_ref.shape[1] - PAD
    loads = [
        [copy(ref.at[i], parts_ref.at[k, i], load_sem.at[k, i]) for k, ref in enumerate(ins)]
        for i in range(frames)
    ]
    for of_frame in loads:
        for load in of_frame:
            load.start()
    stores = []
    for i in range(frames):
        for load in loads[i]:
            load.wait()
        total = parts_ref[0, i].astype(F32)
        for k in range(1, len(ins)):
            total = total + parts_ref[k, i].astype(F32)
        out_ref[i, :patches, :] = total[:patches].astype(BF)
        out_ref[i, patches:, :] = halves(total[patches : patches + 8] + total[patches + 8 :])
        stores.append(copy(out_ref.at[i], out_hbm.at[i], store_sem.at[i]))
        stores[-1].start()
    for store in stores:
        store.wait()


def add_partials(parts):
    shape = parts[0].shape
    frames = shape[0]
    return pl.pallas_call(
        add_partials_kernel,
        in_specs=[ANY] * len(parts),
        out_specs=HBM,
        out_shape=hbm_out(shape),
        scratch_shapes=[
            pltpu.VMEM((len(parts),) + shape, BF),
            pltpu.VMEM(shape, BF),
            DMA((len(parts), frames)),
            DMA((frames,)),
        ],
        compiler_params=params(),
        name="add_partials",
        cost_estimate=cost(4 * parts[0].size, 8 * parts[0].size),
    )(*parts)


def leave_kernel(
    own_hbm, memory_hbm, time_hbm, weight_hbm, out_hbm,
    own_ref, memory_ref, time_ref, combined_ref, weight_ref, out_ref,
    own_sem, memory_sem, time_sem, weight_sem, store_sem,
):
    patches = own_ref.shape[1] - PAD
    quarters = time_ref.shape[0] // G
    rows = time_ref.shape[1]
    steps, _, width = weight_ref.shape
    own_loads = [copy(own_hbm.at[h], own_ref.at[h], own_sem.at[h]) for h in range(G)]
    memory_loads = [copy(memory_hbm.at[h], memory_ref.at[h], memory_sem.at[h]) for h in range(G)]
    time_load = copy(time_hbm, time_ref, time_sem)
    loads, stores = [], []
    for i in range(steps):
        at = pl.ds(i * width, width)
        loads.append(copy(weight_hbm.at[:, at], weight_ref.at[i], weight_sem.at[i]))
        stores.append(copy(out_ref.at[i], out_hbm.at[:, at], store_sem.at[i]))
    for load in own_loads + memory_loads + [time_load] + loads:
        load.start()
    row = lax.broadcasted_iota(jnp.int32, (LINE, C), 0)
    column = lax.broadcasted_iota(jnp.int32, (LINE, C), 1)
    for h in range(G):
        own_loads[h].wait()
        memory_loads[h].wait()
        tail = own_ref[h, patches:, :].astype(F32) + memory_ref[h, patches:, :].astype(F32)
        denominators = tail[:8] + tail[8:]
        for j in range(patches // LINE):
            at = slice(j * LINE, (j + 1) * LINE)
            line = jnp.broadcast_to(denominators[j : j + 1, :], (LINE, C))
            total = jnp.sum(jnp.where(row == column, line, 0.0), axis=1, keepdims=True)
            top = own_ref[h, at, :].astype(F32) + memory_ref[h, at, :].astype(F32)
            combined_ref[at, h * C : (h + 1) * C] = (top / total).astype(BF)
    time_load.wait()
    for h in range(G):
        for z in range(quarters):
            combined_ref[z * rows : (z + 1) * rows, HW + h * C : HW + (h + 1) * C] = time_ref[
                z * G + h
            ]
    for i in range(steps):
        loads[i].wait()
        out_ref[i] = dot(combined_ref[...], weight_ref[i]).astype(BF)
        stores[i].start()
    for store in stores:
        store.wait()


def leave(own, memory, time, weight):
    patches = own.shape[1] - PAD
    depth, width = weight.shape
    steps = 4
    step = width // steps
    return pl.pallas_call(
        leave_kernel,
        in_specs=[HBM, ANY, ANY, HBM],
        out_specs=HBM,
        out_shape=hbm_out((patches, width)),
        scratch_shapes=[
            pltpu.VMEM(own.shape, BF),
            pltpu.VMEM(memory.shape, BF),
            pltpu.VMEM(time.shape, BF),
            pltpu.VMEM((patches, depth), BF),
            pltpu.VMEM((steps, depth, step), BF),
            pltpu.VMEM((steps, patches, step), BF),
            DMA((G,)),
            DMA((G,)),
            DMA,
            DMA((steps,)),
            DMA((steps,)),
        ],
        compiler_params=params(),
        name="leave",
        cost_estimate=cost(
            2 * patches * depth * width,
            2 * depth * width + 2 * patches * width + 6 * patches * depth,
        ),
    )(in_hbm(own), memory, time, in_hbm(weight))


def on_device(
    patch_activation_tensor,
    conditioning_affine,
    entry_projection_matrix,
    exit_projection_matrix,
    softmax_sharpness,
    cached_past_pairs,
    recalled_picture_holder,
    recalled_picture_position,
    lookback_lengths,
):
    rings = lax.axis_size("z")
    patches, depth = patch_activation_tensor.shape[2:]
    held, piece = cached_past_pairs.shape[:2]
    rolls_y, cores = lax.axis_size("y"), lax.axis_size("c")

    def turn(step):
        return [(s, (s + step) % rings) for s in range(rings)]

    other = [(s, cores - 1 - s) for s in range(cores)]

    def swap(blocks, axes):
        return lax.all_to_all(blocks, axes, split_axis=0, concat_axis=0, tiled=True)

    with jax.named_scope("store"):
        split = split_store(cached_past_pairs.reshape(held * piece, 2 * HW))
        pieces = swap(split, "x")

    with jax.named_scope("queries"):
        factor = softmax_sharpness / C
        index = recalled_picture_holder.reshape(TOPM) * held + recalled_picture_position.reshape(
            TOPM
        )
        tail = jnp.zeros((PAD, C), BF).at[0, :TOPM].set(index.astype(BF))
        hidden, query = modulate(
            patch_activation_tensor.reshape(patches, depth),
            conditioning_affine.reshape(2, depth),
            entry_projection_matrix,
            factor,
            tail,
            after=split,
        )
        here = swap(query, "x")

    with jax.named_scope("temporal"):
        parts = temporal_entry(hidden, entry_projection_matrix, factor, rings)

    with jax.named_scope("store"):
        joined = join_pieces(pieces, held, after=parts)
        near = [joined] + [lax.ppermute(joined, "y", turn(-step)) for step in (1, 2, 3)]
        beside = [lax.ppermute(block, "c", other) for block in near]

    with jax.named_scope("queries"):
        here, joined = lax.optimization_barrier((here, joined))
        groups = [here] + [lax.ppermute(here, "z", turn(-step)) for step in (1, 2, 3)]

    with jax.named_scope("temporal"):
        sent = swap(parts.reshape((rings * G,) + parts.shape[2:]), ("z", "x"))

    with jax.named_scope("own"):
        own = own_attend(hidden, entry_projection_matrix, query, after=joined)

    def attend(group, after):
        named = group[:, patches, :TOPM].astype(jnp.int32)
        y = (named // (cores * held) - lax.axis_index("y")) & (rolls_y - 1)
        c = (named // held & (cores - 1)) ^ lax.axis_index("c")
        index = (c * rolls_y + y) * held + (named & (held - 1))
        return memory_attend(index, group, near + beside, after)

    with jax.named_scope("memory"):
        after, sums = own, []
        for step in (2, 1, 3):
            after = attend(groups[step], after)
            sums.append(lax.ppermute(after, "z", turn(step)))
        sum_here = attend(here, after)

    with jax.named_scope("temporal"):
        timed = temporal_attend(lookback_lengths, sent, after=sum_here)
        time = swap(timed, ("z", "x"))

    with jax.named_scope("memory"):
        memory = swap(add_partials([sum_here] + sums), "x")

    with jax.named_scope("exit"):
        attended = leave(own, memory, time, exit_projection_matrix)
    return attended.reshape(1, 1, patches, depth)


def solution(mesh):
    apart = Mesh(mesh.devices.reshape(4, 2, 4, 4), ("y", "c", "z", "x"))
    roll, frame = ("y", "c"), ("z", "x")
    return jax.shard_map(
        on_device,
        mesh=apart,
        in_specs=(
            P(roll, frame, None, None),
            P(roll, frame, None, None),
            P(),
            P(),
            P(),
            P(roll, frame, None, None),
            P(roll, frame, None, None),
            P(roll, frame, None),
            P(roll),
        ),
        out_specs=P(roll, frame, None, None),
        check_vma=False,
    )
```

```python
import functools

import jax
import jax.numpy as jnp
from jax import lax
from jax.experimental import pallas as pl
from jax.experimental.pallas import tpu as pltpu
from jax.sharding import Mesh
from jax.sharding import PartitionSpec as P

G = 4
C = 128
HW = G * C
TOPM = 6
EPSILON = 1e-06
BF = jnp.bfloat16
F32 = jnp.float32
PAD = 16
VMEM_LIMIT = 28 * 1024 * 1024
ANY = pl.BlockSpec(memory_space=pl.ANY)
HBM = pl.BlockSpec(memory_space=pltpu.HBM)
WHOLE = pl.BlockSpec(memory_space=pltpu.VMEM)
SCALARS = pl.BlockSpec(memory_space=pltpu.SMEM)


def params(**more):
    return pltpu.CompilerParams(vmem_limit_bytes=VMEM_LIMIT, **more)


def cost(flops, bytes_accessed):
    return pl.CostEstimate(
        flops=flops // 16, bytes_accessed=bytes_accessed // 16, transcendentals=0
    )


def in_hbm(array):
    return pltpu.with_memory_space_constraint(array, pltpu.HBM)


def hbm_out(shape, dtype=BF):
    return pltpu.HBM(shape, dtype)


def inverse_rms(values):
    return lax.rsqrt(jnp.mean(values * values, axis=-1, keepdims=True) + EPSILON)


def dot(a, b):
    return jnp.dot(a, b, preferred_element_type=F32)


def dot_t(a, b):
    return lax.dot_general(a, b, (((1,), (1,)), ((), ())), preferred_element_type=F32)


DMA = pltpu.SemaphoreType.DMA
copy = pltpu.make_async_copy


def split_store_kernel(x_ref, rows_ref, *refs):
    outs, out_ref, sem = refs[:G], refs[G], refs[G + 1]
    sends = []
    for j in range(G):
        start = lax.rem(x_ref[0] + j, G) * C
        key = rows_ref[:, pl.ds(pl.multiple_of(start, C), C)].astype(F32)
        out_ref[j, :, :C] = (key * inverse_rms(key)).astype(BF)
        out_ref[j, :, C:] = rows_ref[:, pl.ds(pl.multiple_of(HW + start, C), C)]
        sends.append(copy(out_ref.at[j], outs[j], sem.at[j]))
        sends[-1].start()
    for send in sends:
        send.wait()


def split_store(x, rows):
    n = rows.shape[0]
    return pl.pallas_call(
        split_store_kernel,
        in_specs=[SCALARS, WHOLE],
        out_specs=[HBM] * G,
        out_shape=[hbm_out((n, 2 * C))] * G,
        scratch_shapes=[pltpu.VMEM((G, n, 2 * C), BF), DMA((G,))],
        compiler_params=params(),
        name="split_store",
        cost_estimate=cost(8 * n * HW, 8 * n * HW),
    )(x, rows)


def join_pieces_kernel(pieces, *refs):
    ins = refs[:pieces]
    out_hbm, in_ref, wide_ref, joined_ref, out_ref, sem = refs[pieces + 1 :]
    frames = out_ref.shape[0]
    piece = in_ref.shape[1] // frames
    loads = [copy(ins[i], in_ref.at[i], sem.at[i]) for i in range(pieces)]
    for load in loads:
        load.start()
    for i in range(pieces):
        loads[i].wait()
        wide_ref[i] = in_ref[i].astype(F32)
        for m in range(frames):
            joined_ref[m, i * piece : (i + 1) * piece, :] = wide_ref[
                i, m * piece : (m + 1) * piece, :
            ]
    out_ref[...] = joined_ref[...].astype(BF)
    send = copy(out_ref, out_hbm, sem.at[0])
    send.start()
    send.wait()


def join_pieces(parts, frames, after):
    pieces = len(parts)
    rows, width = parts[0].shape
    shape = (frames, pieces * rows // frames, width)
    return pl.pallas_call(
        functools.partial(join_pieces_kernel, pieces),
        in_specs=[ANY] * (pieces + 1),
        out_specs=HBM,
        out_shape=hbm_out(shape),
        scratch_shapes=[
            pltpu.VMEM((pieces, rows, width), BF),
            pltpu.VMEM((pieces, rows, width), F32),
            pltpu.VMEM(shape, F32),
            pltpu.VMEM(shape, BF),
            DMA((pieces,)),
        ],
        compiler_params=params(),
        name="join_pieces",
        cost_estimate=cost(pieces * rows * width, 4 * pieces * rows * width),
    )(*parts, in_hbm(after))


def modulate_kernel(
    act_hbm, affine_ref, weight_hbm, factor_ref, tail_ref, _, hidden_hbm, query_hbm,
    act_ref, weight_ref, hidden_ref, query_ref, load_sem, weight_sem, store_sem, query_sem,
):
    steps, rows, _ = act_ref.shape
    patches = query_ref.shape[1] - PAD
    loads, stores = [], []
    for i in range(steps):
        at = pl.ds(i * rows, rows)
        loads.append(copy(act_hbm.at[at, :], act_ref.at[i], load_sem.at[i]))
        stores.append(copy(hidden_ref.at[i], hidden_hbm.at[at, :], store_sem.at[i]))
    weight_load = copy(weight_hbm.at[:, pl.ds(0, HW)], weight_ref, weight_sem)
    loads[0].start()
    weight_load.start()
    for h in range(G):
        query_ref[h, patches:, :] = tail_ref[...]
    for i in range(steps):
        at = slice(i * rows, (i + 1) * rows)
        loads[i].wait()
        if i + 1 < steps:
            loads[i + 1].start()
        act = act_ref[i].astype(F32)
        hidden = act * inverse_rms(act) * (1.0 + affine_ref[0:1, :]) + affine_ref[1:2, :]
        hidden = hidden.astype(BF)
        hidden_ref[i] = hidden
        stores[i].start()
        if i == 0:
            weight_load.wait()
        mapped = dot(hidden, weight_ref[...]).astype(BF).astype(F32)
        for h in range(G):
            one = mapped[:, h * C : (h + 1) * C]
            query_ref[h, at, :] = (one * inverse_rms(one) * factor_ref[0, h]).astype(BF)
    send = copy(query_ref, query_hbm, query_sem)
    send.start()
    for store in stores:
        store.wait()
    send.wait()


def modulate(act, affine, weight, factor, tail, after):
    patches, depth = act.shape
    steps = 2
    rows = patches // steps
    shape = (G, patches + PAD, C)
    return pl.pallas_call(
        modulate_kernel,
        in_specs=[HBM, WHOLE, HBM, SCALARS, WHOLE, ANY],
        out_specs=[HBM, HBM],
        out_shape=[hbm_out((patches, depth)), hbm_out(shape)],
        scratch_shapes=[
            pltpu.VMEM((steps, rows, depth), BF),
            pltpu.VMEM((depth, HW), BF),
            pltpu.VMEM((steps, rows, depth), BF),
            pltpu.VMEM(shape, BF),
            DMA((steps,)),
            DMA,
            DMA((steps,)),
            DMA,
        ],
        compiler_params=params(),
        name="modulate",
        cost_estimate=cost(
            2 * patches * depth * HW, 4 * patches * depth + 2 * depth * HW + 2 * patches * HW
        ),
    )(in_hbm(act), affine, in_hbm(weight), factor, tail, in_hbm(after))


def temporal_entry_kernel(
    quarters, hidden_hbm, weight_hbm, factor_ref, _, out_hbm,
    hidden_ref, weight_ref, out_ref, hidden_sem, weight_sem, store_sem,
):
    rows = hidden_ref.shape[0] // quarters
    hidden_load = copy(hidden_hbm, hidden_ref, hidden_sem)
    loads = [
        copy(
            weight_hbm.at[:, pl.ds((3 + part) * HW, HW)], weight_ref.at[part], weight_sem.at[part]
        )
        for part in range(3)
    ]
    hidden_load.start()
    loads[0].start()
    hidden_load.wait()
    stores = []
    for part in range(3):
        loads[part].wait()
        if part < 2:
            loads[part + 1].start()
        mapped = dot(hidden_ref[...], weight_ref[part]).astype(BF)
        for h in range(G):
            done = mapped[:, h * C : (h + 1) * C]
            if part < 2:
                one = done.astype(F32)
                one = one * inverse_rms(one)
                if part == 0:
                    one = one * factor_ref[1, h]
                done = one.astype(BF)
            for z in range(quarters):
                out_ref[part, z, h] = done[z * rows : (z + 1) * rows, :]
        stores.append(copy(out_ref.at[part], out_hbm.at[:, :, part], store_sem.at[part]))
        stores[-1].start()
    for store in stores:
        store.wait()


def temporal_entry(hidden, weight, factor, quarters, after):
    patches, depth = hidden.shape
    rows = patches // quarters
    return pl.pallas_call(
        functools.partial(temporal_entry_kernel, quarters),
        in_specs=[HBM, HBM, SCALARS, ANY],
        out_specs=HBM,
        out_shape=hbm_out((quarters, G, 3, rows, C)),
        scratch_shapes=[
            pltpu.VMEM((patches, depth), BF),
            pltpu.VMEM((3, depth, HW), BF),
            pltpu.VMEM((3, quarters, G, rows, C), BF),
            DMA,
            DMA((3,)),
            DMA((3,)),
        ],
        compiler_params=params(),
        name="temporal_entry",
        cost_estimate=cost(
            6 * patches * depth * HW, 2 * patches * depth + 6 * depth * HW + 6 * patches * HW
        ),
    )(in_hbm(hidden), in_hbm(weight), factor, in_hbm(after))


def temporal_attend_kernel(length_ref, in_hbm_ref, _, out_hbm, in_ref, out_ref, sem):
    frames, _, rows, _ = in_ref.shape
    group = 16
    size = frames * group
    load = copy(in_hbm_ref, in_ref, sem)
    load.start()
    length = length_ref[0]
    row = lax.broadcasted_iota(jnp.int32, (size, size), 0)
    column = lax.broadcasted_iota(jnp.int32, (size, size), 1)
    target, source = row // group, column // group
    keep = (row % group == column % group) & (source <= target) & (source > target - length)
    load.wait()
    for g in range(rows // group):
        at = slice(g * group, (g + 1) * group)
        query = in_ref[:, 0, at, :].reshape(size, C)
        key = in_ref[:, 1, at, :].reshape(size, C)
        value = in_ref[:, 2, at, :].reshape(size, C)
        weights = jnp.where(keep, jnp.exp(dot_t(query, key)), 0.0)
        shares = weights / jnp.sum(weights, axis=-1, keepdims=True)
        result = dot(shares.astype(BF), value).astype(BF)
        out_ref[:, at, :] = result.reshape(frames, group, C)
    store = copy(out_ref, out_hbm, sem)
    store.start()
    store.wait()


def temporal_attend(length, parts, after):
    frames, _, rows, _ = parts.shape
    shape = (frames, rows, C)
    return pl.pallas_call(
        temporal_attend_kernel,
        in_specs=[SCALARS, ANY, ANY],
        out_specs=HBM,
        out_shape=hbm_out(shape),
        scratch_shapes=[pltpu.VMEM(parts.shape, BF), pltpu.VMEM(shape, BF), DMA],
        compiler_params=params(),
        name="temporal_attend",
        cost_estimate=cost(4 * frames * rows * 256 * C, 8 * frames * rows * C),
    )(length, parts, in_hbm(after))


LINE = 96
CHUNK = 3 * LINE


def halves(denominators):
    high = denominators.astype(BF).astype(F32)
    return jnp.concatenate([high, denominators - high], axis=0).astype(BF)


def attend_rows(query, keys, both, out_ref):
    patches = out_ref.shape[0] - PAD
    row = lax.broadcasted_iota(jnp.int32, (LINE, C), 0)
    column = lax.broadcasted_iota(jnp.int32, (LINE, C), 1)
    lines = []
    for start in range(0, patches, CHUNK):
        at = slice(start, start + CHUNK)
        weights = jnp.exp(dot_t(query(at), keys)).astype(BF)
        result = dot(weights, both)
        out_ref[at, :] = result[:, :C].astype(BF)
        for j in range(0, CHUNK, LINE):
            diagonal = jnp.where(row == column, result[j : j + LINE, C:], 0.0)
            lines.append(jnp.sum(diagonal, axis=0, keepdims=True))
    lines.append(jnp.zeros((8 - len(lines), C), F32))
    out_ref[patches:, :] = halves(jnp.concatenate(lines, axis=0))


def with_ones(values):
    return jnp.concatenate([values, jnp.ones(values.shape, BF)], axis=1)


def own_attend_kernel(
    hidden_hbm, weight_hbm, query_hbm, _, out_hbm,
    hidden_ref, weight_ref, query_ref, out_ref, hidden_sem, weight_sem, query_sem, store_sem,
):
    hidden_load = copy(hidden_hbm, hidden_ref, hidden_sem)
    query_load = copy(query_hbm, query_ref, query_sem)
    loads = [
        copy(
            weight_hbm.at[:, pl.ds((1 + part) * HW, HW)], weight_ref.at[part], weight_sem.at[part]
        )
        for part in range(2)
    ]
    hidden_load.start()
    loads[0].start()
    hidden_load.wait()
    loads[0].wait()
    loads[1].start()
    query_load.start()
    keys = dot(hidden_ref[...], weight_ref[0]).astype(BF)
    loads[1].wait()
    values = dot(hidden_ref[...], weight_ref[1]).astype(BF)
    query_load.wait()
    stores = []
    for h in range(G):
        key = keys[:, h * C : (h + 1) * C].astype(F32)
        key = (key * inverse_rms(key)).astype(BF)
        both = with_ones(values[:, h * C : (h + 1) * C])
        attend_rows(lambda at, h=h: query_ref[h, at, :], key, both, out_ref.at[h])
        stores.append(copy(out_ref.at[h], out_hbm.at[h], store_sem.at[h]))
        stores[-1].start()
    for store in stores:
        store.wait()


def own_attend(hidden, weight, query, after):
    patches, depth = hidden.shape
    return pl.pallas_call(
        own_attend_kernel,
        in_specs=[HBM, HBM, HBM, ANY],
        out_specs=HBM,
        out_shape=hbm_out(query.shape),
        scratch_shapes=[
            pltpu.VMEM((patches, depth), BF),
            pltpu.VMEM((2, depth, HW), BF),
            pltpu.VMEM(query.shape, BF),
            pltpu.VMEM(query.shape, BF),
            DMA,
            DMA((2,)),
            DMA,
            DMA((G,)),
        ],
        compiler_params=params(),
        name="own_attend",
        cost_estimate=cost(
            4 * patches * depth * HW + 6 * patches * patches * HW,
            2 * patches * depth + 4 * depth * HW + 10 * patches * HW,
        ),
    )(in_hbm(hidden), in_hbm(weight), in_hbm(query), in_hbm(after))


def memory_attend_kernel(groups, count, index_ref, *refs):
    queries, blocks = refs[:groups], refs[groups : groups + count]
    outs = refs[groups + count + 1 : 2 * groups + count + 1]
    query_ref, store_ref, out_ref, query_sem, block_sem, store_sem = refs[2 * groups + count + 1 :]
    frames = queries[0].shape[0]
    loads, start = [], 0
    for i, block in enumerate(blocks):
        held = block.shape[0]
        loads.append(copy(block, store_ref.at[pl.ds(start, held)], block_sem.at[i]))
        start += held
    query_loads = [copy(queries[k], query_ref.at[k], query_sem.at[k]) for k in range(groups)]
    for load in query_loads[:1] + loads + query_loads[1:]:
        load.start()
    for load in loads:
        load.wait()
    stores = []
    for k in range(groups):
        query_loads[k].wait()
        for i in range(frames):
            chosen = [store_ref[index_ref[k * frames + i, j]] for j in range(TOPM)]
            keys = jnp.concatenate([block[:, :C] for block in chosen], axis=0)
            values = jnp.concatenate([block[:, C:] for block in chosen], axis=0)
            attend_rows(
                lambda at, k=k, i=i: query_ref[k, i, at, :],
                keys,
                with_ones(values),
                out_ref.at[k, i],
            )
            stores.append(copy(out_ref.at[k, i], outs[k].at[i], store_sem.at[k, i]))
            stores[-1].start()
    for store in stores:
        store.wait()


def memory_attend(index, queries, blocks, after):
    groups, count = len(queries), len(blocks)
    frames, rows, _ = queries[0].shape
    _, quarter, width = blocks[0].shape
    total = sum(block.shape[0] for block in blocks)
    shape = (groups, frames, rows, C)
    return pl.pallas_call(
        functools.partial(memory_attend_kernel, groups, count),
        in_specs=[SCALARS] + [ANY] * (groups + count + 1),
        out_specs=[HBM] * groups,
        out_shape=[hbm_out(shape[1:])] * groups,
        scratch_shapes=[
            pltpu.VMEM(shape, BF),
            pltpu.VMEM((total, quarter, width), BF),
            pltpu.VMEM(shape, BF),
            DMA((groups,)),
            DMA((count,)),
            DMA((groups, frames)),
        ],
        compiler_params=params(),
        name="memory_attend",
        cost_estimate=cost(
            8 * groups * frames * rows * TOPM * quarter * C,
            4 * groups * frames * rows * C + 2 * total * quarter * width,
        ),
    )(index, *queries, *blocks, in_hbm(after))


def add_partials_kernel(count, x_ref, *refs):
    ins, outs = refs[:count], refs[count : count + G]
    parts_ref, out_ref, load_sem, store_sem = refs[count + G :]
    patches = out_ref.shape[1] - PAD
    loads = []
    for j in range(G):
        frame = lax.rem(x_ref[0] + j, G)
        loads.append(
            [copy(ref.at[frame], parts_ref.at[k, j], load_sem.at[k, j]) for k, ref in enumerate(ins)]
        )
    for of_frame in loads:
        for load in of_frame:
            load.start()
    stores = []
    for j in range(G):
        for load in loads[j]:
            load.wait()
        total = parts_ref[0, j].astype(F32)
        for k in range(1, count):
            total = total + parts_ref[k, j].astype(F32)
        out_ref[j, :patches, :] = total[:patches].astype(BF)
        out_ref[j, patches:, :] = halves(total[patches : patches + 8] + total[patches + 8 :])
        stores.append(copy(out_ref.at[j], outs[j], store_sem.at[j]))
        stores[-1].start()
    for store in stores:
        store.wait()


def add_partials(x, parts):
    shape = parts[0].shape
    return pl.pallas_call(
        functools.partial(add_partials_kernel, len(parts)),
        in_specs=[SCALARS] + [ANY] * len(parts),
        out_specs=[HBM] * G,
        out_shape=[hbm_out(shape[1:])] * G,
        scratch_shapes=[
            pltpu.VMEM((len(parts),) + shape, BF),
            pltpu.VMEM(shape, BF),
            DMA((len(parts), G)),
            DMA((G,)),
        ],
        compiler_params=params(),
        name="add_partials",
        cost_estimate=cost(4 * parts[0].size, 8 * parts[0].size),
    )(x, *parts)


def leave_kernel(
    x_ref, own_hbm, memory_0, memory_1, memory_2, memory_3, time_hbm, weight_hbm, out_hbm,
    own_ref, memory_ref, time_ref, combined_ref, weight_ref, out_ref,
    own_sem, memory_sem, time_sem, weight_sem, store_sem,
):
    patches = own_ref.shape[1] - PAD
    quarters = time_ref.shape[0] // G
    rows = time_ref.shape[1]
    steps, _, width = weight_ref.shape
    heads = [lax.rem(x_ref[0] + G - j, G) for j in range(G)]
    memories = (memory_0, memory_1, memory_2, memory_3)
    own_loads = [copy(own_hbm.at[heads[j]], own_ref.at[j], own_sem.at[j]) for j in range(G)]
    memory_loads = [copy(memories[j], memory_ref.at[j], memory_sem.at[j]) for j in range(G)]
    time_load = copy(time_hbm, time_ref, time_sem)
    loads, stores = [], []
    for i in range(steps):
        at = pl.ds(i * width, width)
        loads.append(copy(weight_hbm.at[:, at], weight_ref.at[i], weight_sem.at[i]))
        stores.append(copy(out_ref.at[i], out_hbm.at[:, at], store_sem.at[i]))
    for load in own_loads + memory_loads + [time_load] + loads:
        load.start()
    row = lax.broadcasted_iota(jnp.int32, (LINE, C), 0)
    column = lax.broadcasted_iota(jnp.int32, (LINE, C), 1)
    for h in range(G):
        own_loads[h].wait()
        memory_loads[h].wait()
        column_at = pl.ds(pl.multiple_of(heads[h] * C, C), C)
        tail = own_ref[h, patches:, :].astype(F32) + memory_ref[h, patches:, :].astype(F32)
        denominators = tail[:8] + tail[8:]
        for j in range(patches // LINE):
            at = slice(j * LINE, (j + 1) * LINE)
            line = jnp.broadcast_to(denominators[j : j + 1, :], (LINE, C))
            total = jnp.sum(jnp.where(row == column, line, 0.0), axis=1, keepdims=True)
            top = own_ref[h, at, :].astype(F32) + memory_ref[h, at, :].astype(F32)
            combined_ref[at, column_at] = (top / total).astype(BF)
    time_load.wait()
    for h in range(G):
        for z in range(quarters):
            combined_ref[z * rows : (z + 1) * rows, HW + h * C : HW + (h + 1) * C] = time_ref[
                z * G + h
            ]
    for i in range(steps):
        loads[i].wait()
        out_ref[i] = dot(combined_ref[...], weight_ref[i]).astype(BF)
        stores[i].start()
    for store in stores:
        store.wait()


def leave(x, own, memory, time, weight):
    patches = own.shape[1] - PAD
    depth, width = weight.shape
    steps = 4
    step = width // steps
    return pl.pallas_call(
        leave_kernel,
        in_specs=[SCALARS, HBM] + [ANY] * (G + 1) + [HBM],
        out_specs=HBM,
        out_shape=hbm_out((patches, width)),
        scratch_shapes=[
            pltpu.VMEM(own.shape, BF),
            pltpu.VMEM(own.shape, BF),
            pltpu.VMEM(time.shape, BF),
            pltpu.VMEM((patches, depth), BF),
            pltpu.VMEM((steps, depth, step), BF),
            pltpu.VMEM((steps, patches, step), BF),
            DMA((G,)),
            DMA((G,)),
            DMA,
            DMA((steps,)),
            DMA((steps,)),
        ],
        compiler_params=params(),
        name="leave",
        cost_estimate=cost(
            2 * patches * depth * width,
            2 * depth * width + 2 * patches * width + 6 * patches * depth,
        ),
    )(x, in_hbm(own), *memory, time, in_hbm(weight))


def on_device(
    patch_activation_tensor,
    conditioning_affine,
    entry_projection_matrix,
    exit_projection_matrix,
    softmax_sharpness,
    cached_past_pairs,
    recalled_picture_holder,
    recalled_picture_position,
    lookback_lengths,
):
    rings = lax.axis_size("z")
    patches, depth = patch_activation_tensor.shape[2:]
    held, piece = cached_past_pairs.shape[:2]
    rolls_y, cores = lax.axis_size("y"), lax.axis_size("c")
    x = lax.axis_index("x").astype(jnp.int32).reshape(1)

    def turn(step):
        return [(s, (s + step) % rings) for s in range(rings)]

    other = [(s, cores - 1 - s) for s in range(cores)]

    def swap(blocks, axes):
        return lax.all_to_all(blocks, axes, split_axis=0, concat_axis=0, tiled=True)

    def swap_apart(blocks):
        return [blocks[0]] + [lax.ppermute(blocks[j], "x", turn(j)) for j in range(1, G)]

    with jax.named_scope("store"):
        split = split_store(x, cached_past_pairs.reshape(held * piece, 2 * HW))
        pieces = swap_apart(split)

    with jax.named_scope("queries"):
        factor = softmax_sharpness / C
        index = recalled_picture_holder.reshape(TOPM) * held + recalled_picture_position.reshape(
            TOPM
        )
        tail = jnp.zeros((PAD, C), BF).at[0, :TOPM].set(index.astype(BF))
        hidden, query = modulate(
            patch_activation_tensor.reshape(patches, depth),
            conditioning_affine.reshape(2, depth),
            entry_projection_matrix,
            factor,
            tail,
            after=split[0],
        )
        here = swap(query, "x")

    with jax.named_scope("store"):
        joined = join_pieces(pieces, held, after=hidden)
        above = lax.ppermute(joined, "y", turn(-1))
        below = lax.ppermute(joined, "y", turn(1))

    with jax.named_scope("queries"):
        here, joined = lax.optimization_barrier((here, joined))
        groups = [here] + [lax.ppermute(here, "z", turn(-step)) for step in (1, 2, 3)]

    with jax.named_scope("own"):
        own = own_attend(hidden, entry_projection_matrix, query, after=joined)

    with jax.named_scope("store"):
        joined, above, below, own = lax.optimization_barrier((joined, above, below, own))
        far_first = lax.ppermute(above[: held // 2], "y", turn(-1))
        far_last = lax.ppermute(below[held // 2 :], "y", turn(1))

    with jax.named_scope("temporal"):
        parts = temporal_entry(hidden, entry_projection_matrix, factor, rings, after=own)
        sent = swap(parts.reshape((rings * G,) + parts.shape[2:]), ("z", "x"))

    with jax.named_scope("store"):
        near = [joined, above, far_first, far_last, below]
        *near, parts = lax.optimization_barrier((*near, parts))
        blocks = near + [lax.ppermute(block, "c", other) for block in near]

    def attend(queries, after):
        named = jnp.concatenate([group[:, patches, :TOPM] for group in queries], axis=0)
        named = named.astype(jnp.int32)
        y = (named // (cores * held) - lax.axis_index("y")) & (rolls_y - 1)
        c = (named // held & (cores - 1)) ^ lax.axis_index("c")
        index = (c * rolls_y + y) * held + (named & (held - 1))
        return memory_attend(index, queries, blocks, after)

    with jax.named_scope("memory"):
        sum_far, sum_above = attend([groups[2], groups[1]], parts)
        from_far = lax.ppermute(sum_far, "z", turn(2))
        from_below = lax.ppermute(sum_above, "z", turn(1))
        sum_below, sum_here = attend([groups[3], here], sum_far)
        from_above = lax.ppermute(sum_below, "z", turn(3))

    with jax.named_scope("temporal"):
        timed = temporal_attend(lookback_lengths, sent, after=sum_below)
        time = swap(timed, ("z", "x"))

    with jax.named_scope("memory"):
        memory = swap_apart(add_partials(x, [sum_here, from_far, from_below, from_above]))

    with jax.named_scope("exit"):
        attended = leave(x, own, memory, time, exit_projection_matrix)
    return attended.reshape(1, 1, patches, depth)


def solution(mesh):
    apart = Mesh(mesh.devices.reshape(4, 2, 4, 4), ("y", "c", "z", "x"))
    roll, frame = ("y", "c"), ("z", "x")
    return jax.shard_map(
        on_device,
        mesh=apart,
        in_specs=(
            P(roll, frame, None, None),
            P(roll, frame, None, None),
            P(),
            P(),
            P(),
            P(roll, frame, None, None),
            P(roll, frame, None, None),
            P(roll, frame, None),
            P(roll),
        ),
        out_specs=P(roll, frame, None, None),
        check_vma=False,
    )
```

```python
import functools

import jax
import jax.numpy as jnp
from jax import lax
from jax.experimental import pallas as pl
from jax.experimental.pallas import tpu as pltpu
from jax.sharding import Mesh
from jax.sharding import PartitionSpec as P

G = 4
C = 128
HW = G * C
TOPM = 6
EPSILON = 1e-06
BF = jnp.bfloat16
F32 = jnp.float32
PAD = 16
VMEM_LIMIT = 28 * 1024 * 1024
ANY = pl.BlockSpec(memory_space=pl.ANY)
HBM = pl.BlockSpec(memory_space=pltpu.HBM)
WHOLE = pl.BlockSpec(memory_space=pltpu.VMEM)
SCALARS = pl.BlockSpec(memory_space=pltpu.SMEM)


def params(**more):
    return pltpu.CompilerParams(vmem_limit_bytes=VMEM_LIMIT, **more)


def cost(flops, bytes_accessed):
    return pl.CostEstimate(
        flops=flops // 16, bytes_accessed=bytes_accessed // 16, transcendentals=0
    )


def in_hbm(array):
    return pltpu.with_memory_space_constraint(array, pltpu.HBM)


def hbm_out(shape, dtype=BF):
    return pltpu.HBM(shape, dtype)


def inverse_rms(values):
    return lax.rsqrt(jnp.mean(values * values, axis=-1, keepdims=True) + EPSILON)


def dot(a, b):
    return jnp.dot(a, b, preferred_element_type=F32)


def dot_t(a, b):
    return lax.dot_general(a, b, (((1,), (1,)), ((), ())), preferred_element_type=F32)


DMA = pltpu.SemaphoreType.DMA
copy = pltpu.make_async_copy


def split_store_kernel(x_ref, rows_ref, *refs):
    outs, out_ref, sem = refs[:G], refs[G], refs[G + 1]
    sends = []
    for j in range(G):
        start = lax.rem(x_ref[0] + j, G) * C
        key = rows_ref[:, pl.ds(pl.multiple_of(start, C), C)].astype(F32)
        out_ref[j, :, :C] = (key * inverse_rms(key)).astype(BF)
        out_ref[j, :, C:] = rows_ref[:, pl.ds(pl.multiple_of(HW + start, C), C)]
        sends.append(copy(out_ref.at[j], outs[j], sem.at[j]))
        sends[-1].start()
    for send in sends:
        send.wait()


def split_store(x, rows):
    n = rows.shape[0]
    return pl.pallas_call(
        split_store_kernel,
        in_specs=[SCALARS, WHOLE],
        out_specs=[HBM] * G,
        out_shape=[hbm_out((n, 2 * C))] * G,
        scratch_shapes=[pltpu.VMEM((G, n, 2 * C), BF), DMA((G,))],
        compiler_params=params(),
        name="split_store",
        cost_estimate=cost(8 * n * HW, 8 * n * HW),
    )(x, rows)


def join_pieces_kernel(pieces, *refs):
    ins = refs[:pieces]
    out_hbm, in_ref, wide_ref, joined_ref, out_ref, sem = refs[pieces + 1 :]
    frames = out_ref.shape[0]
    piece = in_ref.shape[1] // frames
    loads = [copy(ins[i], in_ref.at[i], sem.at[i]) for i in range(pieces)]
    for load in loads:
        load.start()
    for i in range(pieces):
        loads[i].wait()
        wide_ref[i] = in_ref[i].astype(F32)
        for m in range(frames):
            joined_ref[m, i * piece : (i + 1) * piece, :] = wide_ref[
                i, m * piece : (m + 1) * piece, :
            ]
    out_ref[...] = joined_ref[...].astype(BF)
    send = copy(out_ref, out_hbm, sem.at[0])
    send.start()
    send.wait()


def join_pieces(parts, frames, after):
    pieces = len(parts)
    rows, width = parts[0].shape
    shape = (frames, pieces * rows // frames, width)
    return pl.pallas_call(
        functools.partial(join_pieces_kernel, pieces),
        in_specs=[ANY] * (pieces + 1),
        out_specs=HBM,
        out_shape=hbm_out(shape),
        scratch_shapes=[
            pltpu.VMEM((pieces, rows, width), BF),
            pltpu.VMEM((pieces, rows, width), F32),
            pltpu.VMEM(shape, F32),
            pltpu.VMEM(shape, BF),
            DMA((pieces,)),
        ],
        compiler_params=params(),
        name="join_pieces",
        cost_estimate=cost(pieces * rows * width, 4 * pieces * rows * width),
    )(*parts, in_hbm(after))


def modulate_kernel(
    held,
    act_hbm, affine_hbm, weight_hbm, sharpness_ref, owner_ref, slot_ref, _, hidden_hbm, query_hbm,
    act_ref, affine_ref, weight_ref, hidden_ref, query_ref,
    load_sem, affine_sem, weight_sem, store_sem, query_sem,
):
    steps, rows, _ = act_ref.shape
    patches = query_ref.shape[1] - PAD
    loads, stores = [], []
    for i in range(steps):
        at = pl.ds(i * rows, rows)
        loads.append(copy(act_hbm.at[at, :], act_ref.at[i], load_sem.at[i]))
        stores.append(copy(hidden_ref.at[i], hidden_hbm.at[at, :], store_sem.at[i]))
    weight_load = copy(weight_hbm.at[:, pl.ds(0, HW)], weight_ref, weight_sem)
    affine_load = copy(affine_hbm, affine_ref, affine_sem)
    affine_load.start()
    loads[0].start()
    weight_load.start()
    row = lax.broadcasted_iota(jnp.int32, (PAD, C), 0)
    column = lax.broadcasted_iota(jnp.int32, (PAD, C), 1)
    tail = jnp.zeros((PAD, C), jnp.int32)
    for j in range(TOPM):
        tail = jnp.where((row == 0) & (column == j), owner_ref[j] * held + slot_ref[j], tail)
    for h in range(G):
        query_ref[h, patches:, :] = tail.astype(F32).astype(BF)
    affine_load.wait()
    for i in range(steps):
        at = slice(i * rows, (i + 1) * rows)
        loads[i].wait()
        if i + 1 < steps:
            loads[i + 1].start()
        act = act_ref[i].astype(F32)
        hidden = act * inverse_rms(act) * (1.0 + affine_ref[0:1, :]) + affine_ref[1:2, :]
        hidden = hidden.astype(BF)
        hidden_ref[i] = hidden
        stores[i].start()
        if i == 0:
            weight_load.wait()
        mapped = dot(hidden, weight_ref[...]).astype(BF).astype(F32)
        for h in range(G):
            one = mapped[:, h * C : (h + 1) * C]
            query_ref[h, at, :] = (
                one * inverse_rms(one) * (sharpness_ref[0, h] / C)
            ).astype(BF)
    send = copy(query_ref, query_hbm, query_sem)
    send.start()
    for store in stores:
        store.wait()
    send.wait()


def modulate(act, affine, weight, sharpness, owner, slot, held, after):
    patches, depth = act.shape
    steps = 2
    rows = patches // steps
    shape = (G, patches + PAD, C)
    return pl.pallas_call(
        functools.partial(modulate_kernel, held),
        in_specs=[HBM, HBM, HBM, SCALARS, SCALARS, SCALARS, ANY],
        out_specs=[HBM, HBM],
        out_shape=[hbm_out((patches, depth)), hbm_out(shape)],
        scratch_shapes=[
            pltpu.VMEM((steps, rows, depth), BF),
            pltpu.VMEM(affine.shape, F32),
            pltpu.VMEM((depth, HW), BF),
            pltpu.VMEM((steps, rows, depth), BF),
            pltpu.VMEM(shape, BF),
            DMA((steps,)),
            DMA,
            DMA,
            DMA((steps,)),
            DMA,
        ],
        compiler_params=params(),
        name="modulate",
        cost_estimate=cost(
            2 * patches * depth * HW, 4 * patches * depth + 2 * depth * HW + 2 * patches * HW
        ),
    )(in_hbm(act), in_hbm(affine), in_hbm(weight), sharpness, owner, slot, in_hbm(after))


def temporal_entry_kernel(
    quarters, hidden_hbm, weight_hbm, sharpness_ref, _, out_hbm,
    hidden_ref, weight_ref, out_ref, hidden_sem, weight_sem, store_sem,
):
    rows = hidden_ref.shape[0] // quarters
    hidden_load = copy(hidden_hbm, hidden_ref, hidden_sem)
    loads = [
        copy(
            weight_hbm.at[:, pl.ds((3 + part) * HW, HW)], weight_ref.at[part], weight_sem.at[part]
        )
        for part in range(3)
    ]
    hidden_load.start()
    loads[0].start()
    hidden_load.wait()
    stores = []
    for part in range(3):
        loads[part].wait()
        if part < 2:
            loads[part + 1].start()
        mapped = dot(hidden_ref[...], weight_ref[part]).astype(BF)
        for h in range(G):
            done = mapped[:, h * C : (h + 1) * C]
            if part < 2:
                one = done.astype(F32)
                one = one * inverse_rms(one)
                if part == 0:
                    one = one * (sharpness_ref[1, h] / C)
                done = one.astype(BF)
            for z in range(quarters):
                out_ref[part, z, h] = done[z * rows : (z + 1) * rows, :]
        stores.append(copy(out_ref.at[part], out_hbm.at[:, :, part], store_sem.at[part]))
        stores[-1].start()
    for store in stores:
        store.wait()


def temporal_entry(hidden, weight, sharpness, quarters, after):
    patches, depth = hidden.shape
    rows = patches // quarters
    return pl.pallas_call(
        functools.partial(temporal_entry_kernel, quarters),
        in_specs=[HBM, HBM, SCALARS, ANY],
        out_specs=HBM,
        out_shape=hbm_out((quarters, G, 3, rows, C)),
        scratch_shapes=[
            pltpu.VMEM((patches, depth), BF),
            pltpu.VMEM((3, depth, HW), BF),
            pltpu.VMEM((3, quarters, G, rows, C), BF),
            DMA,
            DMA((3,)),
            DMA((3,)),
        ],
        compiler_params=params(),
        name="temporal_entry",
        cost_estimate=cost(
            6 * patches * depth * HW, 2 * patches * depth + 6 * depth * HW + 6 * patches * HW
        ),
    )(in_hbm(hidden), in_hbm(weight), sharpness, in_hbm(after))


def temporal_attend_kernel(length_ref, in_hbm_ref, _, out_hbm, in_ref, out_ref, sem):
    frames, _, rows, _ = in_ref.shape
    group = 16
    size = frames * group
    load = copy(in_hbm_ref, in_ref, sem)
    load.start()
    length = length_ref[0]
    row = lax.broadcasted_iota(jnp.int32, (size, size), 0)
    column = lax.broadcasted_iota(jnp.int32, (size, size), 1)
    target, source = row // group, column // group
    keep = (row % group == column % group) & (source <= target) & (source > target - length)
    load.wait()
    for g in range(rows // group):
        at = slice(g * group, (g + 1) * group)
        query = in_ref[:, 0, at, :].reshape(size, C)
        key = in_ref[:, 1, at, :].reshape(size, C)
        value = in_ref[:, 2, at, :].reshape(size, C)
        weights = jnp.where(keep, jnp.exp(dot_t(query, key)), 0.0)
        shares = weights / jnp.sum(weights, axis=-1, keepdims=True)
        result = dot(shares.astype(BF), value).astype(BF)
        out_ref[:, at, :] = result.reshape(frames, group, C)
    store = copy(out_ref, out_hbm, sem)
    store.start()
    store.wait()


def temporal_attend(length, parts, after):
    frames, _, rows, _ = parts.shape
    shape = (frames, rows, C)
    return pl.pallas_call(
        temporal_attend_kernel,
        in_specs=[SCALARS, ANY, ANY],
        out_specs=HBM,
        out_shape=hbm_out(shape),
        scratch_shapes=[pltpu.VMEM(parts.shape, BF), pltpu.VMEM(shape, BF), DMA],
        compiler_params=params(),
        name="temporal_attend",
        cost_estimate=cost(4 * frames * rows * 256 * C, 8 * frames * rows * C),
    )(length, parts, in_hbm(after))


LINE = 96
CHUNK = 3 * LINE


def halves(denominators):
    high = denominators.astype(BF).astype(F32)
    return jnp.concatenate([high, denominators - high], axis=0).astype(BF)


def attend_rows(query, keys, both, out_ref):
    patches = out_ref.shape[0] - PAD
    row = lax.broadcasted_iota(jnp.int32, (LINE, C), 0)
    column = lax.broadcasted_iota(jnp.int32, (LINE, C), 1)
    lines = []
    for start in range(0, patches, CHUNK):
        at = slice(start, start + CHUNK)
        weights = jnp.exp(dot_t(query(at), keys)).astype(BF)
        result = dot(weights, both)
        out_ref[at, :] = result[:, :C].astype(BF)
        for j in range(0, CHUNK, LINE):
            diagonal = jnp.where(row == column, result[j : j + LINE, C:], 0.0)
            lines.append(jnp.sum(diagonal, axis=0, keepdims=True))
    lines.append(jnp.zeros((8 - len(lines), C), F32))
    out_ref[patches:, :] = halves(jnp.concatenate(lines, axis=0))


def with_ones(values):
    return jnp.concatenate([values, jnp.ones(values.shape, BF)], axis=1)


def own_attend_kernel(
    hidden_hbm, weight_hbm, query_hbm, _, out_hbm,
    hidden_ref, weight_ref, query_ref, out_ref, hidden_sem, weight_sem, query_sem, store_sem,
):
    hidden_load = copy(hidden_hbm, hidden_ref, hidden_sem)
    query_load = copy(query_hbm, query_ref, query_sem)
    loads = [
        copy(
            weight_hbm.at[:, pl.ds((1 + part) * HW, HW)], weight_ref.at[part], weight_sem.at[part]
        )
        for part in range(2)
    ]
    hidden_load.start()
    loads[0].start()
    hidden_load.wait()
    loads[0].wait()
    loads[1].start()
    query_load.start()
    keys = dot(hidden_ref[...], weight_ref[0]).astype(BF)
    loads[1].wait()
    values = dot(hidden_ref[...], weight_ref[1]).astype(BF)
    query_load.wait()
    stores = []
    for h in range(G):
        key = keys[:, h * C : (h + 1) * C].astype(F32)
        key = (key * inverse_rms(key)).astype(BF)
        both = with_ones(values[:, h * C : (h + 1) * C])
        attend_rows(lambda at, h=h: query_ref[h, at, :], key, both, out_ref.at[h])
        stores.append(copy(out_ref.at[h], out_hbm.at[h], store_sem.at[h]))
        stores[-1].start()
    for store in stores:
        store.wait()


def own_attend(hidden, weight, query, after):
    patches, depth = hidden.shape
    return pl.pallas_call(
        own_attend_kernel,
        in_specs=[HBM, HBM, HBM, ANY],
        out_specs=HBM,
        out_shape=hbm_out(query.shape),
        scratch_shapes=[
            pltpu.VMEM((patches, depth), BF),
            pltpu.VMEM((2, depth, HW), BF),
            pltpu.VMEM(query.shape, BF),
            pltpu.VMEM(query.shape, BF),
            DMA,
            DMA((2,)),
            DMA,
            DMA((G,)),
        ],
        compiler_params=params(),
        name="own_attend",
        cost_estimate=cost(
            4 * patches * depth * HW + 6 * patches * patches * HW,
            2 * patches * depth + 4 * depth * HW + 10 * patches * HW,
        ),
    )(in_hbm(hidden), in_hbm(weight), in_hbm(query), in_hbm(after))


def memory_attend_kernel(groups, count, index_ref, *refs):
    queries, blocks = refs[:groups], refs[groups : groups + count]
    outs = refs[groups + count + 1 : 2 * groups + count + 1]
    query_ref, store_ref, out_ref, query_sem, block_sem, store_sem = refs[2 * groups + count + 1 :]
    frames = queries[0].shape[0]
    loads, start = [], 0
    for i, block in enumerate(blocks):
        held = block.shape[0]
        loads.append(copy(block, store_ref.at[pl.ds(start, held)], block_sem.at[i]))
        start += held
    query_loads = [copy(queries[k], query_ref.at[k], query_sem.at[k]) for k in range(groups)]
    for load in query_loads[:1] + loads + query_loads[1:]:
        load.start()
    for load in loads:
        load.wait()
    stores = []
    for k in range(groups):
        query_loads[k].wait()
        for i in range(frames):
            chosen = [store_ref[index_ref[k * frames + i, j]] for j in range(TOPM)]
            keys = jnp.concatenate([block[:, :C] for block in chosen], axis=0)
            values = jnp.concatenate([block[:, C:] for block in chosen], axis=0)
            attend_rows(
                lambda at, k=k, i=i: query_ref[k, i, at, :],
                keys,
                with_ones(values),
                out_ref.at[k, i],
            )
            stores.append(copy(out_ref.at[k, i], outs[k].at[i], store_sem.at[k, i]))
            stores[-1].start()
    for store in stores:
        store.wait()


def memory_attend(index, queries, blocks, after):
    groups, count = len(queries), len(blocks)
    frames, rows, _ = queries[0].shape
    _, quarter, width = blocks[0].shape
    total = sum(block.shape[0] for block in blocks)
    shape = (groups, frames, rows, C)
    return pl.pallas_call(
        functools.partial(memory_attend_kernel, groups, count),
        in_specs=[SCALARS] + [ANY] * (groups + count + 1),
        out_specs=[HBM] * groups,
        out_shape=[hbm_out(shape[1:])] * groups,
        scratch_shapes=[
            pltpu.VMEM(shape, BF),
            pltpu.VMEM((total, quarter, width), BF),
            pltpu.VMEM(shape, BF),
            DMA((groups,)),
            DMA((count,)),
            DMA((groups, frames)),
        ],
        compiler_params=params(),
        name="memory_attend",
        cost_estimate=cost(
            8 * groups * frames * rows * TOPM * quarter * C,
            4 * groups * frames * rows * C + 2 * total * quarter * width,
        ),
    )(index, *queries, *blocks, in_hbm(after))


def add_partials_kernel(count, x_ref, *refs):
    ins, outs = refs[:count], refs[count : count + G]
    parts_ref, out_ref, load_sem, store_sem = refs[count + G :]
    patches = out_ref.shape[1] - PAD
    loads = []
    for j in range(G):
        frame = lax.rem(x_ref[0] + j, G)
        loads.append(
            [copy(ref.at[frame], parts_ref.at[k, j], load_sem.at[k, j]) for k, ref in enumerate(ins)]
        )
    for of_frame in loads:
        for load in of_frame:
            load.start()
    stores = []
    for j in range(G):
        for load in loads[j]:
            load.wait()
        total = parts_ref[0, j].astype(F32)
        for k in range(1, count):
            total = total + parts_ref[k, j].astype(F32)
        out_ref[j, :patches, :] = total[:patches].astype(BF)
        out_ref[j, patches:, :] = halves(total[patches : patches + 8] + total[patches + 8 :])
        stores.append(copy(out_ref.at[j], outs[j], store_sem.at[j]))
        stores[-1].start()
    for store in stores:
        store.wait()


def add_partials(x, parts):
    shape = parts[0].shape
    return pl.pallas_call(
        functools.partial(add_partials_kernel, len(parts)),
        in_specs=[SCALARS] + [ANY] * len(parts),
        out_specs=[HBM] * G,
        out_shape=[hbm_out(shape[1:])] * G,
        scratch_shapes=[
            pltpu.VMEM((len(parts),) + shape, BF),
            pltpu.VMEM(shape, BF),
            DMA((len(parts), G)),
            DMA((G,)),
        ],
        compiler_params=params(),
        name="add_partials",
        cost_estimate=cost(4 * parts[0].size, 8 * parts[0].size),
    )(x, *parts)


def leave_kernel(
    x_ref, own_hbm, memory_0, memory_1, memory_2, memory_3, time_hbm, weight_hbm, out_hbm,
    own_ref, memory_ref, time_ref, combined_ref, weight_ref, out_ref,
    own_sem, memory_sem, time_sem, weight_sem, store_sem,
):
    patches = own_ref.shape[1] - PAD
    quarters = time_ref.shape[0] // G
    rows = time_ref.shape[1]
    steps, _, width = weight_ref.shape
    heads = [lax.rem(x_ref[0] + G - j, G) for j in range(G)]
    memories = (memory_0, memory_1, memory_2, memory_3)
    own_loads = [copy(own_hbm.at[heads[j]], own_ref.at[j], own_sem.at[j]) for j in range(G)]
    memory_loads = [copy(memories[j], memory_ref.at[j], memory_sem.at[j]) for j in range(G)]
    time_load = copy(time_hbm, time_ref, time_sem)
    loads, stores = [], []
    for i in range(steps):
        at = pl.ds(i * width, width)
        loads.append(copy(weight_hbm.at[:, at], weight_ref.at[i], weight_sem.at[i]))
        stores.append(copy(out_ref.at[i], out_hbm.at[:, at], store_sem.at[i]))
    for load in own_loads + memory_loads + [time_load] + loads:
        load.start()
    row = lax.broadcasted_iota(jnp.int32, (LINE, C), 0)
    column = lax.broadcasted_iota(jnp.int32, (LINE, C), 1)
    for h in range(G):
        own_loads[h].wait()
        memory_loads[h].wait()
        column_at = pl.ds(pl.multiple_of(heads[h] * C, C), C)
        tail = own_ref[h, patches:, :].astype(F32) + memory_ref[h, patches:, :].astype(F32)
        denominators = tail[:8] + tail[8:]
        for j in range(patches // LINE):
            at = slice(j * LINE, (j + 1) * LINE)
            line = jnp.broadcast_to(denominators[j : j + 1, :], (LINE, C))
            total = jnp.sum(jnp.where(row == column, line, 0.0), axis=1, keepdims=True)
            top = own_ref[h, at, :].astype(F32) + memory_ref[h, at, :].astype(F32)
            combined_ref[at, column_at] = (top / total).astype(BF)
    time_load.wait()
    for h in range(G):
        for z in range(quarters):
            combined_ref[z * rows : (z + 1) * rows, HW + h * C : HW + (h + 1) * C] = time_ref[
                z * G + h
            ]
    for i in range(steps):
        loads[i].wait()
        out_ref[i] = dot(combined_ref[...], weight_ref[i]).astype(BF)
        stores[i].start()
    for store in stores:
        store.wait()


def leave(x, own, memory, time, weight):
    patches = own.shape[1] - PAD
    depth, width = weight.shape
    steps = 4
    step = width // steps
    return pl.pallas_call(
        leave_kernel,
        in_specs=[SCALARS, HBM] + [ANY] * (G + 1) + [HBM],
        out_specs=HBM,
        out_shape=hbm_out((patches, width)),
        scratch_shapes=[
            pltpu.VMEM(own.shape, BF),
            pltpu.VMEM(own.shape, BF),
            pltpu.VMEM(time.shape, BF),
            pltpu.VMEM((patches, depth), BF),
            pltpu.VMEM((steps, depth, step), BF),
            pltpu.VMEM((steps, patches, step), BF),
            DMA((G,)),
            DMA((G,)),
            DMA,
            DMA((steps,)),
            DMA((steps,)),
        ],
        compiler_params=params(),
        name="leave",
        cost_estimate=cost(
            2 * patches * depth * width,
            2 * depth * width + 2 * patches * width + 6 * patches * depth,
        ),
    )(x, in_hbm(own), *memory, time, in_hbm(weight))


def on_device(
    patch_activation_tensor,
    conditioning_affine,
    entry_projection_matrix,
    exit_projection_matrix,
    softmax_sharpness,
    cached_past_pairs,
    recalled_picture_holder,
    recalled_picture_position,
    lookback_lengths,
):
    rings = lax.axis_size("z")
    patches, depth = patch_activation_tensor.shape[2:]
    held, piece = cached_past_pairs.shape[:2]
    rolls_y, cores = lax.axis_size("y"), lax.axis_size("c")
    x = lax.axis_index("x").astype(jnp.int32).reshape(1)

    def turn(step):
        return [(s, (s + step) % rings) for s in range(rings)]

    other = [(s, cores - 1 - s) for s in range(cores)]

    def swap(blocks, axes):
        return lax.all_to_all(blocks, axes, split_axis=0, concat_axis=0, tiled=True)

    def swap_apart(blocks):
        return [blocks[0]] + [lax.ppermute(blocks[j], "x", turn(j)) for j in range(1, G)]

    with jax.named_scope("store"):
        split = split_store(x, cached_past_pairs.reshape(held * piece, 2 * HW))
        pieces = swap_apart(split)

    with jax.named_scope("queries"):
        hidden, query = modulate(
            patch_activation_tensor.reshape(patches, depth),
            conditioning_affine.reshape(2, depth),
            entry_projection_matrix,
            softmax_sharpness,
            recalled_picture_holder.reshape(TOPM),
            recalled_picture_position.reshape(TOPM),
            held,
            after=split[0],
        )
        here = swap(query, "x")

    with jax.named_scope("store"):
        joined = join_pieces(pieces, held, after=hidden)
        above = lax.ppermute(joined, "y", turn(-1))
        below = lax.ppermute(joined, "y", turn(1))

    with jax.named_scope("temporal"):
        parts = temporal_entry(
            hidden, entry_projection_matrix, softmax_sharpness, rings, after=joined
        )
        sent = swap(parts.reshape((rings * G,) + parts.shape[2:]), ("z", "x"))

    with jax.named_scope("queries"):
        here, parts = lax.optimization_barrier((here, parts))
        z_above = lax.ppermute(here, "z", turn(-1))
        z_below = lax.ppermute(here, "z", turn(1))
        z_far = lax.ppermute(z_below, "z", turn(1))
        groups = [here, z_above, z_far, z_below]

    with jax.named_scope("store"):
        above, below, parts = lax.optimization_barrier((above, below, parts))
        far_first = lax.ppermute(above[: held // 2], "y", turn(-1))
        far_last = lax.ppermute(below[held // 2 :], "y", turn(1))

    with jax.named_scope("own"):
        own = own_attend(hidden, entry_projection_matrix, query, after=parts)

    with jax.named_scope("store"):
        near = [joined, above, far_first, far_last, below]
        *near, own = lax.optimization_barrier((*near, own))
        blocks = near + [lax.ppermute(block, "c", other) for block in near]

    def attend(queries, after):
        named = jnp.concatenate([group[:, patches, :TOPM] for group in queries], axis=0)
        named = named.astype(jnp.int32)
        y = (named // (cores * held) - lax.axis_index("y")) & (rolls_y - 1)
        c = (named // held & (cores - 1)) ^ lax.axis_index("c")
        index = (c * rolls_y + y) * held + (named & (held - 1))
        return memory_attend(index, queries, blocks, after)

    with jax.named_scope("memory"):
        sum_far, sum_above = attend([groups[2], groups[1]], own)
        from_far = lax.ppermute(sum_far, "z", turn(2))
        from_below = lax.ppermute(sum_above, "z", turn(1))
        sum_below, sum_here = attend([groups[3], here], sum_far)
        from_above = lax.ppermute(sum_below, "z", turn(3))

    with jax.named_scope("temporal"):
        timed = temporal_attend(lookback_lengths, sent, after=sum_below)
        time = swap(timed, ("z", "x"))

    with jax.named_scope("memory"):
        memory = swap_apart(add_partials(x, [sum_here, from_far, from_below, from_above]))

    with jax.named_scope("exit"):
        attended = leave(x, own, memory, time, exit_projection_matrix)
    return attended.reshape(1, 1, patches, depth)


def solution(mesh):
    apart = Mesh(mesh.devices.reshape(4, 2, 4, 4), ("y", "c", "z", "x"))
    roll, frame = ("y", "c"), ("z", "x")
    return jax.shard_map(
        on_device,
        mesh=apart,
        in_specs=(
            P(roll, frame, None, None),
            P(roll, frame, None, None),
            P(),
            P(),
            P(),
            P(roll, frame, None, None),
            P(roll, frame, None, None),
            P(roll, frame, None),
            P(roll),
        ),
        out_specs=P(roll, frame, None, None),
        check_vma=False,
    )
```

```python
import functools

import jax
import jax.numpy as jnp
from jax import lax
from jax.experimental import pallas as pl
from jax.experimental.pallas import tpu as pltpu
from jax.sharding import Mesh
from jax.sharding import PartitionSpec as P

G = 4
C = 128
HW = G * C
TOPM = 6
EPSILON = 1e-06
BF = jnp.bfloat16
F32 = jnp.float32
PAD = 16
VMEM_LIMIT = 28 * 1024 * 1024
ANY = pl.BlockSpec(memory_space=pl.ANY)
HBM = pl.BlockSpec(memory_space=pltpu.HBM)
WHOLE = pl.BlockSpec(memory_space=pltpu.VMEM)
SCALARS = pl.BlockSpec(memory_space=pltpu.SMEM)


def params(**more):
    return pltpu.CompilerParams(vmem_limit_bytes=VMEM_LIMIT, **more)


def cost(flops, bytes_accessed):
    return pl.CostEstimate(
        flops=flops // 16, bytes_accessed=bytes_accessed // 16, transcendentals=0
    )


def in_hbm(array):
    return pltpu.with_memory_space_constraint(array, pltpu.HBM)


def hbm_out(shape, dtype=BF):
    return pltpu.HBM(shape, dtype)


def inverse_rms(values):
    return lax.rsqrt(jnp.mean(values * values, axis=-1, keepdims=True) + EPSILON)


def dot(a, b):
    return jnp.dot(a, b, preferred_element_type=F32)


def dot_t(a, b):
    return lax.dot_general(a, b, (((1,), (1,)), ((), ())), preferred_element_type=F32)


DMA = pltpu.SemaphoreType.DMA
copy = pltpu.make_async_copy


def split_store_kernel(rows_ref, out_hbm, out_ref, sem):
    sends = []
    for h in range(G):
        key = rows_ref[:, h * C : (h + 1) * C].astype(F32)
        out_ref[h, :, :C] = (key * inverse_rms(key)).astype(BF)
        out_ref[h, :, C:] = rows_ref[:, HW + h * C : HW + (h + 1) * C]
        sends.append(copy(out_ref.at[h], out_hbm.at[h], sem.at[h]))
        sends[-1].start()
    for send in sends:
        send.wait()


def split_store(rows):
    n = rows.shape[0]
    return pl.pallas_call(
        split_store_kernel,
        in_specs=[WHOLE],
        out_specs=HBM,
        out_shape=hbm_out((G, n, 2 * C)),
        scratch_shapes=[pltpu.VMEM((G, n, 2 * C), BF), DMA((G,))],
        compiler_params=params(),
        name="split_store",
        cost_estimate=cost(8 * n * HW, 8 * n * HW),
    )(rows)


def join_pieces_kernel(piece, in_hbm, _, out_hbm, in_ref, wide_ref, joined_ref, out_ref, sem):
    pieces = in_ref.shape[0]
    loads = [copy(in_hbm.at[i], in_ref.at[i], sem.at[i]) for i in range(pieces)]
    for load in loads:
        load.start()
    for i in range(pieces):
        loads[i].wait()
        wide_ref[i] = in_ref[i].astype(F32)
        for m in range(out_ref.shape[0]):
            joined_ref[m, i * piece : (i + 1) * piece, :] = wide_ref[
                i, m * piece : (m + 1) * piece, :
            ]
    out_ref[...] = joined_ref[...].astype(BF)
    send = copy(out_ref, out_hbm, sem.at[0])
    send.start()
    send.wait()


def join_pieces(parts, frames, after):
    pieces, rows, width = parts.shape
    piece = rows // frames
    shape = (frames, pieces * piece, width)
    return pl.pallas_call(
        functools.partial(join_pieces_kernel, piece),
        in_specs=[ANY, ANY],
        out_specs=HBM,
        out_shape=hbm_out(shape),
        scratch_shapes=[
            pltpu.VMEM(parts.shape, BF),
            pltpu.VMEM(parts.shape, F32),
            pltpu.VMEM(shape, F32),
            pltpu.VMEM(shape, BF),
            DMA((pieces,)),
        ],
        compiler_params=params(),
        name="join_pieces",
        cost_estimate=cost(parts.size, 4 * parts.size),
    )(parts, in_hbm(after))


def modulate_kernel(
    held,
    act_hbm, affine_hbm, weight_hbm, sharpness_ref, owner_ref, slot_ref, _, hidden_hbm, query_hbm,
    act_ref, affine_ref, weight_ref, hidden_ref, query_ref,
    load_sem, affine_sem, weight_sem, store_sem, query_sem,
):
    steps, rows, _ = act_ref.shape
    patches = query_ref.shape[1] - PAD
    loads, stores = [], []
    for i in range(steps):
        at = pl.ds(i * rows, rows)
        loads.append(copy(act_hbm.at[at, :], act_ref.at[i], load_sem.at[i]))
        stores.append(copy(hidden_ref.at[i], hidden_hbm.at[at, :], store_sem.at[i]))
    weight_load = copy(weight_hbm.at[:, pl.ds(0, HW)], weight_ref, weight_sem)
    affine_load = copy(affine_hbm, affine_ref, affine_sem)
    affine_load.start()
    loads[0].start()
    weight_load.start()
    row = lax.broadcasted_iota(jnp.int32, (PAD, C), 0)
    column = lax.broadcasted_iota(jnp.int32, (PAD, C), 1)
    tail = jnp.zeros((PAD, C), jnp.int32)
    for j in range(TOPM):
        tail = jnp.where((row == 0) & (column == j), owner_ref[j] * held + slot_ref[j], tail)
    for h in range(G):
        query_ref[h, patches:, :] = tail.astype(F32).astype(BF)
    affine_load.wait()
    for i in range(steps):
        at = slice(i * rows, (i + 1) * rows)
        loads[i].wait()
        if i + 1 < steps:
            loads[i + 1].start()
        act = act_ref[i].astype(F32)
        hidden = act * inverse_rms(act) * (1.0 + affine_ref[0:1, :]) + affine_ref[1:2, :]
        hidden = hidden.astype(BF)
        hidden_ref[i] = hidden
        stores[i].start()
        if i == 0:
            weight_load.wait()
        mapped = dot(hidden, weight_ref[...]).astype(BF).astype(F32)
        for h in range(G):
            one = mapped[:, h * C : (h + 1) * C]
            query_ref[h, at, :] = (
                one * inverse_rms(one) * (sharpness_ref[0, h] / C)
            ).astype(BF)
    send = copy(query_ref, query_hbm, query_sem)
    send.start()
    for store in stores:
        store.wait()
    send.wait()


def modulate(act, affine, weight, sharpness, owner, slot, held, after):
    patches, depth = act.shape
    steps = 2
    rows = patches // steps
    shape = (G, patches + PAD, C)
    return pl.pallas_call(
        functools.partial(modulate_kernel, held),
        in_specs=[HBM, HBM, HBM, SCALARS, SCALARS, SCALARS, ANY],
        out_specs=[HBM, HBM],
        out_shape=[hbm_out((patches, depth)), hbm_out(shape)],
        scratch_shapes=[
            pltpu.VMEM((steps, rows, depth), BF),
            pltpu.VMEM(affine.shape, F32),
            pltpu.VMEM((depth, HW), BF),
            pltpu.VMEM((steps, rows, depth), BF),
            pltpu.VMEM(shape, BF),
            DMA((steps,)),
            DMA,
            DMA,
            DMA((steps,)),
            DMA,
        ],
        compiler_params=params(),
        name="modulate",
        cost_estimate=cost(
            2 * patches * depth * HW, 4 * patches * depth + 2 * depth * HW + 2 * patches * HW
        ),
    )(in_hbm(act), in_hbm(affine), in_hbm(weight), sharpness, owner, slot, in_hbm(after))


def temporal_entry_kernel(
    quarters, hidden_hbm, weight_hbm, sharpness_ref, _, out_hbm,
    hidden_ref, weight_ref, out_ref, hidden_sem, weight_sem, store_sem,
):
    rows = hidden_ref.shape[0] // quarters
    hidden_load = copy(hidden_hbm, hidden_ref, hidden_sem)
    loads = [
        copy(
            weight_hbm.at[:, pl.ds((3 + part) * HW, HW)], weight_ref.at[part], weight_sem.at[part]
        )
        for part in range(3)
    ]
    hidden_load.start()
    loads[0].start()
    hidden_load.wait()
    stores = []
    for part in range(3):
        loads[part].wait()
        if part < 2:
            loads[part + 1].start()
        mapped = dot(hidden_ref[...], weight_ref[part]).astype(BF)
        for h in range(G):
            done = mapped[:, h * C : (h + 1) * C]
            if part < 2:
                one = done.astype(F32)
                one = one * inverse_rms(one)
                if part == 0:
                    one = one * (sharpness_ref[1, h] / C)
                done = one.astype(BF)
            for z in range(quarters):
                out_ref[part, z, h] = done[z * rows : (z + 1) * rows, :]
        stores.append(copy(out_ref.at[part], out_hbm.at[:, :, part], store_sem.at[part]))
        stores[-1].start()
    for store in stores:
        store.wait()


def temporal_entry(hidden, weight, sharpness, quarters, after):
    patches, depth = hidden.shape
    rows = patches // quarters
    return pl.pallas_call(
        functools.partial(temporal_entry_kernel, quarters),
        in_specs=[HBM, HBM, SCALARS, ANY],
        out_specs=HBM,
        out_shape=hbm_out((quarters, G, 3, rows, C)),
        scratch_shapes=[
            pltpu.VMEM((patches, depth), BF),
            pltpu.VMEM((3, depth, HW), BF),
            pltpu.VMEM((3, quarters, G, rows, C), BF),
            DMA,
            DMA((3,)),
            DMA((3,)),
        ],
        compiler_params=params(),
        name="temporal_entry",
        cost_estimate=cost(
            6 * patches * depth * HW, 2 * patches * depth + 6 * depth * HW + 6 * patches * HW
        ),
    )(in_hbm(hidden), in_hbm(weight), sharpness, in_hbm(after))


def temporal_attend_kernel(length_ref, in_hbm_ref, _, out_hbm, in_ref, out_ref, sem):
    frames, _, rows, _ = in_ref.shape
    group = 16
    size = frames * group
    load = copy(in_hbm_ref, in_ref, sem)
    load.start()
    length = length_ref[0]
    row = lax.broadcasted_iota(jnp.int32, (size, size), 0)
    column = lax.broadcasted_iota(jnp.int32, (size, size), 1)
    target, source = row // group, column // group
    keep = (row % group == column % group) & (source <= target) & (source > target - length)
    load.wait()
    for g in range(rows // group):
        at = slice(g * group, (g + 1) * group)
        query = in_ref[:, 0, at, :].reshape(size, C)
        key = in_ref[:, 1, at, :].reshape(size, C)
        value = in_ref[:, 2, at, :].reshape(size, C)
        weights = jnp.where(keep, jnp.exp(dot_t(query, key)), 0.0)
        shares = weights / jnp.sum(weights, axis=-1, keepdims=True)
        result = dot(shares.astype(BF), value).astype(BF)
        out_ref[:, at, :] = result.reshape(frames, group, C)
    store = copy(out_ref, out_hbm, sem)
    store.start()
    store.wait()


def temporal_attend(length, parts, after):
    frames, _, rows, _ = parts.shape
    shape = (frames, rows, C)
    return pl.pallas_call(
        temporal_attend_kernel,
        in_specs=[SCALARS, ANY, ANY],
        out_specs=HBM,
        out_shape=hbm_out(shape),
        scratch_shapes=[pltpu.VMEM(parts.shape, BF), pltpu.VMEM(shape, BF), DMA],
        compiler_params=params(),
        name="temporal_attend",
        cost_estimate=cost(4 * frames * rows * 256 * C, 8 * frames * rows * C),
    )(length, parts, in_hbm(after))


LINE = 96
CHUNK = 3 * LINE


def halves(denominators):
    high = denominators.astype(BF).astype(F32)
    return jnp.concatenate([high, denominators - high], axis=0).astype(BF)


def attend_rows(query, keys, both, out_ref, carry=None):
    patches = out_ref.shape[0] - PAD
    row = lax.broadcasted_iota(jnp.int32, (LINE, C), 0)
    column = lax.broadcasted_iota(jnp.int32, (LINE, C), 1)
    lines = []
    for start in range(0, patches, CHUNK):
        at = slice(start, start + CHUNK)
        weights = jnp.exp(dot_t(query(at), keys)).astype(BF)
        result = dot(weights, both)
        top = result[:, :C]
        if carry is not None:
            top = top + carry[at, :].astype(F32)
        out_ref[at, :] = top.astype(BF)
        for j in range(0, CHUNK, LINE):
            diagonal = jnp.where(row == column, result[j : j + LINE, C:], 0.0)
            lines.append(jnp.sum(diagonal, axis=0, keepdims=True))
    lines.append(jnp.zeros((8 - len(lines), C), F32))
    total = jnp.concatenate(lines, axis=0)
    if carry is not None:
        tail = carry[patches:, :].astype(F32)
        total = total + tail[:8] + tail[8:]
    out_ref[patches:, :] = halves(total)


def with_ones(values):
    return jnp.concatenate([values, jnp.ones(values.shape, BF)], axis=1)


def own_attend_kernel(
    hidden_hbm, weight_hbm, query_hbm, *refs
):
    out_hbm, hidden_ref, weight_ref, query_ref, out_ref = refs[-9:-4]
    hidden_sem, weight_sem, query_sem, store_sem = refs[-4:]
    hidden_load = copy(hidden_hbm, hidden_ref, hidden_sem)
    query_load = copy(query_hbm, query_ref, query_sem)
    loads = [
        copy(
            weight_hbm.at[:, pl.ds((1 + part) * HW, HW)], weight_ref.at[part], weight_sem.at[part]
        )
        for part in range(2)
    ]
    hidden_load.start()
    loads[0].start()
    hidden_load.wait()
    loads[0].wait()
    loads[1].start()
    query_load.start()
    keys = dot(hidden_ref[...], weight_ref[0]).astype(BF)
    loads[1].wait()
    values = dot(hidden_ref[...], weight_ref[1]).astype(BF)
    query_load.wait()
    stores = []
    for h in range(G):
        key = keys[:, h * C : (h + 1) * C].astype(F32)
        key = (key * inverse_rms(key)).astype(BF)
        both = with_ones(values[:, h * C : (h + 1) * C])
        attend_rows(lambda at, h=h: query_ref[h, at, :], key, both, out_ref.at[h])
        stores.append(copy(out_ref.at[h], out_hbm.at[h], store_sem.at[h]))
        stores[-1].start()
    for store in stores:
        store.wait()


def own_attend(hidden, weight, query, after):
    patches, depth = hidden.shape
    return pl.pallas_call(
        own_attend_kernel,
        in_specs=[HBM, HBM, HBM] + [ANY] * len(after),
        out_specs=HBM,
        out_shape=hbm_out(query.shape),
        scratch_shapes=[
            pltpu.VMEM((patches, depth), BF),
            pltpu.VMEM((2, depth, HW), BF),
            pltpu.VMEM(query.shape, BF),
            pltpu.VMEM(query.shape, BF),
            DMA,
            DMA((2,)),
            DMA,
            DMA((G,)),
        ],
        compiler_params=params(),
        name="own_attend",
        cost_estimate=cost(
            4 * patches * depth * HW + 6 * patches * patches * HW,
            2 * patches * depth + 4 * depth * HW + 10 * patches * HW,
        ),
    )(in_hbm(hidden), in_hbm(weight), in_hbm(query), *after)


def memory_attend_kernel(groups, count, carried, pieces, index_ref, *refs):
    queries, refs = refs[:groups], refs[groups:]
    blocks, refs = refs[:count], refs[count:]
    carries, refs = refs[: len(carried)], refs[len(carried) + 1 :]
    outs, refs = refs[: groups * pieces], refs[groups * pieces :]
    query_ref, store_ref, carry_ref, out_ref, query_sem, block_sem, carry_sem, store_sem = refs
    frames = queries[0].shape[0]
    loads, start = [], 0
    for i, block in enumerate(blocks):
        held = block.shape[0]
        loads.append(copy(block, store_ref.at[pl.ds(start, held)], block_sem.at[i]))
        start += held
    query_loads = [copy(queries[k], query_ref.at[k], query_sem.at[k]) for k in range(groups)]
    carry_loads = [copy(ref, carry_ref.at[i], carry_sem.at[i]) for i, ref in enumerate(carries)]
    for load in query_loads[:1] + loads + carry_loads + query_loads[1:]:
        load.start()
    for load in loads + carry_loads:
        load.wait()
    stores = []
    piece = frames // pieces
    for k in range(groups):
        query_loads[k].wait()
        for i in range(frames):
            chosen = [store_ref[index_ref[k * frames + i, j]] for j in range(TOPM)]
            keys = jnp.concatenate([block[:, :C] for block in chosen], axis=0)
            values = jnp.concatenate([block[:, C:] for block in chosen], axis=0)
            carry = None
            for at, (group, first) in enumerate(carried):
                if group == k and first <= i < first + carries[at].shape[0]:
                    carry = carry_ref.at[at, i - first]
            attend_rows(
                lambda at, k=k, i=i: query_ref[k, i, at, :],
                keys,
                with_ones(values),
                out_ref.at[k, i],
                carry,
            )
            out = outs[k * pieces + i // piece].at[i % piece]
            stores.append(copy(out_ref.at[k, i], out, store_sem.at[k, i]))
            stores[-1].start()
    for store in stores:
        store.wait()


def memory_attend(index, queries, blocks, after, carries=(), carried=(), pieces=1):
    groups, count = len(queries), len(blocks)
    frames, rows, _ = queries[0].shape
    _, quarter, width = blocks[0].shape
    total = sum(block.shape[0] for block in blocks)
    shape = (groups, frames, rows, C)
    held = max([1] + [carry.shape[0] for carry in carries])
    return pl.pallas_call(
        functools.partial(memory_attend_kernel, groups, count, tuple(carried), pieces),
        in_specs=[SCALARS] + [ANY] * (groups + count + len(carries) + 1),
        out_specs=[HBM] * (groups * pieces),
        out_shape=[hbm_out((frames // pieces, rows, C))] * (groups * pieces),
        scratch_shapes=[
            pltpu.VMEM(shape, BF),
            pltpu.VMEM((total, quarter, width), BF),
            pltpu.VMEM((max(1, len(carries)), held, rows, C), BF),
            pltpu.VMEM(shape, BF),
            DMA((groups,)),
            DMA((count,)),
            DMA((max(1, len(carries)),)),
            DMA((groups, frames)),
        ],
        compiler_params=params(),
        name="memory_attend",
        cost_estimate=cost(
            8 * groups * frames * rows * TOPM * quarter * C,
            4 * groups * frames * rows * C + 2 * total * quarter * width,
        ),
    )(index, *queries, *blocks, *carries, in_hbm(after))


def add_partials_kernel(count, x_ref, *refs):
    ins, outs = refs[:count], refs[count : count + G]
    parts_ref, out_ref, load_sem, store_sem = refs[count + G :]
    patches = out_ref.shape[1] - PAD
    loads = []
    for j in range(G):
        frame = lax.rem(x_ref[0] + j, G)
        loads.append(
            [copy(ref.at[frame], parts_ref.at[k, j], load_sem.at[k, j]) for k, ref in enumerate(ins)]
        )
    for of_frame in loads:
        for load in of_frame:
            load.start()
    stores = []
    for j in range(G):
        for load in loads[j]:
            load.wait()
        total = parts_ref[0, j].astype(F32)
        for k in range(1, count):
            total = total + parts_ref[k, j].astype(F32)
        out_ref[j, :patches, :] = total[:patches].astype(BF)
        out_ref[j, patches:, :] = halves(total[patches : patches + 8] + total[patches + 8 :])
        stores.append(copy(out_ref.at[j], outs[j], store_sem.at[j]))
        stores[-1].start()
    for store in stores:
        store.wait()


def add_partials(x, parts):
    shape = parts[0].shape
    return pl.pallas_call(
        functools.partial(add_partials_kernel, len(parts)),
        in_specs=[SCALARS] + [ANY] * len(parts),
        out_specs=[HBM] * G,
        out_shape=[hbm_out(shape[1:])] * G,
        scratch_shapes=[
            pltpu.VMEM((len(parts),) + shape, BF),
            pltpu.VMEM(shape, BF),
            DMA((len(parts), G)),
            DMA((G,)),
        ],
        compiler_params=params(),
        name="add_partials",
        cost_estimate=cost(4 * parts[0].size, 8 * parts[0].size),
    )(x, *parts)


def leave_kernel(
    x_ref, own_hbm, memory_0, memory_1, memory_2, memory_3, time_hbm, weight_hbm, out_hbm,
    own_ref, memory_ref, time_ref, combined_ref, weight_ref, out_ref,
    own_sem, memory_sem, time_sem, weight_sem, store_sem,
):
    patches = own_ref.shape[1] - PAD
    quarters = time_ref.shape[0] // G
    rows = time_ref.shape[1]
    steps, _, width = weight_ref.shape
    heads = [lax.rem(x_ref[0] + G - j, G) for j in range(G)]
    memories = (memory_0, memory_1, memory_2, memory_3)
    own_loads = [copy(own_hbm.at[heads[j]], own_ref.at[j], own_sem.at[j]) for j in range(G)]
    memory_loads = [copy(memories[j], memory_ref.at[j], memory_sem.at[j]) for j in range(G)]
    time_load = copy(time_hbm, time_ref, time_sem)
    loads, stores = [], []
    for i in range(steps):
        at = pl.ds(i * width, width)
        loads.append(copy(weight_hbm.at[:, at], weight_ref.at[i], weight_sem.at[i]))
        stores.append(copy(out_ref.at[i], out_hbm.at[:, at], store_sem.at[i]))
    for load in own_loads + memory_loads + [time_load] + loads:
        load.start()
    row = lax.broadcasted_iota(jnp.int32, (LINE, C), 0)
    column = lax.broadcasted_iota(jnp.int32, (LINE, C), 1)
    for h in range(G):
        own_loads[h].wait()
        memory_loads[h].wait()
        column_at = pl.ds(pl.multiple_of(heads[h] * C, C), C)
        tail = own_ref[h, patches:, :].astype(F32) + memory_ref[h, patches:, :].astype(F32)
        denominators = tail[:8] + tail[8:]
        for j in range(patches // LINE):
            at = slice(j * LINE, (j + 1) * LINE)
            line = jnp.broadcast_to(denominators[j : j + 1, :], (LINE, C))
            total = jnp.sum(jnp.where(row == column, line, 0.0), axis=1, keepdims=True)
            top = own_ref[h, at, :].astype(F32) + memory_ref[h, at, :].astype(F32)
            combined_ref[at, column_at] = (top / total).astype(BF)
    time_load.wait()
    for h in range(G):
        for z in range(quarters):
            combined_ref[z * rows : (z + 1) * rows, HW + h * C : HW + (h + 1) * C] = time_ref[
                z * G + h
            ]
    for i in range(steps):
        loads[i].wait()
        out_ref[i] = dot(combined_ref[...], weight_ref[i]).astype(BF)
        stores[i].start()
    for store in stores:
        store.wait()


def leave(x, own, memory, time, weight):
    patches = own.shape[1] - PAD
    depth, width = weight.shape
    steps = 4
    step = width // steps
    return pl.pallas_call(
        leave_kernel,
        in_specs=[SCALARS, HBM] + [ANY] * (G + 1) + [HBM],
        out_specs=HBM,
        out_shape=hbm_out((patches, width)),
        scratch_shapes=[
            pltpu.VMEM(own.shape, BF),
            pltpu.VMEM(own.shape, BF),
            pltpu.VMEM(time.shape, BF),
            pltpu.VMEM((patches, depth), BF),
            pltpu.VMEM((steps, depth, step), BF),
            pltpu.VMEM((steps, patches, step), BF),
            DMA((G,)),
            DMA((G,)),
            DMA,
            DMA((steps,)),
            DMA((steps,)),
        ],
        compiler_params=params(),
        name="leave",
        cost_estimate=cost(
            2 * patches * depth * width,
            2 * depth * width + 2 * patches * width + 6 * patches * depth,
        ),
    )(x, in_hbm(own), *memory, time, in_hbm(weight))


def on_device(
    patch_activation_tensor,
    conditioning_affine,
    entry_projection_matrix,
    exit_projection_matrix,
    softmax_sharpness,
    cached_past_pairs,
    recalled_picture_holder,
    recalled_picture_position,
    lookback_lengths,
):
    rings = lax.axis_size("z")
    patches, depth = patch_activation_tensor.shape[2:]
    held, piece = cached_past_pairs.shape[:2]
    rolls_y, cores = lax.axis_size("y"), lax.axis_size("c")
    x = lax.axis_index("x").astype(jnp.int32).reshape(1)

    def turn(step):
        return [(s, (s + step) % rings) for s in range(rings)]

    other = [(s, cores - 1 - s) for s in range(cores)]

    def swap(blocks, axes):
        return lax.all_to_all(blocks, axes, split_axis=0, concat_axis=0, tiled=True)

    def swap_apart(blocks):
        return [blocks[0]] + [lax.ppermute(blocks[j], "x", turn(j)) for j in range(1, G)]

    with jax.named_scope("store"):
        split = split_store(cached_past_pairs.reshape(held * piece, 2 * HW))
        pieces = swap(split, "x")

    with jax.named_scope("queries"):
        hidden, query = modulate(
            patch_activation_tensor.reshape(patches, depth),
            conditioning_affine.reshape(2, depth),
            entry_projection_matrix,
            softmax_sharpness,
            recalled_picture_holder.reshape(TOPM),
            recalled_picture_position.reshape(TOPM),
            held,
            after=split,
        )
        here = swap(query, "x")

    with jax.named_scope("store"):
        joined = join_pieces(pieces, held, after=hidden)
        above = lax.ppermute(joined, "y", turn(-1))
        below = lax.ppermute(joined, "y", turn(1))

    with jax.named_scope("temporal"):
        parts = temporal_entry(
            hidden, entry_projection_matrix, softmax_sharpness, rings, after=joined
        )
        sent = swap(parts.reshape((rings * G,) + parts.shape[2:]), ("z", "x"))

    with jax.named_scope("queries"):
        z_above = lax.ppermute(here, "z", turn(-1))
        z_below = lax.ppermute(here, "z", turn(1))

    with jax.named_scope("own"):
        own = own_attend(
            hidden,
            entry_projection_matrix,
            query,
            after=[parts, above, below, z_above, z_below],
        )

    with jax.named_scope("queries"):
        z_far = lax.ppermute(z_below, "z", turn(1))

    with jax.named_scope("store"):
        far_first = lax.ppermute(above[: held // 2], "y", turn(-1))
        far_last = lax.ppermute(below[held // 2 :], "y", turn(1))
        near = [joined, above, far_first, far_last, below]
        *near, own = lax.optimization_barrier((*near, own))
        blocks = near + [lax.ppermute(block, "c", other) for block in near]

    def attend(queries, after, **more):
        named = jnp.concatenate([group[:, patches, :TOPM] for group in queries], axis=0)
        named = named.astype(jnp.int32)
        y = (named // (cores * held) - lax.axis_index("y")) & (rolls_y - 1)
        c = (named // held & (cores - 1)) ^ lax.axis_index("c")
        index = (c * rolls_y + y) * held + (named & (held - 1))
        return memory_attend(index, queries, blocks, after, **more)

    with jax.named_scope("memory"):
        sum_first, sum_last = attend([z_far], own, pieces=2)
        carry_first = lax.ppermute(sum_first, "z", turn(-1))
        carry_last = lax.ppermute(sum_last, "z", turn(1))
        (sum_here,) = attend([here], sum_first)
        sum_below, sum_above = attend(
            [z_below, z_above],
            sum_here,
            carries=[carry_first, carry_last],
            carried=[(0, 0), (1, here.shape[0] // 2)],
        )
        from_above = lax.ppermute(sum_below, "z", turn(-1))
        from_below = lax.ppermute(sum_above, "z", turn(1))

    with jax.named_scope("temporal"):
        timed = temporal_attend(lookback_lengths, sent, after=sum_below)
        time = swap(timed, ("z", "x"))

    with jax.named_scope("memory"):
        memory = swap_apart(add_partials(x, [sum_here, from_below, from_above]))

    with jax.named_scope("exit"):
        attended = leave(x, own, memory, time, exit_projection_matrix)
    return attended.reshape(1, 1, patches, depth)


def solution(mesh):
    apart = Mesh(mesh.devices.reshape(4, 2, 4, 4), ("y", "c", "z", "x"))
    roll, frame = ("y", "c"), ("z", "x")
    return jax.shard_map(
        on_device,
        mesh=apart,
        in_specs=(
            P(roll, frame, None, None),
            P(roll, frame, None, None),
            P(),
            P(),
            P(),
            P(roll, frame, None, None),
            P(roll, frame, None, None),
            P(roll, frame, None),
            P(roll),
        ),
        out_specs=P(roll, frame, None, None),
        check_vma=False,
    )
```

```python
import functools

import jax
import jax.numpy as jnp
from jax import lax
from jax.experimental import pallas as pl
from jax.experimental.pallas import tpu as pltpu
from jax.sharding import Mesh
from jax.sharding import PartitionSpec as P

G = 4
C = 128
HW = G * C
TOPM = 6
EPSILON = 1e-06
BF = jnp.bfloat16
F32 = jnp.float32
PAD = 16
VMEM_LIMIT = 28 * 1024 * 1024
ANY = pl.BlockSpec(memory_space=pl.ANY)
HBM = pl.BlockSpec(memory_space=pltpu.HBM)
WHOLE = pl.BlockSpec(memory_space=pltpu.VMEM)
SCALARS = pl.BlockSpec(memory_space=pltpu.SMEM)


def params(**more):
    return pltpu.CompilerParams(vmem_limit_bytes=VMEM_LIMIT, **more)


def cost(flops, bytes_accessed):
    return pl.CostEstimate(
        flops=flops // 16, bytes_accessed=bytes_accessed // 16, transcendentals=0
    )


def in_hbm(array):
    return pltpu.with_memory_space_constraint(array, pltpu.HBM)


def hbm_out(shape, dtype=BF):
    return pltpu.HBM(shape, dtype)


def inverse_rms(values):
    return lax.rsqrt(jnp.mean(values * values, axis=-1, keepdims=True) + EPSILON)


def dot(a, b):
    return jnp.dot(a, b, preferred_element_type=F32)


def dot_t(a, b):
    return lax.dot_general(a, b, (((1,), (1,)), ((), ())), preferred_element_type=F32)


DMA = pltpu.SemaphoreType.DMA
copy = pltpu.make_async_copy


def split_store_kernel(rows_ref, out_hbm, out_ref, sem):
    sends = []
    for h in range(G):
        key = rows_ref[:, h * C : (h + 1) * C].astype(F32)
        out_ref[h, :, :C] = (key * inverse_rms(key)).astype(BF)
        out_ref[h, :, C:] = rows_ref[:, HW + h * C : HW + (h + 1) * C]
        for k in range(out_hbm.shape[0]):
            sends.append(copy(out_ref.at[h], out_hbm.at[k, h], sem.at[k, h]))
            sends[-1].start()
    for send in sends:
        send.wait()


def split_store(rows, copies):
    n = rows.shape[0]
    return pl.pallas_call(
        split_store_kernel,
        in_specs=[WHOLE],
        out_specs=HBM,
        out_shape=hbm_out((copies, G, n, 2 * C)),
        scratch_shapes=[pltpu.VMEM((G, n, 2 * C), BF), DMA((copies, G))],
        compiler_params=params(),
        name="split_store",
        cost_estimate=cost(8 * n * HW, 8 * n * HW),
    )(rows)


def join_pieces_kernel(piece, in_hbm, _, out_hbm, in_ref, wide_ref, joined_ref, out_ref, sem):
    pieces = in_ref.shape[0]
    loads = [copy(in_hbm.at[i], in_ref.at[i], sem.at[i]) for i in range(pieces)]
    for load in loads:
        load.start()
    for i in range(pieces):
        loads[i].wait()
        wide_ref[i] = in_ref[i].astype(F32)
        for m in range(out_ref.shape[0]):
            joined_ref[m, i * piece : (i + 1) * piece, :] = wide_ref[
                i, m * piece : (m + 1) * piece, :
            ]
    out_ref[...] = joined_ref[...].astype(BF)
    send = copy(out_ref, out_hbm, sem.at[0])
    send.start()
    send.wait()


def join_pieces(parts, frames, after):
    pieces, rows, width = parts.shape
    piece = rows // frames
    shape = (frames, pieces * piece, width)
    return pl.pallas_call(
        functools.partial(join_pieces_kernel, piece),
        in_specs=[ANY, ANY],
        out_specs=HBM,
        out_shape=hbm_out(shape),
        scratch_shapes=[
            pltpu.VMEM(parts.shape, BF),
            pltpu.VMEM(parts.shape, F32),
            pltpu.VMEM(shape, F32),
            pltpu.VMEM(shape, BF),
            DMA((pieces,)),
        ],
        compiler_params=params(),
        name="join_pieces",
        cost_estimate=cost(parts.size, 4 * parts.size),
    )(parts, in_hbm(after))


def modulate_kernel(
    held,
    act_hbm, affine_hbm, weight_hbm, sharpness_ref, owner_ref, slot_ref, _, hidden_hbm, query_hbm,
    act_ref, affine_ref, weight_ref, hidden_ref, query_ref,
    load_sem, affine_sem, weight_sem, store_sem, query_sem,
):
    steps, rows, _ = act_ref.shape
    patches = query_ref.shape[1] - PAD
    loads, stores = [], []
    for i in range(steps):
        at = pl.ds(i * rows, rows)
        loads.append(copy(act_hbm.at[at, :], act_ref.at[i], load_sem.at[i]))
        stores.append(copy(hidden_ref.at[i], hidden_hbm.at[at, :], store_sem.at[i]))
    weight_load = copy(weight_hbm.at[:, pl.ds(0, HW)], weight_ref, weight_sem)
    affine_load = copy(affine_hbm, affine_ref, affine_sem)
    affine_load.start()
    loads[0].start()
    weight_load.start()
    row = lax.broadcasted_iota(jnp.int32, (PAD, C), 0)
    column = lax.broadcasted_iota(jnp.int32, (PAD, C), 1)
    tail = jnp.zeros((PAD, C), jnp.int32)
    for j in range(TOPM):
        tail = jnp.where((row == 0) & (column == j), owner_ref[j] * held + slot_ref[j], tail)
    for h in range(G):
        query_ref[h, patches:, :] = tail.astype(F32).astype(BF)
    affine_load.wait()
    for i in range(steps):
        at = slice(i * rows, (i + 1) * rows)
        loads[i].wait()
        if i + 1 < steps:
            loads[i + 1].start()
        act = act_ref[i].astype(F32)
        hidden = act * inverse_rms(act) * (1.0 + affine_ref[0:1, :]) + affine_ref[1:2, :]
        hidden = hidden.astype(BF)
        hidden_ref[i] = hidden
        stores[i].start()
        if i == 0:
            weight_load.wait()
        mapped = dot(hidden, weight_ref[...]).astype(BF).astype(F32)
        for h in range(G):
            one = mapped[:, h * C : (h + 1) * C]
            query_ref[h, at, :] = (
                one * inverse_rms(one) * (sharpness_ref[0, h] / C)
            ).astype(BF)
    sends = [
        copy(query_ref, query_hbm.at[k], query_sem.at[k]) for k in range(query_hbm.shape[0])
    ]
    for send in sends:
        send.start()
    for store in stores + sends:
        store.wait()


def modulate(act, affine, weight, sharpness, owner, slot, held, copies, after):
    patches, depth = act.shape
    steps = 2
    rows = patches // steps
    shape = (G, patches + PAD, C)
    return pl.pallas_call(
        functools.partial(modulate_kernel, held),
        in_specs=[HBM, HBM, HBM, SCALARS, SCALARS, SCALARS, ANY],
        out_specs=[HBM, HBM],
        out_shape=[hbm_out((patches, depth)), hbm_out((copies,) + shape)],
        scratch_shapes=[
            pltpu.VMEM((steps, rows, depth), BF),
            pltpu.VMEM(affine.shape, F32),
            pltpu.VMEM((depth, HW), BF),
            pltpu.VMEM((steps, rows, depth), BF),
            pltpu.VMEM(shape, BF),
            DMA((steps,)),
            DMA,
            DMA,
            DMA((steps,)),
            DMA((copies,)),
        ],
        compiler_params=params(),
        name="modulate",
        cost_estimate=cost(
            2 * patches * depth * HW, 4 * patches * depth + 2 * depth * HW + 2 * patches * HW
        ),
    )(in_hbm(act), in_hbm(affine), in_hbm(weight), sharpness, owner, slot, in_hbm(after))


def temporal_entry_kernel(
    quarters, hidden_hbm, weight_hbm, sharpness_ref, *refs
):
    out_hbm, hidden_ref, weight_ref, out_ref, hidden_sem, weight_sem, store_sem = refs[-7:]
    rows = hidden_ref.shape[0] // quarters
    hidden_load = copy(hidden_hbm, hidden_ref, hidden_sem)
    loads = [
        copy(
            weight_hbm.at[:, pl.ds((3 + part) * HW, HW)], weight_ref.at[part], weight_sem.at[part]
        )
        for part in range(3)
    ]
    hidden_load.start()
    loads[0].start()
    hidden_load.wait()
    stores = []
    for part in range(3):
        loads[part].wait()
        if part < 2:
            loads[part + 1].start()
        mapped = dot(hidden_ref[...], weight_ref[part]).astype(BF)
        for h in range(G):
            done = mapped[:, h * C : (h + 1) * C]
            if part < 2:
                one = done.astype(F32)
                one = one * inverse_rms(one)
                if part == 0:
                    one = one * (sharpness_ref[1, h] / C)
                done = one.astype(BF)
            for z in range(quarters):
                out_ref[part, z, h] = done[z * rows : (z + 1) * rows, :]
        stores.append(copy(out_ref.at[part], out_hbm.at[:, :, part], store_sem.at[part]))
        stores[-1].start()
    for store in stores:
        store.wait()


def temporal_entry(hidden, weight, sharpness, quarters, after):
    patches, depth = hidden.shape
    rows = patches // quarters
    return pl.pallas_call(
        functools.partial(temporal_entry_kernel, quarters),
        in_specs=[HBM, HBM, SCALARS] + [ANY] * len(after),
        out_specs=HBM,
        out_shape=hbm_out((quarters, G, 3, rows, C)),
        scratch_shapes=[
            pltpu.VMEM((patches, depth), BF),
            pltpu.VMEM((3, depth, HW), BF),
            pltpu.VMEM((3, quarters, G, rows, C), BF),
            DMA,
            DMA((3,)),
            DMA((3,)),
        ],
        compiler_params=params(),
        name="temporal_entry",
        cost_estimate=cost(
            6 * patches * depth * HW, 2 * patches * depth + 6 * depth * HW + 6 * patches * HW
        ),
    )(in_hbm(hidden), in_hbm(weight), sharpness, *after)


def temporal_attend_kernel(length_ref, in_hbm_ref, _, out_hbm, in_ref, out_ref, sem):
    frames, _, rows, _ = in_ref.shape
    group = 16
    size = frames * group
    load = copy(in_hbm_ref, in_ref, sem)
    load.start()
    length = length_ref[0]
    row = lax.broadcasted_iota(jnp.int32, (size, size), 0)
    column = lax.broadcasted_iota(jnp.int32, (size, size), 1)
    target, source = row // group, column // group
    keep = (row % group == column % group) & (source <= target) & (source > target - length)
    load.wait()
    for g in range(rows // group):
        at = slice(g * group, (g + 1) * group)
        query = in_ref[:, 0, at, :].reshape(size, C)
        key = in_ref[:, 1, at, :].reshape(size, C)
        value = in_ref[:, 2, at, :].reshape(size, C)
        weights = jnp.where(keep, jnp.exp(dot_t(query, key)), 0.0)
        shares = weights / jnp.sum(weights, axis=-1, keepdims=True)
        result = dot(shares.astype(BF), value).astype(BF)
        out_ref[:, at, :] = result.reshape(frames, group, C)
    store = copy(out_ref, out_hbm, sem)
    store.start()
    store.wait()


def temporal_attend(length, parts, after):
    frames, _, rows, _ = parts.shape
    shape = (frames, rows, C)
    return pl.pallas_call(
        temporal_attend_kernel,
        in_specs=[SCALARS, ANY, ANY],
        out_specs=HBM,
        out_shape=hbm_out(shape),
        scratch_shapes=[pltpu.VMEM(parts.shape, BF), pltpu.VMEM(shape, BF), DMA],
        compiler_params=params(),
        name="temporal_attend",
        cost_estimate=cost(4 * frames * rows * 256 * C, 8 * frames * rows * C),
    )(length, parts, in_hbm(after))


LINE = 96
CHUNK = 3 * LINE


def halves(denominators):
    high = denominators.astype(BF).astype(F32)
    return jnp.concatenate([high, denominators - high], axis=0).astype(BF)


def attend_rows(query, keys, both, out_ref):
    patches = out_ref.shape[0] - PAD
    row = lax.broadcasted_iota(jnp.int32, (LINE, C), 0)
    column = lax.broadcasted_iota(jnp.int32, (LINE, C), 1)
    lines = []
    for start in range(0, patches, CHUNK):
        at = slice(start, start + CHUNK)
        weights = jnp.exp(dot_t(query(at), keys)).astype(BF)
        result = dot(weights, both)
        out_ref[at, :] = result[:, :C].astype(BF)
        for j in range(0, CHUNK, LINE):
            diagonal = jnp.where(row == column, result[j : j + LINE, C:], 0.0)
            lines.append(jnp.sum(diagonal, axis=0, keepdims=True))
    lines.append(jnp.zeros((8 - len(lines), C), F32))
    out_ref[patches:, :] = halves(jnp.concatenate(lines, axis=0))


def with_ones(values):
    return jnp.concatenate([values, jnp.ones(values.shape, BF)], axis=1)


def own_attend_kernel(
    hidden_hbm, weight_hbm, query_hbm, *refs
):
    out_hbm, hidden_ref, weight_ref, query_ref, out_ref = refs[-9:-4]
    hidden_sem, weight_sem, query_sem, store_sem = refs[-4:]
    hidden_load = copy(hidden_hbm, hidden_ref, hidden_sem)
    query_load = copy(query_hbm.at[0], query_ref, query_sem)
    loads = [
        copy(
            weight_hbm.at[:, pl.ds((1 + part) * HW, HW)], weight_ref.at[part], weight_sem.at[part]
        )
        for part in range(2)
    ]
    hidden_load.start()
    loads[0].start()
    hidden_load.wait()
    loads[0].wait()
    loads[1].start()
    query_load.start()
    keys = dot(hidden_ref[...], weight_ref[0]).astype(BF)
    loads[1].wait()
    values = dot(hidden_ref[...], weight_ref[1]).astype(BF)
    query_load.wait()
    stores = []
    for h in range(G):
        key = keys[:, h * C : (h + 1) * C].astype(F32)
        key = (key * inverse_rms(key)).astype(BF)
        both = with_ones(values[:, h * C : (h + 1) * C])
        attend_rows(lambda at, h=h: query_ref[h, at, :], key, both, out_ref.at[h])
        stores.append(copy(out_ref.at[h], out_hbm.at[h], store_sem.at[h]))
        stores[-1].start()
    for store in stores:
        store.wait()


def own_attend(hidden, weight, query, after):
    patches, depth = hidden.shape
    shape = query.shape[1:]
    return pl.pallas_call(
        own_attend_kernel,
        in_specs=[HBM, HBM, HBM] + [ANY] * len(after),
        out_specs=HBM,
        out_shape=hbm_out(shape),
        scratch_shapes=[
            pltpu.VMEM((patches, depth), BF),
            pltpu.VMEM((2, depth, HW), BF),
            pltpu.VMEM(shape, BF),
            pltpu.VMEM(shape, BF),
            DMA,
            DMA((2,)),
            DMA,
            DMA((G,)),
        ],
        compiler_params=params(),
        name="own_attend",
        cost_estimate=cost(
            4 * patches * depth * HW + 6 * patches * patches * HW,
            2 * patches * depth + 4 * depth * HW + 10 * patches * HW,
        ),
    )(in_hbm(hidden), in_hbm(weight), in_hbm(query), *after)


def memory_attend_kernel(count, base_ref, index_ref, query_hbm, *refs):
    blocks = refs[:count]
    out_hbm, query_ref, store_ref, out_ref, query_sem, block_sem, store_sem = refs[count + 1 :]
    frames = query_ref.shape[0]
    base = base_ref[0]
    query_load = copy(query_hbm.at[pl.ds(base, frames)], query_ref, query_sem)
    query_load.start()

    def fetch(t, carry):
        i, j = t // TOPM, lax.rem(t, TOPM)
        wanted = index_ref[base + i, j]
        start = 0
        for block in blocks:
            held = block.shape[0]

            @pl.when((wanted >= start) & (wanted < start + held))
            def _(block=block, start=start):
                copy(block.at[wanted - start], store_ref.at[i, j], block_sem.at[i]).start()

            start += held
        return carry

    lax.fori_loop(0, frames * TOPM, fetch, 0)
    query_load.wait()
    stores = []
    for i in range(frames):
        copy(store_ref.at[i], store_ref.at[i], block_sem.at[i]).wait()
        keys = jnp.concatenate([store_ref[i, j, :, :C] for j in range(TOPM)], axis=0)
        values = jnp.concatenate([store_ref[i, j, :, C:] for j in range(TOPM)], axis=0)
        attend_rows(
            lambda at, i=i: query_ref[i, at, :], keys, with_ones(values), out_ref.at[i]
        )
        stores.append(copy(out_ref.at[i], out_hbm.at[i], store_sem.at[i]))
        stores[-1].start()
    for store in stores:
        store.wait()


def memory_attend(base, index, query, frames, blocks, after):
    count = len(blocks)
    rows = query.shape[1]
    _, part, width = blocks[0].shape
    shape = (frames, rows, C)
    return pl.pallas_call(
        functools.partial(memory_attend_kernel, count),
        in_specs=[SCALARS, SCALARS] + [ANY] * (count + 2),
        out_specs=HBM,
        out_shape=hbm_out(shape),
        scratch_shapes=[
            pltpu.VMEM(shape, BF),
            pltpu.VMEM((frames, TOPM, part, width), BF),
            pltpu.VMEM(shape, BF),
            DMA,
            DMA((frames,)),
            DMA((frames,)),
        ],
        compiler_params=params(),
        name="memory_attend",
        cost_estimate=cost(
            8 * frames * rows * TOPM * part * C,
            4 * frames * rows * C + 2 * frames * TOPM * part * width,
        ),
    )(base, index, query, *blocks, in_hbm(after))


def add_partials_kernel(count, x_ref, *refs):
    ins, outs = refs[:count], refs[count : count + G]
    parts_ref, out_ref, load_sem, store_sem = refs[count + G :]
    patches = out_ref.shape[1] - PAD
    loads = []
    for j in range(G):
        frame = lax.rem(x_ref[0] + j, G)
        loads.append(
            [copy(ref.at[frame], parts_ref.at[k, j], load_sem.at[k, j]) for k, ref in enumerate(ins)]
        )
    for of_frame in loads:
        for load in of_frame:
            load.start()
    stores = []
    for j in range(G):
        for load in loads[j]:
            load.wait()
        total = parts_ref[0, j].astype(F32)
        for k in range(1, count):
            total = total + parts_ref[k, j].astype(F32)
        out_ref[j, :patches, :] = total[:patches].astype(BF)
        out_ref[j, patches:, :] = halves(total[patches : patches + 8] + total[patches + 8 :])
        stores.append(copy(out_ref.at[j], outs[j], store_sem.at[j]))
        stores[-1].start()
    for store in stores:
        store.wait()


def add_partials(x, parts):
    shape = parts[0].shape
    return pl.pallas_call(
        functools.partial(add_partials_kernel, len(parts)),
        in_specs=[SCALARS] + [ANY] * len(parts),
        out_specs=[HBM] * G,
        out_shape=[hbm_out(shape[1:])] * G,
        scratch_shapes=[
            pltpu.VMEM((len(parts),) + shape, BF),
            pltpu.VMEM(shape, BF),
            DMA((len(parts), G)),
            DMA((G,)),
        ],
        compiler_params=params(),
        name="add_partials",
        cost_estimate=cost(4 * parts[0].size, 8 * parts[0].size),
    )(x, *parts)


def leave_kernel(
    x_ref, own_hbm, memory_0, memory_1, memory_2, memory_3, time_hbm, weight_hbm, out_hbm,
    own_ref, memory_ref, time_ref, combined_ref, weight_ref, out_ref,
    own_sem, memory_sem, time_sem, weight_sem, store_sem,
):
    patches = own_ref.shape[1] - PAD
    quarters = time_ref.shape[0] // G
    rows = time_ref.shape[1]
    steps, _, width = weight_ref.shape
    heads = [lax.rem(x_ref[0] + G - j, G) for j in range(G)]
    memories = (memory_0, memory_1, memory_2, memory_3)
    own_loads = [copy(own_hbm.at[heads[j]], own_ref.at[j], own_sem.at[j]) for j in range(G)]
    memory_loads = [copy(memories[j], memory_ref.at[j], memory_sem.at[j]) for j in range(G)]
    time_load = copy(time_hbm, time_ref, time_sem)
    loads, stores = [], []
    for i in range(steps):
        at = pl.ds(i * width, width)
        loads.append(copy(weight_hbm.at[:, at], weight_ref.at[i], weight_sem.at[i]))
        stores.append(copy(out_ref.at[i], out_hbm.at[:, at], store_sem.at[i]))
    for load in own_loads + memory_loads + [time_load] + loads:
        load.start()
    row = lax.broadcasted_iota(jnp.int32, (LINE, C), 0)
    column = lax.broadcasted_iota(jnp.int32, (LINE, C), 1)
    for h in range(G):
        own_loads[h].wait()
        memory_loads[h].wait()
        column_at = pl.ds(pl.multiple_of(heads[h] * C, C), C)
        tail = own_ref[h, patches:, :].astype(F32) + memory_ref[h, patches:, :].astype(F32)
        denominators = tail[:8] + tail[8:]
        for j in range(patches // LINE):
            at = slice(j * LINE, (j + 1) * LINE)
            line = jnp.broadcast_to(denominators[j : j + 1, :], (LINE, C))
            total = jnp.sum(jnp.where(row == column, line, 0.0), axis=1, keepdims=True)
            top = own_ref[h, at, :].astype(F32) + memory_ref[h, at, :].astype(F32)
            combined_ref[at, column_at] = (top / total).astype(BF)
    time_load.wait()
    for h in range(G):
        for z in range(quarters):
            combined_ref[z * rows : (z + 1) * rows, HW + h * C : HW + (h + 1) * C] = time_ref[
                z * G + h
            ]
    for i in range(steps):
        loads[i].wait()
        out_ref[i] = dot(combined_ref[...], weight_ref[i]).astype(BF)
        stores[i].start()
    for store in stores:
        store.wait()


def leave(x, own, memory, time, weight):
    patches = own.shape[1] - PAD
    depth, width = weight.shape
    steps = 4
    step = width // steps
    return pl.pallas_call(
        leave_kernel,
        in_specs=[SCALARS, HBM] + [ANY] * (G + 1) + [HBM],
        out_specs=HBM,
        out_shape=hbm_out((patches, width)),
        scratch_shapes=[
            pltpu.VMEM(own.shape, BF),
            pltpu.VMEM(own.shape, BF),
            pltpu.VMEM(time.shape, BF),
            pltpu.VMEM((patches, depth), BF),
            pltpu.VMEM((steps, depth, step), BF),
            pltpu.VMEM((steps, patches, step), BF),
            DMA((G,)),
            DMA((G,)),
            DMA,
            DMA((steps,)),
            DMA((steps,)),
        ],
        compiler_params=params(),
        name="leave",
        cost_estimate=cost(
            2 * patches * depth * width,
            2 * depth * width + 2 * patches * width + 6 * patches * depth,
        ),
    )(x, in_hbm(own), *memory, time, in_hbm(weight))


def on_device(
    patch_activation_tensor,
    conditioning_affine,
    entry_projection_matrix,
    exit_projection_matrix,
    softmax_sharpness,
    cached_past_pairs,
    recalled_picture_holder,
    recalled_picture_position,
    lookback_lengths,
):
    frame = ("zq", "zp", "x")
    rings, sides = lax.axis_size("y"), lax.axis_size("zp")
    quarters = lax.axis_size("zq") * sides
    patches, depth = patch_activation_tensor.shape[2:]
    held, piece = cached_past_pairs.shape[:2]
    cores = lax.axis_size("c")
    x = lax.axis_index("x").astype(jnp.int32).reshape(1)
    side = lax.axis_index("zp").astype(jnp.int32).reshape(1)

    def turn(step):
        return [(s, (s + step) % rings) for s in range(rings)]

    def other(size):
        return [(s, size - 1 - s) for s in range(size)]

    def swap(blocks, axes):
        return lax.all_to_all(blocks, axes, split_axis=0, concat_axis=0, tiled=True)

    def swap_apart(blocks):
        return [in_hbm(blocks[0])] + [lax.ppermute(blocks[j], "x", turn(j)) for j in range(1, G)]

    with jax.named_scope("store"):
        split = split_store(
            cached_past_pairs.reshape(held * piece, 2 * HW), lax.axis_size("zq")
        )
        pieces = swap(split.reshape((-1,) + split.shape[2:]), ("zq", "x"))

    with jax.named_scope("queries"):
        hidden, query = modulate(
            patch_activation_tensor.reshape(patches, depth),
            conditioning_affine.reshape(2, depth),
            entry_projection_matrix,
            softmax_sharpness,
            recalled_picture_holder.reshape(TOPM),
            recalled_picture_position.reshape(TOPM),
            held,
            sides,
            after=split,
        )

    with jax.named_scope("store"):
        joined = join_pieces(pieces, held, after=hidden)
        above = lax.ppermute(joined, "y", turn(-1))
        below = lax.ppermute(joined, "y", turn(1))

    with jax.named_scope("queries"):
        asked, joined = lax.optimization_barrier((query, joined))
        asked = swap(asked.reshape((-1,) + asked.shape[2:]), ("zp", "x"))

    with jax.named_scope("temporal"):
        parts = temporal_entry(
            hidden, entry_projection_matrix, softmax_sharpness, quarters, after=[in_hbm(joined)]
        )
        sent = swap(parts.reshape((quarters * G,) + parts.shape[2:]), frame)

    with jax.named_scope("store"):
        above, below, parts = lax.optimization_barrier((above, below, parts))
        far_first = lax.ppermute(above[: held // 2], "y", turn(-1))
        far_last = lax.ppermute(below[held // 2 :], "y", turn(1))
        near = [joined, above, far_first, far_last, below]
        blocks = near + [lax.ppermute(block, "c", other(cores)) for block in near]
        blocks[0] = in_hbm(blocks[0])

    with jax.named_scope("own"):
        own = own_attend(
            hidden, entry_projection_matrix, query, after=[in_hbm(parts), asked]
        )

    with jax.named_scope("queries"):
        named = asked[:, patches, :TOPM].astype(jnp.int32)
        y = (named // (cores * held) - lax.axis_index("y")) & (rings - 1)
        c = (named // held & (cores - 1)) ^ lax.axis_index("c")
        index = (c * rings + y) * held + (named & (held - 1))

    def attend(base, after):
        return memory_attend(base, index, asked, asked.shape[0] // sides, blocks, after)

    with jax.named_scope("memory"):
        count = asked.shape[0] // sides
        sum_beside = attend((sides - 1 - side) * count, own)
        from_beside = lax.ppermute(sum_beside, "zp", other(sides))
        sum_here = attend(side * count, sum_beside)

    with jax.named_scope("temporal"):
        timed = temporal_attend(lookback_lengths, sent, after=sum_here)
        time = swap(timed, frame)

    with jax.named_scope("memory"):
        memory = swap_apart(add_partials(x, [in_hbm(sum_here), from_beside]))

    with jax.named_scope("exit"):
        attended = leave(x, own, memory, time, exit_projection_matrix)
    return attended.reshape(1, 1, patches, depth)


def solution(mesh):
    apart = Mesh(mesh.devices.reshape(4, 2, 2, 2, 4), ("y", "c", "zq", "zp", "x"))
    roll, frame = ("y", "c"), ("zq", "zp", "x")
    return jax.shard_map(
        on_device,
        mesh=apart,
        in_specs=(
            P(roll, frame, None, None),
            P(roll, frame, None, None),
            P(),
            P(),
            P(),
            P(roll, frame, None, None),
            P(roll, frame, None, None),
            P(roll, frame, None),
            P(roll),
        ),
        out_specs=P(roll, frame, None, None),
        check_vma=False,
    )
```

```python
import functools

import jax
import jax.numpy as jnp
from jax import lax
from jax.experimental import pallas as pl
from jax.experimental.pallas import tpu as pltpu
from jax.sharding import Mesh
from jax.sharding import PartitionSpec as P

G = 4
C = 128
HW = G * C
TOPM = 6
EPSILON = 1e-06
BF = jnp.bfloat16
F32 = jnp.float32
PAD = 16
VMEM_LIMIT = 28 * 1024 * 1024
ANY = pl.BlockSpec(memory_space=pl.ANY)
HBM = pl.BlockSpec(memory_space=pltpu.HBM)
WHOLE = pl.BlockSpec(memory_space=pltpu.VMEM)
SCALARS = pl.BlockSpec(memory_space=pltpu.SMEM)


def params(**more):
    return pltpu.CompilerParams(vmem_limit_bytes=VMEM_LIMIT, **more)


def cost(flops, bytes_accessed):
    return pl.CostEstimate(
        flops=flops // 16, bytes_accessed=bytes_accessed // 16, transcendentals=0
    )


def in_hbm(array):
    return pltpu.with_memory_space_constraint(array, pltpu.HBM)


def hbm_out(shape, dtype=BF):
    return pltpu.HBM(shape, dtype)


def inverse_rms(values):
    return lax.rsqrt(jnp.mean(values * values, axis=-1, keepdims=True) + EPSILON)


def dot(a, b):
    return jnp.dot(a, b, preferred_element_type=F32)


def dot_t(a, b):
    return lax.dot_general(a, b, (((1,), (1,)), ((), ())), preferred_element_type=F32)


DMA = pltpu.SemaphoreType.DMA
copy = pltpu.make_async_copy


def split_store_kernel(rows_ref, out_hbm, out_ref, sem):
    sends = []
    for h in range(G):
        key = rows_ref[:, h * C : (h + 1) * C].astype(F32)
        out_ref[h, :, :C] = (key * inverse_rms(key)).astype(BF)
        out_ref[h, :, C:] = rows_ref[:, HW + h * C : HW + (h + 1) * C]
        for k in range(out_hbm.shape[0]):
            sends.append(copy(out_ref.at[h], out_hbm.at[k, h], sem.at[k, h]))
            sends[-1].start()
    for send in sends:
        send.wait()


def split_store(rows, copies):
    n = rows.shape[0]
    return pl.pallas_call(
        split_store_kernel,
        in_specs=[WHOLE],
        out_specs=HBM,
        out_shape=hbm_out((copies, G, n, 2 * C)),
        scratch_shapes=[pltpu.VMEM((G, n, 2 * C), BF), DMA((copies, G))],
        compiler_params=params(),
        name="split_store",
        cost_estimate=cost(8 * n * HW, 8 * n * HW),
    )(rows)


def join_pieces_kernel(piece, in_hbm, _, out_hbm, in_ref, wide_ref, joined_ref, out_ref, sem):
    pieces = in_ref.shape[0]
    loads = [copy(in_hbm.at[i], in_ref.at[i], sem.at[i]) for i in range(pieces)]
    for load in loads:
        load.start()
    for i in range(pieces):
        loads[i].wait()
        wide_ref[i] = in_ref[i].astype(F32)
        for m in range(out_ref.shape[0]):
            joined_ref[m, i * piece : (i + 1) * piece, :] = wide_ref[
                i, m * piece : (m + 1) * piece, :
            ]
    out_ref[...] = joined_ref[...].astype(BF)
    send = copy(out_ref, out_hbm, sem.at[0])
    send.start()
    send.wait()


def join_pieces(parts, frames, after):
    pieces, rows, width = parts.shape
    piece = rows // frames
    shape = (frames, pieces * piece, width)
    return pl.pallas_call(
        functools.partial(join_pieces_kernel, piece),
        in_specs=[ANY, ANY],
        out_specs=HBM,
        out_shape=hbm_out(shape),
        scratch_shapes=[
            pltpu.VMEM(parts.shape, BF),
            pltpu.VMEM(parts.shape, F32),
            pltpu.VMEM(shape, F32),
            pltpu.VMEM(shape, BF),
            DMA((pieces,)),
        ],
        compiler_params=params(),
        name="join_pieces",
        cost_estimate=cost(parts.size, 4 * parts.size),
    )(parts, in_hbm(after))


def modulate_kernel(
    held,
    act_hbm, affine_hbm, weight_hbm, sharpness_ref, owner_ref, slot_ref, _, hidden_hbm, query_hbm,
    act_ref, affine_ref, weight_ref, hidden_ref, query_ref,
    load_sem, affine_sem, weight_sem, store_sem, query_sem,
):
    steps, rows, _ = act_ref.shape
    patches = query_ref.shape[1] - PAD
    loads, stores = [], []
    for i in range(steps):
        at = pl.ds(i * rows, rows)
        loads.append(copy(act_hbm.at[at, :], act_ref.at[i], load_sem.at[i]))
        stores.append(copy(hidden_ref.at[i], hidden_hbm.at[at, :], store_sem.at[i]))
    weight_load = copy(weight_hbm.at[:, pl.ds(0, HW)], weight_ref, weight_sem)
    affine_load = copy(affine_hbm, affine_ref, affine_sem)
    affine_load.start()
    loads[0].start()
    weight_load.start()
    row = lax.broadcasted_iota(jnp.int32, (PAD, C), 0)
    column = lax.broadcasted_iota(jnp.int32, (PAD, C), 1)
    tail = jnp.zeros((PAD, C), jnp.int32)
    for j in range(TOPM):
        tail = jnp.where((row == 0) & (column == j), owner_ref[j] * held + slot_ref[j], tail)
    for h in range(G):
        query_ref[h, patches:, :] = tail.astype(F32).astype(BF)
    affine_load.wait()
    for i in range(steps):
        at = slice(i * rows, (i + 1) * rows)
        loads[i].wait()
        if i + 1 < steps:
            loads[i + 1].start()
        act = act_ref[i].astype(F32)
        hidden = act * inverse_rms(act) * (1.0 + affine_ref[0:1, :]) + affine_ref[1:2, :]
        hidden = hidden.astype(BF)
        hidden_ref[i] = hidden
        stores[i].start()
        if i == 0:
            weight_load.wait()
        mapped = dot(hidden, weight_ref[...]).astype(BF).astype(F32)
        for h in range(G):
            one = mapped[:, h * C : (h + 1) * C]
            query_ref[h, at, :] = (
                one * inverse_rms(one) * (sharpness_ref[0, h] / C)
            ).astype(BF)
    sends = [
        copy(query_ref, query_hbm.at[k], query_sem.at[k]) for k in range(query_hbm.shape[0])
    ]
    for send in sends:
        send.start()
    for store in stores + sends:
        store.wait()


def modulate(act, affine, weight, sharpness, owner, slot, held, copies, after):
    patches, depth = act.shape
    steps = 2
    rows = patches // steps
    shape = (G, patches + PAD, C)
    return pl.pallas_call(
        functools.partial(modulate_kernel, held),
        in_specs=[HBM, HBM, HBM, SCALARS, SCALARS, SCALARS, ANY],
        out_specs=[HBM, HBM],
        out_shape=[hbm_out((patches, depth)), hbm_out((copies,) + shape)],
        scratch_shapes=[
            pltpu.VMEM((steps, rows, depth), BF),
            pltpu.VMEM(affine.shape, F32),
            pltpu.VMEM((depth, HW), BF),
            pltpu.VMEM((steps, rows, depth), BF),
            pltpu.VMEM(shape, BF),
            DMA((steps,)),
            DMA,
            DMA,
            DMA((steps,)),
            DMA((copies,)),
        ],
        compiler_params=params(),
        name="modulate",
        cost_estimate=cost(
            2 * patches * depth * HW, 4 * patches * depth + 2 * depth * HW + 2 * patches * HW
        ),
    )(in_hbm(act), in_hbm(affine), in_hbm(weight), sharpness, owner, slot, in_hbm(after))


def temporal_entry_kernel(
    quarters, hidden_hbm, weight_hbm, sharpness_ref, *refs
):
    out_hbm, hidden_ref, weight_ref, out_ref, hidden_sem, weight_sem, store_sem = refs[-7:]
    rows = hidden_ref.shape[0] // quarters
    hidden_load = copy(hidden_hbm, hidden_ref, hidden_sem)
    loads = [
        copy(
            weight_hbm.at[:, pl.ds((3 + part) * HW, HW)], weight_ref.at[part], weight_sem.at[part]
        )
        for part in range(3)
    ]
    hidden_load.start()
    loads[0].start()
    hidden_load.wait()
    stores = []
    for part in range(3):
        loads[part].wait()
        if part < 2:
            loads[part + 1].start()
        mapped = dot(hidden_ref[...], weight_ref[part]).astype(BF)
        for h in range(G):
            done = mapped[:, h * C : (h + 1) * C]
            if part < 2:
                one = done.astype(F32)
                one = one * inverse_rms(one)
                if part == 0:
                    one = one * (sharpness_ref[1, h] / C)
                done = one.astype(BF)
            for z in range(quarters):
                out_ref[part, z, h] = done[z * rows : (z + 1) * rows, :]
        stores.append(copy(out_ref.at[part], out_hbm.at[:, :, part], store_sem.at[part]))
        stores[-1].start()
    for store in stores:
        store.wait()


def temporal_entry(hidden, weight, sharpness, quarters, after):
    patches, depth = hidden.shape
    rows = patches // quarters
    return pl.pallas_call(
        functools.partial(temporal_entry_kernel, quarters),
        in_specs=[HBM, HBM, SCALARS] + [ANY] * len(after),
        out_specs=HBM,
        out_shape=hbm_out((quarters, G, 3, rows, C)),
        scratch_shapes=[
            pltpu.VMEM((patches, depth), BF),
            pltpu.VMEM((3, depth, HW), BF),
            pltpu.VMEM((3, quarters, G, rows, C), BF),
            DMA,
            DMA((3,)),
            DMA((3,)),
        ],
        compiler_params=params(),
        name="temporal_entry",
        cost_estimate=cost(
            6 * patches * depth * HW, 2 * patches * depth + 6 * depth * HW + 6 * patches * HW
        ),
    )(in_hbm(hidden), in_hbm(weight), sharpness, *after)


def temporal_attend_kernel(length_ref, in_hbm_ref, _, out_hbm, in_ref, out_ref, sem):
    frames, _, rows, _ = in_ref.shape
    group = 16
    size = frames * group
    load = copy(in_hbm_ref, in_ref, sem)
    load.start()
    length = length_ref[0]
    row = lax.broadcasted_iota(jnp.int32, (size, size), 0)
    column = lax.broadcasted_iota(jnp.int32, (size, size), 1)
    target, source = row // group, column // group
    keep = (row % group == column % group) & (source <= target) & (source > target - length)
    load.wait()
    for g in range(rows // group):
        at = slice(g * group, (g + 1) * group)
        query = in_ref[:, 0, at, :].reshape(size, C)
        key = in_ref[:, 1, at, :].reshape(size, C)
        value = in_ref[:, 2, at, :].reshape(size, C)
        weights = jnp.where(keep, jnp.exp(dot_t(query, key)), 0.0)
        shares = weights / jnp.sum(weights, axis=-1, keepdims=True)
        result = dot(shares.astype(BF), value).astype(BF)
        out_ref[:, at, :] = result.reshape(frames, group, C)
    store = copy(out_ref, out_hbm, sem)
    store.start()
    store.wait()


def temporal_attend(length, parts, after):
    frames, _, rows, _ = parts.shape
    shape = (frames, rows, C)
    return pl.pallas_call(
        temporal_attend_kernel,
        in_specs=[SCALARS, ANY, ANY],
        out_specs=HBM,
        out_shape=hbm_out(shape),
        scratch_shapes=[pltpu.VMEM(parts.shape, BF), pltpu.VMEM(shape, BF), DMA],
        compiler_params=params(),
        name="temporal_attend",
        cost_estimate=cost(4 * frames * rows * 256 * C, 8 * frames * rows * C),
    )(length, parts, in_hbm(after))


LINE = 96
CHUNK = 3 * LINE


def halves(denominators):
    high = denominators.astype(BF).astype(F32)
    return jnp.concatenate([high, denominators - high], axis=0).astype(BF)


def attend_rows(query, keys, both, out_ref):
    patches = out_ref.shape[0] - PAD
    row = lax.broadcasted_iota(jnp.int32, (LINE, C), 0)
    column = lax.broadcasted_iota(jnp.int32, (LINE, C), 1)
    lines = []
    for start in range(0, patches, CHUNK):
        at = slice(start, start + CHUNK)
        weights = jnp.exp(dot_t(query(at), keys)).astype(BF)
        result = dot(weights, both)
        out_ref[at, :] = result[:, :C].astype(BF)
        for j in range(0, CHUNK, LINE):
            diagonal = jnp.where(row == column, result[j : j + LINE, C:], 0.0)
            lines.append(jnp.sum(diagonal, axis=0, keepdims=True))
    lines.append(jnp.zeros((8 - len(lines), C), F32))
    out_ref[patches:, :] = halves(jnp.concatenate(lines, axis=0))


def with_ones(values):
    return jnp.concatenate([values, jnp.ones(values.shape, BF)], axis=1)


def own_attend_kernel(
    hidden_hbm, weight_hbm, query_hbm, *refs
):
    out_hbm, hidden_ref, weight_ref, query_ref, out_ref = refs[-9:-4]
    hidden_sem, weight_sem, query_sem, store_sem = refs[-4:]
    hidden_load = copy(hidden_hbm, hidden_ref, hidden_sem)
    query_load = copy(query_hbm.at[0], query_ref, query_sem)
    loads = [
        copy(
            weight_hbm.at[:, pl.ds((1 + part) * HW, HW)], weight_ref.at[part], weight_sem.at[part]
        )
        for part in range(2)
    ]
    hidden_load.start()
    loads[0].start()
    hidden_load.wait()
    loads[0].wait()
    loads[1].start()
    query_load.start()
    keys = dot(hidden_ref[...], weight_ref[0]).astype(BF)
    loads[1].wait()
    values = dot(hidden_ref[...], weight_ref[1]).astype(BF)
    query_load.wait()
    stores = []
    for h in range(G):
        key = keys[:, h * C : (h + 1) * C].astype(F32)
        key = (key * inverse_rms(key)).astype(BF)
        both = with_ones(values[:, h * C : (h + 1) * C])
        attend_rows(lambda at, h=h: query_ref[h, at, :], key, both, out_ref.at[h])
        stores.append(copy(out_ref.at[h], out_hbm.at[h], store_sem.at[h]))
        stores[-1].start()
    for store in stores:
        store.wait()


def own_attend(hidden, weight, query, after):
    patches, depth = hidden.shape
    shape = query.shape[1:]
    return pl.pallas_call(
        own_attend_kernel,
        in_specs=[HBM, HBM, HBM] + [ANY] * len(after),
        out_specs=HBM,
        out_shape=hbm_out(shape),
        scratch_shapes=[
            pltpu.VMEM((patches, depth), BF),
            pltpu.VMEM((2, depth, HW), BF),
            pltpu.VMEM(shape, BF),
            pltpu.VMEM(shape, BF),
            DMA,
            DMA((2,)),
            DMA,
            DMA((G,)),
        ],
        compiler_params=params(),
        name="own_attend",
        cost_estimate=cost(
            4 * patches * depth * HW + 6 * patches * patches * HW,
            2 * patches * depth + 4 * depth * HW + 10 * patches * HW,
        ),
    )(in_hbm(hidden), in_hbm(weight), in_hbm(query), *after)


def memory_attend_kernel(count, base_ref, index_ref, query_hbm, *refs):
    blocks = refs[:count]
    out_hbm, query_ref, store_ref, out_ref, query_sem, block_sem, store_sem = refs[count + 1 :]
    frames = query_ref.shape[0]
    held = blocks[0].shape[0]
    base = base_ref[0]
    query_load = copy(query_hbm.at[pl.ds(base, frames)], query_ref, query_sem)
    query_load.start()

    def fetch(t, carry):
        i, j = t // TOPM, lax.rem(t, TOPM)
        wanted = index_ref[base + i, j]
        for b in range(count // 2):

            @pl.when(wanted // held == b)
            def _(b=b):
                slot = lax.rem(wanted, held)
                for part in range(2):
                    block = blocks[2 * b + part].at[slot]
                    copy(block, store_ref.at[i, j, part], block_sem.at[i]).start()

        return carry

    lax.fori_loop(0, frames * TOPM, fetch, 0)
    query_load.wait()
    stores = []
    for i in range(frames):
        copy(store_ref.at[i], store_ref.at[i], block_sem.at[i]).wait()
        both = [store_ref[i, j, part] for j in range(TOPM) for part in range(2)]
        keys = jnp.concatenate([block[:, :C] for block in both], axis=0)
        values = jnp.concatenate([block[:, C:] for block in both], axis=0)
        attend_rows(
            lambda at, i=i: query_ref[i, at, :], keys, with_ones(values), out_ref.at[i]
        )
        stores.append(copy(out_ref.at[i], out_hbm.at[i], store_sem.at[i]))
        stores[-1].start()
    for store in stores:
        store.wait()


def memory_attend(base, index, query, frames, blocks, after):
    count = len(blocks)
    rows = query.shape[1]
    _, part, width = blocks[0].shape
    shape = (frames, rows, C)
    return pl.pallas_call(
        functools.partial(memory_attend_kernel, count),
        in_specs=[SCALARS, SCALARS] + [ANY] * (count + 2),
        out_specs=HBM,
        out_shape=hbm_out(shape),
        scratch_shapes=[
            pltpu.VMEM(shape, BF),
            pltpu.VMEM((frames, TOPM, 2, part, width), BF),
            pltpu.VMEM(shape, BF),
            DMA,
            DMA((frames,)),
            DMA((frames,)),
        ],
        compiler_params=params(),
        name="memory_attend",
        cost_estimate=cost(
            16 * frames * rows * TOPM * part * C,
            4 * frames * rows * C + 2 * frames * TOPM * part * width,
        ),
    )(base, index, query, *blocks, in_hbm(after))


def add_partials_kernel(count, x_ref, *refs):
    ins, outs = refs[:count], refs[count : count + G]
    parts_ref, out_ref, load_sem, store_sem = refs[count + G :]
    patches = out_ref.shape[1] - PAD
    loads = []
    for j in range(G):
        frame = lax.rem(x_ref[0] + j, G)
        loads.append(
            [copy(ref.at[frame], parts_ref.at[k, j], load_sem.at[k, j]) for k, ref in enumerate(ins)]
        )
    for of_frame in loads:
        for load in of_frame:
            load.start()
    stores = []
    for j in range(G):
        for load in loads[j]:
            load.wait()
        total = parts_ref[0, j].astype(F32)
        for k in range(1, count):
            total = total + parts_ref[k, j].astype(F32)
        out_ref[j, :patches, :] = total[:patches].astype(BF)
        out_ref[j, patches:, :] = halves(total[patches : patches + 8] + total[patches + 8 :])
        stores.append(copy(out_ref.at[j], outs[j], store_sem.at[j]))
        stores[-1].start()
    for store in stores:
        store.wait()


def add_partials(x, parts):
    shape = parts[0].shape
    return pl.pallas_call(
        functools.partial(add_partials_kernel, len(parts)),
        in_specs=[SCALARS] + [ANY] * len(parts),
        out_specs=[HBM] * G,
        out_shape=[hbm_out(shape[1:])] * G,
        scratch_shapes=[
            pltpu.VMEM((len(parts),) + shape, BF),
            pltpu.VMEM(shape, BF),
            DMA((len(parts), G)),
            DMA((G,)),
        ],
        compiler_params=params(),
        name="add_partials",
        cost_estimate=cost(4 * parts[0].size, 8 * parts[0].size),
    )(x, *parts)


def leave_kernel(
    x_ref, own_hbm, memory_0, memory_1, memory_2, memory_3, time_hbm, weight_hbm, out_hbm,
    own_ref, memory_ref, time_ref, combined_ref, weight_ref, out_ref,
    own_sem, memory_sem, time_sem, weight_sem, store_sem,
):
    patches = own_ref.shape[1] - PAD
    quarters = time_ref.shape[0] // G
    rows = time_ref.shape[1]
    steps, _, width = weight_ref.shape
    heads = [lax.rem(x_ref[0] + G - j, G) for j in range(G)]
    memories = (memory_0, memory_1, memory_2, memory_3)
    own_loads = [copy(own_hbm.at[heads[j]], own_ref.at[j], own_sem.at[j]) for j in range(G)]
    memory_loads = [copy(memories[j], memory_ref.at[j], memory_sem.at[j]) for j in range(G)]
    time_load = copy(time_hbm, time_ref, time_sem)
    loads, stores = [], []
    for i in range(steps):
        at = pl.ds(i * width, width)
        loads.append(copy(weight_hbm.at[:, at], weight_ref.at[i], weight_sem.at[i]))
        stores.append(copy(out_ref.at[i], out_hbm.at[:, at], store_sem.at[i]))
    for load in own_loads + memory_loads + [time_load] + loads:
        load.start()
    row = lax.broadcasted_iota(jnp.int32, (LINE, C), 0)
    column = lax.broadcasted_iota(jnp.int32, (LINE, C), 1)
    for h in range(G):
        own_loads[h].wait()
        memory_loads[h].wait()
        column_at = pl.ds(pl.multiple_of(heads[h] * C, C), C)
        tail = own_ref[h, patches:, :].astype(F32) + memory_ref[h, patches:, :].astype(F32)
        denominators = tail[:8] + tail[8:]
        for j in range(patches // LINE):
            at = slice(j * LINE, (j + 1) * LINE)
            line = jnp.broadcast_to(denominators[j : j + 1, :], (LINE, C))
            total = jnp.sum(jnp.where(row == column, line, 0.0), axis=1, keepdims=True)
            top = own_ref[h, at, :].astype(F32) + memory_ref[h, at, :].astype(F32)
            combined_ref[at, column_at] = (top / total).astype(BF)
    time_load.wait()
    for h in range(G):
        for z in range(quarters):
            combined_ref[z * rows : (z + 1) * rows, HW + h * C : HW + (h + 1) * C] = time_ref[
                z * G + h
            ]
    for i in range(steps):
        loads[i].wait()
        out_ref[i] = dot(combined_ref[...], weight_ref[i]).astype(BF)
        stores[i].start()
    for store in stores:
        store.wait()


def leave(x, own, memory, time, weight):
    patches = own.shape[1] - PAD
    depth, width = weight.shape
    steps = 4
    step = width // steps
    return pl.pallas_call(
        leave_kernel,
        in_specs=[SCALARS, HBM] + [ANY] * (G + 1) + [HBM],
        out_specs=HBM,
        out_shape=hbm_out((patches, width)),
        scratch_shapes=[
            pltpu.VMEM(own.shape, BF),
            pltpu.VMEM(own.shape, BF),
            pltpu.VMEM(time.shape, BF),
            pltpu.VMEM((patches, depth), BF),
            pltpu.VMEM((steps, depth, step), BF),
            pltpu.VMEM((steps, patches, step), BF),
            DMA((G,)),
            DMA((G,)),
            DMA,
            DMA((steps,)),
            DMA((steps,)),
        ],
        compiler_params=params(),
        name="leave",
        cost_estimate=cost(
            2 * patches * depth * width,
            2 * depth * width + 2 * patches * width + 6 * patches * depth,
        ),
    )(x, in_hbm(own), *memory, time, in_hbm(weight))


def on_device(
    patch_activation_tensor,
    conditioning_affine,
    entry_projection_matrix,
    exit_projection_matrix,
    softmax_sharpness,
    cached_past_pairs,
    recalled_picture_holder,
    recalled_picture_position,
    lookback_lengths,
):
    frame = ("zq", "zp", "x")
    rings, sides = lax.axis_size("y"), lax.axis_size("zq")
    quarters = lax.axis_size("zp") * sides
    patches, depth = patch_activation_tensor.shape[2:]
    held, piece = cached_past_pairs.shape[:2]
    cores = lax.axis_size("c")
    x = lax.axis_index("x").astype(jnp.int32).reshape(1)
    side = lax.axis_index("zq").astype(jnp.int32).reshape(1)

    def turn(step):
        return [(s, (s + step) % rings) for s in range(rings)]

    def other(size):
        return [(s, size - 1 - s) for s in range(size)]

    def swap(blocks, axes):
        return lax.all_to_all(blocks, axes, split_axis=0, concat_axis=0, tiled=True)

    def swap_apart(blocks):
        return [in_hbm(blocks[0])] + [lax.ppermute(blocks[j], "x", turn(j)) for j in range(1, G)]

    with jax.named_scope("store"):
        split = split_store(cached_past_pairs.reshape(held * piece, 2 * HW), 1)
        pieces = swap(split[0], "x")

    with jax.named_scope("queries"):
        hidden, query = modulate(
            patch_activation_tensor.reshape(patches, depth),
            conditioning_affine.reshape(2, depth),
            entry_projection_matrix,
            softmax_sharpness,
            recalled_picture_holder.reshape(TOPM),
            recalled_picture_position.reshape(TOPM),
            held,
            sides,
            after=split,
        )

    with jax.named_scope("store"):
        joined = join_pieces(pieces, held, after=hidden)
        above = lax.ppermute(joined, "y", turn(-1))
        below = lax.ppermute(joined, "y", turn(1))
        second = lax.ppermute(joined, "zp", other(sides))

    with jax.named_scope("queries"):
        asked, joined = lax.optimization_barrier((query, joined))
        asked = swap(asked.reshape((-1,) + asked.shape[2:]), ("zq", "x"))

    with jax.named_scope("temporal"):
        parts = temporal_entry(
            hidden, entry_projection_matrix, softmax_sharpness, quarters, after=[in_hbm(joined)]
        )
        sent = swap(parts.reshape((quarters * G,) + parts.shape[2:]), frame)

    with jax.named_scope("store"):
        second, parts = lax.optimization_barrier((second, parts))
        second_above = lax.ppermute(second, "y", turn(-1))
        second_below = lax.ppermute(second, "y", turn(1))

    with jax.named_scope("own"):
        own = own_attend(
            hidden, entry_projection_matrix, query, after=[in_hbm(parts), second]
        )

    with jax.named_scope("store"):
        below, second_above, own = lax.optimization_barrier((below, second_above, own))
        far = lax.ppermute(below, "y", turn(1))
        second_far = lax.ppermute(second_above, "y", turn(-1))
        near = [joined, second, above, second_above, far, second_far, below, second_below]
        blocks = near + [lax.ppermute(block, "c", other(cores)) for block in near]
        blocks[0] = in_hbm(blocks[0])

    with jax.named_scope("queries"):
        named = asked[:, patches, :TOPM].astype(jnp.int32)
        y = (named // (cores * held) - lax.axis_index("y")) & (rings - 1)
        c = (named // held & (cores - 1)) ^ lax.axis_index("c")
        index = (c * rings + y) * held + (named & (held - 1))

    def attend(base, after):
        return memory_attend(base, index, asked, asked.shape[0] // sides, blocks, after)

    with jax.named_scope("memory"):
        count = asked.shape[0] // sides
        sum_beside = attend((sides - 1 - side) * count, own)
        from_beside = lax.ppermute(sum_beside, "zq", other(sides))
        sum_here = attend(side * count, sum_beside)

    with jax.named_scope("temporal"):
        timed = temporal_attend(lookback_lengths, sent, after=sum_here)
        time = swap(timed, frame)

    with jax.named_scope("memory"):
        memory = swap_apart(add_partials(x, [in_hbm(sum_here), from_beside]))

    with jax.named_scope("exit"):
        attended = leave(x, own, memory, time, exit_projection_matrix)
    return attended.reshape(1, 1, patches, depth)


def solution(mesh):
    apart = Mesh(mesh.devices.reshape(4, 2, 2, 2, 4), ("y", "c", "zq", "zp", "x"))
    roll, frame = ("y", "c"), ("zq", "zp", "x")
    return jax.shard_map(
        on_device,
        mesh=apart,
        in_specs=(
            P(roll, frame, None, None),
            P(roll, frame, None, None),
            P(),
            P(),
            P(),
            P(roll, frame, None, None),
            P(roll, frame, None, None),
            P(roll, frame, None),
            P(roll),
        ),
        out_specs=P(roll, frame, None, None),
        check_vma=False,
    )
```

```python
import functools

import jax
import jax.numpy as jnp
from jax import lax
from jax.experimental import pallas as pl
from jax.experimental.pallas import tpu as pltpu
from jax.sharding import Mesh
from jax.sharding import PartitionSpec as P

G = 4
C = 128
HW = G * C
TOPM = 6
EPSILON = 1e-06
BF = jnp.bfloat16
F32 = jnp.float32
PAD = 16
VMEM_LIMIT = 28 * 1024 * 1024
ANY = pl.BlockSpec(memory_space=pl.ANY)
HBM = pl.BlockSpec(memory_space=pltpu.HBM)
WHOLE = pl.BlockSpec(memory_space=pltpu.VMEM)
SCALARS = pl.BlockSpec(memory_space=pltpu.SMEM)


def params(**more):
    return pltpu.CompilerParams(vmem_limit_bytes=VMEM_LIMIT, **more)


def cost(flops, bytes_accessed):
    return pl.CostEstimate(
        flops=flops // 16, bytes_accessed=bytes_accessed // 16, transcendentals=0
    )


def in_hbm(array):
    return pltpu.with_memory_space_constraint(array, pltpu.HBM)


def hbm_out(shape, dtype=BF):
    return pltpu.HBM(shape, dtype)


def inverse_rms(values):
    return lax.rsqrt(jnp.mean(values * values, axis=-1, keepdims=True) + EPSILON)


def dot(a, b):
    return jnp.dot(a, b, preferred_element_type=F32)


def dot_t(a, b):
    return lax.dot_general(a, b, (((1,), (1,)), ((), ())), preferred_element_type=F32)


DMA = pltpu.SemaphoreType.DMA
copy = pltpu.make_async_copy


def split_store_kernel(rows_ref, out_hbm, out_ref, sem):
    sends = []
    for h in range(G):
        key = rows_ref[:, h * C : (h + 1) * C].astype(F32)
        out_ref[h, :, :C] = (key * inverse_rms(key)).astype(BF)
        out_ref[h, :, C:] = rows_ref[:, HW + h * C : HW + (h + 1) * C]
        for k in range(out_hbm.shape[0]):
            sends.append(copy(out_ref.at[h], out_hbm.at[k, h], sem.at[k, h]))
            sends[-1].start()
    for send in sends:
        send.wait()


def split_store(rows, copies):
    n = rows.shape[0]
    return pl.pallas_call(
        split_store_kernel,
        in_specs=[WHOLE],
        out_specs=HBM,
        out_shape=hbm_out((copies, G, n, 2 * C)),
        scratch_shapes=[pltpu.VMEM((G, n, 2 * C), BF), DMA((copies, G))],
        compiler_params=params(),
        name="split_store",
        cost_estimate=cost(8 * n * HW, 8 * n * HW),
    )(rows)


def join_pieces_kernel(piece, in_hbm, _, out_hbm, in_ref, wide_ref, joined_ref, out_ref, sem):
    pieces = in_ref.shape[0]
    loads = [copy(in_hbm.at[i], in_ref.at[i], sem.at[i]) for i in range(pieces)]
    for load in loads:
        load.start()
    for i in range(pieces):
        loads[i].wait()
        wide_ref[i] = in_ref[i].astype(F32)
        for m in range(out_ref.shape[0]):
            joined_ref[m, i * piece : (i + 1) * piece, :] = wide_ref[
                i, m * piece : (m + 1) * piece, :
            ]
    out_ref[...] = joined_ref[...].astype(BF)
    send = copy(out_ref, out_hbm, sem.at[0])
    send.start()
    send.wait()


def join_pieces(parts, frames, after):
    pieces, rows, width = parts.shape
    piece = rows // frames
    shape = (frames, pieces * piece, width)
    return pl.pallas_call(
        functools.partial(join_pieces_kernel, piece),
        in_specs=[ANY, ANY],
        out_specs=HBM,
        out_shape=hbm_out(shape),
        scratch_shapes=[
            pltpu.VMEM(parts.shape, BF),
            pltpu.VMEM(parts.shape, F32),
            pltpu.VMEM(shape, F32),
            pltpu.VMEM(shape, BF),
            DMA((pieces,)),
        ],
        compiler_params=params(),
        name="join_pieces",
        cost_estimate=cost(parts.size, 4 * parts.size),
    )(parts, in_hbm(after))


def modulate_kernel(
    held,
    act_hbm, affine_hbm, weight_hbm, sharpness_ref, owner_ref, slot_ref, _, hidden_hbm, query_hbm,
    act_ref, affine_ref, weight_ref, hidden_ref, query_ref,
    load_sem, affine_sem, weight_sem, store_sem, query_sem,
):
    steps, rows, _ = act_ref.shape
    patches = query_ref.shape[1] - PAD
    loads, stores = [], []
    for i in range(steps):
        at = pl.ds(i * rows, rows)
        loads.append(copy(act_hbm.at[at, :], act_ref.at[i], load_sem.at[i]))
        stores.append(copy(hidden_ref.at[i], hidden_hbm.at[at, :], store_sem.at[i]))
    weight_load = copy(weight_hbm.at[:, pl.ds(0, HW)], weight_ref, weight_sem)
    affine_load = copy(affine_hbm, affine_ref, affine_sem)
    affine_load.start()
    loads[0].start()
    weight_load.start()
    row = lax.broadcasted_iota(jnp.int32, (PAD, C), 0)
    column = lax.broadcasted_iota(jnp.int32, (PAD, C), 1)
    tail = jnp.zeros((PAD, C), jnp.int32)
    for j in range(TOPM):
        tail = jnp.where((row == 0) & (column == j), owner_ref[j] * held + slot_ref[j], tail)
    for h in range(G):
        query_ref[h, patches:, :] = tail.astype(F32).astype(BF)
    affine_load.wait()
    for i in range(steps):
        at = slice(i * rows, (i + 1) * rows)
        loads[i].wait()
        if i + 1 < steps:
            loads[i + 1].start()
        act = act_ref[i].astype(F32)
        hidden = act * inverse_rms(act) * (1.0 + affine_ref[0:1, :]) + affine_ref[1:2, :]
        hidden = hidden.astype(BF)
        hidden_ref[i] = hidden
        stores[i].start()
        if i == 0:
            weight_load.wait()
        mapped = dot(hidden, weight_ref[...]).astype(BF).astype(F32)
        for h in range(G):
            one = mapped[:, h * C : (h + 1) * C]
            query_ref[h, at, :] = (
                one * inverse_rms(one) * (sharpness_ref[0, h] / C)
            ).astype(BF)
    sends = [
        copy(query_ref, query_hbm.at[k], query_sem.at[k]) for k in range(query_hbm.shape[0])
    ]
    for send in sends:
        send.start()
    for store in stores + sends:
        store.wait()


def modulate(act, affine, weight, sharpness, owner, slot, held, copies, after):
    patches, depth = act.shape
    steps = 2
    rows = patches // steps
    shape = (G, patches + PAD, C)
    return pl.pallas_call(
        functools.partial(modulate_kernel, held),
        in_specs=[HBM, HBM, HBM, SCALARS, SCALARS, SCALARS, ANY],
        out_specs=[HBM, HBM],
        out_shape=[hbm_out((patches, depth)), hbm_out((copies,) + shape)],
        scratch_shapes=[
            pltpu.VMEM((steps, rows, depth), BF),
            pltpu.VMEM(affine.shape, F32),
            pltpu.VMEM((depth, HW), BF),
            pltpu.VMEM((steps, rows, depth), BF),
            pltpu.VMEM(shape, BF),
            DMA((steps,)),
            DMA,
            DMA,
            DMA((steps,)),
            DMA((copies,)),
        ],
        compiler_params=params(),
        name="modulate",
        cost_estimate=cost(
            2 * patches * depth * HW, 4 * patches * depth + 2 * depth * HW + 2 * patches * HW
        ),
    )(in_hbm(act), in_hbm(affine), in_hbm(weight), sharpness, owner, slot, in_hbm(after))


def temporal_entry_kernel(
    quarters, hidden_hbm, weight_hbm, sharpness_ref, *refs
):
    out_hbm, hidden_ref, weight_ref, out_ref, hidden_sem, weight_sem, store_sem = refs[-7:]
    rows = hidden_ref.shape[0] // quarters
    hidden_load = copy(hidden_hbm, hidden_ref, hidden_sem)
    loads = [
        copy(
            weight_hbm.at[:, pl.ds((3 + part) * HW, HW)], weight_ref.at[part], weight_sem.at[part]
        )
        for part in range(3)
    ]
    hidden_load.start()
    loads[0].start()
    hidden_load.wait()
    stores = []
    for part in range(3):
        loads[part].wait()
        if part < 2:
            loads[part + 1].start()
        mapped = dot(hidden_ref[...], weight_ref[part]).astype(BF)
        for h in range(G):
            done = mapped[:, h * C : (h + 1) * C]
            if part < 2:
                one = done.astype(F32)
                one = one * inverse_rms(one)
                if part == 0:
                    one = one * (sharpness_ref[1, h] / C)
                done = one.astype(BF)
            for z in range(quarters):
                out_ref[part, z, h] = done[z * rows : (z + 1) * rows, :]
        stores.append(copy(out_ref.at[part], out_hbm.at[:, :, part], store_sem.at[part]))
        stores[-1].start()
    for store in stores:
        store.wait()


def temporal_entry(hidden, weight, sharpness, quarters, after):
    patches, depth = hidden.shape
    rows = patches // quarters
    return pl.pallas_call(
        functools.partial(temporal_entry_kernel, quarters),
        in_specs=[HBM, HBM, SCALARS] + [ANY] * len(after),
        out_specs=HBM,
        out_shape=hbm_out((quarters, G, 3, rows, C)),
        scratch_shapes=[
            pltpu.VMEM((patches, depth), BF),
            pltpu.VMEM((3, depth, HW), BF),
            pltpu.VMEM((3, quarters, G, rows, C), BF),
            DMA,
            DMA((3,)),
            DMA((3,)),
        ],
        compiler_params=params(),
        name="temporal_entry",
        cost_estimate=cost(
            6 * patches * depth * HW, 2 * patches * depth + 6 * depth * HW + 6 * patches * HW
        ),
    )(in_hbm(hidden), in_hbm(weight), sharpness, *after)


def temporal_attend_kernel(length_ref, in_hbm_ref, _, out_hbm, in_ref, out_ref, sem):
    frames, _, rows, _ = in_ref.shape
    group = 16
    size = frames * group
    load = copy(in_hbm_ref, in_ref, sem)
    load.start()
    length = length_ref[0]
    row = lax.broadcasted_iota(jnp.int32, (size, size), 0)
    column = lax.broadcasted_iota(jnp.int32, (size, size), 1)
    target, source = row // group, column // group
    keep = (row % group == column % group) & (source <= target) & (source > target - length)
    load.wait()
    for g in range(rows // group):
        at = slice(g * group, (g + 1) * group)
        query = in_ref[:, 0, at, :].reshape(size, C)
        key = in_ref[:, 1, at, :].reshape(size, C)
        value = in_ref[:, 2, at, :].reshape(size, C)
        weights = jnp.where(keep, jnp.exp(dot_t(query, key)), 0.0)
        shares = weights / jnp.sum(weights, axis=-1, keepdims=True)
        result = dot(shares.astype(BF), value).astype(BF)
        out_ref[:, at, :] = result.reshape(frames, group, C)
    store = copy(out_ref, out_hbm, sem)
    store.start()
    store.wait()


def temporal_attend(length, parts, after):
    frames, _, rows, _ = parts.shape
    shape = (frames, rows, C)
    return pl.pallas_call(
        temporal_attend_kernel,
        in_specs=[SCALARS, ANY, ANY],
        out_specs=HBM,
        out_shape=hbm_out(shape),
        scratch_shapes=[pltpu.VMEM(parts.shape, BF), pltpu.VMEM(shape, BF), DMA],
        compiler_params=params(),
        name="temporal_attend",
        cost_estimate=cost(4 * frames * rows * 256 * C, 8 * frames * rows * C),
    )(length, parts, in_hbm(after))


LINE = 96
CHUNK = 3 * LINE


def halves(denominators):
    high = denominators.astype(BF).astype(F32)
    return jnp.concatenate([high, denominators - high], axis=0).astype(BF)


def attend_rows(query, keys, both, out_ref):
    patches = out_ref.shape[0] - PAD
    row = lax.broadcasted_iota(jnp.int32, (LINE, C), 0)
    column = lax.broadcasted_iota(jnp.int32, (LINE, C), 1)
    lines = []
    for start in range(0, patches, CHUNK):
        at = slice(start, start + CHUNK)
        weights = jnp.exp(dot_t(query(at), keys)).astype(BF)
        result = dot(weights, both)
        out_ref[at, :] = result[:, :C].astype(BF)
        for j in range(0, CHUNK, LINE):
            diagonal = jnp.where(row == column, result[j : j + LINE, C:], 0.0)
            lines.append(jnp.sum(diagonal, axis=0, keepdims=True))
    lines.append(jnp.zeros((8 - len(lines), C), F32))
    out_ref[patches:, :] = halves(jnp.concatenate(lines, axis=0))


def with_ones(values):
    return jnp.concatenate([values, jnp.ones(values.shape, BF)], axis=1)


def own_attend_kernel(
    hidden_hbm, weight_hbm, query_hbm, *refs
):
    out_hbm, hidden_ref, weight_ref, query_ref, out_ref = refs[-9:-4]
    hidden_sem, weight_sem, query_sem, store_sem = refs[-4:]
    hidden_load = copy(hidden_hbm, hidden_ref, hidden_sem)
    query_load = copy(query_hbm.at[0], query_ref, query_sem)
    loads = [
        copy(
            weight_hbm.at[:, pl.ds((1 + part) * HW, HW)], weight_ref.at[part], weight_sem.at[part]
        )
        for part in range(2)
    ]
    hidden_load.start()
    loads[0].start()
    hidden_load.wait()
    loads[0].wait()
    loads[1].start()
    query_load.start()
    keys = dot(hidden_ref[...], weight_ref[0]).astype(BF)
    loads[1].wait()
    values = dot(hidden_ref[...], weight_ref[1]).astype(BF)
    query_load.wait()
    stores = []
    for h in range(G):
        key = keys[:, h * C : (h + 1) * C].astype(F32)
        key = (key * inverse_rms(key)).astype(BF)
        both = with_ones(values[:, h * C : (h + 1) * C])
        attend_rows(lambda at, h=h: query_ref[h, at, :], key, both, out_ref.at[h])
        stores.append(copy(out_ref.at[h], out_hbm.at[h], store_sem.at[h]))
        stores[-1].start()
    for store in stores:
        store.wait()


def own_attend(hidden, weight, query, after):
    patches, depth = hidden.shape
    shape = query.shape[1:]
    return pl.pallas_call(
        own_attend_kernel,
        in_specs=[HBM, HBM, HBM] + [ANY] * len(after),
        out_specs=HBM,
        out_shape=hbm_out(shape),
        scratch_shapes=[
            pltpu.VMEM((patches, depth), BF),
            pltpu.VMEM((2, depth, HW), BF),
            pltpu.VMEM(shape, BF),
            pltpu.VMEM(shape, BF),
            DMA,
            DMA((2,)),
            DMA,
            DMA((G,)),
        ],
        compiler_params=params(),
        name="own_attend",
        cost_estimate=cost(
            4 * patches * depth * HW + 6 * patches * patches * HW,
            2 * patches * depth + 4 * depth * HW + 10 * patches * HW,
        ),
    )(in_hbm(hidden), in_hbm(weight), in_hbm(query), *after)


def memory_attend_kernel(count, base_ref, index_ref, query_hbm, *refs):
    blocks = refs[:count]
    out_hbm, query_ref, store_ref, out_ref, query_sem, block_sem, store_sem = refs[count + 1 :]
    frames = query_ref.shape[0]
    held = blocks[0].shape[0]
    base = base_ref[0]
    query_load = copy(query_hbm.at[pl.ds(base, frames)], query_ref, query_sem)
    query_load.start()

    def fetch(t, carry):
        i, j = t // TOPM, lax.rem(t, TOPM)
        wanted = index_ref[base + i, j]
        for b in range(count // 2):

            @pl.when(wanted // held == b)
            def _(b=b):
                slot = lax.rem(wanted, held)
                for part in range(2):
                    block = blocks[2 * b + part].at[slot]
                    copy(block, store_ref.at[i, j, part], block_sem.at[i]).start()

        return carry

    lax.fori_loop(0, frames * TOPM, fetch, 0)
    query_load.wait()
    stores = []
    for i in range(frames):
        copy(store_ref.at[i], store_ref.at[i], block_sem.at[i]).wait()
        both = [store_ref[i, j, part] for j in range(TOPM) for part in range(2)]
        keys = jnp.concatenate([block[:, :C] for block in both], axis=0)
        values = jnp.concatenate([block[:, C:] for block in both], axis=0)
        attend_rows(
            lambda at, i=i: query_ref[i, at, :], keys, with_ones(values), out_ref.at[i]
        )
        stores.append(copy(out_ref.at[i], out_hbm.at[i], store_sem.at[i]))
        stores[-1].start()
    for store in stores:
        store.wait()


def memory_attend(base, index, query, frames, blocks, after):
    count = len(blocks)
    rows = query.shape[1]
    _, part, width = blocks[0].shape
    shape = (frames, rows, C)
    return pl.pallas_call(
        functools.partial(memory_attend_kernel, count),
        in_specs=[SCALARS, SCALARS] + [ANY] * (count + 2),
        out_specs=HBM,
        out_shape=hbm_out(shape),
        scratch_shapes=[
            pltpu.VMEM(shape, BF),
            pltpu.VMEM((frames, TOPM, 2, part, width), BF),
            pltpu.VMEM(shape, BF),
            DMA,
            DMA((frames,)),
            DMA((frames,)),
        ],
        compiler_params=params(),
        name="memory_attend",
        cost_estimate=cost(
            16 * frames * rows * TOPM * part * C,
            4 * frames * rows * C + 2 * frames * TOPM * part * width,
        ),
    )(base, index, query, *blocks, in_hbm(after))


def add_partials_kernel(count, x_ref, *refs):
    ins, outs = refs[:count], refs[count : count + G]
    parts_ref, out_ref, load_sem, store_sem = refs[count + G :]
    patches = out_ref.shape[1] - PAD
    loads = []
    for j in range(G):
        frame = lax.rem(x_ref[0] + j, G)
        loads.append(
            [copy(ref.at[frame], parts_ref.at[k, j], load_sem.at[k, j]) for k, ref in enumerate(ins)]
        )
    for of_frame in loads:
        for load in of_frame:
            load.start()
    stores = []
    for j in range(G):
        for load in loads[j]:
            load.wait()
        total = parts_ref[0, j].astype(F32)
        for k in range(1, count):
            total = total + parts_ref[k, j].astype(F32)
        out_ref[j, :patches, :] = total[:patches].astype(BF)
        out_ref[j, patches:, :] = halves(total[patches : patches + 8] + total[patches + 8 :])
        stores.append(copy(out_ref.at[j], outs[j], store_sem.at[j]))
        stores[-1].start()
    for store in stores:
        store.wait()


def add_partials(x, parts):
    shape = parts[0].shape
    return pl.pallas_call(
        functools.partial(add_partials_kernel, len(parts)),
        in_specs=[SCALARS] + [ANY] * len(parts),
        out_specs=[HBM] * G,
        out_shape=[hbm_out(shape[1:])] * G,
        scratch_shapes=[
            pltpu.VMEM((len(parts),) + shape, BF),
            pltpu.VMEM(shape, BF),
            DMA((len(parts), G)),
            DMA((G,)),
        ],
        compiler_params=params(),
        name="add_partials",
        cost_estimate=cost(4 * parts[0].size, 8 * parts[0].size),
    )(x, *parts)


def leave_kernel(
    x_ref, own_hbm, memory_0, memory_1, memory_2, memory_3, time_hbm, weight_hbm, out_hbm,
    own_ref, memory_ref, time_ref, combined_ref, weight_ref, out_ref,
    own_sem, memory_sem, time_sem, weight_sem, store_sem,
):
    patches = own_ref.shape[1] - PAD
    quarters = time_ref.shape[0] // G
    rows = time_ref.shape[1]
    steps, _, width = weight_ref.shape
    heads = [lax.rem(x_ref[0] + G - j, G) for j in range(G)]
    memories = (memory_0, memory_1, memory_2, memory_3)
    own_loads = [copy(own_hbm.at[heads[j]], own_ref.at[j], own_sem.at[j]) for j in range(G)]
    memory_loads = [copy(memories[j], memory_ref.at[j], memory_sem.at[j]) for j in range(G)]
    time_load = copy(time_hbm, time_ref, time_sem)
    loads, stores = [], []
    for i in range(steps):
        at = pl.ds(i * width, width)
        loads.append(copy(weight_hbm.at[:, at], weight_ref.at[i], weight_sem.at[i]))
        stores.append(copy(out_ref.at[i], out_hbm.at[:, at], store_sem.at[i]))
    for load in own_loads + memory_loads + [time_load] + loads:
        load.start()
    row = lax.broadcasted_iota(jnp.int32, (LINE, C), 0)
    column = lax.broadcasted_iota(jnp.int32, (LINE, C), 1)
    for h in range(G):
        own_loads[h].wait()
        memory_loads[h].wait()
        column_at = pl.ds(pl.multiple_of(heads[h] * C, C), C)
        tail = own_ref[h, patches:, :].astype(F32) + memory_ref[h, patches:, :].astype(F32)
        denominators = tail[:8] + tail[8:]
        for j in range(patches // LINE):
            at = slice(j * LINE, (j + 1) * LINE)
            line = jnp.broadcast_to(denominators[j : j + 1, :], (LINE, C))
            total = jnp.sum(jnp.where(row == column, line, 0.0), axis=1, keepdims=True)
            top = own_ref[h, at, :].astype(F32) + memory_ref[h, at, :].astype(F32)
            combined_ref[at, column_at] = (top / total).astype(BF)
    time_load.wait()
    for h in range(G):
        for z in range(quarters):
            combined_ref[z * rows : (z + 1) * rows, HW + h * C : HW + (h + 1) * C] = time_ref[
                z * G + h
            ]
    for i in range(steps):
        loads[i].wait()
        out_ref[i] = dot(combined_ref[...], weight_ref[i]).astype(BF)
        stores[i].start()
    for store in stores:
        store.wait()


def leave(x, own, memory, time, weight):
    patches = own.shape[1] - PAD
    depth, width = weight.shape
    steps = 4
    step = width // steps
    return pl.pallas_call(
        leave_kernel,
        in_specs=[SCALARS, HBM] + [ANY] * (G + 1) + [HBM],
        out_specs=HBM,
        out_shape=hbm_out((patches, width)),
        scratch_shapes=[
            pltpu.VMEM(own.shape, BF),
            pltpu.VMEM(own.shape, BF),
            pltpu.VMEM(time.shape, BF),
            pltpu.VMEM((patches, depth), BF),
            pltpu.VMEM((steps, depth, step), BF),
            pltpu.VMEM((steps, patches, step), BF),
            DMA((G,)),
            DMA((G,)),
            DMA,
            DMA((steps,)),
            DMA((steps,)),
        ],
        compiler_params=params(),
        name="leave",
        cost_estimate=cost(
            2 * patches * depth * width,
            2 * depth * width + 2 * patches * width + 6 * patches * depth,
        ),
    )(x, in_hbm(own), *memory, time, in_hbm(weight))


def on_device(
    patch_activation_tensor,
    conditioning_affine,
    entry_projection_matrix,
    exit_projection_matrix,
    softmax_sharpness,
    cached_past_pairs,
    recalled_picture_holder,
    recalled_picture_position,
    lookback_lengths,
):
    frame = ("zq", "zp", "x")
    rings, sides = lax.axis_size("y"), lax.axis_size("zq")
    quarters = lax.axis_size("zp") * sides
    patches, depth = patch_activation_tensor.shape[2:]
    held, piece = cached_past_pairs.shape[:2]
    cores = lax.axis_size("c")
    x = lax.axis_index("x").astype(jnp.int32).reshape(1)
    side = lax.axis_index("zq").astype(jnp.int32).reshape(1)

    def turn(step):
        return [(s, (s + step) % rings) for s in range(rings)]

    def other(size):
        return [(s, size - 1 - s) for s in range(size)]

    def swap(blocks, axes):
        return lax.all_to_all(blocks, axes, split_axis=0, concat_axis=0, tiled=True)

    def swap_apart(blocks):
        return [in_hbm(blocks[0])] + [lax.ppermute(blocks[j], "x", turn(j)) for j in range(1, G)]

    with jax.named_scope("store"):
        split = split_store(cached_past_pairs.reshape(held * piece, 2 * HW), 1)
        pieces = swap(split[0], "x")

    with jax.named_scope("queries"):
        hidden, query = modulate(
            patch_activation_tensor.reshape(patches, depth),
            conditioning_affine.reshape(2, depth),
            entry_projection_matrix,
            softmax_sharpness,
            recalled_picture_holder.reshape(TOPM),
            recalled_picture_position.reshape(TOPM),
            held,
            sides,
            after=split,
        )

    with jax.named_scope("store"):
        joined = join_pieces(pieces, held, after=hidden)
        above = lax.ppermute(joined, "y", turn(-1))
        below = lax.ppermute(joined, "y", turn(1))
        second = lax.ppermute(joined, "zp", other(sides))

    with jax.named_scope("queries"):
        asked, second = lax.optimization_barrier((query, second))
        asked = swap(asked.reshape((-1,) + asked.shape[2:]), ("zq", "x"))

    with jax.named_scope("temporal"):
        parts = temporal_entry(
            hidden, entry_projection_matrix, softmax_sharpness, quarters, after=[in_hbm(joined)]
        )
        sent = swap(parts.reshape((quarters * G,) + parts.shape[2:]), frame)

    with jax.named_scope("store"):
        second, parts = lax.optimization_barrier((second, parts))
        second_above = lax.ppermute(second, "y", turn(-1))
        second_below = lax.ppermute(second, "y", turn(1))

    with jax.named_scope("own"):
        own = own_attend(
            hidden, entry_projection_matrix, query, after=[in_hbm(parts), second]
        )

    with jax.named_scope("store"):
        below, second_above, own = lax.optimization_barrier((below, second_above, own))
        far = lax.ppermute(below, "y", turn(1))
        second_far = lax.ppermute(second_above, "y", turn(-1))
        near = [joined, second, above, second_above, far, second_far, below, second_below]
        blocks = near + [lax.ppermute(block, "c", other(cores)) for block in near]
        blocks = [in_hbm(block) for block in blocks]

    with jax.named_scope("queries"):
        named = asked[:, patches, :TOPM].astype(jnp.int32)
        y = (named // (cores * held) - lax.axis_index("y")) & (rings - 1)
        c = (named // held & (cores - 1)) ^ lax.axis_index("c")
        index = (c * rings + y) * held + (named & (held - 1))

    def attend(base, after):
        return memory_attend(base, index, asked, asked.shape[0] // sides, blocks, after)

    with jax.named_scope("memory"):
        count = asked.shape[0] // sides
        sum_beside = attend((sides - 1 - side) * count, own)
        from_beside = lax.ppermute(sum_beside, "zq", other(sides))
        sum_here = attend(side * count, sum_beside)

    with jax.named_scope("temporal"):
        timed = temporal_attend(lookback_lengths, sent, after=sum_here)
        time = swap(timed, frame)

    with jax.named_scope("memory"):
        memory = swap_apart(add_partials(x, [in_hbm(sum_here), from_beside]))

    with jax.named_scope("exit"):
        attended = leave(x, own, memory, time, exit_projection_matrix)
    return attended.reshape(1, 1, patches, depth)


def solution(mesh):
    apart = Mesh(mesh.devices.reshape(4, 2, 2, 2, 4), ("y", "c", "zq", "zp", "x"))
    roll, frame = ("y", "c"), ("zq", "zp", "x")
    return jax.shard_map(
        on_device,
        mesh=apart,
        in_specs=(
            P(roll, frame, None, None),
            P(roll, frame, None, None),
            P(),
            P(),
            P(),
            P(roll, frame, None, None),
            P(roll, frame, None, None),
            P(roll, frame, None),
            P(roll),
        ),
        out_specs=P(roll, frame, None, None),
        check_vma=False,
    )
```

```python
import functools

import jax
import jax.numpy as jnp
from jax import lax
from jax.experimental import pallas as pl
from jax.experimental.pallas import tpu as pltpu
from jax.sharding import Mesh
from jax.sharding import PartitionSpec as P

G = 4
C = 128
HW = G * C
TOPM = 6
EPSILON = 1e-06
BF = jnp.bfloat16
F32 = jnp.float32
PAD = 16
VMEM_LIMIT = 28 * 1024 * 1024
ANY = pl.BlockSpec(memory_space=pl.ANY)
HBM = pl.BlockSpec(memory_space=pltpu.HBM)
WHOLE = pl.BlockSpec(memory_space=pltpu.VMEM)
SCALARS = pl.BlockSpec(memory_space=pltpu.SMEM)


def params(**more):
    return pltpu.CompilerParams(vmem_limit_bytes=VMEM_LIMIT, **more)


def cost(flops, bytes_accessed):
    return pl.CostEstimate(
        flops=flops // 16, bytes_accessed=bytes_accessed // 16, transcendentals=0
    )


def in_hbm(array):
    return pltpu.with_memory_space_constraint(array, pltpu.HBM)


def hbm_out(shape, dtype=BF):
    return pltpu.HBM(shape, dtype)


def inverse_rms(values):
    return lax.rsqrt(jnp.mean(values * values, axis=-1, keepdims=True) + EPSILON)


def dot(a, b):
    return jnp.dot(a, b, preferred_element_type=F32)


def dot_t(a, b):
    return lax.dot_general(a, b, (((1,), (1,)), ((), ())), preferred_element_type=F32)


DMA = pltpu.SemaphoreType.DMA
copy = pltpu.make_async_copy


def split_store_kernel(rows_ref, out_hbm, out_ref, sem):
    sends = []
    for h in range(G):
        key = rows_ref[:, h * C : (h + 1) * C].astype(F32)
        out_ref[h, :, :C] = (key * inverse_rms(key)).astype(BF)
        out_ref[h, :, C:] = rows_ref[:, HW + h * C : HW + (h + 1) * C]
        for k in range(out_hbm.shape[0]):
            sends.append(copy(out_ref.at[h], out_hbm.at[k, h], sem.at[k, h]))
            sends[-1].start()
    for send in sends:
        send.wait()


def split_store(rows, copies):
    n = rows.shape[0]
    return pl.pallas_call(
        split_store_kernel,
        in_specs=[WHOLE],
        out_specs=HBM,
        out_shape=hbm_out((copies, G, n, 2 * C)),
        scratch_shapes=[pltpu.VMEM((G, n, 2 * C), BF), DMA((copies, G))],
        compiler_params=params(),
        name="split_store",
        cost_estimate=cost(8 * n * HW, 8 * n * HW),
    )(rows)


def join_pieces_kernel(piece, in_hbm, _, out_hbm, in_ref, wide_ref, joined_ref, out_ref, sem):
    pieces = in_ref.shape[0]
    loads = [copy(in_hbm.at[i], in_ref.at[i], sem.at[i]) for i in range(pieces)]
    for load in loads:
        load.start()
    for i in range(pieces):
        loads[i].wait()
        wide_ref[i] = in_ref[i].astype(F32)
        for m in range(out_ref.shape[0]):
            joined_ref[m, i * piece : (i + 1) * piece, :] = wide_ref[
                i, m * piece : (m + 1) * piece, :
            ]
    out_ref[...] = joined_ref[...].astype(BF)
    send = copy(out_ref, out_hbm, sem.at[0])
    send.start()
    send.wait()


def join_pieces(parts, frames, after):
    pieces, rows, width = parts.shape
    piece = rows // frames
    shape = (frames, pieces * piece, width)
    return pl.pallas_call(
        functools.partial(join_pieces_kernel, piece),
        in_specs=[ANY, ANY],
        out_specs=HBM,
        out_shape=hbm_out(shape),
        scratch_shapes=[
            pltpu.VMEM(parts.shape, BF),
            pltpu.VMEM(parts.shape, F32),
            pltpu.VMEM(shape, F32),
            pltpu.VMEM(shape, BF),
            DMA((pieces,)),
        ],
        compiler_params=params(),
        name="join_pieces",
        cost_estimate=cost(parts.size, 4 * parts.size),
    )(parts, in_hbm(after))


def modulate_kernel(
    held,
    act_hbm, affine_hbm, weight_hbm, sharpness_ref, owner_ref, slot_ref, _, hidden_hbm, query_hbm,
    act_ref, affine_ref, weight_ref, hidden_ref, query_ref,
    load_sem, affine_sem, weight_sem, store_sem, query_sem,
):
    steps, rows, _ = act_ref.shape
    patches = query_ref.shape[1] - PAD
    loads, stores = [], []
    for i in range(steps):
        at = pl.ds(i * rows, rows)
        loads.append(copy(act_hbm.at[at, :], act_ref.at[i], load_sem.at[i]))
        stores.append(copy(hidden_ref.at[i], hidden_hbm.at[at, :], store_sem.at[i]))
    weight_load = copy(weight_hbm.at[:, pl.ds(0, HW)], weight_ref, weight_sem)
    affine_load = copy(affine_hbm, affine_ref, affine_sem)
    affine_load.start()
    loads[0].start()
    weight_load.start()
    row = lax.broadcasted_iota(jnp.int32, (PAD, C), 0)
    column = lax.broadcasted_iota(jnp.int32, (PAD, C), 1)
    tail = jnp.zeros((PAD, C), jnp.int32)
    for j in range(TOPM):
        tail = jnp.where((row == 0) & (column == j), owner_ref[j] * held + slot_ref[j], tail)
    for h in range(G):
        query_ref[h, patches:, :] = tail.astype(F32).astype(BF)
    affine_load.wait()
    for i in range(steps):
        at = slice(i * rows, (i + 1) * rows)
        loads[i].wait()
        if i + 1 < steps:
            loads[i + 1].start()
        act = act_ref[i].astype(F32)
        hidden = act * inverse_rms(act) * (1.0 + affine_ref[0:1, :]) + affine_ref[1:2, :]
        hidden = hidden.astype(BF)
        hidden_ref[i] = hidden
        stores[i].start()
        if i == 0:
            weight_load.wait()
        mapped = dot(hidden, weight_ref[...]).astype(BF).astype(F32)
        for h in range(G):
            one = mapped[:, h * C : (h + 1) * C]
            query_ref[h, at, :] = (
                one * inverse_rms(one) * (sharpness_ref[0, h] / C)
            ).astype(BF)
    sends = [
        copy(query_ref, query_hbm.at[k], query_sem.at[k]) for k in range(query_hbm.shape[0])
    ]
    for send in sends:
        send.start()
    for store in stores + sends:
        store.wait()


def modulate(act, affine, weight, sharpness, owner, slot, held, copies, after):
    patches, depth = act.shape
    steps = 2
    rows = patches // steps
    shape = (G, patches + PAD, C)
    return pl.pallas_call(
        functools.partial(modulate_kernel, held),
        in_specs=[HBM, HBM, HBM, SCALARS, SCALARS, SCALARS, ANY],
        out_specs=[HBM, HBM],
        out_shape=[hbm_out((patches, depth)), hbm_out((copies,) + shape)],
        scratch_shapes=[
            pltpu.VMEM((steps, rows, depth), BF),
            pltpu.VMEM(affine.shape, F32),
            pltpu.VMEM((depth, HW), BF),
            pltpu.VMEM((steps, rows, depth), BF),
            pltpu.VMEM(shape, BF),
            DMA((steps,)),
            DMA,
            DMA,
            DMA((steps,)),
            DMA((copies,)),
        ],
        compiler_params=params(),
        name="modulate",
        cost_estimate=cost(
            2 * patches * depth * HW, 4 * patches * depth + 2 * depth * HW + 2 * patches * HW
        ),
    )(in_hbm(act), in_hbm(affine), in_hbm(weight), sharpness, owner, slot, in_hbm(after))


def temporal_entry_kernel(
    quarters, hidden_hbm, weight_hbm, sharpness_ref, *refs
):
    out_hbm, hidden_ref, weight_ref, out_ref, hidden_sem, weight_sem, store_sem = refs[-7:]
    rows = hidden_ref.shape[0] // quarters
    hidden_load = copy(hidden_hbm, hidden_ref, hidden_sem)
    loads = [
        copy(
            weight_hbm.at[:, pl.ds((3 + part) * HW, HW)], weight_ref.at[part], weight_sem.at[part]
        )
        for part in range(3)
    ]
    hidden_load.start()
    loads[0].start()
    hidden_load.wait()
    stores = []
    for part in range(3):
        loads[part].wait()
        if part < 2:
            loads[part + 1].start()
        mapped = dot(hidden_ref[...], weight_ref[part]).astype(BF)
        for h in range(G):
            done = mapped[:, h * C : (h + 1) * C]
            if part < 2:
                one = done.astype(F32)
                one = one * inverse_rms(one)
                if part == 0:
                    one = one * (sharpness_ref[1, h] / C)
                done = one.astype(BF)
            for z in range(quarters):
                out_ref[part, z, h] = done[z * rows : (z + 1) * rows, :]
        stores.append(copy(out_ref.at[part], out_hbm.at[:, :, part], store_sem.at[part]))
        stores[-1].start()
    for store in stores:
        store.wait()


def temporal_entry(hidden, weight, sharpness, quarters, after):
    patches, depth = hidden.shape
    rows = patches // quarters
    return pl.pallas_call(
        functools.partial(temporal_entry_kernel, quarters),
        in_specs=[HBM, HBM, SCALARS] + [ANY] * len(after),
        out_specs=HBM,
        out_shape=hbm_out((quarters, G, 3, rows, C)),
        scratch_shapes=[
            pltpu.VMEM((patches, depth), BF),
            pltpu.VMEM((3, depth, HW), BF),
            pltpu.VMEM((3, quarters, G, rows, C), BF),
            DMA,
            DMA((3,)),
            DMA((3,)),
        ],
        compiler_params=params(),
        name="temporal_entry",
        cost_estimate=cost(
            6 * patches * depth * HW, 2 * patches * depth + 6 * depth * HW + 6 * patches * HW
        ),
    )(in_hbm(hidden), in_hbm(weight), sharpness, *after)


def temporal_attend_kernel(length_ref, in_hbm_ref, _, out_hbm, in_ref, out_ref, sem):
    frames, _, rows, _ = in_ref.shape
    group = 16
    size = frames * group
    load = copy(in_hbm_ref, in_ref, sem)
    load.start()
    length = length_ref[0]
    row = lax.broadcasted_iota(jnp.int32, (size, size), 0)
    column = lax.broadcasted_iota(jnp.int32, (size, size), 1)
    target, source = row // group, column // group
    keep = (row % group == column % group) & (source <= target) & (source > target - length)
    load.wait()
    for g in range(rows // group):
        at = slice(g * group, (g + 1) * group)
        query = in_ref[:, 0, at, :].reshape(size, C)
        key = in_ref[:, 1, at, :].reshape(size, C)
        value = in_ref[:, 2, at, :].reshape(size, C)
        weights = jnp.where(keep, jnp.exp(dot_t(query, key)), 0.0)
        shares = weights / jnp.sum(weights, axis=-1, keepdims=True)
        result = dot(shares.astype(BF), value).astype(BF)
        out_ref[:, at, :] = result.reshape(frames, group, C)
    store = copy(out_ref, out_hbm, sem)
    store.start()
    store.wait()


def temporal_attend(length, parts, after):
    frames, _, rows, _ = parts.shape
    shape = (frames, rows, C)
    return pl.pallas_call(
        temporal_attend_kernel,
        in_specs=[SCALARS, ANY, ANY],
        out_specs=HBM,
        out_shape=hbm_out(shape),
        scratch_shapes=[pltpu.VMEM(parts.shape, BF), pltpu.VMEM(shape, BF), DMA],
        compiler_params=params(),
        name="temporal_attend",
        cost_estimate=cost(4 * frames * rows * 256 * C, 8 * frames * rows * C),
    )(length, parts, in_hbm(after))


LINE = 96
CHUNK = 3 * LINE


def halves(denominators):
    high = denominators.astype(BF).astype(F32)
    return jnp.concatenate([high, denominators - high], axis=0).astype(BF)


def attend_rows(query, keys, both, out_ref):
    patches = out_ref.shape[0] - PAD
    row = lax.broadcasted_iota(jnp.int32, (LINE, C), 0)
    column = lax.broadcasted_iota(jnp.int32, (LINE, C), 1)
    lines = []
    for start in range(0, patches, CHUNK):
        at = slice(start, start + CHUNK)
        weights = jnp.exp(dot_t(query(at), keys)).astype(BF)
        result = dot(weights, both)
        out_ref[at, :] = result[:, :C].astype(BF)
        for j in range(0, CHUNK, LINE):
            diagonal = jnp.where(row == column, result[j : j + LINE, C:], 0.0)
            lines.append(jnp.sum(diagonal, axis=0, keepdims=True))
    lines.append(jnp.zeros((8 - len(lines), C), F32))
    out_ref[patches:, :] = halves(jnp.concatenate(lines, axis=0))


def with_ones(values):
    return jnp.concatenate([values, jnp.ones(values.shape, BF)], axis=1)


def own_attend_kernel(
    hidden_hbm, weight_hbm, query_hbm, *refs
):
    out_hbm, hidden_ref, weight_ref, query_ref, out_ref = refs[-9:-4]
    hidden_sem, weight_sem, query_sem, store_sem = refs[-4:]
    hidden_load = copy(hidden_hbm, hidden_ref, hidden_sem)
    query_load = copy(query_hbm.at[0], query_ref, query_sem)
    loads = [
        copy(
            weight_hbm.at[:, pl.ds((1 + part) * HW, HW)], weight_ref.at[part], weight_sem.at[part]
        )
        for part in range(2)
    ]
    hidden_load.start()
    loads[0].start()
    hidden_load.wait()
    loads[0].wait()
    loads[1].start()
    query_load.start()
    keys = dot(hidden_ref[...], weight_ref[0]).astype(BF)
    loads[1].wait()
    values = dot(hidden_ref[...], weight_ref[1]).astype(BF)
    query_load.wait()
    stores = []
    for h in range(G):
        key = keys[:, h * C : (h + 1) * C].astype(F32)
        key = (key * inverse_rms(key)).astype(BF)
        both = with_ones(values[:, h * C : (h + 1) * C])
        attend_rows(lambda at, h=h: query_ref[h, at, :], key, both, out_ref.at[h])
        stores.append(copy(out_ref.at[h], out_hbm.at[h], store_sem.at[h]))
        stores[-1].start()
    for store in stores:
        store.wait()


def own_attend(hidden, weight, query, after):
    patches, depth = hidden.shape
    shape = query.shape[1:]
    return pl.pallas_call(
        own_attend_kernel,
        in_specs=[HBM, HBM, HBM] + [ANY] * len(after),
        out_specs=HBM,
        out_shape=hbm_out(shape),
        scratch_shapes=[
            pltpu.VMEM((patches, depth), BF),
            pltpu.VMEM((2, depth, HW), BF),
            pltpu.VMEM(shape, BF),
            pltpu.VMEM(shape, BF),
            DMA,
            DMA((2,)),
            DMA,
            DMA((G,)),
        ],
        compiler_params=params(),
        name="own_attend",
        cost_estimate=cost(
            4 * patches * depth * HW + 6 * patches * patches * HW,
            2 * patches * depth + 4 * depth * HW + 10 * patches * HW,
        ),
    )(in_hbm(hidden), in_hbm(weight), in_hbm(query), *after)


def memory_attend_kernel(count, base_ref, index_ref, query_hbm, *refs):
    blocks = refs[:count]
    out_hbm, query_ref, store_ref, out_ref, query_sem, block_sem, store_sem = refs[count + 1 :]
    frames = query_ref.shape[0]
    held = blocks[0].shape[0]
    base = base_ref[0]
    query_load = copy(query_hbm.at[pl.ds(base, frames)], query_ref, query_sem)
    query_load.start()

    def fetch(t, carry):
        i, j = t // TOPM, lax.rem(t, TOPM)
        wanted = index_ref[base + i, j]
        for b in range(count // 2):

            @pl.when(wanted // held == b)
            def _(b=b):
                slot = lax.rem(wanted, held)
                for part in range(2):
                    block = blocks[2 * b + part].at[slot]
                    copy(block, store_ref.at[i, j, part], block_sem.at[i]).start()

        return carry

    lax.fori_loop(0, frames * TOPM, fetch, 0)
    query_load.wait()
    stores = []
    for i in range(frames):
        copy(store_ref.at[i], store_ref.at[i], block_sem.at[i]).wait()
        both = [store_ref[i, j, part] for j in range(TOPM) for part in range(2)]
        keys = jnp.concatenate([block[:, :C] for block in both], axis=0)
        values = jnp.concatenate([block[:, C:] for block in both], axis=0)
        attend_rows(
            lambda at, i=i: query_ref[i, at, :], keys, with_ones(values), out_ref.at[i]
        )
        stores.append(copy(out_ref.at[i], out_hbm.at[i], store_sem.at[i]))
        stores[-1].start()
    for store in stores:
        store.wait()


def memory_attend(base, index, query, frames, blocks, after):
    count = len(blocks)
    rows = query.shape[1]
    _, part, width = blocks[0].shape
    shape = (frames, rows, C)
    return pl.pallas_call(
        functools.partial(memory_attend_kernel, count),
        in_specs=[SCALARS, SCALARS] + [ANY] * (count + 2),
        out_specs=HBM,
        out_shape=hbm_out(shape),
        scratch_shapes=[
            pltpu.VMEM(shape, BF),
            pltpu.VMEM((frames, TOPM, 2, part, width), BF),
            pltpu.VMEM(shape, BF),
            DMA,
            DMA((frames,)),
            DMA((frames,)),
        ],
        compiler_params=params(),
        name="memory_attend",
        cost_estimate=cost(
            16 * frames * rows * TOPM * part * C,
            4 * frames * rows * C + 2 * frames * TOPM * part * width,
        ),
    )(base, index, query, *blocks, in_hbm(after))


def add_partials_kernel(count, x_ref, *refs):
    ins, outs = refs[:count], refs[count : count + G]
    parts_ref, out_ref, load_sem, store_sem = refs[count + G :]
    patches = out_ref.shape[1] - PAD
    loads = []
    for j in range(G):
        frame = lax.rem(x_ref[0] + j, G)
        loads.append(
            [copy(ref.at[frame], parts_ref.at[k, j], load_sem.at[k, j]) for k, ref in enumerate(ins)]
        )
    for of_frame in loads:
        for load in of_frame:
            load.start()
    stores = []
    for j in range(G):
        for load in loads[j]:
            load.wait()
        total = parts_ref[0, j].astype(F32)
        for k in range(1, count):
            total = total + parts_ref[k, j].astype(F32)
        out_ref[j, :patches, :] = total[:patches].astype(BF)
        out_ref[j, patches:, :] = halves(total[patches : patches + 8] + total[patches + 8 :])
        stores.append(copy(out_ref.at[j], outs[j], store_sem.at[j]))
        stores[-1].start()
    for store in stores:
        store.wait()


def add_partials(x, parts):
    shape = parts[0].shape
    return pl.pallas_call(
        functools.partial(add_partials_kernel, len(parts)),
        in_specs=[SCALARS] + [ANY] * len(parts),
        out_specs=[HBM] * G,
        out_shape=[hbm_out(shape[1:])] * G,
        scratch_shapes=[
            pltpu.VMEM((len(parts),) + shape, BF),
            pltpu.VMEM(shape, BF),
            DMA((len(parts), G)),
            DMA((G,)),
        ],
        compiler_params=params(),
        name="add_partials",
        cost_estimate=cost(4 * parts[0].size, 8 * parts[0].size),
    )(x, *parts)


def leave_kernel(
    x_ref, own_hbm, memory_0, memory_1, memory_2, memory_3, time_hbm, weight_hbm, out_hbm,
    own_ref, memory_ref, time_ref, combined_ref, weight_ref, out_ref,
    own_sem, memory_sem, time_sem, weight_sem, store_sem,
):
    patches = own_ref.shape[1] - PAD
    quarters = time_ref.shape[0] // G
    rows = time_ref.shape[1]
    steps, _, width = weight_ref.shape
    heads = [lax.rem(x_ref[0] + G - j, G) for j in range(G)]
    memories = (memory_0, memory_1, memory_2, memory_3)
    own_loads = [copy(own_hbm.at[heads[j]], own_ref.at[j], own_sem.at[j]) for j in range(G)]
    memory_loads = [copy(memories[j], memory_ref.at[j], memory_sem.at[j]) for j in range(G)]
    time_load = copy(time_hbm, time_ref, time_sem)
    loads, stores = [], []
    for i in range(steps):
        at = pl.ds(i * width, width)
        loads.append(copy(weight_hbm.at[:, at], weight_ref.at[i], weight_sem.at[i]))
        stores.append(copy(out_ref.at[i], out_hbm.at[:, at], store_sem.at[i]))
    for load in own_loads + memory_loads + [time_load] + loads:
        load.start()
    row = lax.broadcasted_iota(jnp.int32, (LINE, C), 0)
    column = lax.broadcasted_iota(jnp.int32, (LINE, C), 1)
    for h in range(G):
        own_loads[h].wait()
        memory_loads[h].wait()
        column_at = pl.ds(pl.multiple_of(heads[h] * C, C), C)
        tail = own_ref[h, patches:, :].astype(F32) + memory_ref[h, patches:, :].astype(F32)
        denominators = tail[:8] + tail[8:]
        for j in range(patches // LINE):
            at = slice(j * LINE, (j + 1) * LINE)
            line = jnp.broadcast_to(denominators[j : j + 1, :], (LINE, C))
            total = jnp.sum(jnp.where(row == column, line, 0.0), axis=1, keepdims=True)
            top = own_ref[h, at, :].astype(F32) + memory_ref[h, at, :].astype(F32)
            combined_ref[at, column_at] = (top / total).astype(BF)
    time_load.wait()
    for h in range(G):
        for z in range(quarters):
            combined_ref[z * rows : (z + 1) * rows, HW + h * C : HW + (h + 1) * C] = time_ref[
                z * G + h
            ]
    for i in range(steps):
        loads[i].wait()
        out_ref[i] = dot(combined_ref[...], weight_ref[i]).astype(BF)
        stores[i].start()
    for store in stores:
        store.wait()


def leave(x, own, memory, time, weight):
    patches = own.shape[1] - PAD
    depth, width = weight.shape
    steps = 4
    step = width // steps
    return pl.pallas_call(
        leave_kernel,
        in_specs=[SCALARS, HBM] + [ANY] * (G + 1) + [HBM],
        out_specs=HBM,
        out_shape=hbm_out((patches, width)),
        scratch_shapes=[
            pltpu.VMEM(own.shape, BF),
            pltpu.VMEM(own.shape, BF),
            pltpu.VMEM(time.shape, BF),
            pltpu.VMEM((patches, depth), BF),
            pltpu.VMEM((steps, depth, step), BF),
            pltpu.VMEM((steps, patches, step), BF),
            DMA((G,)),
            DMA((G,)),
            DMA,
            DMA((steps,)),
            DMA((steps,)),
        ],
        compiler_params=params(),
        name="leave",
        cost_estimate=cost(
            2 * patches * depth * width,
            2 * depth * width + 2 * patches * width + 6 * patches * depth,
        ),
    )(x, in_hbm(own), *memory, time, in_hbm(weight))


def on_device(
    patch_activation_tensor,
    conditioning_affine,
    entry_projection_matrix,
    exit_projection_matrix,
    softmax_sharpness,
    cached_past_pairs,
    recalled_picture_holder,
    recalled_picture_position,
    lookback_lengths,
):
    frame = ("zq", "zp", "x")
    rings, sides = lax.axis_size("y"), lax.axis_size("zq")
    quarters = lax.axis_size("zp") * sides
    patches, depth = patch_activation_tensor.shape[2:]
    held, piece = cached_past_pairs.shape[:2]
    cores = lax.axis_size("c")
    x = lax.axis_index("x").astype(jnp.int32).reshape(1)
    side = lax.axis_index("zq").astype(jnp.int32).reshape(1)

    def turn(step):
        return [(s, (s + step) % rings) for s in range(rings)]

    def other(size):
        return [(s, size - 1 - s) for s in range(size)]

    def swap(blocks, axes):
        return lax.all_to_all(blocks, axes, split_axis=0, concat_axis=0, tiled=True)

    def swap_apart(blocks):
        return [in_hbm(blocks[0])] + [lax.ppermute(blocks[j], "x", turn(j)) for j in range(1, G)]

    with jax.named_scope("store"):
        split = split_store(cached_past_pairs.reshape(held * piece, 2 * HW), 1)
        pieces = swap(split[0], "x")

    with jax.named_scope("queries"):
        hidden, query = modulate(
            patch_activation_tensor.reshape(patches, depth),
            conditioning_affine.reshape(2, depth),
            entry_projection_matrix,
            softmax_sharpness,
            recalled_picture_holder.reshape(TOPM),
            recalled_picture_position.reshape(TOPM),
            held,
            sides,
            after=split,
        )

    with jax.named_scope("store"):
        joined = join_pieces(pieces, held, after=hidden)
        above = lax.ppermute(joined, "y", turn(-1))
        below = lax.ppermute(joined, "y", turn(1))
        second = lax.ppermute(joined, "zp", other(sides))

        second_above = lax.ppermute(second, "y", turn(-1))
        second_below = lax.ppermute(second, "y", turn(1))

    with jax.named_scope("queries"):
        asked, second, above, below = lax.optimization_barrier((query, second, above, below))
        asked = swap(asked.reshape((-1,) + asked.shape[2:]), ("zq", "x"))

    with jax.named_scope("temporal"):
        parts = temporal_entry(
            hidden, entry_projection_matrix, softmax_sharpness, quarters, after=[in_hbm(joined)]
        )
        sent = swap(parts.reshape((quarters * G,) + parts.shape[2:]), frame)

    with jax.named_scope("own"):
        own = own_attend(
            hidden, entry_projection_matrix, query, after=[in_hbm(parts)]
        )

    with jax.named_scope("store"):
        below, second_above, parts = lax.optimization_barrier((below, second_above, parts))
        far = lax.ppermute(below, "y", turn(1))
        second_far = lax.ppermute(second_above, "y", turn(-1))
        near = [joined, second, above, second_above, far, second_far, below, second_below]
        blocks = near + [lax.ppermute(block, "c", other(cores)) for block in near]
        blocks = [in_hbm(block) for block in blocks]

    with jax.named_scope("queries"):
        named = asked[:, patches, :TOPM].astype(jnp.int32)
        y = (named // (cores * held) - lax.axis_index("y")) & (rings - 1)
        c = (named // held & (cores - 1)) ^ lax.axis_index("c")
        index = (c * rings + y) * held + (named & (held - 1))

    def attend(base, after):
        return memory_attend(base, index, asked, asked.shape[0] // sides, blocks, after)

    with jax.named_scope("memory"):
        count = asked.shape[0] // sides
        sum_beside = attend((sides - 1 - side) * count, own)
        from_beside = lax.ppermute(sum_beside, "zq", other(sides))
        sum_here = attend(side * count, sum_beside)

    with jax.named_scope("temporal"):
        timed = temporal_attend(lookback_lengths, sent, after=sum_here)
        time = swap(timed, frame)

    with jax.named_scope("memory"):
        memory = swap_apart(add_partials(x, [in_hbm(sum_here), from_beside]))

    with jax.named_scope("exit"):
        attended = leave(x, own, memory, time, exit_projection_matrix)
    return attended.reshape(1, 1, patches, depth)


def solution(mesh):
    apart = Mesh(mesh.devices.reshape(4, 2, 2, 2, 4), ("y", "c", "zq", "zp", "x"))
    roll, frame = ("y", "c"), ("zq", "zp", "x")
    return jax.shard_map(
        on_device,
        mesh=apart,
        in_specs=(
            P(roll, frame, None, None),
            P(roll, frame, None, None),
            P(),
            P(),
            P(),
            P(roll, frame, None, None),
            P(roll, frame, None, None),
            P(roll, frame, None),
            P(roll),
        ),
        out_specs=P(roll, frame, None, None),
        check_vma=False,
    )
```

```python
import functools

import jax
import jax.numpy as jnp
from jax import lax
from jax.experimental import pallas as pl
from jax.experimental.pallas import tpu as pltpu
from jax.sharding import Mesh
from jax.sharding import PartitionSpec as P

G = 4
C = 128
HW = G * C
TOPM = 6
EPSILON = 1e-06
BF = jnp.bfloat16
F32 = jnp.float32
PAD = 16
VMEM_LIMIT = 28 * 1024 * 1024
ANY = pl.BlockSpec(memory_space=pl.ANY)
HBM = pl.BlockSpec(memory_space=pltpu.HBM)
WHOLE = pl.BlockSpec(memory_space=pltpu.VMEM)
SCALARS = pl.BlockSpec(memory_space=pltpu.SMEM)


def params(**more):
    return pltpu.CompilerParams(vmem_limit_bytes=VMEM_LIMIT, **more)


def cost(flops, bytes_accessed):
    return pl.CostEstimate(
        flops=flops // 16, bytes_accessed=bytes_accessed // 16, transcendentals=0
    )


def in_hbm(array):
    return pltpu.with_memory_space_constraint(array, pltpu.HBM)


def hbm_out(shape, dtype=BF):
    return pltpu.HBM(shape, dtype)


def inverse_rms(values):
    return lax.rsqrt(jnp.mean(values * values, axis=-1, keepdims=True) + EPSILON)


def dot(a, b):
    return jnp.dot(a, b, preferred_element_type=F32)


def dot_t(a, b):
    return lax.dot_general(a, b, (((1,), (1,)), ((), ())), preferred_element_type=F32)


DMA = pltpu.SemaphoreType.DMA
copy = pltpu.make_async_copy


def split_store_kernel(rows_ref, out_hbm, out_ref, sem):
    sends = []
    for h in range(G):
        key = rows_ref[:, h * C : (h + 1) * C].astype(F32)
        out_ref[h, :, :C] = (key * inverse_rms(key)).astype(BF)
        out_ref[h, :, C:] = rows_ref[:, HW + h * C : HW + (h + 1) * C]
        for k in range(out_hbm.shape[0]):
            sends.append(copy(out_ref.at[h], out_hbm.at[k, h], sem.at[k, h]))
            sends[-1].start()
    for send in sends:
        send.wait()


def split_store(rows, copies):
    n = rows.shape[0]
    return pl.pallas_call(
        split_store_kernel,
        in_specs=[WHOLE],
        out_specs=HBM,
        out_shape=hbm_out((copies, G, n, 2 * C)),
        scratch_shapes=[pltpu.VMEM((G, n, 2 * C), BF), DMA((copies, G))],
        compiler_params=params(),
        name="split_store",
        cost_estimate=cost(8 * n * HW, 8 * n * HW),
    )(rows)


def join_pieces_kernel(piece, in_hbm, _, out_hbm, in_ref, wide_ref, joined_ref, out_ref, sem):
    pieces = in_ref.shape[0]
    loads = [copy(in_hbm.at[i], in_ref.at[i], sem.at[i]) for i in range(pieces)]
    for load in loads:
        load.start()
    for i in range(pieces):
        loads[i].wait()
        wide_ref[i] = in_ref[i].astype(F32)
        for m in range(out_ref.shape[0]):
            joined_ref[m, i * piece : (i + 1) * piece, :] = wide_ref[
                i, m * piece : (m + 1) * piece, :
            ]
    out_ref[...] = joined_ref[...].astype(BF)
    send = copy(out_ref, out_hbm, sem.at[0])
    send.start()
    send.wait()


def join_pieces(parts, frames, after):
    pieces, rows, width = parts.shape
    piece = rows // frames
    shape = (frames, pieces * piece, width)
    return pl.pallas_call(
        functools.partial(join_pieces_kernel, piece),
        in_specs=[ANY, ANY],
        out_specs=HBM,
        out_shape=hbm_out(shape),
        scratch_shapes=[
            pltpu.VMEM(parts.shape, BF),
            pltpu.VMEM(parts.shape, F32),
            pltpu.VMEM(shape, F32),
            pltpu.VMEM(shape, BF),
            DMA((pieces,)),
        ],
        compiler_params=params(),
        name="join_pieces",
        cost_estimate=cost(parts.size, 4 * parts.size),
    )(parts, in_hbm(after))


def modulate_kernel(
    held,
    act_hbm, affine_hbm, weight_hbm, sharpness_ref, owner_ref, slot_ref, _, hidden_hbm, query_hbm,
    act_ref, affine_ref, weight_ref, hidden_ref, query_ref,
    load_sem, affine_sem, weight_sem, store_sem, query_sem,
):
    steps, rows, _ = act_ref.shape
    patches = query_ref.shape[1] - PAD
    loads, stores = [], []
    for i in range(steps):
        at = pl.ds(i * rows, rows)
        loads.append(copy(act_hbm.at[at, :], act_ref.at[i], load_sem.at[i]))
        stores.append(copy(hidden_ref.at[i], hidden_hbm.at[at, :], store_sem.at[i]))
    weight_load = copy(weight_hbm.at[:, pl.ds(0, HW)], weight_ref, weight_sem)
    affine_load = copy(affine_hbm, affine_ref, affine_sem)
    affine_load.start()
    loads[0].start()
    weight_load.start()
    row = lax.broadcasted_iota(jnp.int32, (PAD, C), 0)
    column = lax.broadcasted_iota(jnp.int32, (PAD, C), 1)
    tail = jnp.zeros((PAD, C), jnp.int32)
    for j in range(TOPM):
        tail = jnp.where((row == 0) & (column == j), owner_ref[j] * held + slot_ref[j], tail)
    for h in range(G):
        query_ref[h, patches:, :] = tail.astype(F32).astype(BF)
    affine_load.wait()
    for i in range(steps):
        at = slice(i * rows, (i + 1) * rows)
        loads[i].wait()
        if i + 1 < steps:
            loads[i + 1].start()
        act = act_ref[i].astype(F32)
        hidden = act * inverse_rms(act) * (1.0 + affine_ref[0:1, :]) + affine_ref[1:2, :]
        hidden = hidden.astype(BF)
        hidden_ref[i] = hidden
        stores[i].start()
        if i == 0:
            weight_load.wait()
        mapped = dot(hidden, weight_ref[...]).astype(BF).astype(F32)
        for h in range(G):
            one = mapped[:, h * C : (h + 1) * C]
            query_ref[h, at, :] = (
                one * inverse_rms(one) * (sharpness_ref[0, h] / C)
            ).astype(BF)
    sends = [
        copy(query_ref, query_hbm.at[k], query_sem.at[k]) for k in range(query_hbm.shape[0])
    ]
    for send in sends:
        send.start()
    for store in stores + sends:
        store.wait()


def modulate(act, affine, weight, sharpness, owner, slot, held, copies, after):
    patches, depth = act.shape
    steps = 2
    rows = patches // steps
    shape = (G, patches + PAD, C)
    return pl.pallas_call(
        functools.partial(modulate_kernel, held),
        in_specs=[HBM, HBM, HBM, SCALARS, SCALARS, SCALARS, ANY],
        out_specs=[HBM, HBM],
        out_shape=[hbm_out((patches, depth)), hbm_out((copies,) + shape)],
        scratch_shapes=[
            pltpu.VMEM((steps, rows, depth), BF),
            pltpu.VMEM(affine.shape, F32),
            pltpu.VMEM((depth, HW), BF),
            pltpu.VMEM((steps, rows, depth), BF),
            pltpu.VMEM(shape, BF),
            DMA((steps,)),
            DMA,
            DMA,
            DMA((steps,)),
            DMA((copies,)),
        ],
        compiler_params=params(),
        name="modulate",
        cost_estimate=cost(
            2 * patches * depth * HW, 4 * patches * depth + 2 * depth * HW + 2 * patches * HW
        ),
    )(in_hbm(act), in_hbm(affine), in_hbm(weight), sharpness, owner, slot, in_hbm(after))


def temporal_entry_kernel(
    quarters, hidden_hbm, weight_hbm, sharpness_ref, *refs
):
    out_hbm, hidden_ref, weight_ref, out_ref, hidden_sem, weight_sem, store_sem = refs[-7:]
    rows = hidden_ref.shape[0] // quarters
    hidden_load = copy(hidden_hbm, hidden_ref, hidden_sem)
    loads = [
        copy(
            weight_hbm.at[:, pl.ds((3 + part) * HW, HW)], weight_ref.at[part], weight_sem.at[part]
        )
        for part in range(3)
    ]
    hidden_load.start()
    loads[0].start()
    hidden_load.wait()
    stores = []
    for part in range(3):
        loads[part].wait()
        if part < 2:
            loads[part + 1].start()
        mapped = dot(hidden_ref[...], weight_ref[part]).astype(BF)
        for h in range(G):
            done = mapped[:, h * C : (h + 1) * C]
            if part < 2:
                one = done.astype(F32)
                one = one * inverse_rms(one)
                if part == 0:
                    one = one * (sharpness_ref[1, h] / C)
                done = one.astype(BF)
            for z in range(quarters):
                out_ref[part, z, h] = done[z * rows : (z + 1) * rows, :]
        stores.append(copy(out_ref.at[part], out_hbm.at[:, :, part], store_sem.at[part]))
        stores[-1].start()
    for store in stores:
        store.wait()


def temporal_entry(hidden, weight, sharpness, quarters, after):
    patches, depth = hidden.shape
    rows = patches // quarters
    return pl.pallas_call(
        functools.partial(temporal_entry_kernel, quarters),
        in_specs=[HBM, HBM, SCALARS] + [ANY] * len(after),
        out_specs=HBM,
        out_shape=hbm_out((quarters, G, 3, rows, C)),
        scratch_shapes=[
            pltpu.VMEM((patches, depth), BF),
            pltpu.VMEM((3, depth, HW), BF),
            pltpu.VMEM((3, quarters, G, rows, C), BF),
            DMA,
            DMA((3,)),
            DMA((3,)),
        ],
        compiler_params=params(),
        name="temporal_entry",
        cost_estimate=cost(
            6 * patches * depth * HW, 2 * patches * depth + 6 * depth * HW + 6 * patches * HW
        ),
    )(in_hbm(hidden), in_hbm(weight), sharpness, *after)


def temporal_attend_kernel(length_ref, in_hbm_ref, _, out_hbm, in_ref, out_ref, sem):
    frames, _, rows, _ = in_ref.shape
    group = 16
    size = frames * group
    load = copy(in_hbm_ref, in_ref, sem)
    load.start()
    length = length_ref[0]
    row = lax.broadcasted_iota(jnp.int32, (size, size), 0)
    column = lax.broadcasted_iota(jnp.int32, (size, size), 1)
    target, source = row // group, column // group
    keep = (row % group == column % group) & (source <= target) & (source > target - length)
    load.wait()
    for g in range(rows // group):
        at = slice(g * group, (g + 1) * group)
        query = in_ref[:, 0, at, :].reshape(size, C)
        key = in_ref[:, 1, at, :].reshape(size, C)
        value = in_ref[:, 2, at, :].reshape(size, C)
        weights = jnp.where(keep, jnp.exp(dot_t(query, key)), 0.0)
        shares = weights / jnp.sum(weights, axis=-1, keepdims=True)
        result = dot(shares.astype(BF), value).astype(BF)
        out_ref[:, at, :] = result.reshape(frames, group, C)
    store = copy(out_ref, out_hbm, sem)
    store.start()
    store.wait()


def temporal_attend(length, parts, after):
    frames, _, rows, _ = parts.shape
    shape = (frames, rows, C)
    return pl.pallas_call(
        temporal_attend_kernel,
        in_specs=[SCALARS, ANY, ANY],
        out_specs=HBM,
        out_shape=hbm_out(shape),
        scratch_shapes=[pltpu.VMEM(parts.shape, BF), pltpu.VMEM(shape, BF), DMA],
        compiler_params=params(),
        name="temporal_attend",
        cost_estimate=cost(4 * frames * rows * 256 * C, 8 * frames * rows * C),
    )(length, parts, in_hbm(after))


LINE = 96
CHUNK = 3 * LINE


def halves(denominators):
    high = denominators.astype(BF).astype(F32)
    return jnp.concatenate([high, denominators - high], axis=0).astype(BF)


def attend_rows(query, keys, both, out_ref):
    patches = out_ref.shape[0] - PAD
    row = lax.broadcasted_iota(jnp.int32, (LINE, C), 0)
    column = lax.broadcasted_iota(jnp.int32, (LINE, C), 1)
    lines = []
    for start in range(0, patches, CHUNK):
        at = slice(start, start + CHUNK)
        weights = jnp.exp(dot_t(query(at), keys)).astype(BF)
        result = dot(weights, both)
        out_ref[at, :] = result[:, :C].astype(BF)
        for j in range(0, CHUNK, LINE):
            diagonal = jnp.where(row == column, result[j : j + LINE, C:], 0.0)
            lines.append(jnp.sum(diagonal, axis=0, keepdims=True))
    lines.append(jnp.zeros((8 - len(lines), C), F32))
    out_ref[patches:, :] = halves(jnp.concatenate(lines, axis=0))


def with_ones(values):
    return jnp.concatenate([values, jnp.ones(values.shape, BF)], axis=1)


def own_attend_kernel(
    hidden_hbm, weight_hbm, query_hbm, *refs
):
    out_hbm, hidden_ref, weight_ref, query_ref, out_ref = refs[-9:-4]
    hidden_sem, weight_sem, query_sem, store_sem = refs[-4:]
    hidden_load = copy(hidden_hbm, hidden_ref, hidden_sem)
    query_load = copy(query_hbm.at[0], query_ref, query_sem)
    loads = [
        copy(
            weight_hbm.at[:, pl.ds((1 + part) * HW, HW)], weight_ref.at[part], weight_sem.at[part]
        )
        for part in range(2)
    ]
    hidden_load.start()
    loads[0].start()
    hidden_load.wait()
    loads[0].wait()
    loads[1].start()
    query_load.start()
    keys = dot(hidden_ref[...], weight_ref[0]).astype(BF)
    loads[1].wait()
    values = dot(hidden_ref[...], weight_ref[1]).astype(BF)
    query_load.wait()
    stores = []
    for h in range(G):
        key = keys[:, h * C : (h + 1) * C].astype(F32)
        key = (key * inverse_rms(key)).astype(BF)
        both = with_ones(values[:, h * C : (h + 1) * C])
        attend_rows(lambda at, h=h: query_ref[h, at, :], key, both, out_ref.at[h])
        stores.append(copy(out_ref.at[h], out_hbm.at[h], store_sem.at[h]))
        stores[-1].start()
    for store in stores:
        store.wait()


def own_attend(hidden, weight, query, after):
    patches, depth = hidden.shape
    shape = query.shape[1:]
    return pl.pallas_call(
        own_attend_kernel,
        in_specs=[HBM, HBM, HBM] + [ANY] * len(after),
        out_specs=HBM,
        out_shape=hbm_out(shape),
        scratch_shapes=[
            pltpu.VMEM((patches, depth), BF),
            pltpu.VMEM((2, depth, HW), BF),
            pltpu.VMEM(shape, BF),
            pltpu.VMEM(shape, BF),
            DMA,
            DMA((2,)),
            DMA,
            DMA((G,)),
        ],
        compiler_params=params(),
        name="own_attend",
        cost_estimate=cost(
            4 * patches * depth * HW + 6 * patches * patches * HW,
            2 * patches * depth + 4 * depth * HW + 10 * patches * HW,
        ),
    )(in_hbm(hidden), in_hbm(weight), in_hbm(query), *after)


def memory_attend_kernel(count, base_ref, index_ref, query_hbm, *refs):
    blocks = refs[:count]
    out_hbm, query_ref, store_ref, out_ref, query_sem, block_sem, store_sem = refs[count + 1 :]
    frames = query_ref.shape[0]
    held = blocks[0].shape[0]
    base = base_ref[0]
    query_load = copy(query_hbm.at[pl.ds(base, frames)], query_ref, query_sem)
    query_load.start()

    def fetch(t, carry):
        i, j = t // TOPM, lax.rem(t, TOPM)
        wanted = index_ref[base + i, j]
        for b in range(count // 2):

            @pl.when(wanted // held == b)
            def _(b=b):
                slot = lax.rem(wanted, held)
                for part in range(2):
                    block = blocks[2 * b + part].at[slot]
                    copy(block, store_ref.at[i, j, part], block_sem.at[i]).start()

        return carry

    lax.fori_loop(0, frames * TOPM, fetch, 0)
    query_load.wait()
    stores = []
    for i in range(frames):
        copy(store_ref.at[i], store_ref.at[i], block_sem.at[i]).wait()
        both = [store_ref[i, j, part] for j in range(TOPM) for part in range(2)]
        keys = jnp.concatenate([block[:, :C] for block in both], axis=0)
        values = jnp.concatenate([block[:, C:] for block in both], axis=0)
        attend_rows(
            lambda at, i=i: query_ref[i, at, :], keys, with_ones(values), out_ref.at[i]
        )
        stores.append(copy(out_ref.at[i], out_hbm.at[i], store_sem.at[i]))
        stores[-1].start()
    for store in stores:
        store.wait()


def memory_attend(base, index, query, frames, blocks, after):
    count = len(blocks)
    rows = query.shape[1]
    _, part, width = blocks[0].shape
    shape = (frames, rows, C)
    return pl.pallas_call(
        functools.partial(memory_attend_kernel, count),
        in_specs=[SCALARS, SCALARS] + [ANY] * (count + 2),
        out_specs=HBM,
        out_shape=hbm_out(shape),
        scratch_shapes=[
            pltpu.VMEM(shape, BF),
            pltpu.VMEM((frames, TOPM, 2, part, width), BF),
            pltpu.VMEM(shape, BF),
            DMA,
            DMA((frames,)),
            DMA((frames,)),
        ],
        compiler_params=params(),
        name="memory_attend",
        cost_estimate=cost(
            16 * frames * rows * TOPM * part * C,
            4 * frames * rows * C + 2 * frames * TOPM * part * width,
        ),
    )(base, index, query, *blocks, in_hbm(after))


def add_partials_kernel(count, x_ref, *refs):
    ins, outs = refs[:count], refs[count : count + G]
    parts_ref, out_ref, load_sem, store_sem = refs[count + G :]
    patches = out_ref.shape[1] - PAD
    loads = []
    for j in range(G):
        frame = lax.rem(x_ref[0] + j, G)
        loads.append(
            [copy(ref.at[frame], parts_ref.at[k, j], load_sem.at[k, j]) for k, ref in enumerate(ins)]
        )
    for of_frame in loads:
        for load in of_frame:
            load.start()
    stores = []
    for j in range(G):
        for load in loads[j]:
            load.wait()
        total = parts_ref[0, j].astype(F32)
        for k in range(1, count):
            total = total + parts_ref[k, j].astype(F32)
        out_ref[j, :patches, :] = total[:patches].astype(BF)
        out_ref[j, patches:, :] = halves(total[patches : patches + 8] + total[patches + 8 :])
        stores.append(copy(out_ref.at[j], outs[j], store_sem.at[j]))
        stores[-1].start()
    for store in stores:
        store.wait()


def add_partials(x, parts):
    shape = parts[0].shape
    return pl.pallas_call(
        functools.partial(add_partials_kernel, len(parts)),
        in_specs=[SCALARS] + [ANY] * len(parts),
        out_specs=[HBM] * G,
        out_shape=[hbm_out(shape[1:])] * G,
        scratch_shapes=[
            pltpu.VMEM((len(parts),) + shape, BF),
            pltpu.VMEM(shape, BF),
            DMA((len(parts), G)),
            DMA((G,)),
        ],
        compiler_params=params(),
        name="add_partials",
        cost_estimate=cost(4 * parts[0].size, 8 * parts[0].size),
    )(x, *parts)


def leave_kernel(
    x_ref, own_hbm, memory_0, memory_1, memory_2, memory_3, time_hbm, weight_hbm, out_hbm,
    own_ref, memory_ref, time_ref, combined_ref, weight_ref, out_ref,
    own_sem, memory_sem, time_sem, weight_sem, store_sem,
):
    patches = own_ref.shape[1] - PAD
    quarters = time_ref.shape[0] // G
    rows = time_ref.shape[1]
    steps, _, width = weight_ref.shape
    heads = [lax.rem(x_ref[0] + G - j, G) for j in range(G)]
    memories = (memory_0, memory_1, memory_2, memory_3)
    own_loads = [copy(own_hbm.at[heads[j]], own_ref.at[j], own_sem.at[j]) for j in range(G)]
    memory_loads = [copy(memories[j], memory_ref.at[j], memory_sem.at[j]) for j in range(G)]
    time_load = copy(time_hbm, time_ref, time_sem)
    loads, stores = [], []
    for i in range(steps):
        at = pl.ds(i * width, width)
        loads.append(copy(weight_hbm.at[:, at], weight_ref.at[i], weight_sem.at[i]))
        stores.append(copy(out_ref.at[i], out_hbm.at[:, at], store_sem.at[i]))
    for load in own_loads + memory_loads + [time_load] + loads:
        load.start()
    row = lax.broadcasted_iota(jnp.int32, (LINE, C), 0)
    column = lax.broadcasted_iota(jnp.int32, (LINE, C), 1)
    for h in range(G):
        own_loads[h].wait()
        memory_loads[h].wait()
        column_at = pl.ds(pl.multiple_of(heads[h] * C, C), C)
        tail = own_ref[h, patches:, :].astype(F32) + memory_ref[h, patches:, :].astype(F32)
        denominators = tail[:8] + tail[8:]
        for j in range(patches // LINE):
            at = slice(j * LINE, (j + 1) * LINE)
            line = jnp.broadcast_to(denominators[j : j + 1, :], (LINE, C))
            total = jnp.sum(jnp.where(row == column, line, 0.0), axis=1, keepdims=True)
            top = own_ref[h, at, :].astype(F32) + memory_ref[h, at, :].astype(F32)
            combined_ref[at, column_at] = (top / total).astype(BF)
    time_load.wait()
    for h in range(G):
        for z in range(quarters):
            combined_ref[z * rows : (z + 1) * rows, HW + h * C : HW + (h + 1) * C] = time_ref[
                z * G + h
            ]
    for i in range(steps):
        loads[i].wait()
        out_ref[i] = dot(combined_ref[...], weight_ref[i]).astype(BF)
        stores[i].start()
    for store in stores:
        store.wait()


def leave(x, own, memory, time, weight):
    patches = own.shape[1] - PAD
    depth, width = weight.shape
    steps = 4
    step = width // steps
    return pl.pallas_call(
        leave_kernel,
        in_specs=[SCALARS, HBM] + [ANY] * (G + 1) + [HBM],
        out_specs=HBM,
        out_shape=hbm_out((patches, width)),
        scratch_shapes=[
            pltpu.VMEM(own.shape, BF),
            pltpu.VMEM(own.shape, BF),
            pltpu.VMEM(time.shape, BF),
            pltpu.VMEM((patches, depth), BF),
            pltpu.VMEM((steps, depth, step), BF),
            pltpu.VMEM((steps, patches, step), BF),
            DMA((G,)),
            DMA((G,)),
            DMA,
            DMA((steps,)),
            DMA((steps,)),
        ],
        compiler_params=params(),
        name="leave",
        cost_estimate=cost(
            2 * patches * depth * width,
            2 * depth * width + 2 * patches * width + 6 * patches * depth,
        ),
    )(x, in_hbm(own), *memory, time, in_hbm(weight))


def on_device(
    patch_activation_tensor,
    conditioning_affine,
    entry_projection_matrix,
    exit_projection_matrix,
    softmax_sharpness,
    cached_past_pairs,
    recalled_picture_holder,
    recalled_picture_position,
    lookback_lengths,
):
    frame = ("zq", "zp", "x")
    rings, sides = lax.axis_size("y"), lax.axis_size("zq")
    quarters = lax.axis_size("zp") * sides
    patches, depth = patch_activation_tensor.shape[2:]
    held, piece = cached_past_pairs.shape[:2]
    cores = lax.axis_size("c")
    x = lax.axis_index("x").astype(jnp.int32).reshape(1)
    side = lax.axis_index("zq").astype(jnp.int32).reshape(1)

    def turn(step):
        return [(s, (s + step) % rings) for s in range(rings)]

    def other(size):
        return [(s, size - 1 - s) for s in range(size)]

    def swap(blocks, axes):
        return lax.all_to_all(blocks, axes, split_axis=0, concat_axis=0, tiled=True)

    def swap_apart(blocks):
        return [in_hbm(blocks[0])] + [lax.ppermute(blocks[j], "x", turn(j)) for j in range(1, G)]

    with jax.named_scope("store"):
        split = split_store(cached_past_pairs.reshape(held * piece, 2 * HW), 1)
        pieces = swap(split[0], "x")

    with jax.named_scope("queries"):
        hidden, query = modulate(
            patch_activation_tensor.reshape(patches, depth),
            conditioning_affine.reshape(2, depth),
            entry_projection_matrix,
            softmax_sharpness,
            recalled_picture_holder.reshape(TOPM),
            recalled_picture_position.reshape(TOPM),
            held,
            sides,
            after=split,
        )

    with jax.named_scope("store"):
        joined = join_pieces(pieces, held, after=hidden)
        above = lax.ppermute(joined, "y", turn(-1))
        below = lax.ppermute(joined, "y", turn(1))
        second = lax.ppermute(joined, "zp", other(sides))

        second_above = lax.ppermute(second, "y", turn(-1))
        second_below = lax.ppermute(second, "y", turn(1))

    with jax.named_scope("temporal"):
        parts = temporal_entry(
            hidden, entry_projection_matrix, softmax_sharpness, quarters, after=[in_hbm(joined)]
        )

    with jax.named_scope("queries"):
        asked, *_ = lax.optimization_barrier((query, second, above, below, parts))
        asked = swap(asked.reshape((-1,) + asked.shape[2:]), ("zq", "x"))

    with jax.named_scope("own"):
        own = own_attend(
            hidden, entry_projection_matrix, query, after=[in_hbm(parts), above]
        )

    with jax.named_scope("temporal"):
        sent, *_ = lax.optimization_barrier((parts, second_above, second_below))
        sent = swap(sent.reshape((quarters * G,) + parts.shape[2:]), frame)

    with jax.named_scope("store"):
        below, second_above, second_below, own = lax.optimization_barrier(
            (below, second_above, second_below, own)
        )
        far = lax.ppermute(below, "y", turn(1))
        second_far = lax.ppermute(second_above, "y", turn(-1))
        near = [joined, second, above, second_above, far, second_far, below, second_below]
        blocks = near + [lax.ppermute(block, "c", other(cores)) for block in near]
        blocks = [in_hbm(block) for block in blocks]

    with jax.named_scope("queries"):
        named = asked[:, patches, :TOPM].astype(jnp.int32)
        y = (named // (cores * held) - lax.axis_index("y")) & (rings - 1)
        c = (named // held & (cores - 1)) ^ lax.axis_index("c")
        index = (c * rings + y) * held + (named & (held - 1))

    def attend(base, after):
        return memory_attend(base, index, asked, asked.shape[0] // sides, blocks, after)

    with jax.named_scope("memory"):
        count = asked.shape[0] // sides
        sum_beside = attend((sides - 1 - side) * count, own)
        from_beside = lax.ppermute(sum_beside, "zq", other(sides))
        sum_here = attend(side * count, sum_beside)

    with jax.named_scope("temporal"):
        timed = temporal_attend(lookback_lengths, sent, after=sum_here)
        time = swap(timed, frame)

    with jax.named_scope("memory"):
        memory = swap_apart(add_partials(x, [in_hbm(sum_here), from_beside]))

    with jax.named_scope("exit"):
        attended = leave(x, own, memory, time, exit_projection_matrix)
    return attended.reshape(1, 1, patches, depth)


def solution(mesh):
    apart = Mesh(mesh.devices.reshape(4, 2, 2, 2, 4), ("y", "c", "zq", "zp", "x"))
    roll, frame = ("y", "c"), ("zq", "zp", "x")
    return jax.shard_map(
        on_device,
        mesh=apart,
        in_specs=(
            P(roll, frame, None, None),
            P(roll, frame, None, None),
            P(),
            P(),
            P(),
            P(roll, frame, None, None),
            P(roll, frame, None, None),
            P(roll, frame, None),
            P(roll),
        ),
        out_specs=P(roll, frame, None, None),
        check_vma=False,
    )
```

```python
import functools

import jax
import jax.numpy as jnp
from jax import lax
from jax.experimental import pallas as pl
from jax.experimental.pallas import tpu as pltpu
from jax.sharding import Mesh
from jax.sharding import PartitionSpec as P

G = 4
C = 128
HW = G * C
TOPM = 6
EPSILON = 1e-06
BF = jnp.bfloat16
F32 = jnp.float32
PAD = 16
VMEM_LIMIT = 28 * 1024 * 1024
ANY = pl.BlockSpec(memory_space=pl.ANY)
HBM = pl.BlockSpec(memory_space=pltpu.HBM)
WHOLE = pl.BlockSpec(memory_space=pltpu.VMEM)
SCALARS = pl.BlockSpec(memory_space=pltpu.SMEM)


def params(**more):
    return pltpu.CompilerParams(vmem_limit_bytes=VMEM_LIMIT, **more)


def cost(flops, bytes_accessed):
    return pl.CostEstimate(
        flops=flops // 16, bytes_accessed=bytes_accessed // 16, transcendentals=0
    )


def in_hbm(array):
    return pltpu.with_memory_space_constraint(array, pltpu.HBM)


def hbm_out(shape, dtype=BF):
    return pltpu.HBM(shape, dtype)


def inverse_rms(values):
    return lax.rsqrt(jnp.mean(values * values, axis=-1, keepdims=True) + EPSILON)


def dot(a, b):
    return jnp.dot(a, b, preferred_element_type=F32)


def dot_t(a, b):
    return lax.dot_general(a, b, (((1,), (1,)), ((), ())), preferred_element_type=F32)


DMA = pltpu.SemaphoreType.DMA
copy = pltpu.make_async_copy


def split_store_kernel(rows_ref, out_hbm, out_ref, sem):
    sends = []
    for h in range(G):
        key = rows_ref[:, h * C : (h + 1) * C].astype(F32)
        out_ref[h, :, :C] = (key * inverse_rms(key)).astype(BF)
        out_ref[h, :, C:] = rows_ref[:, HW + h * C : HW + (h + 1) * C]
        for k in range(out_hbm.shape[0]):
            sends.append(copy(out_ref.at[h], out_hbm.at[k, h], sem.at[k, h]))
            sends[-1].start()
    for send in sends:
        send.wait()


def split_store(rows, copies):
    n = rows.shape[0]
    return pl.pallas_call(
        split_store_kernel,
        in_specs=[WHOLE],
        out_specs=HBM,
        out_shape=hbm_out((copies, G, n, 2 * C)),
        scratch_shapes=[pltpu.VMEM((G, n, 2 * C), BF), DMA((copies, G))],
        compiler_params=params(),
        name="split_store",
        cost_estimate=cost(8 * n * HW, 8 * n * HW),
    )(rows)


def join_pieces_kernel(piece, in_hbm, _, out_hbm, in_ref, wide_ref, joined_ref, out_ref, sem):
    pieces = in_ref.shape[0]
    loads = [copy(in_hbm.at[i], in_ref.at[i], sem.at[i]) for i in range(pieces)]
    for load in loads:
        load.start()
    for i in range(pieces):
        loads[i].wait()
        wide_ref[i] = in_ref[i].astype(F32)
        for m in range(out_ref.shape[0]):
            joined_ref[m, i * piece : (i + 1) * piece, :] = wide_ref[
                i, m * piece : (m + 1) * piece, :
            ]
    out_ref[...] = joined_ref[...].astype(BF)
    send = copy(out_ref, out_hbm, sem.at[0])
    send.start()
    send.wait()


def join_pieces(parts, frames, after):
    pieces, rows, width = parts.shape
    piece = rows // frames
    shape = (frames, pieces * piece, width)
    return pl.pallas_call(
        functools.partial(join_pieces_kernel, piece),
        in_specs=[ANY, ANY],
        out_specs=HBM,
        out_shape=hbm_out(shape),
        scratch_shapes=[
            pltpu.VMEM(parts.shape, BF),
            pltpu.VMEM(parts.shape, F32),
            pltpu.VMEM(shape, F32),
            pltpu.VMEM(shape, BF),
            DMA((pieces,)),
        ],
        compiler_params=params(),
        name="join_pieces",
        cost_estimate=cost(parts.size, 4 * parts.size),
    )(parts, in_hbm(after))


def modulate_kernel(
    held,
    act_hbm, affine_hbm, weight_hbm, sharpness_ref, owner_ref, slot_ref, _, hidden_hbm, query_hbm,
    act_ref, affine_ref, weight_ref, hidden_ref, query_ref,
    load_sem, affine_sem, weight_sem, store_sem, query_sem,
):
    steps, rows, _ = act_ref.shape
    patches = query_ref.shape[1] - PAD
    loads, stores = [], []
    for i in range(steps):
        at = pl.ds(i * rows, rows)
        loads.append(copy(act_hbm.at[at, :], act_ref.at[i], load_sem.at[i]))
        stores.append(copy(hidden_ref.at[i], hidden_hbm.at[at, :], store_sem.at[i]))
    weight_load = copy(weight_hbm.at[:, pl.ds(0, HW)], weight_ref, weight_sem)
    affine_load = copy(affine_hbm, affine_ref, affine_sem)
    affine_load.start()
    loads[0].start()
    weight_load.start()
    row = lax.broadcasted_iota(jnp.int32, (PAD, C), 0)
    column = lax.broadcasted_iota(jnp.int32, (PAD, C), 1)
    tail = jnp.zeros((PAD, C), jnp.int32)
    for j in range(TOPM):
        tail = jnp.where((row == 0) & (column == j), owner_ref[j] * held + slot_ref[j], tail)
    for h in range(G):
        query_ref[h, patches:, :] = tail.astype(F32).astype(BF)
    affine_load.wait()
    for i in range(steps):
        at = slice(i * rows, (i + 1) * rows)
        loads[i].wait()
        if i + 1 < steps:
            loads[i + 1].start()
        act = act_ref[i].astype(F32)
        hidden = act * inverse_rms(act) * (1.0 + affine_ref[0:1, :]) + affine_ref[1:2, :]
        hidden = hidden.astype(BF)
        hidden_ref[i] = hidden
        stores[i].start()
        if i == 0:
            weight_load.wait()
        mapped = dot(hidden, weight_ref[...]).astype(BF).astype(F32)
        for h in range(G):
            one = mapped[:, h * C : (h + 1) * C]
            query_ref[h, at, :] = (
                one * inverse_rms(one) * (sharpness_ref[0, h] / C)
            ).astype(BF)
    sends = [
        copy(query_ref, query_hbm.at[k], query_sem.at[k]) for k in range(query_hbm.shape[0])
    ]
    for send in sends:
        send.start()
    for store in stores + sends:
        store.wait()


def modulate(act, affine, weight, sharpness, owner, slot, held, copies, after):
    patches, depth = act.shape
    steps = 2
    rows = patches // steps
    shape = (G, patches + PAD, C)
    return pl.pallas_call(
        functools.partial(modulate_kernel, held),
        in_specs=[HBM, HBM, HBM, SCALARS, SCALARS, SCALARS, ANY],
        out_specs=[HBM, HBM],
        out_shape=[hbm_out((patches, depth)), hbm_out((copies,) + shape)],
        scratch_shapes=[
            pltpu.VMEM((steps, rows, depth), BF),
            pltpu.VMEM(affine.shape, F32),
            pltpu.VMEM((depth, HW), BF),
            pltpu.VMEM((steps, rows, depth), BF),
            pltpu.VMEM(shape, BF),
            DMA((steps,)),
            DMA,
            DMA,
            DMA((steps,)),
            DMA((copies,)),
        ],
        compiler_params=params(),
        name="modulate",
        cost_estimate=cost(
            2 * patches * depth * HW, 4 * patches * depth + 2 * depth * HW + 2 * patches * HW
        ),
    )(in_hbm(act), in_hbm(affine), in_hbm(weight), sharpness, owner, slot, in_hbm(after))


def temporal_entry_kernel(
    quarters, hidden_hbm, weight_hbm, sharpness_ref, *refs
):
    out_hbm, hidden_ref, weight_ref, out_ref, hidden_sem, weight_sem, store_sem = refs[-7:]
    rows = hidden_ref.shape[0] // quarters
    hidden_load = copy(hidden_hbm, hidden_ref, hidden_sem)
    loads = [
        copy(
            weight_hbm.at[:, pl.ds((3 + part) * HW, HW)], weight_ref.at[part], weight_sem.at[part]
        )
        for part in range(3)
    ]
    hidden_load.start()
    loads[0].start()
    hidden_load.wait()
    stores = []
    for part in range(3):
        loads[part].wait()
        if part < 2:
            loads[part + 1].start()
        mapped = dot(hidden_ref[...], weight_ref[part]).astype(BF)
        for h in range(G):
            done = mapped[:, h * C : (h + 1) * C]
            if part < 2:
                one = done.astype(F32)
                one = one * inverse_rms(one)
                if part == 0:
                    one = one * (sharpness_ref[1, h] / C)
                done = one.astype(BF)
            for z in range(quarters):
                out_ref[part, z, h] = done[z * rows : (z + 1) * rows, :]
        stores.append(copy(out_ref.at[part], out_hbm.at[:, :, part], store_sem.at[part]))
        stores[-1].start()
    for store in stores:
        store.wait()


def temporal_entry(hidden, weight, sharpness, quarters, after):
    patches, depth = hidden.shape
    rows = patches // quarters
    return pl.pallas_call(
        functools.partial(temporal_entry_kernel, quarters),
        in_specs=[HBM, HBM, SCALARS] + [ANY] * len(after),
        out_specs=HBM,
        out_shape=hbm_out((quarters, G, 3, rows, C)),
        scratch_shapes=[
            pltpu.VMEM((patches, depth), BF),
            pltpu.VMEM((3, depth, HW), BF),
            pltpu.VMEM((3, quarters, G, rows, C), BF),
            DMA,
            DMA((3,)),
            DMA((3,)),
        ],
        compiler_params=params(),
        name="temporal_entry",
        cost_estimate=cost(
            6 * patches * depth * HW, 2 * patches * depth + 6 * depth * HW + 6 * patches * HW
        ),
    )(in_hbm(hidden), in_hbm(weight), sharpness, *after)


def temporal_attend_kernel(length_ref, in_hbm_ref, _, out_hbm, in_ref, out_ref, sem):
    frames, _, rows, _ = in_ref.shape
    group = 16
    size = frames * group
    load = copy(in_hbm_ref, in_ref, sem)
    load.start()
    length = length_ref[0]
    row = lax.broadcasted_iota(jnp.int32, (size, size), 0)
    column = lax.broadcasted_iota(jnp.int32, (size, size), 1)
    target, source = row // group, column // group
    keep = (row % group == column % group) & (source <= target) & (source > target - length)
    load.wait()
    for g in range(rows // group):
        at = slice(g * group, (g + 1) * group)
        query = in_ref[:, 0, at, :].reshape(size, C)
        key = in_ref[:, 1, at, :].reshape(size, C)
        value = in_ref[:, 2, at, :].reshape(size, C)
        weights = jnp.where(keep, jnp.exp(dot_t(query, key)), 0.0)
        shares = weights / jnp.sum(weights, axis=-1, keepdims=True)
        result = dot(shares.astype(BF), value).astype(BF)
        out_ref[:, at, :] = result.reshape(frames, group, C)
    store = copy(out_ref, out_hbm, sem)
    store.start()
    store.wait()


def temporal_attend(length, parts, after):
    frames, _, rows, _ = parts.shape
    shape = (frames, rows, C)
    return pl.pallas_call(
        temporal_attend_kernel,
        in_specs=[SCALARS, ANY, ANY],
        out_specs=HBM,
        out_shape=hbm_out(shape),
        scratch_shapes=[pltpu.VMEM(parts.shape, BF), pltpu.VMEM(shape, BF), DMA],
        compiler_params=params(),
        name="temporal_attend",
        cost_estimate=cost(4 * frames * rows * 256 * C, 8 * frames * rows * C),
    )(length, parts, in_hbm(after))


LINE = 96
CHUNK = 3 * LINE


def halves(denominators):
    high = denominators.astype(BF).astype(F32)
    return jnp.concatenate([high, denominators - high], axis=0).astype(BF)


def attend_rows(query, keys, both, out_ref):
    patches = out_ref.shape[0] - PAD
    row = lax.broadcasted_iota(jnp.int32, (LINE, C), 0)
    column = lax.broadcasted_iota(jnp.int32, (LINE, C), 1)
    lines = []
    for start in range(0, patches, CHUNK):
        at = slice(start, start + CHUNK)
        weights = jnp.exp(dot_t(query(at), keys)).astype(BF)
        result = dot(weights, both)
        out_ref[at, :] = result[:, :C].astype(BF)
        for j in range(0, CHUNK, LINE):
            diagonal = jnp.where(row == column, result[j : j + LINE, C:], 0.0)
            lines.append(jnp.sum(diagonal, axis=0, keepdims=True))
    lines.append(jnp.zeros((8 - len(lines), C), F32))
    out_ref[patches:, :] = halves(jnp.concatenate(lines, axis=0))


def with_ones(values):
    return jnp.concatenate([values, jnp.ones(values.shape, BF)], axis=1)


def own_attend_kernel(
    hidden_hbm, weight_hbm, query_hbm, *refs
):
    out_hbm, hidden_ref, weight_ref, query_ref, out_ref = refs[-9:-4]
    hidden_sem, weight_sem, query_sem, store_sem = refs[-4:]
    hidden_load = copy(hidden_hbm, hidden_ref, hidden_sem)
    query_load = copy(query_hbm.at[0], query_ref, query_sem)
    loads = [
        copy(
            weight_hbm.at[:, pl.ds((1 + part) * HW, HW)], weight_ref.at[part], weight_sem.at[part]
        )
        for part in range(2)
    ]
    hidden_load.start()
    loads[0].start()
    hidden_load.wait()
    loads[0].wait()
    loads[1].start()
    query_load.start()
    keys = dot(hidden_ref[...], weight_ref[0]).astype(BF)
    loads[1].wait()
    values = dot(hidden_ref[...], weight_ref[1]).astype(BF)
    query_load.wait()
    stores = []
    for h in range(G):
        key = keys[:, h * C : (h + 1) * C].astype(F32)
        key = (key * inverse_rms(key)).astype(BF)
        both = with_ones(values[:, h * C : (h + 1) * C])
        attend_rows(lambda at, h=h: query_ref[h, at, :], key, both, out_ref.at[h])
        stores.append(copy(out_ref.at[h], out_hbm.at[h], store_sem.at[h]))
        stores[-1].start()
    for store in stores:
        store.wait()


def own_attend(hidden, weight, query, after):
    patches, depth = hidden.shape
    shape = query.shape[1:]
    return pl.pallas_call(
        own_attend_kernel,
        in_specs=[HBM, HBM, HBM] + [ANY] * len(after),
        out_specs=HBM,
        out_shape=hbm_out(shape),
        scratch_shapes=[
            pltpu.VMEM((patches, depth), BF),
            pltpu.VMEM((2, depth, HW), BF),
            pltpu.VMEM(shape, BF),
            pltpu.VMEM(shape, BF),
            DMA,
            DMA((2,)),
            DMA,
            DMA((G,)),
        ],
        compiler_params=params(),
        name="own_attend",
        cost_estimate=cost(
            4 * patches * depth * HW + 6 * patches * patches * HW,
            2 * patches * depth + 4 * depth * HW + 10 * patches * HW,
        ),
    )(in_hbm(hidden), in_hbm(weight), in_hbm(query), *after)


def memory_attend_kernel(count, base_ref, index_ref, query_hbm, *refs):
    blocks = refs[:count]
    out_hbm, query_ref, store_ref, out_ref, query_sem, block_sem, store_sem = refs[count + 1 :]
    frames = query_ref.shape[0]
    held = blocks[0].shape[0]
    base = base_ref[0]
    query_load = copy(query_hbm.at[pl.ds(base, frames)], query_ref, query_sem)
    query_load.start()

    def fetch(t, carry):
        i, j = t // TOPM, lax.rem(t, TOPM)
        wanted = index_ref[base + i, j]
        for b in range(count // 2):

            @pl.when(wanted // held == b)
            def _(b=b):
                slot = lax.rem(wanted, held)
                for part in range(2):
                    block = blocks[2 * b + part].at[slot]
                    copy(block, store_ref.at[i, j, part], block_sem.at[i]).start()

        return carry

    lax.fori_loop(0, frames * TOPM, fetch, 0)
    query_load.wait()
    stores = []
    for i in range(frames):
        copy(store_ref.at[i], store_ref.at[i], block_sem.at[i]).wait()
        both = [store_ref[i, j, part] for j in range(TOPM) for part in range(2)]
        keys = jnp.concatenate([block[:, :C] for block in both], axis=0)
        values = jnp.concatenate([block[:, C:] for block in both], axis=0)
        attend_rows(
            lambda at, i=i: query_ref[i, at, :], keys, with_ones(values), out_ref.at[i]
        )
        stores.append(copy(out_ref.at[i], out_hbm.at[i], store_sem.at[i]))
        stores[-1].start()
    for store in stores:
        store.wait()


def memory_attend(base, index, query, frames, blocks, after):
    count = len(blocks)
    rows = query.shape[1]
    _, part, width = blocks[0].shape
    shape = (frames, rows, C)
    return pl.pallas_call(
        functools.partial(memory_attend_kernel, count),
        in_specs=[SCALARS, SCALARS] + [ANY] * (count + 2),
        out_specs=HBM,
        out_shape=hbm_out(shape),
        scratch_shapes=[
            pltpu.VMEM(shape, BF),
            pltpu.VMEM((frames, TOPM, 2, part, width), BF),
            pltpu.VMEM(shape, BF),
            DMA,
            DMA((frames,)),
            DMA((frames,)),
        ],
        compiler_params=params(),
        name="memory_attend",
        cost_estimate=cost(
            16 * frames * rows * TOPM * part * C,
            4 * frames * rows * C + 2 * frames * TOPM * part * width,
        ),
    )(base, index, query, *blocks, in_hbm(after))


def add_partials_kernel(count, x_ref, *refs):
    ins, outs = refs[:count], refs[count : count + G]
    parts_ref, out_ref, load_sem, store_sem = refs[count + G :]
    patches = out_ref.shape[1] - PAD
    loads = []
    for j in range(G):
        frame = lax.rem(x_ref[0] + j, G)
        loads.append(
            [copy(ref.at[frame], parts_ref.at[k, j], load_sem.at[k, j]) for k, ref in enumerate(ins)]
        )
    for of_frame in loads:
        for load in of_frame:
            load.start()
    stores = []
    for j in range(G):
        for load in loads[j]:
            load.wait()
        total = parts_ref[0, j].astype(F32)
        for k in range(1, count):
            total = total + parts_ref[k, j].astype(F32)
        out_ref[j, :patches, :] = total[:patches].astype(BF)
        out_ref[j, patches:, :] = halves(total[patches : patches + 8] + total[patches + 8 :])
        stores.append(copy(out_ref.at[j], outs[j], store_sem.at[j]))
        stores[-1].start()
    for store in stores:
        store.wait()


def add_partials(x, parts):
    shape = parts[0].shape
    return pl.pallas_call(
        functools.partial(add_partials_kernel, len(parts)),
        in_specs=[SCALARS] + [ANY] * len(parts),
        out_specs=[HBM] * G,
        out_shape=[hbm_out(shape[1:])] * G,
        scratch_shapes=[
            pltpu.VMEM((len(parts),) + shape, BF),
            pltpu.VMEM(shape, BF),
            DMA((len(parts), G)),
            DMA((G,)),
        ],
        compiler_params=params(),
        name="add_partials",
        cost_estimate=cost(4 * parts[0].size, 8 * parts[0].size),
    )(x, *parts)


def leave_kernel(
    x_ref, own_hbm, memory_0, memory_1, memory_2, memory_3, time_hbm, weight_hbm, out_hbm,
    own_ref, memory_ref, time_ref, combined_ref, weight_ref, out_ref,
    own_sem, memory_sem, time_sem, weight_sem, store_sem,
):
    patches = own_ref.shape[1] - PAD
    quarters = time_ref.shape[0] // G
    rows = time_ref.shape[1]
    steps, _, width = weight_ref.shape
    heads = [lax.rem(x_ref[0] + G - j, G) for j in range(G)]
    memories = (memory_0, memory_1, memory_2, memory_3)
    own_loads = [copy(own_hbm.at[heads[j]], own_ref.at[j], own_sem.at[j]) for j in range(G)]
    memory_loads = [copy(memories[j], memory_ref.at[j], memory_sem.at[j]) for j in range(G)]
    time_load = copy(time_hbm, time_ref, time_sem)
    loads, stores = [], []
    for i in range(steps):
        at = pl.ds(i * width, width)
        loads.append(copy(weight_hbm.at[:, at], weight_ref.at[i], weight_sem.at[i]))
        stores.append(copy(out_ref.at[i], out_hbm.at[:, at], store_sem.at[i]))
    for load in own_loads + memory_loads + [time_load] + loads:
        load.start()
    row = lax.broadcasted_iota(jnp.int32, (LINE, C), 0)
    column = lax.broadcasted_iota(jnp.int32, (LINE, C), 1)
    for h in range(G):
        own_loads[h].wait()
        memory_loads[h].wait()
        column_at = pl.ds(pl.multiple_of(heads[h] * C, C), C)
        tail = own_ref[h, patches:, :].astype(F32) + memory_ref[h, patches:, :].astype(F32)
        denominators = tail[:8] + tail[8:]
        for j in range(patches // LINE):
            at = slice(j * LINE, (j + 1) * LINE)
            line = jnp.broadcast_to(denominators[j : j + 1, :], (LINE, C))
            total = jnp.sum(jnp.where(row == column, line, 0.0), axis=1, keepdims=True)
            top = own_ref[h, at, :].astype(F32) + memory_ref[h, at, :].astype(F32)
            combined_ref[at, column_at] = (top / total).astype(BF)
    time_load.wait()
    for h in range(G):
        for z in range(quarters):
            combined_ref[z * rows : (z + 1) * rows, HW + h * C : HW + (h + 1) * C] = time_ref[
                z * G + h
            ]
    for i in range(steps):
        loads[i].wait()
        out_ref[i] = dot(combined_ref[...], weight_ref[i]).astype(BF)
        stores[i].start()
    for store in stores:
        store.wait()


def leave(x, own, memory, time, weight):
    patches = own.shape[1] - PAD
    depth, width = weight.shape
    steps = 4
    step = width // steps
    return pl.pallas_call(
        leave_kernel,
        in_specs=[SCALARS, HBM] + [ANY] * (G + 1) + [HBM],
        out_specs=HBM,
        out_shape=hbm_out((patches, width)),
        scratch_shapes=[
            pltpu.VMEM(own.shape, BF),
            pltpu.VMEM(own.shape, BF),
            pltpu.VMEM(time.shape, BF),
            pltpu.VMEM((patches, depth), BF),
            pltpu.VMEM((steps, depth, step), BF),
            pltpu.VMEM((steps, patches, step), BF),
            DMA((G,)),
            DMA((G,)),
            DMA,
            DMA((steps,)),
            DMA((steps,)),
        ],
        compiler_params=params(),
        name="leave",
        cost_estimate=cost(
            2 * patches * depth * width,
            2 * depth * width + 2 * patches * width + 6 * patches * depth,
        ),
    )(x, in_hbm(own), *memory, time, in_hbm(weight))


def on_device(
    patch_activation_tensor,
    conditioning_affine,
    entry_projection_matrix,
    exit_projection_matrix,
    softmax_sharpness,
    cached_past_pairs,
    recalled_picture_holder,
    recalled_picture_position,
    lookback_lengths,
):
    frame = ("zq", "zp", "x")
    rings, sides = lax.axis_size("y"), lax.axis_size("zq")
    quarters = lax.axis_size("zp") * sides
    patches, depth = patch_activation_tensor.shape[2:]
    held, piece = cached_past_pairs.shape[:2]
    cores = lax.axis_size("c")
    x = lax.axis_index("x").astype(jnp.int32).reshape(1)
    side = lax.axis_index("zq").astype(jnp.int32).reshape(1)

    def turn(step):
        return [(s, (s + step) % rings) for s in range(rings)]

    def other(size):
        return [(s, size - 1 - s) for s in range(size)]

    def swap(blocks, axes):
        return lax.all_to_all(blocks, axes, split_axis=0, concat_axis=0, tiled=True)

    def swap_apart(blocks):
        return [in_hbm(blocks[0])] + [lax.ppermute(blocks[j], "x", turn(j)) for j in range(1, G)]

    with jax.named_scope("store"):
        split = split_store(cached_past_pairs.reshape(held * piece, 2 * HW), 1)
        pieces = swap(split[0], "x")

    with jax.named_scope("queries"):
        hidden, query = modulate(
            patch_activation_tensor.reshape(patches, depth),
            conditioning_affine.reshape(2, depth),
            entry_projection_matrix,
            softmax_sharpness,
            recalled_picture_holder.reshape(TOPM),
            recalled_picture_position.reshape(TOPM),
            held,
            sides,
            after=split,
        )

    with jax.named_scope("store"):
        joined = join_pieces(pieces, held, after=hidden)
        above = lax.ppermute(joined, "y", turn(-1))
        below = lax.ppermute(joined, "y", turn(1))
        second = lax.ppermute(joined, "zp", other(sides))

        second_above = lax.ppermute(second, "y", turn(-1))
        second_below = lax.ppermute(second, "y", turn(1))

    with jax.named_scope("temporal"):
        parts = temporal_entry(
            hidden, entry_projection_matrix, softmax_sharpness, quarters, after=[in_hbm(joined)]
        )

    with jax.named_scope("queries"):
        asked, *_ = lax.optimization_barrier((query, second, above, below, parts))
        asked = swap(asked.reshape((-1,) + asked.shape[2:]), ("zq", "x"))

    with jax.named_scope("own"):
        own = own_attend(
            hidden, entry_projection_matrix, query, after=[in_hbm(parts), above]
        )

    with jax.named_scope("temporal"):
        sent, *_ = lax.optimization_barrier((parts, own))
        sent = swap(sent.reshape((quarters * G,) + parts.shape[2:]), frame)

    with jax.named_scope("store"):
        below, second_above, second_below = lax.optimization_barrier(
            (below, second_above, second_below)
        )
        far = lax.ppermute(below, "y", turn(1))
        second_far = lax.ppermute(second_above, "y", turn(-1))
        near = [joined, second, above, second_above, far, second_far, below, second_below]
        blocks = near + [lax.ppermute(block, "c", other(cores)) for block in near]
        blocks = [in_hbm(block) for block in blocks]

    with jax.named_scope("queries"):
        named = asked[:, patches, :TOPM].astype(jnp.int32)
        y = (named // (cores * held) - lax.axis_index("y")) & (rings - 1)
        c = (named // held & (cores - 1)) ^ lax.axis_index("c")
        index = (c * rings + y) * held + (named & (held - 1))

    def attend(base, after):
        return memory_attend(base, index, asked, asked.shape[0] // sides, blocks, after)

    with jax.named_scope("memory"):
        count = asked.shape[0] // sides
        sum_beside = attend((sides - 1 - side) * count, own)
        from_beside = lax.ppermute(sum_beside, "zq", other(sides))

    with jax.named_scope("temporal"):
        timed = temporal_attend(lookback_lengths, sent, after=sum_beside)
        time = swap(timed, frame)

    with jax.named_scope("memory"):
        sum_here = attend(side * count, timed)
        memory = swap_apart(add_partials(x, [in_hbm(sum_here), from_beside]))

    with jax.named_scope("exit"):
        attended = leave(x, own, memory, time, exit_projection_matrix)
    return attended.reshape(1, 1, patches, depth)


def solution(mesh):
    apart = Mesh(mesh.devices.reshape(4, 2, 2, 2, 4), ("y", "c", "zq", "zp", "x"))
    roll, frame = ("y", "c"), ("zq", "zp", "x")
    return jax.shard_map(
        on_device,
        mesh=apart,
        in_specs=(
            P(roll, frame, None, None),
            P(roll, frame, None, None),
            P(),
            P(),
            P(),
            P(roll, frame, None, None),
            P(roll, frame, None, None),
            P(roll, frame, None),
            P(roll),
        ),
        out_specs=P(roll, frame, None, None),
        check_vma=False,
    )
```

```python
import functools

import jax
import jax.numpy as jnp
from jax import lax
from jax.experimental import pallas as pl
from jax.experimental.pallas import tpu as pltpu
from jax.sharding import Mesh
from jax.sharding import PartitionSpec as P

G = 4
C = 128
HW = G * C
TOPM = 6
EPSILON = 1e-06
BF = jnp.bfloat16
F32 = jnp.float32
PAD = 16
VMEM_LIMIT = 28 * 1024 * 1024
ANY = pl.BlockSpec(memory_space=pl.ANY)
HBM = pl.BlockSpec(memory_space=pltpu.HBM)
WHOLE = pl.BlockSpec(memory_space=pltpu.VMEM)
SCALARS = pl.BlockSpec(memory_space=pltpu.SMEM)


def params(**more):
    return pltpu.CompilerParams(vmem_limit_bytes=VMEM_LIMIT, **more)


def cost(flops, bytes_accessed):
    return pl.CostEstimate(
        flops=flops // 16, bytes_accessed=bytes_accessed // 16, transcendentals=0
    )


def in_hbm(array):
    return pltpu.with_memory_space_constraint(array, pltpu.HBM)


def hbm_out(shape, dtype=BF):
    return pltpu.HBM(shape, dtype)


def inverse_rms(values):
    return lax.rsqrt(jnp.mean(values * values, axis=-1, keepdims=True) + EPSILON)


def dot(a, b):
    return jnp.dot(a, b, preferred_element_type=F32)


def dot_t(a, b):
    return lax.dot_general(a, b, (((1,), (1,)), ((), ())), preferred_element_type=F32)


DMA = pltpu.SemaphoreType.DMA
copy = pltpu.make_async_copy


def split_store_kernel(rows_ref, out_hbm, out_ref, sem):
    sends = []
    for h in range(G):
        key = rows_ref[:, h * C : (h + 1) * C].astype(F32)
        out_ref[h, :, :C] = (key * inverse_rms(key)).astype(BF)
        out_ref[h, :, C:] = rows_ref[:, HW + h * C : HW + (h + 1) * C]
        for k in range(out_hbm.shape[0]):
            sends.append(copy(out_ref.at[h], out_hbm.at[k, h], sem.at[k, h]))
            sends[-1].start()
    for send in sends:
        send.wait()


def split_store(rows, copies):
    n = rows.shape[0]
    return pl.pallas_call(
        split_store_kernel,
        in_specs=[WHOLE],
        out_specs=HBM,
        out_shape=hbm_out((copies, G, n, 2 * C)),
        scratch_shapes=[pltpu.VMEM((G, n, 2 * C), BF), DMA((copies, G))],
        compiler_params=params(),
        name="split_store",
        cost_estimate=cost(8 * n * HW, 8 * n * HW),
    )(rows)


def join_pieces_kernel(piece, in_hbm, _, out_hbm, in_ref, wide_ref, joined_ref, out_ref, sem):
    pieces = in_ref.shape[0]
    loads = [copy(in_hbm.at[i], in_ref.at[i], sem.at[i]) for i in range(pieces)]
    for load in loads:
        load.start()
    for i in range(pieces):
        loads[i].wait()
        wide_ref[i] = in_ref[i].astype(F32)
        for m in range(out_ref.shape[0]):
            joined_ref[m, i * piece : (i + 1) * piece, :] = wide_ref[
                i, m * piece : (m + 1) * piece, :
            ]
    out_ref[...] = joined_ref[...].astype(BF)
    send = copy(out_ref, out_hbm, sem.at[0])
    send.start()
    send.wait()


def join_pieces(parts, frames, after):
    pieces, rows, width = parts.shape
    piece = rows // frames
    shape = (frames, pieces * piece, width)
    return pl.pallas_call(
        functools.partial(join_pieces_kernel, piece),
        in_specs=[ANY, ANY],
        out_specs=HBM,
        out_shape=hbm_out(shape),
        scratch_shapes=[
            pltpu.VMEM(parts.shape, BF),
            pltpu.VMEM(parts.shape, F32),
            pltpu.VMEM(shape, F32),
            pltpu.VMEM(shape, BF),
            DMA((pieces,)),
        ],
        compiler_params=params(),
        name="join_pieces",
        cost_estimate=cost(parts.size, 4 * parts.size),
    )(parts, in_hbm(after))


def modulate_kernel(
    held,
    act_hbm, affine_hbm, weight_hbm, sharpness_ref, owner_ref, slot_ref, _, hidden_hbm, query_hbm,
    act_ref, affine_ref, weight_ref, hidden_ref, query_ref,
    load_sem, affine_sem, weight_sem, store_sem, query_sem,
):
    steps, rows, _ = act_ref.shape
    patches = query_ref.shape[1] - PAD
    loads, stores = [], []
    for i in range(steps):
        at = pl.ds(i * rows, rows)
        loads.append(copy(act_hbm.at[at, :], act_ref.at[i], load_sem.at[i]))
        stores.append(copy(hidden_ref.at[i], hidden_hbm.at[at, :], store_sem.at[i]))
    weight_load = copy(weight_hbm.at[:, pl.ds(0, HW)], weight_ref, weight_sem)
    affine_load = copy(affine_hbm, affine_ref, affine_sem)
    affine_load.start()
    loads[0].start()
    weight_load.start()
    row = lax.broadcasted_iota(jnp.int32, (PAD, C), 0)
    column = lax.broadcasted_iota(jnp.int32, (PAD, C), 1)
    tail = jnp.zeros((PAD, C), jnp.int32)
    for j in range(TOPM):
        tail = jnp.where((row == 0) & (column == j), owner_ref[j] * held + slot_ref[j], tail)
    for h in range(G):
        query_ref[h, patches:, :] = tail.astype(F32).astype(BF)
    affine_load.wait()
    for i in range(steps):
        at = slice(i * rows, (i + 1) * rows)
        loads[i].wait()
        if i + 1 < steps:
            loads[i + 1].start()
        act = act_ref[i].astype(F32)
        hidden = act * inverse_rms(act) * (1.0 + affine_ref[0:1, :]) + affine_ref[1:2, :]
        hidden = hidden.astype(BF)
        hidden_ref[i] = hidden
        stores[i].start()
        if i == 0:
            weight_load.wait()
        mapped = dot(hidden, weight_ref[...]).astype(BF).astype(F32)
        for h in range(G):
            one = mapped[:, h * C : (h + 1) * C]
            query_ref[h, at, :] = (
                one * inverse_rms(one) * (sharpness_ref[0, h] / C)
            ).astype(BF)
    sends = [
        copy(query_ref, query_hbm.at[k], query_sem.at[k]) for k in range(query_hbm.shape[0])
    ]
    for send in sends:
        send.start()
    for store in stores + sends:
        store.wait()


def modulate(act, affine, weight, sharpness, owner, slot, held, copies, after):
    patches, depth = act.shape
    steps = 2
    rows = patches // steps
    shape = (G, patches + PAD, C)
    return pl.pallas_call(
        functools.partial(modulate_kernel, held),
        in_specs=[HBM, HBM, HBM, SCALARS, SCALARS, SCALARS, ANY],
        out_specs=[HBM, HBM],
        out_shape=[hbm_out((patches, depth)), hbm_out((copies,) + shape)],
        scratch_shapes=[
            pltpu.VMEM((steps, rows, depth), BF),
            pltpu.VMEM(affine.shape, F32),
            pltpu.VMEM((depth, HW), BF),
            pltpu.VMEM((steps, rows, depth), BF),
            pltpu.VMEM(shape, BF),
            DMA((steps,)),
            DMA,
            DMA,
            DMA((steps,)),
            DMA((copies,)),
        ],
        compiler_params=params(),
        name="modulate",
        cost_estimate=cost(
            2 * patches * depth * HW, 4 * patches * depth + 2 * depth * HW + 2 * patches * HW
        ),
    )(in_hbm(act), in_hbm(affine), in_hbm(weight), sharpness, owner, slot, in_hbm(after))


def temporal_entry_kernel(
    quarters, hidden_hbm, weight_hbm, sharpness_ref, *refs
):
    out_hbm, hidden_ref, weight_ref, out_ref, hidden_sem, weight_sem, store_sem = refs[-7:]
    rows = hidden_ref.shape[0] // quarters
    hidden_load = copy(hidden_hbm, hidden_ref, hidden_sem)
    loads = [
        copy(
            weight_hbm.at[:, pl.ds((3 + part) * HW, HW)], weight_ref.at[part], weight_sem.at[part]
        )
        for part in range(3)
    ]
    hidden_load.start()
    loads[0].start()
    hidden_load.wait()
    stores = []
    for part in range(3):
        loads[part].wait()
        if part < 2:
            loads[part + 1].start()
        mapped = dot(hidden_ref[...], weight_ref[part]).astype(BF)
        for h in range(G):
            done = mapped[:, h * C : (h + 1) * C]
            if part < 2:
                one = done.astype(F32)
                one = one * inverse_rms(one)
                if part == 0:
                    one = one * (sharpness_ref[1, h] / C)
                done = one.astype(BF)
            for z in range(quarters):
                out_ref[part, z, h] = done[z * rows : (z + 1) * rows, :]
        stores.append(copy(out_ref.at[part], out_hbm.at[:, :, part], store_sem.at[part]))
        stores[-1].start()
    for store in stores:
        store.wait()


def temporal_entry(hidden, weight, sharpness, quarters, after):
    patches, depth = hidden.shape
    rows = patches // quarters
    return pl.pallas_call(
        functools.partial(temporal_entry_kernel, quarters),
        in_specs=[HBM, HBM, SCALARS] + [ANY] * len(after),
        out_specs=HBM,
        out_shape=hbm_out((quarters, G, 3, rows, C)),
        scratch_shapes=[
            pltpu.VMEM((patches, depth), BF),
            pltpu.VMEM((3, depth, HW), BF),
            pltpu.VMEM((3, quarters, G, rows, C), BF),
            DMA,
            DMA((3,)),
            DMA((3,)),
        ],
        compiler_params=params(),
        name="temporal_entry",
        cost_estimate=cost(
            6 * patches * depth * HW, 2 * patches * depth + 6 * depth * HW + 6 * patches * HW
        ),
    )(in_hbm(hidden), in_hbm(weight), sharpness, *after)


def temporal_attend_kernel(length_ref, in_hbm_ref, _, out_hbm, in_ref, out_ref, sem):
    frames, _, rows, _ = in_ref.shape
    group = 16
    size = frames * group
    load = copy(in_hbm_ref, in_ref, sem)
    load.start()
    length = length_ref[0]
    row = lax.broadcasted_iota(jnp.int32, (size, size), 0)
    column = lax.broadcasted_iota(jnp.int32, (size, size), 1)
    target, source = row // group, column // group
    keep = (row % group == column % group) & (source <= target) & (source > target - length)
    load.wait()
    for g in range(rows // group):
        at = slice(g * group, (g + 1) * group)
        query = in_ref[:, 0, at, :].reshape(size, C)
        key = in_ref[:, 1, at, :].reshape(size, C)
        value = in_ref[:, 2, at, :].reshape(size, C)
        weights = jnp.where(keep, jnp.exp(dot_t(query, key)), 0.0)
        shares = weights / jnp.sum(weights, axis=-1, keepdims=True)
        result = dot(shares.astype(BF), value).astype(BF)
        out_ref[:, at, :] = result.reshape(frames, group, C)
    store = copy(out_ref, out_hbm, sem)
    store.start()
    store.wait()


def temporal_attend(length, parts, after):
    frames, _, rows, _ = parts.shape
    shape = (frames, rows, C)
    return pl.pallas_call(
        temporal_attend_kernel,
        in_specs=[SCALARS, ANY, ANY],
        out_specs=HBM,
        out_shape=hbm_out(shape),
        scratch_shapes=[pltpu.VMEM(parts.shape, BF), pltpu.VMEM(shape, BF), DMA],
        compiler_params=params(),
        name="temporal_attend",
        cost_estimate=cost(4 * frames * rows * 256 * C, 8 * frames * rows * C),
    )(length, parts, in_hbm(after))


LINE = 96
CHUNK = 3 * LINE


def halves(denominators):
    high = denominators.astype(BF).astype(F32)
    return jnp.concatenate([high, denominators - high], axis=0).astype(BF)


def attend_rows(query, keys, both, out_ref):
    patches = out_ref.shape[0] - PAD
    row = lax.broadcasted_iota(jnp.int32, (LINE, C), 0)
    column = lax.broadcasted_iota(jnp.int32, (LINE, C), 1)
    lines = []
    for start in range(0, patches, CHUNK):
        at = slice(start, start + CHUNK)
        weights = jnp.exp(dot_t(query(at), keys)).astype(BF)
        result = dot(weights, both)
        out_ref[at, :] = result[:, :C].astype(BF)
        for j in range(0, CHUNK, LINE):
            diagonal = jnp.where(row == column, result[j : j + LINE, C:], 0.0)
            lines.append(jnp.sum(diagonal, axis=0, keepdims=True))
    lines.append(jnp.zeros((8 - len(lines), C), F32))
    out_ref[patches:, :] = halves(jnp.concatenate(lines, axis=0))


def with_ones(values):
    return jnp.concatenate([values, jnp.ones(values.shape, BF)], axis=1)


def own_attend_kernel(
    hidden_hbm, weight_hbm, query_hbm, *refs
):
    out_hbm, hidden_ref, weight_ref, query_ref, out_ref = refs[-9:-4]
    hidden_sem, weight_sem, query_sem, store_sem = refs[-4:]
    hidden_load = copy(hidden_hbm, hidden_ref, hidden_sem)
    query_load = copy(query_hbm.at[0], query_ref, query_sem)
    loads = [
        copy(
            weight_hbm.at[:, pl.ds((1 + part) * HW, HW)], weight_ref.at[part], weight_sem.at[part]
        )
        for part in range(2)
    ]
    hidden_load.start()
    loads[0].start()
    hidden_load.wait()
    loads[0].wait()
    loads[1].start()
    query_load.start()
    keys = dot(hidden_ref[...], weight_ref[0]).astype(BF)
    loads[1].wait()
    values = dot(hidden_ref[...], weight_ref[1]).astype(BF)
    query_load.wait()
    stores = []
    for h in range(G):
        key = keys[:, h * C : (h + 1) * C].astype(F32)
        key = (key * inverse_rms(key)).astype(BF)
        both = with_ones(values[:, h * C : (h + 1) * C])
        attend_rows(lambda at, h=h: query_ref[h, at, :], key, both, out_ref.at[h])
        stores.append(copy(out_ref.at[h], out_hbm.at[h], store_sem.at[h]))
        stores[-1].start()
    for store in stores:
        store.wait()


def own_attend(hidden, weight, query, after):
    patches, depth = hidden.shape
    shape = query.shape[1:]
    return pl.pallas_call(
        own_attend_kernel,
        in_specs=[HBM, HBM, HBM] + [ANY] * len(after),
        out_specs=HBM,
        out_shape=hbm_out(shape),
        scratch_shapes=[
            pltpu.VMEM((patches, depth), BF),
            pltpu.VMEM((2, depth, HW), BF),
            pltpu.VMEM(shape, BF),
            pltpu.VMEM(shape, BF),
            DMA,
            DMA((2,)),
            DMA,
            DMA((G,)),
        ],
        compiler_params=params(),
        name="own_attend",
        cost_estimate=cost(
            4 * patches * depth * HW + 6 * patches * patches * HW,
            2 * patches * depth + 4 * depth * HW + 10 * patches * HW,
        ),
    )(in_hbm(hidden), in_hbm(weight), in_hbm(query), *after)


def memory_attend_kernel(count, first, index_ref, query_hbm, *refs):
    blocks = refs[:count]
    out_hbm, query_ref, store_ref, out_ref, query_sem, block_sem, store_sem = refs[count + 1 :]
    frames = query_ref.shape[0]
    held = blocks[0].shape[0]
    query_load = copy(query_hbm, query_ref, query_sem)
    query_load.start()

    def fetch(t, carry):
        i, j = t // TOPM, lax.rem(t, TOPM)
        wanted = index_ref[first + i, j]
        for b in range(count // 2):

            @pl.when(wanted // held == b)
            def _(b=b):
                slot = lax.rem(wanted, held)
                for part in range(2):
                    block = blocks[2 * b + part].at[slot]
                    copy(block, store_ref.at[i, j, part], block_sem.at[i]).start()

        return carry

    lax.fori_loop(0, frames * TOPM, fetch, 0)
    query_load.wait()
    stores = []
    for i in range(frames):
        copy(store_ref.at[i], store_ref.at[i], block_sem.at[i]).wait()
        both = [store_ref[i, j, part] for j in range(TOPM) for part in range(2)]
        keys = jnp.concatenate([block[:, :C] for block in both], axis=0)
        values = jnp.concatenate([block[:, C:] for block in both], axis=0)
        attend_rows(
            lambda at, i=i: query_ref[i, at, :], keys, with_ones(values), out_ref.at[i]
        )
        stores.append(copy(out_ref.at[i], out_hbm.at[i], store_sem.at[i]))
        stores[-1].start()
    for store in stores:
        store.wait()


def memory_attend(first, index, query, blocks, after):
    count = len(blocks)
    frames, rows, _ = query.shape
    _, part, width = blocks[0].shape
    shape = (frames, rows, C)
    return pl.pallas_call(
        functools.partial(memory_attend_kernel, count, first),
        in_specs=[SCALARS] + [ANY] * (count + 2),
        out_specs=HBM,
        out_shape=hbm_out(shape),
        scratch_shapes=[
            pltpu.VMEM(shape, BF),
            pltpu.VMEM((frames, TOPM, 2, part, width), BF),
            pltpu.VMEM(shape, BF),
            DMA,
            DMA((frames,)),
            DMA((frames,)),
        ],
        compiler_params=params(),
        name="memory_attend",
        cost_estimate=cost(
            16 * frames * rows * TOPM * part * C,
            4 * frames * rows * C + 2 * frames * TOPM * part * width,
        ),
    )(index, query, *blocks, in_hbm(after))


def add_partials_kernel(count, x_ref, *refs):
    ins, outs = refs[:count], refs[count : count + G]
    parts_ref, out_ref, load_sem, store_sem = refs[count + G :]
    patches = out_ref.shape[1] - PAD
    loads = []
    for j in range(G):
        frame = lax.rem(x_ref[0] + j, G)
        loads.append(
            [copy(ref.at[frame], parts_ref.at[k, j], load_sem.at[k, j]) for k, ref in enumerate(ins)]
        )
    for of_frame in loads:
        for load in of_frame:
            load.start()
    stores = []
    for j in range(G):
        for load in loads[j]:
            load.wait()
        total = parts_ref[0, j].astype(F32)
        for k in range(1, count):
            total = total + parts_ref[k, j].astype(F32)
        out_ref[j, :patches, :] = total[:patches].astype(BF)
        out_ref[j, patches:, :] = halves(total[patches : patches + 8] + total[patches + 8 :])
        stores.append(copy(out_ref.at[j], outs[j], store_sem.at[j]))
        stores[-1].start()
    for store in stores:
        store.wait()


def add_partials(x, parts):
    shape = parts[0].shape
    return pl.pallas_call(
        functools.partial(add_partials_kernel, len(parts)),
        in_specs=[SCALARS] + [ANY] * len(parts),
        out_specs=[HBM] * G,
        out_shape=[hbm_out(shape[1:])] * G,
        scratch_shapes=[
            pltpu.VMEM((len(parts),) + shape, BF),
            pltpu.VMEM(shape, BF),
            DMA((len(parts), G)),
            DMA((G,)),
        ],
        compiler_params=params(),
        name="add_partials",
        cost_estimate=cost(4 * parts[0].size, 8 * parts[0].size),
    )(x, *parts)


def leave_kernel(
    x_ref, own_hbm, memory_0, memory_1, memory_2, memory_3, time_hbm, weight_hbm, out_hbm,
    own_ref, memory_ref, time_ref, combined_ref, weight_ref, out_ref,
    own_sem, memory_sem, time_sem, weight_sem, store_sem,
):
    patches = own_ref.shape[1] - PAD
    quarters = time_ref.shape[0] // G
    rows = time_ref.shape[1]
    steps, _, width = weight_ref.shape
    heads = [lax.rem(x_ref[0] + G - j, G) for j in range(G)]
    memories = (memory_0, memory_1, memory_2, memory_3)
    own_loads = [copy(own_hbm.at[heads[j]], own_ref.at[j], own_sem.at[j]) for j in range(G)]
    memory_loads = [copy(memories[j], memory_ref.at[j], memory_sem.at[j]) for j in range(G)]
    time_load = copy(time_hbm, time_ref, time_sem)
    loads, stores = [], []
    for i in range(steps):
        at = pl.ds(i * width, width)
        loads.append(copy(weight_hbm.at[:, at], weight_ref.at[i], weight_sem.at[i]))
        stores.append(copy(out_ref.at[i], out_hbm.at[:, at], store_sem.at[i]))
    for load in own_loads + memory_loads + [time_load] + loads:
        load.start()
    row = lax.broadcasted_iota(jnp.int32, (LINE, C), 0)
    column = lax.broadcasted_iota(jnp.int32, (LINE, C), 1)
    for h in range(G):
        own_loads[h].wait()
        memory_loads[h].wait()
        column_at = pl.ds(pl.multiple_of(heads[h] * C, C), C)
        tail = own_ref[h, patches:, :].astype(F32) + memory_ref[h, patches:, :].astype(F32)
        denominators = tail[:8] + tail[8:]
        for j in range(patches // LINE):
            at = slice(j * LINE, (j + 1) * LINE)
            line = jnp.broadcast_to(denominators[j : j + 1, :], (LINE, C))
            total = jnp.sum(jnp.where(row == column, line, 0.0), axis=1, keepdims=True)
            top = own_ref[h, at, :].astype(F32) + memory_ref[h, at, :].astype(F32)
            combined_ref[at, column_at] = (top / total).astype(BF)
    time_load.wait()
    for h in range(G):
        for z in range(quarters):
            combined_ref[z * rows : (z + 1) * rows, HW + h * C : HW + (h + 1) * C] = time_ref[
                z * G + h
            ]
    for i in range(steps):
        loads[i].wait()
        out_ref[i] = dot(combined_ref[...], weight_ref[i]).astype(BF)
        stores[i].start()
    for store in stores:
        store.wait()


def leave(x, own, memory, time, weight):
    patches = own.shape[1] - PAD
    depth, width = weight.shape
    steps = 4
    step = width // steps
    return pl.pallas_call(
        leave_kernel,
        in_specs=[SCALARS, HBM] + [ANY] * (G + 1) + [HBM],
        out_specs=HBM,
        out_shape=hbm_out((patches, width)),
        scratch_shapes=[
            pltpu.VMEM(own.shape, BF),
            pltpu.VMEM(own.shape, BF),
            pltpu.VMEM(time.shape, BF),
            pltpu.VMEM((patches, depth), BF),
            pltpu.VMEM((steps, depth, step), BF),
            pltpu.VMEM((steps, patches, step), BF),
            DMA((G,)),
            DMA((G,)),
            DMA,
            DMA((steps,)),
            DMA((steps,)),
        ],
        compiler_params=params(),
        name="leave",
        cost_estimate=cost(
            2 * patches * depth * width,
            2 * depth * width + 2 * patches * width + 6 * patches * depth,
        ),
    )(x, in_hbm(own), *memory, time, in_hbm(weight))


def on_device(
    patch_activation_tensor,
    conditioning_affine,
    entry_projection_matrix,
    exit_projection_matrix,
    softmax_sharpness,
    cached_past_pairs,
    recalled_picture_holder,
    recalled_picture_position,
    lookback_lengths,
):
    frame = ("zq", "zp", "x")
    rings, sides = lax.axis_size("y"), lax.axis_size("zq")
    quarters = lax.axis_size("zp") * sides
    patches, depth = patch_activation_tensor.shape[2:]
    held, piece = cached_past_pairs.shape[:2]
    cores = lax.axis_size("c")
    x = lax.axis_index("x").astype(jnp.int32).reshape(1)

    def turn(step):
        return [(s, (s + step) % rings) for s in range(rings)]

    def other(size):
        return [(s, size - 1 - s) for s in range(size)]

    def swap(blocks, axes):
        return lax.all_to_all(blocks, axes, split_axis=0, concat_axis=0, tiled=True)

    def swap_apart(blocks):
        return [in_hbm(blocks[0])] + [lax.ppermute(blocks[j], "x", turn(j)) for j in range(1, G)]

    with jax.named_scope("store"):
        split = split_store(cached_past_pairs.reshape(held * piece, 2 * HW), 1)
        pieces = swap(split[0], "x")

    with jax.named_scope("queries"):
        hidden, query = modulate(
            patch_activation_tensor.reshape(patches, depth),
            conditioning_affine.reshape(2, depth),
            entry_projection_matrix,
            softmax_sharpness,
            recalled_picture_holder.reshape(TOPM),
            recalled_picture_position.reshape(TOPM),
            held,
            1,
            after=split,
        )
        here = swap(query[0], "x")

    with jax.named_scope("store"):
        joined = join_pieces(pieces, held, after=hidden)
        above = lax.ppermute(joined, "y", turn(-1))
        below = lax.ppermute(joined, "y", turn(1))
        second = lax.ppermute(joined, "zp", other(sides))

        second_above = lax.ppermute(second, "y", turn(-1))
        second_below = lax.ppermute(second, "y", turn(1))

    with jax.named_scope("temporal"):
        parts = temporal_entry(
            hidden, entry_projection_matrix, softmax_sharpness, quarters, after=[in_hbm(joined)]
        )

    with jax.named_scope("queries"):
        here, *_ = lax.optimization_barrier((here, second, above, below, parts))
        beside = lax.ppermute(here, "zq", other(sides))

    with jax.named_scope("own"):
        own = own_attend(
            hidden, entry_projection_matrix, query, after=[in_hbm(parts), above]
        )

    with jax.named_scope("temporal"):
        sent, *_ = lax.optimization_barrier((parts, own, beside))
        sent = swap(sent.reshape((quarters * G,) + parts.shape[2:]), frame)

    with jax.named_scope("store"):
        below, second_above, second_below = lax.optimization_barrier(
            (below, second_above, second_below)
        )
        far = lax.ppermute(below, "y", turn(1))
        second_far = lax.ppermute(second_above, "y", turn(-1))
        near = [joined, second, above, second_above, far, second_far, below, second_below]
        blocks = near + [lax.ppermute(block, "c", other(cores)) for block in near]
        blocks = [in_hbm(block) for block in blocks]

    with jax.named_scope("queries"):
        named = jnp.concatenate([group[:, patches, :TOPM] for group in (beside, here)], axis=0)
        named = named.astype(jnp.int32)
        y = (named // (cores * held) - lax.axis_index("y")) & (rings - 1)
        c = (named // held & (cores - 1)) ^ lax.axis_index("c")
        index = (c * rings + y) * held + (named & (held - 1))

    with jax.named_scope("memory"):
        sum_beside = memory_attend(0, index, beside, blocks, own)
        from_beside = lax.ppermute(sum_beside, "zq", other(sides))

    with jax.named_scope("temporal"):
        timed = temporal_attend(lookback_lengths, sent, after=sum_beside)
        time = swap(timed, frame)

    with jax.named_scope("memory"):
        sum_here = memory_attend(beside.shape[0], index, here, blocks, timed)
        memory = swap_apart(add_partials(x, [in_hbm(sum_here), from_beside]))

    with jax.named_scope("exit"):
        attended = leave(x, own, memory, time, exit_projection_matrix)
    return attended.reshape(1, 1, patches, depth)


def solution(mesh):
    apart = Mesh(mesh.devices.reshape(4, 2, 2, 2, 4), ("y", "c", "zq", "zp", "x"))
    roll, frame = ("y", "c"), ("zq", "zp", "x")
    return jax.shard_map(
        on_device,
        mesh=apart,
        in_specs=(
            P(roll, frame, None, None),
            P(roll, frame, None, None),
            P(),
            P(),
            P(),
            P(roll, frame, None, None),
            P(roll, frame, None, None),
            P(roll, frame, None),
            P(roll),
        ),
        out_specs=P(roll, frame, None, None),
        check_vma=False,
    )
```

```python
import functools

import jax
import jax.numpy as jnp
from jax import lax
from jax.experimental import pallas as pl
from jax.experimental.pallas import tpu as pltpu
from jax.sharding import Mesh
from jax.sharding import PartitionSpec as P

G = 4
C = 128
HW = G * C
TOPM = 6
EPSILON = 1e-06
BF = jnp.bfloat16
F32 = jnp.float32
PAD = 16
VMEM_LIMIT = 28 * 1024 * 1024
ANY = pl.BlockSpec(memory_space=pl.ANY)
HBM = pl.BlockSpec(memory_space=pltpu.HBM)
WHOLE = pl.BlockSpec(memory_space=pltpu.VMEM)
SCALARS = pl.BlockSpec(memory_space=pltpu.SMEM)


def params(**more):
    return pltpu.CompilerParams(vmem_limit_bytes=VMEM_LIMIT, **more)


def cost(flops, bytes_accessed):
    return pl.CostEstimate(
        flops=flops // 16, bytes_accessed=bytes_accessed // 16, transcendentals=0
    )


def in_hbm(array):
    return pltpu.with_memory_space_constraint(array, pltpu.HBM)


def hbm_out(shape, dtype=BF):
    return pltpu.HBM(shape, dtype)


def inverse_rms(values):
    return lax.rsqrt(jnp.mean(values * values, axis=-1, keepdims=True) + EPSILON)


def dot(a, b):
    return jnp.dot(a, b, preferred_element_type=F32)


def dot_t(a, b):
    return lax.dot_general(a, b, (((1,), (1,)), ((), ())), preferred_element_type=F32)


DMA = pltpu.SemaphoreType.DMA
copy = pltpu.make_async_copy


def split_store_kernel(rows_ref, out_hbm, out_ref, sem):
    sends = []
    for h in range(G):
        key = rows_ref[:, h * C : (h + 1) * C].astype(F32)
        out_ref[h, :, :C] = (key * inverse_rms(key)).astype(BF)
        out_ref[h, :, C:] = rows_ref[:, HW + h * C : HW + (h + 1) * C]
        for k in range(out_hbm.shape[0]):
            sends.append(copy(out_ref.at[h], out_hbm.at[k, h], sem.at[k, h]))
            sends[-1].start()
    for send in sends:
        send.wait()


def split_store(rows, copies):
    n = rows.shape[0]
    return pl.pallas_call(
        split_store_kernel,
        in_specs=[WHOLE],
        out_specs=HBM,
        out_shape=hbm_out((copies, G, n, 2 * C)),
        scratch_shapes=[pltpu.VMEM((G, n, 2 * C), BF), DMA((copies, G))],
        compiler_params=params(),
        name="split_store",
        cost_estimate=cost(8 * n * HW, 8 * n * HW),
    )(rows)


def join_pieces_kernel(piece, in_hbm, _, out_hbm, in_ref, wide_ref, joined_ref, out_ref, sem):
    pieces = in_ref.shape[0]
    loads = [copy(in_hbm.at[i], in_ref.at[i], sem.at[i]) for i in range(pieces)]
    for load in loads:
        load.start()
    for i in range(pieces):
        loads[i].wait()
        wide_ref[i] = in_ref[i].astype(F32)
        for m in range(out_ref.shape[0]):
            joined_ref[m, i * piece : (i + 1) * piece, :] = wide_ref[
                i, m * piece : (m + 1) * piece, :
            ]
    out_ref[...] = joined_ref[...].astype(BF)
    send = copy(out_ref, out_hbm, sem.at[0])
    send.start()
    send.wait()


def join_pieces(parts, frames, after):
    pieces, rows, width = parts.shape
    piece = rows // frames
    shape = (frames, pieces * piece, width)
    return pl.pallas_call(
        functools.partial(join_pieces_kernel, piece),
        in_specs=[ANY, ANY],
        out_specs=HBM,
        out_shape=hbm_out(shape),
        scratch_shapes=[
            pltpu.VMEM(parts.shape, BF),
            pltpu.VMEM(parts.shape, F32),
            pltpu.VMEM(shape, F32),
            pltpu.VMEM(shape, BF),
            DMA((pieces,)),
        ],
        compiler_params=params(),
        name="join_pieces",
        cost_estimate=cost(parts.size, 4 * parts.size),
    )(parts, in_hbm(after))


def modulate_kernel(
    held,
    act_hbm, affine_hbm, weight_hbm, sharpness_ref, owner_ref, slot_ref, _, hidden_hbm, query_hbm,
    act_ref, affine_ref, weight_ref, hidden_ref, query_ref,
    load_sem, affine_sem, weight_sem, store_sem, query_sem,
):
    steps, rows, _ = act_ref.shape
    patches = query_ref.shape[1] - PAD
    loads, stores = [], []
    for i in range(steps):
        at = pl.ds(i * rows, rows)
        loads.append(copy(act_hbm.at[at, :], act_ref.at[i], load_sem.at[i]))
        stores.append(copy(hidden_ref.at[i], hidden_hbm.at[at, :], store_sem.at[i]))
    weight_load = copy(weight_hbm.at[:, pl.ds(0, HW)], weight_ref, weight_sem)
    affine_load = copy(affine_hbm, affine_ref, affine_sem)
    affine_load.start()
    loads[0].start()
    weight_load.start()
    row = lax.broadcasted_iota(jnp.int32, (PAD, C), 0)
    column = lax.broadcasted_iota(jnp.int32, (PAD, C), 1)
    tail = jnp.zeros((PAD, C), jnp.int32)
    for j in range(TOPM):
        tail = jnp.where((row == 0) & (column == j), owner_ref[j] * held + slot_ref[j], tail)
    for h in range(G):
        query_ref[h, patches:, :] = tail.astype(F32).astype(BF)
    affine_load.wait()
    for i in range(steps):
        at = slice(i * rows, (i + 1) * rows)
        loads[i].wait()
        if i + 1 < steps:
            loads[i + 1].start()
        act = act_ref[i].astype(F32)
        hidden = act * inverse_rms(act) * (1.0 + affine_ref[0:1, :]) + affine_ref[1:2, :]
        hidden = hidden.astype(BF)
        hidden_ref[i] = hidden
        stores[i].start()
        if i == 0:
            weight_load.wait()
        mapped = dot(hidden, weight_ref[...]).astype(BF).astype(F32)
        for h in range(G):
            one = mapped[:, h * C : (h + 1) * C]
            query_ref[h, at, :] = (
                one * inverse_rms(one) * (sharpness_ref[0, h] / C)
            ).astype(BF)
    sends = [
        copy(query_ref, query_hbm.at[k], query_sem.at[k]) for k in range(query_hbm.shape[0])
    ]
    for send in sends:
        send.start()
    for store in stores + sends:
        store.wait()


def modulate(act, affine, weight, sharpness, owner, slot, held, copies, after):
    patches, depth = act.shape
    steps = 2
    rows = patches // steps
    shape = (G, patches + PAD, C)
    return pl.pallas_call(
        functools.partial(modulate_kernel, held),
        in_specs=[HBM, HBM, HBM, SCALARS, SCALARS, SCALARS, ANY],
        out_specs=[HBM, HBM],
        out_shape=[hbm_out((patches, depth)), hbm_out((copies,) + shape)],
        scratch_shapes=[
            pltpu.VMEM((steps, rows, depth), BF),
            pltpu.VMEM(affine.shape, F32),
            pltpu.VMEM((depth, HW), BF),
            pltpu.VMEM((steps, rows, depth), BF),
            pltpu.VMEM(shape, BF),
            DMA((steps,)),
            DMA,
            DMA,
            DMA((steps,)),
            DMA((copies,)),
        ],
        compiler_params=params(),
        name="modulate",
        cost_estimate=cost(
            2 * patches * depth * HW, 4 * patches * depth + 2 * depth * HW + 2 * patches * HW
        ),
    )(in_hbm(act), in_hbm(affine), in_hbm(weight), sharpness, owner, slot, in_hbm(after))


def temporal_entry_kernel(
    quarters, hidden_hbm, weight_hbm, sharpness_ref, *refs
):
    out_hbm, hidden_ref, weight_ref, out_ref, hidden_sem, weight_sem, store_sem = refs[-7:]
    rows = hidden_ref.shape[0] // quarters
    hidden_load = copy(hidden_hbm, hidden_ref, hidden_sem)
    loads = [
        copy(
            weight_hbm.at[:, pl.ds((3 + part) * HW, HW)], weight_ref.at[part], weight_sem.at[part]
        )
        for part in range(3)
    ]
    hidden_load.start()
    loads[0].start()
    hidden_load.wait()
    stores = []
    for part in range(3):
        loads[part].wait()
        if part < 2:
            loads[part + 1].start()
        mapped = dot(hidden_ref[...], weight_ref[part]).astype(BF)
        for h in range(G):
            done = mapped[:, h * C : (h + 1) * C]
            if part < 2:
                one = done.astype(F32)
                one = one * inverse_rms(one)
                if part == 0:
                    one = one * (sharpness_ref[1, h] / C)
                done = one.astype(BF)
            for z in range(quarters):
                out_ref[part, z, h] = done[z * rows : (z + 1) * rows, :]
        stores.append(copy(out_ref.at[part], out_hbm.at[:, :, part], store_sem.at[part]))
        stores[-1].start()
    for store in stores:
        store.wait()


def temporal_entry(hidden, weight, sharpness, quarters, after):
    patches, depth = hidden.shape
    rows = patches // quarters
    return pl.pallas_call(
        functools.partial(temporal_entry_kernel, quarters),
        in_specs=[HBM, HBM, SCALARS] + [ANY] * len(after),
        out_specs=HBM,
        out_shape=hbm_out((quarters, G, 3, rows, C)),
        scratch_shapes=[
            pltpu.VMEM((patches, depth), BF),
            pltpu.VMEM((3, depth, HW), BF),
            pltpu.VMEM((3, quarters, G, rows, C), BF),
            DMA,
            DMA((3,)),
            DMA((3,)),
        ],
        compiler_params=params(),
        name="temporal_entry",
        cost_estimate=cost(
            6 * patches * depth * HW, 2 * patches * depth + 6 * depth * HW + 6 * patches * HW
        ),
    )(in_hbm(hidden), in_hbm(weight), sharpness, *after)


def temporal_attend_kernel(length_ref, in_hbm_ref, _, out_hbm, in_ref, out_ref, sem):
    frames, _, rows, _ = in_ref.shape
    group = 16
    size = frames * group
    load = copy(in_hbm_ref, in_ref, sem)
    load.start()
    length = length_ref[0]
    row = lax.broadcasted_iota(jnp.int32, (size, size), 0)
    column = lax.broadcasted_iota(jnp.int32, (size, size), 1)
    target, source = row // group, column // group
    keep = (row % group == column % group) & (source <= target) & (source > target - length)
    load.wait()
    for g in range(rows // group):
        at = slice(g * group, (g + 1) * group)
        query = in_ref[:, 0, at, :].reshape(size, C)
        key = in_ref[:, 1, at, :].reshape(size, C)
        value = in_ref[:, 2, at, :].reshape(size, C)
        weights = jnp.where(keep, jnp.exp(dot_t(query, key)), 0.0)
        shares = weights / jnp.sum(weights, axis=-1, keepdims=True)
        result = dot(shares.astype(BF), value).astype(BF)
        out_ref[:, at, :] = result.reshape(frames, group, C)
    store = copy(out_ref, out_hbm, sem)
    store.start()
    store.wait()


def temporal_attend(length, parts, after):
    frames, _, rows, _ = parts.shape
    shape = (frames, rows, C)
    return pl.pallas_call(
        temporal_attend_kernel,
        in_specs=[SCALARS, ANY, ANY],
        out_specs=HBM,
        out_shape=hbm_out(shape),
        scratch_shapes=[pltpu.VMEM(parts.shape, BF), pltpu.VMEM(shape, BF), DMA],
        compiler_params=params(),
        name="temporal_attend",
        cost_estimate=cost(4 * frames * rows * 256 * C, 8 * frames * rows * C),
    )(length, parts, in_hbm(after))


LINE = 96
CHUNK = 3 * LINE


def halves(denominators):
    high = denominators.astype(BF).astype(F32)
    return jnp.concatenate([high, denominators - high], axis=0).astype(BF)


def attend_rows(query, keys, both, out_ref):
    patches = out_ref.shape[0] - PAD
    row = lax.broadcasted_iota(jnp.int32, (LINE, C), 0)
    column = lax.broadcasted_iota(jnp.int32, (LINE, C), 1)
    lines = []
    for start in range(0, patches, CHUNK):
        at = slice(start, start + CHUNK)
        weights = jnp.exp(dot_t(query(at), keys)).astype(BF)
        result = dot(weights, both)
        out_ref[at, :] = result[:, :C].astype(BF)
        for j in range(0, CHUNK, LINE):
            diagonal = jnp.where(row == column, result[j : j + LINE, C:], 0.0)
            lines.append(jnp.sum(diagonal, axis=0, keepdims=True))
    lines.append(jnp.zeros((8 - len(lines), C), F32))
    out_ref[patches:, :] = halves(jnp.concatenate(lines, axis=0))


def with_ones(values):
    return jnp.concatenate([values, jnp.ones(values.shape, BF)], axis=1)


def own_attend_kernel(
    hidden_hbm, weight_hbm, query_hbm, *refs
):
    out_hbm, hidden_ref, weight_ref, query_ref, out_ref = refs[-9:-4]
    hidden_sem, weight_sem, query_sem, store_sem = refs[-4:]
    hidden_load = copy(hidden_hbm, hidden_ref, hidden_sem)
    query_load = copy(query_hbm.at[0], query_ref, query_sem)
    loads = [
        copy(
            weight_hbm.at[:, pl.ds((1 + part) * HW, HW)], weight_ref.at[part], weight_sem.at[part]
        )
        for part in range(2)
    ]
    hidden_load.start()
    loads[0].start()
    hidden_load.wait()
    loads[0].wait()
    loads[1].start()
    query_load.start()
    keys = dot(hidden_ref[...], weight_ref[0]).astype(BF)
    loads[1].wait()
    values = dot(hidden_ref[...], weight_ref[1]).astype(BF)
    query_load.wait()
    stores = []
    for h in range(G):
        key = keys[:, h * C : (h + 1) * C].astype(F32)
        key = (key * inverse_rms(key)).astype(BF)
        both = with_ones(values[:, h * C : (h + 1) * C])
        attend_rows(lambda at, h=h: query_ref[h, at, :], key, both, out_ref.at[h])
        stores.append(copy(out_ref.at[h], out_hbm.at[h], store_sem.at[h]))
        stores[-1].start()
    for store in stores:
        store.wait()


def own_attend(hidden, weight, query, after):
    patches, depth = hidden.shape
    shape = query.shape[1:]
    return pl.pallas_call(
        own_attend_kernel,
        in_specs=[HBM, HBM, HBM] + [ANY] * len(after),
        out_specs=HBM,
        out_shape=hbm_out(shape),
        scratch_shapes=[
            pltpu.VMEM((patches, depth), BF),
            pltpu.VMEM((2, depth, HW), BF),
            pltpu.VMEM(shape, BF),
            pltpu.VMEM(shape, BF),
            DMA,
            DMA((2,)),
            DMA,
            DMA((G,)),
        ],
        compiler_params=params(),
        name="own_attend",
        cost_estimate=cost(
            4 * patches * depth * HW + 6 * patches * patches * HW,
            2 * patches * depth + 4 * depth * HW + 10 * patches * HW,
        ),
    )(in_hbm(hidden), in_hbm(weight), in_hbm(query), *after)


def memory_attend_kernel(count, first, index_ref, query_hbm, *refs):
    blocks = refs[:count]
    out_hbm, query_ref, store_ref, out_ref, query_sem, block_sem, store_sem = refs[count + 1 :]
    frames = query_ref.shape[0]
    held = blocks[0].shape[0]
    query_load = copy(query_hbm, query_ref, query_sem)
    query_load.start()

    def fetch(t, carry):
        i, j = t // TOPM, lax.rem(t, TOPM)
        wanted = index_ref[first + i, j]
        for b in range(count // 2):

            @pl.when(wanted // held == b)
            def _(b=b):
                slot = lax.rem(wanted, held)
                for part in range(2):
                    block = blocks[2 * b + part].at[slot]
                    copy(block, store_ref.at[i, j, part], block_sem.at[i]).start()

        return carry

    lax.fori_loop(0, frames * TOPM, fetch, 0)
    query_load.wait()
    stores = []
    for i in range(frames):
        copy(store_ref.at[i], store_ref.at[i], block_sem.at[i]).wait()
        both = [store_ref[i, j, part] for j in range(TOPM) for part in range(2)]
        keys = jnp.concatenate([block[:, :C] for block in both], axis=0)
        values = jnp.concatenate([block[:, C:] for block in both], axis=0)
        attend_rows(
            lambda at, i=i: query_ref[i, at, :], keys, with_ones(values), out_ref.at[i]
        )
        stores.append(copy(out_ref.at[i], out_hbm.at[i], store_sem.at[i]))
        stores[-1].start()
    for store in stores:
        store.wait()


def memory_attend(first, index, query, blocks, after):
    count = len(blocks)
    frames, rows, _ = query.shape
    _, part, width = blocks[0].shape
    shape = (frames, rows, C)
    return pl.pallas_call(
        functools.partial(memory_attend_kernel, count, first),
        in_specs=[SCALARS] + [ANY] * (count + 2),
        out_specs=HBM,
        out_shape=hbm_out(shape),
        scratch_shapes=[
            pltpu.VMEM(shape, BF),
            pltpu.VMEM((frames, TOPM, 2, part, width), BF),
            pltpu.VMEM(shape, BF),
            DMA,
            DMA((frames,)),
            DMA((frames,)),
        ],
        compiler_params=params(),
        name="memory_attend",
        cost_estimate=cost(
            16 * frames * rows * TOPM * part * C,
            4 * frames * rows * C + 2 * frames * TOPM * part * width,
        ),
    )(index, query, *blocks, in_hbm(after))


def add_partials_kernel(count, x_ref, *refs):
    ins, outs = refs[:count], refs[count : count + G]
    parts_ref, out_ref, load_sem, store_sem = refs[count + G :]
    patches = out_ref.shape[1] - PAD
    loads = []
    for j in range(G):
        frame = lax.rem(x_ref[0] + j, G)
        loads.append(
            [copy(ref.at[frame], parts_ref.at[k, j], load_sem.at[k, j]) for k, ref in enumerate(ins)]
        )
    for of_frame in loads:
        for load in of_frame:
            load.start()
    stores = []
    for j in range(G):
        for load in loads[j]:
            load.wait()
        total = parts_ref[0, j].astype(F32)
        for k in range(1, count):
            total = total + parts_ref[k, j].astype(F32)
        out_ref[j, :patches, :] = total[:patches].astype(BF)
        out_ref[j, patches:, :] = halves(total[patches : patches + 8] + total[patches + 8 :])
        stores.append(copy(out_ref.at[j], outs[j], store_sem.at[j]))
        stores[-1].start()
    for store in stores:
        store.wait()


def add_partials(x, parts):
    shape = parts[0].shape
    return pl.pallas_call(
        functools.partial(add_partials_kernel, len(parts)),
        in_specs=[SCALARS] + [ANY] * len(parts),
        out_specs=[HBM] * G,
        out_shape=[hbm_out(shape[1:])] * G,
        scratch_shapes=[
            pltpu.VMEM((len(parts),) + shape, BF),
            pltpu.VMEM(shape, BF),
            DMA((len(parts), G)),
            DMA((G,)),
        ],
        compiler_params=params(),
        name="add_partials",
        cost_estimate=cost(4 * parts[0].size, 8 * parts[0].size),
    )(x, *parts)


def leave_kernel(
    x_ref, own_hbm, memory_0, memory_1, memory_2, memory_3, time_hbm, weight_hbm, out_hbm,
    own_ref, memory_ref, time_ref, combined_ref, weight_ref, out_ref,
    own_sem, memory_sem, time_sem, weight_sem, store_sem,
):
    patches = own_ref.shape[1] - PAD
    quarters = time_ref.shape[0] // G
    rows = time_ref.shape[1]
    steps, _, width = weight_ref.shape
    heads = [lax.rem(x_ref[0] + G - j, G) for j in range(G)]
    memories = (memory_0, memory_1, memory_2, memory_3)
    own_loads = [copy(own_hbm.at[heads[j]], own_ref.at[j], own_sem.at[j]) for j in range(G)]
    memory_loads = [copy(memories[j], memory_ref.at[j], memory_sem.at[j]) for j in range(G)]
    time_load = copy(time_hbm, time_ref, time_sem)
    loads, stores = [], []
    for i in range(steps):
        at = pl.ds(i * width, width)
        loads.append(copy(weight_hbm.at[:, at], weight_ref.at[i], weight_sem.at[i]))
        stores.append(copy(out_ref.at[i], out_hbm.at[:, at], store_sem.at[i]))
    for load in own_loads + memory_loads + [time_load] + loads:
        load.start()
    row = lax.broadcasted_iota(jnp.int32, (LINE, C), 0)
    column = lax.broadcasted_iota(jnp.int32, (LINE, C), 1)
    for h in range(G):
        own_loads[h].wait()
        memory_loads[h].wait()
        column_at = pl.ds(pl.multiple_of(heads[h] * C, C), C)
        tail = own_ref[h, patches:, :].astype(F32) + memory_ref[h, patches:, :].astype(F32)
        denominators = tail[:8] + tail[8:]
        for j in range(patches // LINE):
            at = slice(j * LINE, (j + 1) * LINE)
            line = jnp.broadcast_to(denominators[j : j + 1, :], (LINE, C))
            total = jnp.sum(jnp.where(row == column, line, 0.0), axis=1, keepdims=True)
            top = own_ref[h, at, :].astype(F32) + memory_ref[h, at, :].astype(F32)
            combined_ref[at, column_at] = (top / total).astype(BF)
    time_load.wait()
    for h in range(G):
        for z in range(quarters):
            combined_ref[z * rows : (z + 1) * rows, HW + h * C : HW + (h + 1) * C] = time_ref[
                z * G + h
            ]
    for i in range(steps):
        loads[i].wait()
        out_ref[i] = dot(combined_ref[...], weight_ref[i]).astype(BF)
        stores[i].start()
    for store in stores:
        store.wait()


def leave(x, own, memory, time, weight):
    patches = own.shape[1] - PAD
    depth, width = weight.shape
    steps = 4
    step = width // steps
    return pl.pallas_call(
        leave_kernel,
        in_specs=[SCALARS, HBM] + [ANY] * (G + 1) + [HBM],
        out_specs=HBM,
        out_shape=hbm_out((patches, width)),
        scratch_shapes=[
            pltpu.VMEM(own.shape, BF),
            pltpu.VMEM(own.shape, BF),
            pltpu.VMEM(time.shape, BF),
            pltpu.VMEM((patches, depth), BF),
            pltpu.VMEM((steps, depth, step), BF),
            pltpu.VMEM((steps, patches, step), BF),
            DMA((G,)),
            DMA((G,)),
            DMA,
            DMA((steps,)),
            DMA((steps,)),
        ],
        compiler_params=params(),
        name="leave",
        cost_estimate=cost(
            2 * patches * depth * width,
            2 * depth * width + 2 * patches * width + 6 * patches * depth,
        ),
    )(x, in_hbm(own), *memory, time, in_hbm(weight))


def on_device(
    patch_activation_tensor,
    conditioning_affine,
    entry_projection_matrix,
    exit_projection_matrix,
    softmax_sharpness,
    cached_past_pairs,
    recalled_picture_holder,
    recalled_picture_position,
    lookback_lengths,
):
    frame = ("zq", "zp", "x")
    rings, sides = lax.axis_size("y"), lax.axis_size("zq")
    quarters = lax.axis_size("zp") * sides
    patches, depth = patch_activation_tensor.shape[2:]
    held, piece = cached_past_pairs.shape[:2]
    cores = lax.axis_size("c")
    x = lax.axis_index("x").astype(jnp.int32).reshape(1)

    def turn(step):
        return [(s, (s + step) % rings) for s in range(rings)]

    def other(size):
        return [(s, size - 1 - s) for s in range(size)]

    def swap(blocks, axes):
        return lax.all_to_all(blocks, axes, split_axis=0, concat_axis=0, tiled=True)

    def swap_apart(blocks):
        return [in_hbm(blocks[0])] + [lax.ppermute(blocks[j], "x", turn(j)) for j in range(1, G)]

    with jax.named_scope("store"):
        split = split_store(cached_past_pairs.reshape(held * piece, 2 * HW), 1)
        pieces = swap(split[0], "x")

    with jax.named_scope("queries"):
        hidden, query = modulate(
            patch_activation_tensor.reshape(patches, depth),
            conditioning_affine.reshape(2, depth),
            entry_projection_matrix,
            softmax_sharpness,
            recalled_picture_holder.reshape(TOPM),
            recalled_picture_position.reshape(TOPM),
            held,
            1,
            after=split,
        )
        here = swap(query[0], "x")

    with jax.named_scope("store"):
        joined = join_pieces(pieces, held, after=hidden)
        above = lax.ppermute(joined, "y", turn(-1))
        below = lax.ppermute(joined, "y", turn(1))
        second = lax.ppermute(joined, "zp", other(sides))

        second_above = lax.ppermute(second, "y", turn(-1))
        second_below = lax.ppermute(second, "y", turn(1))

    with jax.named_scope("temporal"):
        parts = temporal_entry(
            hidden, entry_projection_matrix, softmax_sharpness, quarters, after=[in_hbm(joined)]
        )

    with jax.named_scope("queries"):
        here, *_ = lax.optimization_barrier((here, second, above, below, parts))
        beside = lax.ppermute(here, "zq", other(sides))

    with jax.named_scope("own"):
        own = own_attend(
            hidden,
            entry_projection_matrix,
            query,
            after=[in_hbm(parts), second_above, second_below],
        )

    with jax.named_scope("temporal"):
        sent, *_ = lax.optimization_barrier((parts, beside, second_above, second_below))
        sent = swap(sent.reshape((quarters * G,) + parts.shape[2:]), frame)

    with jax.named_scope("store"):
        below, second_above, second_below = lax.optimization_barrier(
            (below, second_above, second_below)
        )
        far = lax.ppermute(below, "y", turn(1))
        second_far = lax.ppermute(second_above, "y", turn(-1))
        near = [joined, second, above, second_above, far, second_far, below, second_below]
        blocks = near + [lax.ppermute(block, "c", other(cores)) for block in near]
        blocks = [in_hbm(block) for block in blocks]

    with jax.named_scope("queries"):
        named = jnp.concatenate([group[:, patches, :TOPM] for group in (beside, here)], axis=0)
        named = named.astype(jnp.int32)
        y = (named // (cores * held) - lax.axis_index("y")) & (rings - 1)
        c = (named // held & (cores - 1)) ^ lax.axis_index("c")
        index = (c * rings + y) * held + (named & (held - 1))

    with jax.named_scope("memory"):
        sum_beside = memory_attend(0, index, beside, blocks, own)
        from_beside = lax.ppermute(sum_beside, "zq", other(sides))
        sum_here = memory_attend(beside.shape[0], index, here, blocks, sum_beside)

    with jax.named_scope("temporal"):
        timed = temporal_attend(lookback_lengths, sent, after=sum_here)
        time = swap(timed, frame)

    with jax.named_scope("memory"):
        memory = swap_apart(add_partials(x, [in_hbm(sum_here), from_beside]))

    with jax.named_scope("exit"):
        attended = leave(x, own, memory, time, exit_projection_matrix)
    return attended.reshape(1, 1, patches, depth)


def solution(mesh):
    apart = Mesh(mesh.devices.reshape(4, 2, 2, 2, 4), ("y", "c", "zq", "zp", "x"))
    roll, frame = ("y", "c"), ("zq", "zp", "x")
    return jax.shard_map(
        on_device,
        mesh=apart,
        in_specs=(
            P(roll, frame, None, None),
            P(roll, frame, None, None),
            P(),
            P(),
            P(),
            P(roll, frame, None, None),
            P(roll, frame, None, None),
            P(roll, frame, None),
            P(roll),
        ),
        out_specs=P(roll, frame, None, None),
        check_vma=False,
    )
```

```python
import functools

import jax
import jax.numpy as jnp
from jax import lax
from jax.experimental import pallas as pl
from jax.experimental.pallas import tpu as pltpu
from jax.sharding import Mesh
from jax.sharding import PartitionSpec as P

G = 4
C = 128
HW = G * C
TOPM = 6
EPSILON = 1e-06
BF = jnp.bfloat16
F32 = jnp.float32
PAD = 16
VMEM_LIMIT = 28 * 1024 * 1024
ANY = pl.BlockSpec(memory_space=pl.ANY)
HBM = pl.BlockSpec(memory_space=pltpu.HBM)
WHOLE = pl.BlockSpec(memory_space=pltpu.VMEM)
SCALARS = pl.BlockSpec(memory_space=pltpu.SMEM)


def params(**more):
    return pltpu.CompilerParams(vmem_limit_bytes=VMEM_LIMIT, **more)


def cost(flops, bytes_accessed):
    return pl.CostEstimate(
        flops=flops // 16, bytes_accessed=bytes_accessed // 16, transcendentals=0
    )


def in_hbm(array):
    return pltpu.with_memory_space_constraint(array, pltpu.HBM)


def hbm_out(shape, dtype=BF):
    return pltpu.HBM(shape, dtype)


def inverse_rms(values):
    return lax.rsqrt(jnp.mean(values * values, axis=-1, keepdims=True) + EPSILON)


def dot(a, b):
    return jnp.dot(a, b, preferred_element_type=F32)


def dot_t(a, b):
    return lax.dot_general(a, b, (((1,), (1,)), ((), ())), preferred_element_type=F32)


DMA = pltpu.SemaphoreType.DMA
copy = pltpu.make_async_copy


def split_store_kernel(rows_ref, out_hbm, out_ref, sem):
    sends = []
    for h in range(G):
        key = rows_ref[:, h * C : (h + 1) * C].astype(F32)
        out_ref[h, :, :C] = (key * inverse_rms(key)).astype(BF)
        out_ref[h, :, C:] = rows_ref[:, HW + h * C : HW + (h + 1) * C]
        for k in range(out_hbm.shape[0]):
            sends.append(copy(out_ref.at[h], out_hbm.at[k, h], sem.at[k, h]))
            sends[-1].start()
    for send in sends:
        send.wait()


def split_store(rows, copies):
    n = rows.shape[0]
    return pl.pallas_call(
        split_store_kernel,
        in_specs=[WHOLE],
        out_specs=HBM,
        out_shape=hbm_out((copies, G, n, 2 * C)),
        scratch_shapes=[pltpu.VMEM((G, n, 2 * C), BF), DMA((copies, G))],
        compiler_params=params(),
        name="split_store",
        cost_estimate=cost(8 * n * HW, 8 * n * HW),
    )(rows)


def join_pieces_kernel(piece, in_hbm, _, out_hbm, in_ref, wide_ref, joined_ref, out_ref, sem):
    pieces = in_ref.shape[0]
    loads = [copy(in_hbm.at[i], in_ref.at[i], sem.at[i]) for i in range(pieces)]
    for load in loads:
        load.start()
    for i in range(pieces):
        loads[i].wait()
        wide_ref[i] = in_ref[i].astype(F32)
        for m in range(out_ref.shape[0]):
            joined_ref[m, i * piece : (i + 1) * piece, :] = wide_ref[
                i, m * piece : (m + 1) * piece, :
            ]
    out_ref[...] = joined_ref[...].astype(BF)
    send = copy(out_ref, out_hbm, sem.at[0])
    send.start()
    send.wait()


def join_pieces(parts, frames, after):
    pieces, rows, width = parts.shape
    piece = rows // frames
    shape = (frames, pieces * piece, width)
    return pl.pallas_call(
        functools.partial(join_pieces_kernel, piece),
        in_specs=[ANY, ANY],
        out_specs=HBM,
        out_shape=hbm_out(shape),
        scratch_shapes=[
            pltpu.VMEM(parts.shape, BF),
            pltpu.VMEM(parts.shape, F32),
            pltpu.VMEM(shape, F32),
            pltpu.VMEM(shape, BF),
            DMA((pieces,)),
        ],
        compiler_params=params(),
        name="join_pieces",
        cost_estimate=cost(parts.size, 4 * parts.size),
    )(parts, in_hbm(after))


def modulate_kernel(
    held,
    act_hbm, affine_hbm, weight_hbm, sharpness_ref, owner_ref, slot_ref, _, hidden_hbm, query_hbm,
    act_ref, affine_ref, weight_ref, hidden_ref, query_ref,
    load_sem, affine_sem, weight_sem, store_sem, query_sem,
):
    steps, rows, _ = act_ref.shape
    patches = query_ref.shape[1] - PAD
    loads, stores = [], []
    for i in range(steps):
        at = pl.ds(i * rows, rows)
        loads.append(copy(act_hbm.at[at, :], act_ref.at[i], load_sem.at[i]))
        stores.append(copy(hidden_ref.at[i], hidden_hbm.at[at, :], store_sem.at[i]))
    weight_load = copy(weight_hbm.at[:, pl.ds(0, HW)], weight_ref, weight_sem)
    affine_load = copy(affine_hbm, affine_ref, affine_sem)
    affine_load.start()
    loads[0].start()
    weight_load.start()
    row = lax.broadcasted_iota(jnp.int32, (PAD, C), 0)
    column = lax.broadcasted_iota(jnp.int32, (PAD, C), 1)
    tail = jnp.zeros((PAD, C), jnp.int32)
    for j in range(TOPM):
        tail = jnp.where((row == 0) & (column == j), owner_ref[j] * held + slot_ref[j], tail)
    for h in range(G):
        query_ref[h, patches:, :] = tail.astype(F32).astype(BF)
    affine_load.wait()
    for i in range(steps):
        at = slice(i * rows, (i + 1) * rows)
        loads[i].wait()
        if i + 1 < steps:
            loads[i + 1].start()
        act = act_ref[i].astype(F32)
        hidden = act * inverse_rms(act) * (1.0 + affine_ref[0:1, :]) + affine_ref[1:2, :]
        hidden = hidden.astype(BF)
        hidden_ref[i] = hidden
        stores[i].start()
        if i == 0:
            weight_load.wait()
        mapped = dot(hidden, weight_ref[...]).astype(BF).astype(F32)
        for h in range(G):
            one = mapped[:, h * C : (h + 1) * C]
            query_ref[h, at, :] = (
                one * inverse_rms(one) * (sharpness_ref[0, h] / C)
            ).astype(BF)
    sends = [
        copy(query_ref, query_hbm.at[k], query_sem.at[k]) for k in range(query_hbm.shape[0])
    ]
    for send in sends:
        send.start()
    for store in stores + sends:
        store.wait()


def modulate(act, affine, weight, sharpness, owner, slot, held, copies, after):
    patches, depth = act.shape
    steps = 2
    rows = patches // steps
    shape = (G, patches + PAD, C)
    return pl.pallas_call(
        functools.partial(modulate_kernel, held),
        in_specs=[HBM, HBM, HBM, SCALARS, SCALARS, SCALARS, ANY],
        out_specs=[HBM, HBM],
        out_shape=[hbm_out((patches, depth)), hbm_out((copies,) + shape)],
        scratch_shapes=[
            pltpu.VMEM((steps, rows, depth), BF),
            pltpu.VMEM(affine.shape, F32),
            pltpu.VMEM((depth, HW), BF),
            pltpu.VMEM((steps, rows, depth), BF),
            pltpu.VMEM(shape, BF),
            DMA((steps,)),
            DMA,
            DMA,
            DMA((steps,)),
            DMA((copies,)),
        ],
        compiler_params=params(),
        name="modulate",
        cost_estimate=cost(
            2 * patches * depth * HW, 4 * patches * depth + 2 * depth * HW + 2 * patches * HW
        ),
    )(in_hbm(act), in_hbm(affine), in_hbm(weight), sharpness, owner, slot, in_hbm(after))


def temporal_entry_kernel(
    quarters, hidden_hbm, weight_hbm, sharpness_ref, *refs
):
    out_hbm, hidden_ref, weight_ref, out_ref, hidden_sem, weight_sem, store_sem = refs[-7:]
    rows = hidden_ref.shape[0] // quarters
    hidden_load = copy(hidden_hbm, hidden_ref, hidden_sem)
    loads = [
        copy(
            weight_hbm.at[:, pl.ds((3 + part) * HW, HW)], weight_ref.at[part], weight_sem.at[part]
        )
        for part in range(3)
    ]
    hidden_load.start()
    loads[0].start()
    hidden_load.wait()
    stores = []
    for part in range(3):
        loads[part].wait()
        if part < 2:
            loads[part + 1].start()
        mapped = dot(hidden_ref[...], weight_ref[part]).astype(BF)
        for h in range(G):
            done = mapped[:, h * C : (h + 1) * C]
            if part < 2:
                one = done.astype(F32)
                one = one * inverse_rms(one)
                if part == 0:
                    one = one * (sharpness_ref[1, h] / C)
                done = one.astype(BF)
            for z in range(quarters):
                out_ref[part, z, h] = done[z * rows : (z + 1) * rows, :]
        stores.append(copy(out_ref.at[part], out_hbm.at[:, :, part], store_sem.at[part]))
        stores[-1].start()
    for store in stores:
        store.wait()


def temporal_entry(hidden, weight, sharpness, quarters, after):
    patches, depth = hidden.shape
    rows = patches // quarters
    return pl.pallas_call(
        functools.partial(temporal_entry_kernel, quarters),
        in_specs=[HBM, HBM, SCALARS] + [ANY] * len(after),
        out_specs=HBM,
        out_shape=hbm_out((quarters, G, 3, rows, C)),
        scratch_shapes=[
            pltpu.VMEM((patches, depth), BF),
            pltpu.VMEM((3, depth, HW), BF),
            pltpu.VMEM((3, quarters, G, rows, C), BF),
            DMA,
            DMA((3,)),
            DMA((3,)),
        ],
        compiler_params=params(),
        name="temporal_entry",
        cost_estimate=cost(
            6 * patches * depth * HW, 2 * patches * depth + 6 * depth * HW + 6 * patches * HW
        ),
    )(in_hbm(hidden), in_hbm(weight), sharpness, *after)


def temporal_attend_kernel(length_ref, in_hbm_ref, _, out_hbm, in_ref, out_ref, sem):
    frames, _, rows, _ = in_ref.shape
    group = 16
    size = frames * group
    load = copy(in_hbm_ref, in_ref, sem)
    load.start()
    length = length_ref[0]
    row = lax.broadcasted_iota(jnp.int32, (size, size), 0)
    column = lax.broadcasted_iota(jnp.int32, (size, size), 1)
    target, source = row // group, column // group
    keep = (row % group == column % group) & (source <= target) & (source > target - length)
    load.wait()
    for g in range(rows // group):
        at = slice(g * group, (g + 1) * group)
        query = in_ref[:, 0, at, :].reshape(size, C)
        key = in_ref[:, 1, at, :].reshape(size, C)
        value = in_ref[:, 2, at, :].reshape(size, C)
        weights = jnp.where(keep, jnp.exp(dot_t(query, key)), 0.0)
        shares = weights / jnp.sum(weights, axis=-1, keepdims=True)
        result = dot(shares.astype(BF), value).astype(BF)
        out_ref[:, at, :] = result.reshape(frames, group, C)
    store = copy(out_ref, out_hbm, sem)
    store.start()
    store.wait()


def temporal_attend(length, parts, after):
    frames, _, rows, _ = parts.shape
    shape = (frames, rows, C)
    return pl.pallas_call(
        temporal_attend_kernel,
        in_specs=[SCALARS, ANY, ANY],
        out_specs=HBM,
        out_shape=hbm_out(shape),
        scratch_shapes=[pltpu.VMEM(parts.shape, BF), pltpu.VMEM(shape, BF), DMA],
        compiler_params=params(),
        name="temporal_attend",
        cost_estimate=cost(4 * frames * rows * 256 * C, 8 * frames * rows * C),
    )(length, parts, in_hbm(after))


LINE = 96
CHUNK = 3 * LINE


def halves(denominators):
    high = denominators.astype(BF).astype(F32)
    return jnp.concatenate([high, denominators - high], axis=0).astype(BF)


def attend_rows(query, keys, both, out_ref):
    patches = out_ref.shape[0] - PAD
    row = lax.broadcasted_iota(jnp.int32, (LINE, C), 0)
    column = lax.broadcasted_iota(jnp.int32, (LINE, C), 1)
    lines = []
    for start in range(0, patches, CHUNK):
        at = slice(start, start + CHUNK)
        weights = jnp.exp(dot_t(query(at), keys)).astype(BF)
        result = dot(weights, both)
        out_ref[at, :] = result[:, :C].astype(BF)
        for j in range(0, CHUNK, LINE):
            diagonal = jnp.where(row == column, result[j : j + LINE, C:], 0.0)
            lines.append(jnp.sum(diagonal, axis=0, keepdims=True))
    lines.append(jnp.zeros((8 - len(lines), C), F32))
    out_ref[patches:, :] = halves(jnp.concatenate(lines, axis=0))


def with_ones(values):
    return jnp.concatenate([values, jnp.ones(values.shape, BF)], axis=1)


def own_attend_kernel(
    hidden_hbm, weight_hbm, query_hbm, *refs
):
    out_hbm, hidden_ref, weight_ref, query_ref, out_ref = refs[-9:-4]
    hidden_sem, weight_sem, query_sem, store_sem = refs[-4:]
    hidden_load = copy(hidden_hbm, hidden_ref, hidden_sem)
    query_load = copy(query_hbm.at[0], query_ref, query_sem)
    loads = [
        copy(
            weight_hbm.at[:, pl.ds((1 + part) * HW, HW)], weight_ref.at[part], weight_sem.at[part]
        )
        for part in range(2)
    ]
    hidden_load.start()
    loads[0].start()
    hidden_load.wait()
    loads[0].wait()
    loads[1].start()
    query_load.start()
    keys = dot(hidden_ref[...], weight_ref[0]).astype(BF)
    loads[1].wait()
    values = dot(hidden_ref[...], weight_ref[1]).astype(BF)
    query_load.wait()
    stores = []
    for h in range(G):
        key = keys[:, h * C : (h + 1) * C].astype(F32)
        key = (key * inverse_rms(key)).astype(BF)
        both = with_ones(values[:, h * C : (h + 1) * C])
        attend_rows(lambda at, h=h: query_ref[h, at, :], key, both, out_ref.at[h])
        stores.append(copy(out_ref.at[h], out_hbm.at[h], store_sem.at[h]))
        stores[-1].start()
    for store in stores:
        store.wait()


def own_attend(hidden, weight, query, after):
    patches, depth = hidden.shape
    shape = query.shape[1:]
    return pl.pallas_call(
        own_attend_kernel,
        in_specs=[HBM, HBM, HBM] + [ANY] * len(after),
        out_specs=HBM,
        out_shape=hbm_out(shape),
        scratch_shapes=[
            pltpu.VMEM((patches, depth), BF),
            pltpu.VMEM((2, depth, HW), BF),
            pltpu.VMEM(shape, BF),
            pltpu.VMEM(shape, BF),
            DMA,
            DMA((2,)),
            DMA,
            DMA((G,)),
        ],
        compiler_params=params(),
        name="own_attend",
        cost_estimate=cost(
            4 * patches * depth * HW + 6 * patches * patches * HW,
            2 * patches * depth + 4 * depth * HW + 10 * patches * HW,
        ),
    )(in_hbm(hidden), in_hbm(weight), in_hbm(query), *after)


def memory_attend_kernel(count, first, index_ref, query_hbm, *refs):
    blocks = refs[:count]
    out_hbm, query_ref, store_ref, out_ref, query_sem, block_sem, store_sem = refs[count + 1 :]
    frames = query_ref.shape[0]
    held = blocks[0].shape[0]
    query_load = copy(query_hbm, query_ref, query_sem)
    query_load.start()

    def fetch(t, carry):
        i, j = t // TOPM, lax.rem(t, TOPM)
        wanted = index_ref[first + i, j]
        for b in range(count // 2):

            @pl.when(wanted // held == b)
            def _(b=b):
                slot = lax.rem(wanted, held)
                for part in range(2):
                    block = blocks[2 * b + part].at[slot]
                    copy(block, store_ref.at[i, j, part], block_sem.at[i]).start()

        return carry

    lax.fori_loop(0, frames * TOPM, fetch, 0)
    query_load.wait()
    stores = []
    for i in range(frames):
        copy(store_ref.at[i], store_ref.at[i], block_sem.at[i]).wait()
        both = [store_ref[i, j, part] for j in range(TOPM) for part in range(2)]
        keys = jnp.concatenate([block[:, :C] for block in both], axis=0)
        values = jnp.concatenate([block[:, C:] for block in both], axis=0)
        attend_rows(
            lambda at, i=i: query_ref[i, at, :], keys, with_ones(values), out_ref.at[i]
        )
        stores.append(copy(out_ref.at[i], out_hbm.at[i], store_sem.at[i]))
        stores[-1].start()
    for store in stores:
        store.wait()


def memory_attend(first, index, query, blocks, after):
    count = len(blocks)
    frames, rows, _ = query.shape
    _, part, width = blocks[0].shape
    shape = (frames, rows, C)
    return pl.pallas_call(
        functools.partial(memory_attend_kernel, count, first),
        in_specs=[SCALARS] + [ANY] * (count + 2),
        out_specs=HBM,
        out_shape=hbm_out(shape),
        scratch_shapes=[
            pltpu.VMEM(shape, BF),
            pltpu.VMEM((frames, TOPM, 2, part, width), BF),
            pltpu.VMEM(shape, BF),
            DMA,
            DMA((frames,)),
            DMA((frames,)),
        ],
        compiler_params=params(),
        name="memory_attend",
        cost_estimate=cost(
            16 * frames * rows * TOPM * part * C,
            4 * frames * rows * C + 2 * frames * TOPM * part * width,
        ),
    )(index, query, *blocks, in_hbm(after))


def add_partials_kernel(count, x_ref, *refs):
    ins, outs = refs[:count], refs[count : count + G]
    parts_ref, out_ref, load_sem, store_sem = refs[count + G :]
    patches = out_ref.shape[1] - PAD
    loads = []
    for j in range(G):
        frame = lax.rem(x_ref[0] + j, G)
        loads.append(
            [copy(ref.at[frame], parts_ref.at[k, j], load_sem.at[k, j]) for k, ref in enumerate(ins)]
        )
    for of_frame in loads:
        for load in of_frame:
            load.start()
    stores = []
    for j in range(G):
        for load in loads[j]:
            load.wait()
        total = parts_ref[0, j].astype(F32)
        for k in range(1, count):
            total = total + parts_ref[k, j].astype(F32)
        out_ref[j, :patches, :] = total[:patches].astype(BF)
        out_ref[j, patches:, :] = halves(total[patches : patches + 8] + total[patches + 8 :])
        stores.append(copy(out_ref.at[j], outs[j], store_sem.at[j]))
        stores[-1].start()
    for store in stores:
        store.wait()


def add_partials(x, parts):
    shape = parts[0].shape
    return pl.pallas_call(
        functools.partial(add_partials_kernel, len(parts)),
        in_specs=[SCALARS] + [ANY] * len(parts),
        out_specs=[HBM] * G,
        out_shape=[hbm_out(shape[1:])] * G,
        scratch_shapes=[
            pltpu.VMEM((len(parts),) + shape, BF),
            pltpu.VMEM(shape, BF),
            DMA((len(parts), G)),
            DMA((G,)),
        ],
        compiler_params=params(),
        name="add_partials",
        cost_estimate=cost(4 * parts[0].size, 8 * parts[0].size),
    )(x, *parts)


def leave_kernel(
    x_ref, own_hbm, memory_0, memory_1, memory_2, memory_3, time_hbm, weight_hbm, out_hbm,
    own_ref, memory_ref, time_ref, combined_ref, weight_ref, out_ref,
    own_sem, memory_sem, time_sem, weight_sem, store_sem,
):
    patches = own_ref.shape[1] - PAD
    quarters = time_ref.shape[0] // G
    rows = time_ref.shape[1]
    steps, _, width = weight_ref.shape
    heads = [lax.rem(x_ref[0] + G - j, G) for j in range(G)]
    memories = (memory_0, memory_1, memory_2, memory_3)
    own_loads = [copy(own_hbm.at[heads[j]], own_ref.at[j], own_sem.at[j]) for j in range(G)]
    memory_loads = [copy(memories[j], memory_ref.at[j], memory_sem.at[j]) for j in range(G)]
    time_load = copy(time_hbm, time_ref, time_sem)
    loads, stores = [], []
    for i in range(steps):
        at = pl.ds(i * width, width)
        loads.append(copy(weight_hbm.at[:, at], weight_ref.at[i], weight_sem.at[i]))
        stores.append(copy(out_ref.at[i], out_hbm.at[:, at], store_sem.at[i]))
    for load in own_loads + memory_loads + [time_load] + loads:
        load.start()
    row = lax.broadcasted_iota(jnp.int32, (LINE, C), 0)
    column = lax.broadcasted_iota(jnp.int32, (LINE, C), 1)
    for h in range(G):
        own_loads[h].wait()
        memory_loads[h].wait()
        column_at = pl.ds(pl.multiple_of(heads[h] * C, C), C)
        tail = own_ref[h, patches:, :].astype(F32) + memory_ref[h, patches:, :].astype(F32)
        denominators = tail[:8] + tail[8:]
        for j in range(patches // LINE):
            at = slice(j * LINE, (j + 1) * LINE)
            line = jnp.broadcast_to(denominators[j : j + 1, :], (LINE, C))
            total = jnp.sum(jnp.where(row == column, line, 0.0), axis=1, keepdims=True)
            top = own_ref[h, at, :].astype(F32) + memory_ref[h, at, :].astype(F32)
            combined_ref[at, column_at] = (top / total).astype(BF)
    time_load.wait()
    for h in range(G):
        for z in range(quarters):
            combined_ref[z * rows : (z + 1) * rows, HW + h * C : HW + (h + 1) * C] = time_ref[
                z * G + h
            ]
    for i in range(steps):
        loads[i].wait()
        out_ref[i] = dot(combined_ref[...], weight_ref[i]).astype(BF)
        stores[i].start()
    for store in stores:
        store.wait()


def leave(x, own, memory, time, weight):
    patches = own.shape[1] - PAD
    depth, width = weight.shape
    steps = 4
    step = width // steps
    return pl.pallas_call(
        leave_kernel,
        in_specs=[SCALARS, HBM] + [ANY] * (G + 1) + [HBM],
        out_specs=HBM,
        out_shape=hbm_out((patches, width)),
        scratch_shapes=[
            pltpu.VMEM(own.shape, BF),
            pltpu.VMEM(own.shape, BF),
            pltpu.VMEM(time.shape, BF),
            pltpu.VMEM((patches, depth), BF),
            pltpu.VMEM((steps, depth, step), BF),
            pltpu.VMEM((steps, patches, step), BF),
            DMA((G,)),
            DMA((G,)),
            DMA,
            DMA((steps,)),
            DMA((steps,)),
        ],
        compiler_params=params(),
        name="leave",
        cost_estimate=cost(
            2 * patches * depth * width,
            2 * depth * width + 2 * patches * width + 6 * patches * depth,
        ),
    )(x, in_hbm(own), *memory, time, in_hbm(weight))


def on_device(
    patch_activation_tensor,
    conditioning_affine,
    entry_projection_matrix,
    exit_projection_matrix,
    softmax_sharpness,
    cached_past_pairs,
    recalled_picture_holder,
    recalled_picture_position,
    lookback_lengths,
):
    frame = ("zq", "zp", "x")
    rings, sides = lax.axis_size("y"), lax.axis_size("zq")
    quarters = lax.axis_size("zp") * sides
    patches, depth = patch_activation_tensor.shape[2:]
    held, piece = cached_past_pairs.shape[:2]
    cores = lax.axis_size("c")
    x = lax.axis_index("x").astype(jnp.int32).reshape(1)

    def turn(step):
        return [(s, (s + step) % rings) for s in range(rings)]

    def other(size):
        return [(s, size - 1 - s) for s in range(size)]

    def swap(blocks, axes):
        return lax.all_to_all(blocks, axes, split_axis=0, concat_axis=0, tiled=True)

    def swap_apart(blocks):
        return [in_hbm(blocks[0])] + [lax.ppermute(blocks[j], "x", turn(j)) for j in range(1, G)]

    with jax.named_scope("store"):
        split = split_store(cached_past_pairs.reshape(held * piece, 2 * HW), 1)
        pieces = swap(split[0], "x")

    with jax.named_scope("queries"):
        hidden, query = modulate(
            patch_activation_tensor.reshape(patches, depth),
            conditioning_affine.reshape(2, depth),
            entry_projection_matrix,
            softmax_sharpness,
            recalled_picture_holder.reshape(TOPM),
            recalled_picture_position.reshape(TOPM),
            held,
            1,
            after=split,
        )
        here = swap(query[0], "x")

    with jax.named_scope("store"):
        joined = join_pieces(pieces, held, after=hidden)
        above = lax.ppermute(joined, "y", turn(-1))
        below = lax.ppermute(joined, "y", turn(1))
        second = lax.ppermute(joined, "zp", other(sides))

        second_above = lax.ppermute(second, "y", turn(-1))
        second_below = lax.ppermute(second, "y", turn(1))

    with jax.named_scope("temporal"):
        parts = temporal_entry(
            hidden, entry_projection_matrix, softmax_sharpness, quarters, after=[in_hbm(joined)]
        )

    with jax.named_scope("queries"):
        here, *_ = lax.optimization_barrier((here, second, above, below, parts))
        beside = lax.ppermute(here, "zq", other(sides))

    with jax.named_scope("own"):
        own = own_attend(
            hidden, entry_projection_matrix, query, after=[in_hbm(parts), above]
        )

    with jax.named_scope("temporal"):
        sent, *_ = lax.optimization_barrier((parts, second))
        sent = swap(sent.reshape((quarters * G,) + parts.shape[2:]), frame)

    with jax.named_scope("store"):
        below, second_above, second_below = lax.optimization_barrier(
            (below, second_above, second_below)
        )
        far = lax.ppermute(below, "y", turn(1))
        second_far = lax.ppermute(second_above, "y", turn(-1))
        near = [joined, second, above, second_above, far, second_far, below, second_below]
        blocks = near + [lax.ppermute(block, "c", other(cores)) for block in near]
        blocks = [in_hbm(block) for block in blocks]

    with jax.named_scope("queries"):
        named = jnp.concatenate([group[:, patches, :TOPM] for group in (beside, here)], axis=0)
        named = named.astype(jnp.int32)
        y = (named // (cores * held) - lax.axis_index("y")) & (rings - 1)
        c = (named // held & (cores - 1)) ^ lax.axis_index("c")
        index = (c * rings + y) * held + (named & (held - 1))

    with jax.named_scope("temporal"):
        timed = temporal_attend(lookback_lengths, sent, after=own)
        time = swap(timed, frame)

    with jax.named_scope("memory"):
        sum_beside = memory_attend(0, index, beside, blocks, timed)
        from_beside = lax.ppermute(sum_beside, "zq", other(sides))
        sum_here = memory_attend(beside.shape[0], index, here, blocks, sum_beside)
        memory = swap_apart(add_partials(x, [in_hbm(sum_here), from_beside]))

    with jax.named_scope("exit"):
        attended = leave(x, own, memory, time, exit_projection_matrix)
    return attended.reshape(1, 1, patches, depth)


def solution(mesh):
    apart = Mesh(mesh.devices.reshape(4, 2, 2, 2, 4), ("y", "c", "zq", "zp", "x"))
    roll, frame = ("y", "c"), ("zq", "zp", "x")
    return jax.shard_map(
        on_device,
        mesh=apart,
        in_specs=(
            P(roll, frame, None, None),
            P(roll, frame, None, None),
            P(),
            P(),
            P(),
            P(roll, frame, None, None),
            P(roll, frame, None, None),
            P(roll, frame, None),
            P(roll),
        ),
        out_specs=P(roll, frame, None, None),
        check_vma=False,
    )
```

```python
import functools

import jax
import jax.numpy as jnp
from jax import lax
from jax.experimental import pallas as pl
from jax.experimental.pallas import tpu as pltpu
from jax.sharding import Mesh
from jax.sharding import PartitionSpec as P

G = 4
C = 128
HW = G * C
TOPM = 6
EPSILON = 1e-06
BF = jnp.bfloat16
F32 = jnp.float32
PAD = 16
VMEM_LIMIT = 28 * 1024 * 1024
ANY = pl.BlockSpec(memory_space=pl.ANY)
HBM = pl.BlockSpec(memory_space=pltpu.HBM)
WHOLE = pl.BlockSpec(memory_space=pltpu.VMEM)
SCALARS = pl.BlockSpec(memory_space=pltpu.SMEM)


def params(**more):
    return pltpu.CompilerParams(vmem_limit_bytes=VMEM_LIMIT, **more)


def cost(flops, bytes_accessed):
    return pl.CostEstimate(
        flops=flops // 16, bytes_accessed=bytes_accessed // 16, transcendentals=0
    )


def in_hbm(array):
    return pltpu.with_memory_space_constraint(array, pltpu.HBM)


def hbm_out(shape, dtype=BF):
    return pltpu.HBM(shape, dtype)


def inverse_rms(values):
    return lax.rsqrt(jnp.mean(values * values, axis=-1, keepdims=True) + EPSILON)


def dot(a, b):
    return jnp.dot(a, b, preferred_element_type=F32)


def dot_t(a, b):
    return lax.dot_general(a, b, (((1,), (1,)), ((), ())), preferred_element_type=F32)


DMA = pltpu.SemaphoreType.DMA
copy = pltpu.make_async_copy


def split_store_kernel(rows_ref, out_hbm, out_ref, sem):
    sends = []
    for h in range(G):
        key = rows_ref[:, h * C : (h + 1) * C].astype(F32)
        out_ref[h, :, :C] = (key * inverse_rms(key)).astype(BF)
        out_ref[h, :, C:] = rows_ref[:, HW + h * C : HW + (h + 1) * C]
        for k in range(out_hbm.shape[0]):
            sends.append(copy(out_ref.at[h], out_hbm.at[k, h], sem.at[k, h]))
            sends[-1].start()
    for send in sends:
        send.wait()


def split_store(rows, copies):
    n = rows.shape[0]
    return pl.pallas_call(
        split_store_kernel,
        in_specs=[WHOLE],
        out_specs=HBM,
        out_shape=hbm_out((copies, G, n, 2 * C)),
        scratch_shapes=[pltpu.VMEM((G, n, 2 * C), BF), DMA((copies, G))],
        compiler_params=params(),
        name="split_store",
        cost_estimate=cost(8 * n * HW, 8 * n * HW),
    )(rows)


def join_pieces_kernel(piece, in_hbm, _, out_hbm, in_ref, wide_ref, joined_ref, out_ref, sem):
    pieces = in_ref.shape[0]
    loads = [copy(in_hbm.at[i], in_ref.at[i], sem.at[i]) for i in range(pieces)]
    for load in loads:
        load.start()
    for i in range(pieces):
        loads[i].wait()
        wide_ref[i] = in_ref[i].astype(F32)
        for m in range(out_ref.shape[0]):
            joined_ref[m, i * piece : (i + 1) * piece, :] = wide_ref[
                i, m * piece : (m + 1) * piece, :
            ]
    out_ref[...] = joined_ref[...].astype(BF)
    send = copy(out_ref, out_hbm, sem.at[0])
    send.start()
    send.wait()


def join_pieces(parts, frames, after):
    pieces, rows, width = parts.shape
    piece = rows // frames
    shape = (frames, pieces * piece, width)
    return pl.pallas_call(
        functools.partial(join_pieces_kernel, piece),
        in_specs=[ANY, ANY],
        out_specs=HBM,
        out_shape=hbm_out(shape),
        scratch_shapes=[
            pltpu.VMEM(parts.shape, BF),
            pltpu.VMEM(parts.shape, F32),
            pltpu.VMEM(shape, F32),
            pltpu.VMEM(shape, BF),
            DMA((pieces,)),
        ],
        compiler_params=params(),
        name="join_pieces",
        cost_estimate=cost(parts.size, 4 * parts.size),
    )(parts, in_hbm(after))


def modulate_kernel(
    held,
    act_hbm, affine_hbm, weight_hbm, sharpness_ref, owner_ref, slot_ref, _, hidden_hbm, query_hbm,
    act_ref, affine_ref, weight_ref, hidden_ref, query_ref,
    load_sem, affine_sem, weight_sem, store_sem, query_sem,
):
    steps, rows, _ = act_ref.shape
    patches = query_ref.shape[1] - PAD
    loads, stores = [], []
    for i in range(steps):
        at = pl.ds(i * rows, rows)
        loads.append(copy(act_hbm.at[at, :], act_ref.at[i], load_sem.at[i]))
        stores.append(copy(hidden_ref.at[i], hidden_hbm.at[at, :], store_sem.at[i]))
    weight_load = copy(weight_hbm.at[:, pl.ds(0, HW)], weight_ref, weight_sem)
    affine_load = copy(affine_hbm, affine_ref, affine_sem)
    affine_load.start()
    loads[0].start()
    weight_load.start()
    row = lax.broadcasted_iota(jnp.int32, (PAD, C), 0)
    column = lax.broadcasted_iota(jnp.int32, (PAD, C), 1)
    tail = jnp.zeros((PAD, C), jnp.int32)
    for j in range(TOPM):
        tail = jnp.where((row == 0) & (column == j), owner_ref[j] * held + slot_ref[j], tail)
    for h in range(G):
        query_ref[h, patches:, :] = tail.astype(F32).astype(BF)
    affine_load.wait()
    for i in range(steps):
        at = slice(i * rows, (i + 1) * rows)
        loads[i].wait()
        if i + 1 < steps:
            loads[i + 1].start()
        act = act_ref[i].astype(F32)
        hidden = act * inverse_rms(act) * (1.0 + affine_ref[0:1, :]) + affine_ref[1:2, :]
        hidden = hidden.astype(BF)
        hidden_ref[i] = hidden
        stores[i].start()
        if i == 0:
            weight_load.wait()
        mapped = dot(hidden, weight_ref[...]).astype(BF).astype(F32)
        for h in range(G):
            one = mapped[:, h * C : (h + 1) * C]
            query_ref[h, at, :] = (
                one * inverse_rms(one) * (sharpness_ref[0, h] / C)
            ).astype(BF)
    sends = [
        copy(query_ref, query_hbm.at[k], query_sem.at[k]) for k in range(query_hbm.shape[0])
    ]
    for send in sends:
        send.start()
    for store in stores + sends:
        store.wait()


def modulate(act, affine, weight, sharpness, owner, slot, held, copies, after):
    patches, depth = act.shape
    steps = 2
    rows = patches // steps
    shape = (G, patches + PAD, C)
    return pl.pallas_call(
        functools.partial(modulate_kernel, held),
        in_specs=[HBM, HBM, HBM, SCALARS, SCALARS, SCALARS, ANY],
        out_specs=[HBM, HBM],
        out_shape=[hbm_out((patches, depth)), hbm_out((copies,) + shape)],
        scratch_shapes=[
            pltpu.VMEM((steps, rows, depth), BF),
            pltpu.VMEM(affine.shape, F32),
            pltpu.VMEM((depth, HW), BF),
            pltpu.VMEM((steps, rows, depth), BF),
            pltpu.VMEM(shape, BF),
            DMA((steps,)),
            DMA,
            DMA,
            DMA((steps,)),
            DMA((copies,)),
        ],
        compiler_params=params(),
        name="modulate",
        cost_estimate=cost(
            2 * patches * depth * HW, 4 * patches * depth + 2 * depth * HW + 2 * patches * HW
        ),
    )(in_hbm(act), in_hbm(affine), in_hbm(weight), sharpness, owner, slot, in_hbm(after))


def temporal_entry_kernel(
    quarters, hidden_hbm, weight_hbm, sharpness_ref, *refs
):
    out_hbm, hidden_ref, weight_ref, out_ref, hidden_sem, weight_sem, store_sem = refs[-7:]
    rows = hidden_ref.shape[0] // quarters
    hidden_load = copy(hidden_hbm, hidden_ref, hidden_sem)
    loads = [
        copy(
            weight_hbm.at[:, pl.ds((3 + part) * HW, HW)], weight_ref.at[part], weight_sem.at[part]
        )
        for part in range(3)
    ]
    hidden_load.start()
    loads[0].start()
    hidden_load.wait()
    stores = []
    for part in range(3):
        loads[part].wait()
        if part < 2:
            loads[part + 1].start()
        mapped = dot(hidden_ref[...], weight_ref[part]).astype(BF)
        for h in range(G):
            done = mapped[:, h * C : (h + 1) * C]
            if part < 2:
                one = done.astype(F32)
                one = one * inverse_rms(one)
                if part == 0:
                    one = one * (sharpness_ref[1, h] / C)
                done = one.astype(BF)
            for z in range(quarters):
                out_ref[part, z, h] = done[z * rows : (z + 1) * rows, :]
        stores.append(copy(out_ref.at[part], out_hbm.at[:, :, part], store_sem.at[part]))
        stores[-1].start()
    for store in stores:
        store.wait()


def temporal_entry(hidden, weight, sharpness, quarters, after):
    patches, depth = hidden.shape
    rows = patches // quarters
    return pl.pallas_call(
        functools.partial(temporal_entry_kernel, quarters),
        in_specs=[HBM, HBM, SCALARS] + [ANY] * len(after),
        out_specs=HBM,
        out_shape=hbm_out((quarters, G, 3, rows, C)),
        scratch_shapes=[
            pltpu.VMEM((patches, depth), BF),
            pltpu.VMEM((3, depth, HW), BF),
            pltpu.VMEM((3, quarters, G, rows, C), BF),
            DMA,
            DMA((3,)),
            DMA((3,)),
        ],
        compiler_params=params(),
        name="temporal_entry",
        cost_estimate=cost(
            6 * patches * depth * HW, 2 * patches * depth + 6 * depth * HW + 6 * patches * HW
        ),
    )(in_hbm(hidden), in_hbm(weight), sharpness, *after)


def temporal_attend_kernel(length_ref, in_hbm_ref, _, out_hbm, in_ref, out_ref, sem):
    frames, _, rows, _ = in_ref.shape
    group = 16
    size = frames * group
    load = copy(in_hbm_ref, in_ref, sem)
    load.start()
    length = length_ref[0]
    row = lax.broadcasted_iota(jnp.int32, (size, size), 0)
    column = lax.broadcasted_iota(jnp.int32, (size, size), 1)
    target, source = row // group, column // group
    keep = (row % group == column % group) & (source <= target) & (source > target - length)
    load.wait()
    for g in range(rows // group):
        at = slice(g * group, (g + 1) * group)
        query = in_ref[:, 0, at, :].reshape(size, C)
        key = in_ref[:, 1, at, :].reshape(size, C)
        value = in_ref[:, 2, at, :].reshape(size, C)
        weights = jnp.where(keep, jnp.exp(dot_t(query, key)), 0.0)
        shares = weights / jnp.sum(weights, axis=-1, keepdims=True)
        result = dot(shares.astype(BF), value).astype(BF)
        out_ref[:, at, :] = result.reshape(frames, group, C)
    store = copy(out_ref, out_hbm, sem)
    store.start()
    store.wait()


def temporal_attend(length, parts, after):
    frames, _, rows, _ = parts.shape
    shape = (frames, rows, C)
    return pl.pallas_call(
        temporal_attend_kernel,
        in_specs=[SCALARS, ANY, ANY],
        out_specs=HBM,
        out_shape=hbm_out(shape),
        scratch_shapes=[pltpu.VMEM(parts.shape, BF), pltpu.VMEM(shape, BF), DMA],
        compiler_params=params(),
        name="temporal_attend",
        cost_estimate=cost(4 * frames * rows * 256 * C, 8 * frames * rows * C),
    )(length, parts, in_hbm(after))


LINE = 96
CHUNK = 3 * LINE


def halves(denominators):
    high = denominators.astype(BF).astype(F32)
    return jnp.concatenate([high, denominators - high], axis=0).astype(BF)


def attend_rows(query, keys, both, out_ref):
    patches = out_ref.shape[0] - PAD
    row = lax.broadcasted_iota(jnp.int32, (LINE, C), 0)
    column = lax.broadcasted_iota(jnp.int32, (LINE, C), 1)
    lines = []
    for start in range(0, patches, CHUNK):
        at = slice(start, start + CHUNK)
        weights = jnp.exp(dot_t(query(at), keys)).astype(BF)
        result = dot(weights, both)
        out_ref[at, :] = result[:, :C].astype(BF)
        for j in range(0, CHUNK, LINE):
            diagonal = jnp.where(row == column, result[j : j + LINE, C:], 0.0)
            lines.append(jnp.sum(diagonal, axis=0, keepdims=True))
    lines.append(jnp.zeros((8 - len(lines), C), F32))
    out_ref[patches:, :] = halves(jnp.concatenate(lines, axis=0))


def with_ones(values):
    return jnp.concatenate([values, jnp.ones(values.shape, BF)], axis=1)


def own_attend_kernel(
    hidden_hbm, weight_hbm, query_hbm, *refs
):
    out_hbm, hidden_ref, weight_ref, query_ref, out_ref = refs[-9:-4]
    hidden_sem, weight_sem, query_sem, store_sem = refs[-4:]
    hidden_load = copy(hidden_hbm, hidden_ref, hidden_sem)
    query_load = copy(query_hbm.at[0], query_ref, query_sem)
    loads = [
        copy(
            weight_hbm.at[:, pl.ds((1 + part) * HW, HW)], weight_ref.at[part], weight_sem.at[part]
        )
        for part in range(2)
    ]
    hidden_load.start()
    loads[0].start()
    hidden_load.wait()
    loads[0].wait()
    loads[1].start()
    query_load.start()
    keys = dot(hidden_ref[...], weight_ref[0]).astype(BF)
    loads[1].wait()
    values = dot(hidden_ref[...], weight_ref[1]).astype(BF)
    query_load.wait()
    stores = []
    for h in range(G):
        key = keys[:, h * C : (h + 1) * C].astype(F32)
        key = (key * inverse_rms(key)).astype(BF)
        both = with_ones(values[:, h * C : (h + 1) * C])
        attend_rows(lambda at, h=h: query_ref[h, at, :], key, both, out_ref.at[h])
        stores.append(copy(out_ref.at[h], out_hbm.at[h], store_sem.at[h]))
        stores[-1].start()
    for store in stores:
        store.wait()


def own_attend(hidden, weight, query, after):
    patches, depth = hidden.shape
    shape = query.shape[1:]
    return pl.pallas_call(
        own_attend_kernel,
        in_specs=[HBM, HBM, HBM] + [ANY] * len(after),
        out_specs=HBM,
        out_shape=hbm_out(shape),
        scratch_shapes=[
            pltpu.VMEM((patches, depth), BF),
            pltpu.VMEM((2, depth, HW), BF),
            pltpu.VMEM(shape, BF),
            pltpu.VMEM(shape, BF),
            DMA,
            DMA((2,)),
            DMA,
            DMA((G,)),
        ],
        compiler_params=params(),
        name="own_attend",
        cost_estimate=cost(
            4 * patches * depth * HW + 6 * patches * patches * HW,
            2 * patches * depth + 4 * depth * HW + 10 * patches * HW,
        ),
    )(in_hbm(hidden), in_hbm(weight), in_hbm(query), *after)


def memory_attend_kernel(count, first, index_ref, query_hbm, *refs):
    blocks = refs[:count]
    out_hbm, query_ref, store_ref, out_ref, query_sem, block_sem, store_sem = refs[count + 1 :]
    frames = query_ref.shape[0]
    held = blocks[0].shape[0]
    query_load = copy(query_hbm, query_ref, query_sem)
    query_load.start()

    def fetch(t, carry):
        i, j = t // TOPM, lax.rem(t, TOPM)
        wanted = index_ref[first + i, j]
        for b in range(count // 2):

            @pl.when(wanted // held == b)
            def _(b=b):
                slot = lax.rem(wanted, held)
                for part in range(2):
                    block = blocks[2 * b + part].at[slot]
                    copy(block, store_ref.at[i, j, part], block_sem.at[i]).start()

        return carry

    lax.fori_loop(0, frames * TOPM, fetch, 0)
    query_load.wait()
    stores = []
    for i in range(frames):
        copy(store_ref.at[i], store_ref.at[i], block_sem.at[i]).wait()
        both = [store_ref[i, j, part] for j in range(TOPM) for part in range(2)]
        keys = jnp.concatenate([block[:, :C] for block in both], axis=0)
        values = jnp.concatenate([block[:, C:] for block in both], axis=0)
        attend_rows(
            lambda at, i=i: query_ref[i, at, :], keys, with_ones(values), out_ref.at[i]
        )
        stores.append(copy(out_ref.at[i], out_hbm.at[i], store_sem.at[i]))
        stores[-1].start()
    for store in stores:
        store.wait()


def memory_attend(first, index, query, blocks, after):
    count = len(blocks)
    frames, rows, _ = query.shape
    _, part, width = blocks[0].shape
    shape = (frames, rows, C)
    return pl.pallas_call(
        functools.partial(memory_attend_kernel, count, first),
        in_specs=[SCALARS] + [ANY] * (count + 2),
        out_specs=HBM,
        out_shape=hbm_out(shape),
        scratch_shapes=[
            pltpu.VMEM(shape, BF),
            pltpu.VMEM((frames, TOPM, 2, part, width), BF),
            pltpu.VMEM(shape, BF),
            DMA,
            DMA((frames,)),
            DMA((frames,)),
        ],
        compiler_params=params(),
        name="memory_attend",
        cost_estimate=cost(
            16 * frames * rows * TOPM * part * C,
            4 * frames * rows * C + 2 * frames * TOPM * part * width,
        ),
    )(index, in_hbm(query), *blocks, in_hbm(after))


def add_partials_kernel(count, x_ref, *refs):
    ins, outs = refs[:count], refs[count : count + G]
    parts_ref, out_ref, load_sem, store_sem = refs[count + G :]
    patches = out_ref.shape[1] - PAD
    loads = []
    for j in range(G):
        frame = lax.rem(x_ref[0] + j, G)
        loads.append(
            [copy(ref.at[frame], parts_ref.at[k, j], load_sem.at[k, j]) for k, ref in enumerate(ins)]
        )
    for of_frame in loads:
        for load in of_frame:
            load.start()
    stores = []
    for j in range(G):
        for load in loads[j]:
            load.wait()
        total = parts_ref[0, j].astype(F32)
        for k in range(1, count):
            total = total + parts_ref[k, j].astype(F32)
        out_ref[j, :patches, :] = total[:patches].astype(BF)
        out_ref[j, patches:, :] = halves(total[patches : patches + 8] + total[patches + 8 :])
        stores.append(copy(out_ref.at[j], outs[j], store_sem.at[j]))
        stores[-1].start()
    for store in stores:
        store.wait()


def add_partials(x, parts):
    shape = parts[0].shape
    return pl.pallas_call(
        functools.partial(add_partials_kernel, len(parts)),
        in_specs=[SCALARS] + [ANY] * len(parts),
        out_specs=[HBM] * G,
        out_shape=[hbm_out(shape[1:])] * G,
        scratch_shapes=[
            pltpu.VMEM((len(parts),) + shape, BF),
            pltpu.VMEM(shape, BF),
            DMA((len(parts), G)),
            DMA((G,)),
        ],
        compiler_params=params(),
        name="add_partials",
        cost_estimate=cost(4 * parts[0].size, 8 * parts[0].size),
    )(x, *parts)


STEPS = 4


def leave_time_kernel(
    time_hbm, weight_hbm, _, out_hbm,
    time_ref, combined_ref, weight_ref, out_ref, time_sem, weight_sem, store_sem,
):
    quarters = time_ref.shape[0] // G
    rows = time_ref.shape[1]
    depth, width = weight_ref.shape[1:]
    time_load = copy(time_hbm, time_ref, time_sem)
    time_load.start()
    loads, stores = [], []
    for i in range(STEPS):
        at = pl.ds(i * width, width)
        loads.append(
            copy(weight_hbm.at[pl.ds(HW, depth), at], weight_ref.at[i], weight_sem.at[i])
        )
        stores.append(copy(out_ref.at[i], out_hbm.at[i], store_sem.at[i]))
        loads[i].start()
    time_load.wait()
    for h in range(G):
        for z in range(quarters):
            combined_ref[z * rows : (z + 1) * rows, h * C : (h + 1) * C] = time_ref[z * G + h]
    for i in range(STEPS):
        loads[i].wait()
        out_ref[i] = dot(combined_ref[...], weight_ref[i])
        stores[i].start()
    for store in stores:
        store.wait()


def leave_time(time, weight, after):
    patches = time.shape[0] // G * time.shape[1]
    depth, width = weight.shape
    step = width // STEPS
    shape = (STEPS, patches, step)
    return pl.pallas_call(
        leave_time_kernel,
        in_specs=[ANY, HBM, ANY],
        out_specs=HBM,
        out_shape=hbm_out(shape, F32),
        scratch_shapes=[
            pltpu.VMEM(time.shape, BF),
            pltpu.VMEM((patches, depth - HW), BF),
            pltpu.VMEM((STEPS, depth - HW, step), BF),
            pltpu.VMEM(shape, F32),
            DMA,
            DMA((STEPS,)),
            DMA((STEPS,)),
        ],
        compiler_params=params(),
        name="leave_time",
        cost_estimate=cost(
            patches * depth * width, depth * width + 4 * patches * width + 2 * time.size
        ),
    )(time, in_hbm(weight), in_hbm(after))


def leave_kernel(
    x_ref, own_hbm, memory_0, memory_1, memory_2, memory_3, partial_hbm, weight_hbm, out_hbm,
    own_ref, memory_ref, combined_ref, partial_ref, weight_ref, out_ref,
    own_sem, memory_sem, partial_sem, weight_sem, store_sem,
):
    patches = own_ref.shape[1] - PAD
    width = weight_ref.shape[2]
    heads = [lax.rem(x_ref[0] + G - j, G) for j in range(G)]
    memories = (memory_0, memory_1, memory_2, memory_3)
    own_loads = [copy(own_hbm.at[heads[j]], own_ref.at[j], own_sem.at[j]) for j in range(G)]
    memory_loads = [copy(memories[j], memory_ref.at[j], memory_sem.at[j]) for j in range(G)]
    loads, partial_loads, stores = [], [], []
    for i in range(STEPS):
        at = pl.ds(i * width, width)
        loads.append(copy(weight_hbm.at[pl.ds(0, HW), at], weight_ref.at[i], weight_sem.at[i]))
        partial_loads.append(copy(partial_hbm.at[i], partial_ref.at[i], partial_sem.at[i]))
        stores.append(copy(out_ref.at[i], out_hbm.at[:, at], store_sem.at[i]))
    for load in own_loads + memory_loads:
        load.start()
    for i in range(STEPS):
        loads[i].start()
        partial_loads[i].start()
    row = lax.broadcasted_iota(jnp.int32, (LINE, C), 0)
    column = lax.broadcasted_iota(jnp.int32, (LINE, C), 1)
    for h in range(G):
        own_loads[h].wait()
        memory_loads[h].wait()
        column_at = pl.ds(pl.multiple_of(heads[h] * C, C), C)
        tail = own_ref[h, patches:, :].astype(F32) + memory_ref[h, patches:, :].astype(F32)
        denominators = tail[:8] + tail[8:]
        for j in range(patches // LINE):
            at = slice(j * LINE, (j + 1) * LINE)
            line = jnp.broadcast_to(denominators[j : j + 1, :], (LINE, C))
            total = jnp.sum(jnp.where(row == column, line, 0.0), axis=1, keepdims=True)
            top = own_ref[h, at, :].astype(F32) + memory_ref[h, at, :].astype(F32)
            combined_ref[at, column_at] = (top / total).astype(BF)
    for i in range(STEPS):
        loads[i].wait()
        partial_loads[i].wait()
        out_ref[i] = (dot(combined_ref[...], weight_ref[i]) + partial_ref[i]).astype(BF)
        stores[i].start()
    for store in stores:
        store.wait()


def leave(x, own, memory, partial, weight):
    patches = own.shape[1] - PAD
    width = weight.shape[1]
    step = width // STEPS
    return pl.pallas_call(
        leave_kernel,
        in_specs=[SCALARS, HBM] + [ANY] * G + [HBM, HBM],
        out_specs=HBM,
        out_shape=hbm_out((patches, width)),
        scratch_shapes=[
            pltpu.VMEM(own.shape, BF),
            pltpu.VMEM(own.shape, BF),
            pltpu.VMEM((patches, HW), BF),
            pltpu.VMEM(partial.shape, F32),
            pltpu.VMEM((STEPS, HW, step), BF),
            pltpu.VMEM((STEPS, patches, step), BF),
            DMA((G,)),
            DMA((G,)),
            DMA((STEPS,)),
            DMA((STEPS,)),
            DMA((STEPS,)),
        ],
        compiler_params=params(),
        name="leave",
        cost_estimate=cost(
            2 * patches * HW * width, 2 * HW * width + 6 * patches * width + 4 * patches * HW
        ),
    )(x, in_hbm(own), *memory, in_hbm(partial), in_hbm(weight))


def on_device(
    patch_activation_tensor,
    conditioning_affine,
    entry_projection_matrix,
    exit_projection_matrix,
    softmax_sharpness,
    cached_past_pairs,
    recalled_picture_holder,
    recalled_picture_position,
    lookback_lengths,
):
    frame = ("zq", "zp", "x")
    rings, sides = lax.axis_size("y"), lax.axis_size("zq")
    quarters = lax.axis_size("zp") * sides
    patches, depth = patch_activation_tensor.shape[2:]
    held, piece = cached_past_pairs.shape[:2]
    cores = lax.axis_size("c")
    x = lax.axis_index("x").astype(jnp.int32).reshape(1)

    def turn(step):
        return [(s, (s + step) % rings) for s in range(rings)]

    def other(size):
        return [(s, size - 1 - s) for s in range(size)]

    def swap(blocks, axes):
        return lax.all_to_all(blocks, axes, split_axis=0, concat_axis=0, tiled=True)

    def swap_apart(blocks):
        return [in_hbm(blocks[0])] + [lax.ppermute(blocks[j], "x", turn(j)) for j in range(1, G)]

    with jax.named_scope("store"):
        split = split_store(cached_past_pairs.reshape(held * piece, 2 * HW), 1)
        pieces = swap(split[0], "x")

    with jax.named_scope("queries"):
        hidden, query = modulate(
            patch_activation_tensor.reshape(patches, depth),
            conditioning_affine.reshape(2, depth),
            entry_projection_matrix,
            softmax_sharpness,
            recalled_picture_holder.reshape(TOPM),
            recalled_picture_position.reshape(TOPM),
            held,
            1,
            after=split,
        )
        here = swap(query[0], "x")

    with jax.named_scope("store"):
        joined = join_pieces(pieces, held, after=hidden)
        above = lax.ppermute(joined, "y", turn(-1))
        below = lax.ppermute(joined, "y", turn(1))
        second = lax.ppermute(joined, "zp", other(sides))

        second_above = lax.ppermute(second, "y", turn(-1))
        second_below = lax.ppermute(second, "y", turn(1))

    with jax.named_scope("temporal"):
        parts = temporal_entry(
            hidden, entry_projection_matrix, softmax_sharpness, quarters, after=[in_hbm(joined)]
        )

    with jax.named_scope("queries"):
        here, *_ = lax.optimization_barrier((here, second, above, below, parts))
        beside = lax.ppermute(here, "zq", other(sides))

    with jax.named_scope("own"):
        own = own_attend(
            hidden, entry_projection_matrix, query, after=[in_hbm(parts), above]
        )

    with jax.named_scope("temporal"):
        sent, *_ = lax.optimization_barrier((parts, own, beside))
        sent = swap(sent.reshape((quarters * G,) + parts.shape[2:]), frame)

    with jax.named_scope("store"):
        below, second_above, second_below = lax.optimization_barrier(
            (below, second_above, second_below)
        )
        far = lax.ppermute(below, "y", turn(1))
        second_far = lax.ppermute(second_above, "y", turn(-1))
        near = [joined, second, above, second_above, far, second_far, below, second_below]
        blocks = near + [lax.ppermute(block, "c", other(cores)) for block in near]
        blocks = [in_hbm(block) for block in blocks]

    with jax.named_scope("queries"):
        named = jnp.concatenate([group[:, patches, :TOPM] for group in (beside, here)], axis=0)
        named = named.astype(jnp.int32)
        y = (named // (cores * held) - lax.axis_index("y")) & (rings - 1)
        c = (named // held & (cores - 1)) ^ lax.axis_index("c")
        index = (c * rings + y) * held + (named & (held - 1))

    with jax.named_scope("memory"):
        sum_beside = memory_attend(0, index, beside, blocks, own)
        from_beside = lax.ppermute(sum_beside, "zq", other(sides))

    with jax.named_scope("temporal"):
        timed = temporal_attend(lookback_lengths, sent, after=sum_beside)
        time = swap(timed, frame)

    with jax.named_scope("memory"):
        sum_here = memory_attend(beside.shape[0], index, here, blocks, timed)
        memory = swap_apart(add_partials(x, [in_hbm(sum_here), from_beside]))

    with jax.named_scope("exit"):
        partial = leave_time(time, exit_projection_matrix, after=memory[0])
        attended = leave(x, own, memory, partial, exit_projection_matrix)
    return attended.reshape(1, 1, patches, depth)


def solution(mesh):
    apart = Mesh(mesh.devices.reshape(4, 2, 2, 2, 4), ("y", "c", "zq", "zp", "x"))
    roll, frame = ("y", "c"), ("zq", "zp", "x")
    return jax.shard_map(
        on_device,
        mesh=apart,
        in_specs=(
            P(roll, frame, None, None),
            P(roll, frame, None, None),
            P(),
            P(),
            P(),
            P(roll, frame, None, None),
            P(roll, frame, None, None),
            P(roll, frame, None),
            P(roll),
        ),
        out_specs=P(roll, frame, None, None),
        check_vma=False,
    )
```

```python
import functools

import jax
import jax.numpy as jnp
from jax import lax
from jax.experimental import pallas as pl
from jax.experimental.pallas import tpu as pltpu
from jax.sharding import Mesh
from jax.sharding import PartitionSpec as P

G = 4
C = 128
HW = G * C
TOPM = 6
EPSILON = 1e-06
BF = jnp.bfloat16
F32 = jnp.float32
PAD = 16
VMEM_LIMIT = 28 * 1024 * 1024
ANY = pl.BlockSpec(memory_space=pl.ANY)
HBM = pl.BlockSpec(memory_space=pltpu.HBM)
WHOLE = pl.BlockSpec(memory_space=pltpu.VMEM)
SCALARS = pl.BlockSpec(memory_space=pltpu.SMEM)


def params(**more):
    return pltpu.CompilerParams(vmem_limit_bytes=VMEM_LIMIT, **more)


def cost(flops, bytes_accessed):
    return pl.CostEstimate(
        flops=flops // 16, bytes_accessed=bytes_accessed // 16, transcendentals=0
    )


def in_hbm(array):
    return pltpu.with_memory_space_constraint(array, pltpu.HBM)


def hbm_out(shape, dtype=BF):
    return pltpu.HBM(shape, dtype)


def inverse_rms(values):
    return lax.rsqrt(jnp.mean(values * values, axis=-1, keepdims=True) + EPSILON)


def dot(a, b):
    return jnp.dot(a, b, preferred_element_type=F32)


def dot_t(a, b):
    return lax.dot_general(a, b, (((1,), (1,)), ((), ())), preferred_element_type=F32)


DMA = pltpu.SemaphoreType.DMA
copy = pltpu.make_async_copy


def split_store_kernel(rows_ref, out_hbm, out_ref, sem):
    sends = []
    for h in range(G):
        key = rows_ref[:, h * C : (h + 1) * C].astype(F32)
        out_ref[h, :, :C] = (key * inverse_rms(key)).astype(BF)
        out_ref[h, :, C:] = rows_ref[:, HW + h * C : HW + (h + 1) * C]
        for k in range(out_hbm.shape[0]):
            sends.append(copy(out_ref.at[h], out_hbm.at[k, h], sem.at[k, h]))
            sends[-1].start()
    for send in sends:
        send.wait()


def split_store(rows, copies):
    n = rows.shape[0]
    return pl.pallas_call(
        split_store_kernel,
        in_specs=[WHOLE],
        out_specs=HBM,
        out_shape=hbm_out((copies, G, n, 2 * C)),
        scratch_shapes=[pltpu.VMEM((G, n, 2 * C), BF), DMA((copies, G))],
        compiler_params=params(),
        name="split_store",
        cost_estimate=cost(8 * n * HW, 8 * n * HW),
    )(rows)


def join_pieces_kernel(piece, in_hbm, _, out_hbm, in_ref, wide_ref, joined_ref, out_ref, sem):
    pieces = in_ref.shape[0]
    loads = [copy(in_hbm.at[i], in_ref.at[i], sem.at[i]) for i in range(pieces)]
    for load in loads:
        load.start()
    for i in range(pieces):
        loads[i].wait()
        wide_ref[i] = in_ref[i].astype(F32)
        for m in range(out_ref.shape[0]):
            joined_ref[m, i * piece : (i + 1) * piece, :] = wide_ref[
                i, m * piece : (m + 1) * piece, :
            ]
    out_ref[...] = joined_ref[...].astype(BF)
    send = copy(out_ref, out_hbm, sem.at[0])
    send.start()
    send.wait()


def join_pieces(parts, frames, after):
    pieces, rows, width = parts.shape
    piece = rows // frames
    shape = (frames, pieces * piece, width)
    return pl.pallas_call(
        functools.partial(join_pieces_kernel, piece),
        in_specs=[ANY, ANY],
        out_specs=HBM,
        out_shape=hbm_out(shape),
        scratch_shapes=[
            pltpu.VMEM(parts.shape, BF),
            pltpu.VMEM(parts.shape, F32),
            pltpu.VMEM(shape, F32),
            pltpu.VMEM(shape, BF),
            DMA((pieces,)),
        ],
        compiler_params=params(),
        name="join_pieces",
        cost_estimate=cost(parts.size, 4 * parts.size),
    )(parts, in_hbm(after))


def modulate_kernel(
    held,
    act_hbm, affine_hbm, weight_hbm, sharpness_ref, owner_ref, slot_ref, _, hidden_hbm, query_hbm,
    act_ref, affine_ref, weight_ref, hidden_ref, query_ref,
    load_sem, affine_sem, weight_sem, store_sem, query_sem,
):
    steps, rows, _ = act_ref.shape
    patches = query_ref.shape[1] - PAD
    loads, stores = [], []
    for i in range(steps):
        at = pl.ds(i * rows, rows)
        loads.append(copy(act_hbm.at[at, :], act_ref.at[i], load_sem.at[i]))
        stores.append(copy(hidden_ref.at[i], hidden_hbm.at[at, :], store_sem.at[i]))
    weight_load = copy(weight_hbm.at[:, pl.ds(0, HW)], weight_ref, weight_sem)
    affine_load = copy(affine_hbm, affine_ref, affine_sem)
    affine_load.start()
    loads[0].start()
    weight_load.start()
    row = lax.broadcasted_iota(jnp.int32, (PAD, C), 0)
    column = lax.broadcasted_iota(jnp.int32, (PAD, C), 1)
    tail = jnp.zeros((PAD, C), jnp.int32)
    for j in range(TOPM):
        tail = jnp.where((row == 0) & (column == j), owner_ref[j] * held + slot_ref[j], tail)
    for h in range(G):
        query_ref[h, patches:, :] = tail.astype(F32).astype(BF)
    affine_load.wait()
    for i in range(steps):
        at = slice(i * rows, (i + 1) * rows)
        loads[i].wait()
        if i + 1 < steps:
            loads[i + 1].start()
        act = act_ref[i].astype(F32)
        hidden = act * inverse_rms(act) * (1.0 + affine_ref[0:1, :]) + affine_ref[1:2, :]
        hidden = hidden.astype(BF)
        hidden_ref[i] = hidden
        stores[i].start()
        if i == 0:
            weight_load.wait()
        mapped = dot(hidden, weight_ref[...]).astype(BF).astype(F32)
        for h in range(G):
            one = mapped[:, h * C : (h + 1) * C]
            query_ref[h, at, :] = (
                one * inverse_rms(one) * (sharpness_ref[0, h] / C)
            ).astype(BF)
    sends = [
        copy(query_ref, query_hbm.at[k], query_sem.at[k]) for k in range(query_hbm.shape[0])
    ]
    for send in sends:
        send.start()
    for store in stores + sends:
        store.wait()


def modulate(act, affine, weight, sharpness, owner, slot, held, copies, after):
    patches, depth = act.shape
    steps = 2
    rows = patches // steps
    shape = (G, patches + PAD, C)
    return pl.pallas_call(
        functools.partial(modulate_kernel, held),
        in_specs=[HBM, HBM, HBM, SCALARS, SCALARS, SCALARS, ANY],
        out_specs=[HBM, HBM],
        out_shape=[hbm_out((patches, depth)), hbm_out((copies,) + shape)],
        scratch_shapes=[
            pltpu.VMEM((steps, rows, depth), BF),
            pltpu.VMEM(affine.shape, F32),
            pltpu.VMEM((depth, HW), BF),
            pltpu.VMEM((steps, rows, depth), BF),
            pltpu.VMEM(shape, BF),
            DMA((steps,)),
            DMA,
            DMA,
            DMA((steps,)),
            DMA((copies,)),
        ],
        compiler_params=params(),
        name="modulate",
        cost_estimate=cost(
            2 * patches * depth * HW, 4 * patches * depth + 2 * depth * HW + 2 * patches * HW
        ),
    )(in_hbm(act), in_hbm(affine), in_hbm(weight), sharpness, owner, slot, in_hbm(after))


def temporal_entry_kernel(
    quarters, hidden_hbm, weight_hbm, sharpness_ref, *refs
):
    out_hbm, hidden_ref, weight_ref, out_ref, hidden_sem, weight_sem, store_sem = refs[-7:]
    rows = hidden_ref.shape[0] // quarters
    hidden_load = copy(hidden_hbm, hidden_ref, hidden_sem)
    loads = [
        copy(
            weight_hbm.at[:, pl.ds((3 + part) * HW, HW)], weight_ref.at[part], weight_sem.at[part]
        )
        for part in range(3)
    ]
    hidden_load.start()
    loads[0].start()
    hidden_load.wait()
    stores = []
    for part in range(3):
        loads[part].wait()
        if part < 2:
            loads[part + 1].start()
        mapped = dot(hidden_ref[...], weight_ref[part]).astype(BF)
        for h in range(G):
            done = mapped[:, h * C : (h + 1) * C]
            if part < 2:
                one = done.astype(F32)
                one = one * inverse_rms(one)
                if part == 0:
                    one = one * (sharpness_ref[1, h] / C)
                done = one.astype(BF)
            for z in range(quarters):
                out_ref[part, z, h] = done[z * rows : (z + 1) * rows, :]
        stores.append(copy(out_ref.at[part], out_hbm.at[:, :, part], store_sem.at[part]))
        stores[-1].start()
    for store in stores:
        store.wait()


def temporal_entry(hidden, weight, sharpness, quarters, after):
    patches, depth = hidden.shape
    rows = patches // quarters
    return pl.pallas_call(
        functools.partial(temporal_entry_kernel, quarters),
        in_specs=[HBM, HBM, SCALARS] + [ANY] * len(after),
        out_specs=HBM,
        out_shape=hbm_out((quarters, G, 3, rows, C)),
        scratch_shapes=[
            pltpu.VMEM((patches, depth), BF),
            pltpu.VMEM((3, depth, HW), BF),
            pltpu.VMEM((3, quarters, G, rows, C), BF),
            DMA,
            DMA((3,)),
            DMA((3,)),
        ],
        compiler_params=params(),
        name="temporal_entry",
        cost_estimate=cost(
            6 * patches * depth * HW, 2 * patches * depth + 6 * depth * HW + 6 * patches * HW
        ),
    )(in_hbm(hidden), in_hbm(weight), sharpness, *after)


def temporal_attend_kernel(length_ref, in_hbm_ref, _, out_hbm, in_ref, out_ref, sem):
    frames, _, rows, _ = in_ref.shape
    group = 16
    size = frames * group
    load = copy(in_hbm_ref, in_ref, sem)
    load.start()
    length = length_ref[0]
    row = lax.broadcasted_iota(jnp.int32, (size, size), 0)
    column = lax.broadcasted_iota(jnp.int32, (size, size), 1)
    target, source = row // group, column // group
    keep = (row % group == column % group) & (source <= target) & (source > target - length)
    load.wait()
    for g in range(rows // group):
        at = slice(g * group, (g + 1) * group)
        query = in_ref[:, 0, at, :].reshape(size, C)
        key = in_ref[:, 1, at, :].reshape(size, C)
        value = in_ref[:, 2, at, :].reshape(size, C)
        weights = jnp.where(keep, jnp.exp(dot_t(query, key)), 0.0)
        shares = weights / jnp.sum(weights, axis=-1, keepdims=True)
        result = dot(shares.astype(BF), value).astype(BF)
        out_ref[:, at, :] = result.reshape(frames, group, C)
    store = copy(out_ref, out_hbm, sem)
    store.start()
    store.wait()


def temporal_attend(length, parts, after):
    frames, _, rows, _ = parts.shape
    shape = (frames, rows, C)
    return pl.pallas_call(
        temporal_attend_kernel,
        in_specs=[SCALARS, ANY, ANY],
        out_specs=HBM,
        out_shape=hbm_out(shape),
        scratch_shapes=[pltpu.VMEM(parts.shape, BF), pltpu.VMEM(shape, BF), DMA],
        compiler_params=params(),
        name="temporal_attend",
        cost_estimate=cost(4 * frames * rows * 256 * C, 8 * frames * rows * C),
    )(length, parts, in_hbm(after))


LINE = 96
CHUNK = 3 * LINE


def halves(denominators):
    high = denominators.astype(BF).astype(F32)
    return jnp.concatenate([high, denominators - high], axis=0).astype(BF)


def attend_rows(query, keys, both, out_ref):
    patches = out_ref.shape[0] - PAD
    row = lax.broadcasted_iota(jnp.int32, (LINE, C), 0)
    column = lax.broadcasted_iota(jnp.int32, (LINE, C), 1)
    lines = []
    for start in range(0, patches, CHUNK):
        at = slice(start, start + CHUNK)
        weights = jnp.exp(dot_t(query(at), keys)).astype(BF)
        result = dot(weights, both)
        out_ref[at, :] = result[:, :C].astype(BF)
        for j in range(0, CHUNK, LINE):
            diagonal = jnp.where(row == column, result[j : j + LINE, C:], 0.0)
            lines.append(jnp.sum(diagonal, axis=0, keepdims=True))
    lines.append(jnp.zeros((8 - len(lines), C), F32))
    out_ref[patches:, :] = halves(jnp.concatenate(lines, axis=0))


def with_ones(values):
    return jnp.concatenate([values, jnp.ones(values.shape, BF)], axis=1)


def own_attend_kernel(
    hidden_hbm, weight_hbm, query_hbm, *refs
):
    out_hbm, hidden_ref, weight_ref, query_ref, out_ref = refs[-9:-4]
    hidden_sem, weight_sem, query_sem, store_sem = refs[-4:]
    hidden_load = copy(hidden_hbm, hidden_ref, hidden_sem)
    query_load = copy(query_hbm.at[0], query_ref, query_sem)
    loads = [
        copy(
            weight_hbm.at[:, pl.ds((1 + part) * HW, HW)], weight_ref.at[part], weight_sem.at[part]
        )
        for part in range(2)
    ]
    hidden_load.start()
    loads[0].start()
    hidden_load.wait()
    loads[0].wait()
    loads[1].start()
    query_load.start()
    keys = dot(hidden_ref[...], weight_ref[0]).astype(BF)
    loads[1].wait()
    values = dot(hidden_ref[...], weight_ref[1]).astype(BF)
    query_load.wait()
    stores = []
    for h in range(G):
        key = keys[:, h * C : (h + 1) * C].astype(F32)
        key = (key * inverse_rms(key)).astype(BF)
        both = with_ones(values[:, h * C : (h + 1) * C])
        attend_rows(lambda at, h=h: query_ref[h, at, :], key, both, out_ref.at[h])
        stores.append(copy(out_ref.at[h], out_hbm.at[h], store_sem.at[h]))
        stores[-1].start()
    for store in stores:
        store.wait()


def own_attend(hidden, weight, query, after):
    patches, depth = hidden.shape
    shape = query.shape[1:]
    return pl.pallas_call(
        own_attend_kernel,
        in_specs=[HBM, HBM, HBM] + [ANY] * len(after),
        out_specs=HBM,
        out_shape=hbm_out(shape),
        scratch_shapes=[
            pltpu.VMEM((patches, depth), BF),
            pltpu.VMEM((2, depth, HW), BF),
            pltpu.VMEM(shape, BF),
            pltpu.VMEM(shape, BF),
            DMA,
            DMA((2,)),
            DMA,
            DMA((G,)),
        ],
        compiler_params=params(),
        name="own_attend",
        cost_estimate=cost(
            4 * patches * depth * HW + 6 * patches * patches * HW,
            2 * patches * depth + 4 * depth * HW + 10 * patches * HW,
        ),
    )(in_hbm(hidden), in_hbm(weight), in_hbm(query), *after)


def memory_attend_kernel(count, first, index_ref, query_hbm, *refs):
    blocks = refs[:count]
    out_hbm, query_ref, store_ref, out_ref, query_sem, block_sem, store_sem = refs[count + 1 :]
    frames = query_ref.shape[0]
    query_load = copy(query_hbm, query_ref, query_sem)
    query_load.start()

    def fetch(t, carry):
        i, j = t // TOPM, lax.rem(t, TOPM)
        wanted = index_ref[first + i, j]
        start = 0
        for b in range(count // 2):
            held = blocks[2 * b].shape[0]

            @pl.when((wanted >= start) & (wanted < start + held))
            def _(b=b, start=start):
                for part in range(2):
                    block = blocks[2 * b + part].at[wanted - start]
                    copy(block, store_ref.at[i, j, part], block_sem.at[i]).start()

            start += held
        return carry

    lax.fori_loop(0, frames * TOPM, fetch, 0)
    query_load.wait()
    stores = []
    for i in range(frames):
        copy(store_ref.at[i], store_ref.at[i], block_sem.at[i]).wait()
        both = [store_ref[i, j, part] for j in range(TOPM) for part in range(2)]
        keys = jnp.concatenate([block[:, :C] for block in both], axis=0)
        values = jnp.concatenate([block[:, C:] for block in both], axis=0)
        attend_rows(
            lambda at, i=i: query_ref[i, at, :], keys, with_ones(values), out_ref.at[i]
        )
        stores.append(copy(out_ref.at[i], out_hbm.at[i], store_sem.at[i]))
        stores[-1].start()
    for store in stores:
        store.wait()


def memory_attend(first, index, query, blocks, after):
    count = len(blocks)
    frames, rows, _ = query.shape
    _, part, width = blocks[0].shape
    shape = (frames, rows, C)
    return pl.pallas_call(
        functools.partial(memory_attend_kernel, count, first),
        in_specs=[SCALARS] + [ANY] * (count + 2),
        out_specs=HBM,
        out_shape=hbm_out(shape),
        scratch_shapes=[
            pltpu.VMEM(shape, BF),
            pltpu.VMEM((frames, TOPM, 2, part, width), BF),
            pltpu.VMEM(shape, BF),
            DMA,
            DMA((frames,)),
            DMA((frames,)),
        ],
        compiler_params=params(),
        name="memory_attend",
        cost_estimate=cost(
            16 * frames * rows * TOPM * part * C,
            4 * frames * rows * C + 2 * frames * TOPM * part * width,
        ),
    )(index, in_hbm(query), *blocks, in_hbm(after))


def add_partials_kernel(count, x_ref, *refs):
    ins, outs = refs[:count], refs[count : count + G]
    parts_ref, out_ref, load_sem, store_sem = refs[count + G :]
    patches = out_ref.shape[1] - PAD
    loads = []
    for j in range(G):
        frame = lax.rem(x_ref[0] + j, G)
        loads.append(
            [copy(ref.at[frame], parts_ref.at[k, j], load_sem.at[k, j]) for k, ref in enumerate(ins)]
        )
    for of_frame in loads:
        for load in of_frame:
            load.start()
    stores = []
    for j in range(G):
        for load in loads[j]:
            load.wait()
        total = parts_ref[0, j].astype(F32)
        for k in range(1, count):
            total = total + parts_ref[k, j].astype(F32)
        out_ref[j, :patches, :] = total[:patches].astype(BF)
        out_ref[j, patches:, :] = halves(total[patches : patches + 8] + total[patches + 8 :])
        stores.append(copy(out_ref.at[j], outs[j], store_sem.at[j]))
        stores[-1].start()
    for store in stores:
        store.wait()


def add_partials(x, parts):
    shape = parts[0].shape
    return pl.pallas_call(
        functools.partial(add_partials_kernel, len(parts)),
        in_specs=[SCALARS] + [ANY] * len(parts),
        out_specs=[HBM] * G,
        out_shape=[hbm_out(shape[1:])] * G,
        scratch_shapes=[
            pltpu.VMEM((len(parts),) + shape, BF),
            pltpu.VMEM(shape, BF),
            DMA((len(parts), G)),
            DMA((G,)),
        ],
        compiler_params=params(),
        name="add_partials",
        cost_estimate=cost(4 * parts[0].size, 8 * parts[0].size),
    )(x, *parts)


STEPS = 4


def leave_time_kernel(
    time_hbm, weight_hbm, _, out_hbm,
    time_ref, combined_ref, weight_ref, out_ref, time_sem, weight_sem, store_sem,
):
    quarters = time_ref.shape[0] // G
    rows = time_ref.shape[1]
    depth, width = weight_ref.shape[1:]
    time_load = copy(time_hbm, time_ref, time_sem)
    time_load.start()
    loads, stores = [], []
    for i in range(STEPS):
        at = pl.ds(i * width, width)
        loads.append(
            copy(weight_hbm.at[pl.ds(HW, depth), at], weight_ref.at[i], weight_sem.at[i])
        )
        stores.append(copy(out_ref.at[i], out_hbm.at[i], store_sem.at[i]))
        loads[i].start()
    time_load.wait()
    for h in range(G):
        for z in range(quarters):
            combined_ref[z * rows : (z + 1) * rows, h * C : (h + 1) * C] = time_ref[z * G + h]
    for i in range(STEPS):
        loads[i].wait()
        out_ref[i] = dot(combined_ref[...], weight_ref[i])
        stores[i].start()
    for store in stores:
        store.wait()


def leave_time(time, weight, after):
    patches = time.shape[0] // G * time.shape[1]
    depth, width = weight.shape
    step = width // STEPS
    shape = (STEPS, patches, step)
    return pl.pallas_call(
        leave_time_kernel,
        in_specs=[ANY, HBM, ANY],
        out_specs=HBM,
        out_shape=hbm_out(shape, F32),
        scratch_shapes=[
            pltpu.VMEM(time.shape, BF),
            pltpu.VMEM((patches, depth - HW), BF),
            pltpu.VMEM((STEPS, depth - HW, step), BF),
            pltpu.VMEM(shape, F32),
            DMA,
            DMA((STEPS,)),
            DMA((STEPS,)),
        ],
        compiler_params=params(),
        name="leave_time",
        cost_estimate=cost(
            patches * depth * width, depth * width + 4 * patches * width + 2 * time.size
        ),
    )(time, in_hbm(weight), in_hbm(after))


def leave_kernel(
    x_ref, own_hbm, memory_0, memory_1, memory_2, memory_3, partial_hbm, weight_hbm, out_hbm,
    own_ref, memory_ref, combined_ref, partial_ref, weight_ref, out_ref,
    own_sem, memory_sem, partial_sem, weight_sem, store_sem,
):
    patches = own_ref.shape[1] - PAD
    width = weight_ref.shape[2]
    heads = [lax.rem(x_ref[0] + G - j, G) for j in range(G)]
    memories = (memory_0, memory_1, memory_2, memory_3)
    own_loads = [copy(own_hbm.at[heads[j]], own_ref.at[j], own_sem.at[j]) for j in range(G)]
    memory_loads = [copy(memories[j], memory_ref.at[j], memory_sem.at[j]) for j in range(G)]
    loads, partial_loads, stores = [], [], []
    for i in range(STEPS):
        at = pl.ds(i * width, width)
        loads.append(copy(weight_hbm.at[pl.ds(0, HW), at], weight_ref.at[i], weight_sem.at[i]))
        partial_loads.append(copy(partial_hbm.at[i], partial_ref.at[i], partial_sem.at[i]))
        stores.append(copy(out_ref.at[i], out_hbm.at[:, at], store_sem.at[i]))
    for load in own_loads + memory_loads:
        load.start()
    for i in range(STEPS):
        loads[i].start()
        partial_loads[i].start()
    row = lax.broadcasted_iota(jnp.int32, (LINE, C), 0)
    column = lax.broadcasted_iota(jnp.int32, (LINE, C), 1)
    for h in range(G):
        own_loads[h].wait()
        memory_loads[h].wait()
        column_at = pl.ds(pl.multiple_of(heads[h] * C, C), C)
        tail = own_ref[h, patches:, :].astype(F32) + memory_ref[h, patches:, :].astype(F32)
        denominators = tail[:8] + tail[8:]
        for j in range(patches // LINE):
            at = slice(j * LINE, (j + 1) * LINE)
            line = jnp.broadcast_to(denominators[j : j + 1, :], (LINE, C))
            total = jnp.sum(jnp.where(row == column, line, 0.0), axis=1, keepdims=True)
            top = own_ref[h, at, :].astype(F32) + memory_ref[h, at, :].astype(F32)
            combined_ref[at, column_at] = (top / total).astype(BF)
    for i in range(STEPS):
        loads[i].wait()
        partial_loads[i].wait()
        out_ref[i] = (dot(combined_ref[...], weight_ref[i]) + partial_ref[i]).astype(BF)
        stores[i].start()
    for store in stores:
        store.wait()


def leave(x, own, memory, partial, weight):
    patches = own.shape[1] - PAD
    width = weight.shape[1]
    step = width // STEPS
    return pl.pallas_call(
        leave_kernel,
        in_specs=[SCALARS, HBM] + [ANY] * G + [HBM, HBM],
        out_specs=HBM,
        out_shape=hbm_out((patches, width)),
        scratch_shapes=[
            pltpu.VMEM(own.shape, BF),
            pltpu.VMEM(own.shape, BF),
            pltpu.VMEM((patches, HW), BF),
            pltpu.VMEM(partial.shape, F32),
            pltpu.VMEM((STEPS, HW, step), BF),
            pltpu.VMEM((STEPS, patches, step), BF),
            DMA((G,)),
            DMA((G,)),
            DMA((STEPS,)),
            DMA((STEPS,)),
            DMA((STEPS,)),
        ],
        compiler_params=params(),
        name="leave",
        cost_estimate=cost(
            2 * patches * HW * width, 2 * HW * width + 6 * patches * width + 4 * patches * HW
        ),
    )(x, in_hbm(own), *memory, in_hbm(partial), in_hbm(weight))


def on_device(
    patch_activation_tensor,
    conditioning_affine,
    entry_projection_matrix,
    exit_projection_matrix,
    softmax_sharpness,
    cached_past_pairs,
    recalled_picture_holder,
    recalled_picture_position,
    lookback_lengths,
):
    frame = ("zq", "zp", "x")
    rings, sides = lax.axis_size("y"), lax.axis_size("zq")
    quarters = lax.axis_size("zp") * sides
    patches, depth = patch_activation_tensor.shape[2:]
    held, piece = cached_past_pairs.shape[:2]
    cores = lax.axis_size("c")
    x = lax.axis_index("x").astype(jnp.int32).reshape(1)

    def turn(step):
        return [(s, (s + step) % rings) for s in range(rings)]

    def other(size):
        return [(s, size - 1 - s) for s in range(size)]

    def swap(blocks, axes):
        return lax.all_to_all(blocks, axes, split_axis=0, concat_axis=0, tiled=True)

    def swap_apart(blocks):
        return [in_hbm(blocks[0])] + [lax.ppermute(blocks[j], "x", turn(j)) for j in range(1, G)]

    with jax.named_scope("store"):
        split = split_store(cached_past_pairs.reshape(held * piece, 2 * HW), 1)
        pieces = swap(split[0], "x")

    with jax.named_scope("queries"):
        hidden, query = modulate(
            patch_activation_tensor.reshape(patches, depth),
            conditioning_affine.reshape(2, depth),
            entry_projection_matrix,
            softmax_sharpness,
            recalled_picture_holder.reshape(TOPM),
            recalled_picture_position.reshape(TOPM),
            held,
            1,
            after=split,
        )
        here = swap(query[0], "x")

    with jax.named_scope("store"):
        joined = join_pieces(pieces, held, after=hidden)
        above = lax.ppermute(joined, "y", turn(-1))
        below = lax.ppermute(joined, "y", turn(1))
        second = lax.ppermute(joined, "zp", other(sides))

        second_above = lax.ppermute(second, "y", turn(-1))
        second_below = lax.ppermute(second, "y", turn(1))

    with jax.named_scope("temporal"):
        parts = temporal_entry(
            hidden, entry_projection_matrix, softmax_sharpness, quarters, after=[in_hbm(joined)]
        )

    with jax.named_scope("queries"):
        here, second, above, below, parts = lax.optimization_barrier(
            (here, second, above, below, parts)
        )
        half = held // 2
        far_first = lax.ppermute(above[:half], "y", turn(-1))
        far_last = lax.ppermute(below[half:], "y", turn(1))
        beside = lax.ppermute(here, "zq", other(sides))

    with jax.named_scope("own"):
        own = own_attend(
            hidden, entry_projection_matrix, query, after=[in_hbm(parts), above]
        )

    with jax.named_scope("temporal"):
        sent, *_ = lax.optimization_barrier((parts, own, beside, far_first, far_last))
        sent = swap(sent.reshape((quarters * G,) + parts.shape[2:]), frame)

    with jax.named_scope("store"):
        second_above, second_below = lax.optimization_barrier((second_above, second_below))
        near = [joined, second, above, second_above]
        near += [far_first, lax.ppermute(second_above[:half], "y", turn(-1))]
        near += [far_last, lax.ppermute(second_below[half:], "y", turn(1))]
        near += [below, second_below]
        blocks = near + [lax.ppermute(block, "c", other(cores)) for block in near]
        blocks = [in_hbm(block) for block in blocks]

    with jax.named_scope("queries"):
        named = jnp.concatenate([group[:, patches, :TOPM] for group in (beside, here)], axis=0)
        named = named.astype(jnp.int32)
        y = (named // (cores * held) - lax.axis_index("y")) & (rings - 1)
        c = (named // held & (cores - 1)) ^ lax.axis_index("c")
        index = (c * rings + y) * held + (named & (held - 1))

    with jax.named_scope("memory"):
        sum_beside = memory_attend(0, index, beside, blocks, own)
        from_beside = lax.ppermute(sum_beside, "zq", other(sides))

    with jax.named_scope("temporal"):
        timed = temporal_attend(lookback_lengths, sent, after=sum_beside)
        time = swap(timed, frame)

    with jax.named_scope("memory"):
        sum_here = memory_attend(beside.shape[0], index, here, blocks, timed)
        memory = swap_apart(add_partials(x, [in_hbm(sum_here), from_beside]))

    with jax.named_scope("exit"):
        partial = leave_time(time, exit_projection_matrix, after=memory[0])
        attended = leave(x, own, memory, partial, exit_projection_matrix)
    return attended.reshape(1, 1, patches, depth)


def solution(mesh):
    apart = Mesh(mesh.devices.reshape(4, 2, 2, 2, 4), ("y", "c", "zq", "zp", "x"))
    roll, frame = ("y", "c"), ("zq", "zp", "x")
    return jax.shard_map(
        on_device,
        mesh=apart,
        in_specs=(
            P(roll, frame, None, None),
            P(roll, frame, None, None),
            P(),
            P(),
            P(),
            P(roll, frame, None, None),
            P(roll, frame, None, None),
            P(roll, frame, None),
            P(roll),
        ),
        out_specs=P(roll, frame, None, None),
        check_vma=False,
    )
```
